32 devices in a mesh: dp: 4 (over z), seq: 8 (over y, x, core).
Axes of the slice: x: 2, y: 2, z: 4, core: 2. Of those that a mesh axis runs over, the one named last changes fastest.
Arguments:
- block_input: bfloat16 [8, 1024, 1536], P('dp', 'seq'), may hold values from -6 to 6
- cotangent: bfloat16 [8, 1024, 1536], P('dp', 'seq'), may hold values from -6 to 6
- lengths: int32 [8], P('dp'), may hold values from 256 to 1024, as said below
- in_weight: bfloat16 [1536, 6448], P(('dp', 'seq')), may hold values from -0.15625 to 0.15625
- out_weight: bfloat16 [3072, 1536], P(('dp', 'seq')), may hold values from -0.109375 to 0.109375
- norm_gain: bfloat16 [1536], P(('dp', 'seq')), may hold values from 0.5 to 1.5
- gate_gain: bfloat16 [3072], P(('dp', 'seq')), may hold values from 0.5 to 1.5
- conv_weight: bfloat16 [4, 3328], P(None, ('dp', 'seq')), may hold values from -3 to 3
- conv_bias: bfloat16 [3328], P(('dp', 'seq')), may hold values from -0.5 to 0.5
- dt_bias: float32 [48], replicated, may hold values from -12 to -3
- a_log: float32 [48], replicated, may hold values from -0.7 to 0.7
- d_skip: float32 [48], replicated, may hold values from 0.5 to 1.5
Outputs:
- output: bfloat16 [8, 1024, 1536], P('dp', 'seq')
- input_grad: bfloat16 [8, 1024, 1536], P('dp', 'seq')
- in_weight_grad: float32 [1536, 6448], P(('dp', 'seq'))
- out_weight_grad: float32 [3072, 1536], P(('dp', 'seq'))
- norm_gain_grad: float32 [1536], P(('dp', 'seq'))
- gate_gain_grad: float32 [3072], P(('dp', 'seq'))
- conv_weight_grad: float32 [4, 3328], P(None, ('dp', 'seq'))
- conv_bias_grad: float32 [3328], P(('dp', 'seq'))
- dt_bias_grad: float32 [48], replicated
- a_log_grad: float32 [48], replicated
- d_skip_grad: float32 [48], replicated
The draws below stay inside these ranges and needn't reach their ends.
Inputs may be any that keep to these rules, and one draw needn't show every extreme that they name: `lengths`: in every aligned block of 2 slots one or more slots have length 1024.
All inputs are finite; a program needn't handle non-finite values.
Results may differ from the reference program's by a relative error of at most 0.007.
Values may be sent and summed in bfloat16 or wider, within the bound.
A program may use at most 448 MiB of HBM per device.

```python
import math
import jax
import jax.numpy as jnp
from jax import lax

D = 1536
HEADS = 48
HEAD_DIM = 64
STATE = 128
KW = 4
INNER = 3072
CONV_CH = 3328
PROJ = 6448
LEN = 1024
SLOTS_DEV = 2
SLOTS = 8


def draw_lengths(key, part):
    key = jax.random.fold_in(key, 5)
    span_key, pick_key = jax.random.split(key)
    drawn = jax.random.randint(span_key, (SLOTS,), LEN // 4, LEN + 1)
    chosen = jax.random.randint(pick_key, (SLOTS // SLOTS_DEV,), 0, SLOTS_DEV)
    within = jnp.arange(SLOTS) % SLOTS_DEV
    full_slot = within == jnp.repeat(chosen, SLOTS_DEV)
    return jnp.where(full_slot, LEN, drawn).astype(jnp.int32)


def draw_dt_bias(key, part):
    key = jax.random.fold_in(key, 11)
    pick_key, fast_key, slow_key = jax.random.split(key, 3)
    share = 0.5
    quick = jax.random.uniform(pick_key, (HEADS,)) < share
    fast_rate = jnp.exp(jax.random.uniform(fast_key, (HEADS,), minval=math.log(1.0 / 50.0), maxval=math.log(1.0 / 25.0)))
    slow_rate = jnp.exp(jax.random.uniform(slow_key, (HEADS,), minval=math.log(0.1), maxval=0.0)) / LEN
    chosen_rate = jnp.where(quick, fast_rate, slow_rate)
    return (jnp.log(chosen_rate) - 0.5).astype(jnp.float32)


def levels(own_key, dims, shards, least, largest):
    def one(position, blocks):
        draws = jax.random.uniform(jax.random.fold_in(jax.random.fold_in(own_key, 6), position), (blocks,), jnp.float32, least / len(shards), largest / len(shards))
        return jnp.repeat(jnp.exp(draws), dims[position] // blocks).reshape((-1,) + (1,) * (len(dims) - position - 1))

    level = one(*shards[0])
    for cut in shards[1:]:
        level = level * one(*cut)
    return level


def gaussian(key, extent, spread, bound, shards=(), held_as=jnp.bfloat16):
    factor_of = levels(key, extent, shards, -0.22, 0.18) if shards else 1.0
    entries = jax.random.normal(key, extent, jnp.float32) * spread * factor_of
    return jnp.minimum(jnp.maximum(entries, -bound), bound).astype(held_as)


def setup_inputs(seed: int = 0) -> dict:
    seeds = jax.random.split(jax.random.key(seed), 13)
    return {
        "block_input": gaussian(seeds[0], (SLOTS, LEN, D), 1.0, 6.0, ((0, 4), (1, 8))),
        "cotangent": gaussian(seeds[1], (SLOTS, LEN, D), 1.0, 6.0, ((0, 4), (1, 8))),
        "lengths": draw_lengths(jax.random.fold_in(seeds[12], 71), 0),
        "in_weight": gaussian(seeds[3], (D, PROJ), D ** -0.5, 0.15625, ((0, 32),)),
        "out_weight": gaussian(seeds[4], (INNER, D), INNER ** -0.5, 0.109375, ((0, 32),)),
        "norm_gain": jnp.clip(1.0 + 0.1 * jax.random.normal(seeds[5], (D,), jnp.float32), 0.5, 1.5).astype(jnp.bfloat16),
        "gate_gain": jnp.clip(1.0 + 0.1 * jax.random.normal(seeds[6], (INNER,), jnp.float32), 0.5, 1.5).astype(jnp.bfloat16),
        "conv_weight": gaussian(seeds[7], (KW, CONV_CH), KW ** -0.5, 3.0, ((1, 32),)),
        "conv_bias": jnp.clip(jax.random.uniform(seeds[8], (CONV_CH,), jnp.float32, -0.5, 0.5) * levels(seeds[8], (CONV_CH,), ((0, 32),), -0.4, 0.0), -0.5, 0.5).astype(jnp.bfloat16),
        "dt_bias": draw_dt_bias(jax.random.fold_in(seeds[12], 71), 0),
        "a_log": jnp.clip(jax.random.uniform(seeds[10], (HEADS,), jnp.float32, -0.7, 0.7), -0.7, 0.7),
        "d_skip": jnp.clip(jax.random.uniform(seeds[11], (HEADS,), jnp.float32, 0.5, 1.5), 0.5, 1.5),
    }


EPS = 1e-05
HIGH = lax.Precision.HIGHEST

@jax.custom_vjp
def low(v):
    return lax.optimization_barrier(v.astype(jnp.bfloat16)).astype(jnp.float32)

@jax.custom_vjp
def low_back(v):
    return v

def low_keep(v):
    return (low(v), None)

def low_pass(kept, grad):
    return (grad,)

def back_keep(v):
    return (v, None)

def back_low(kept, grad):
    return (low(grad),)
low.defvjp(low_keep, low_pass)
low_back.defvjp(back_keep, back_low)

def scan_block(state_in, block_data):
    x_heads, b_rows, c_rows, dt_vals, log_step = block_data
    log_cum = jnp.cumsum(log_step, axis=0)
    log_tot = log_cum[-1]
    spots = jnp.arange(log_cum.shape[0])
    causal = (spots[:, None] >= spots[None, :])[None]
    cum_heads = log_cum.T
    gap_vals = jnp.where(causal, cum_heads[:, :, None] - cum_heads[:, None, :], 0.0)
    decay_mat = jnp.where(causal, jnp.exp(gap_vals), 0.0)
    cb_mat = jnp.dot(c_rows, b_rows.T, precision=HIGH, preferred_element_type=jnp.float32)
    mixing = decay_mat * cb_mat[None] * dt_vals.T[:, None, :]
    y_intra = jnp.einsum('htu,uhp->thp', mixing, x_heads, precision=HIGH)
    state_read = jnp.einsum('tn,hpn->thp', c_rows, state_in, precision=HIGH)
    y_block = y_intra + jnp.exp(log_cum)[:, :, None] * state_read
    weights_in = jnp.exp(log_tot[None] - log_cum) * dt_vals
    state_out = jnp.exp(log_tot)[:, None, None] * state_in + jnp.einsum('thp,tn->hpn', weights_in[:, :, None] * x_heads, b_rows, precision=HIGH)
    return (state_out, y_block)

def mixer_block(block_in, in_weight, out_weight, norm_gain, gate_gain, conv_weight, conv_bias, dt_bias, a_log, d_skip):
    inv_rms = lax.rsqrt(lax.optimization_barrier(jnp.mean(block_in * block_in, axis=-1, keepdims=True)) + EPS)
    normed = low(block_in * inv_rms * norm_gain)
    projected = low_back(jnp.dot(normed, in_weight, precision=HIGH, preferred_element_type=jnp.float32))
    gate_part = projected[:, :INNER]
    conv_in = projected[:, INNER:INNER + CONV_CH]
    dt_raw = projected[:, INNER + CONV_CH:]
    padded = jnp.pad(conv_in, ((KW - 1, 0), (0, 0)))
    pre_act = conv_bias + sum((conv_weight[tap_index] * padded[tap_index:tap_index + LEN] for tap_index in range(KW)))
    activated = jax.nn.silu(pre_act)
    x_heads = activated[:, :INNER].reshape(LEN, HEADS, HEAD_DIM)
    b_rows = activated[:, INNER:INNER + STATE]
    c_rows = activated[:, INNER + STATE:]
    dt_vals = jax.nn.softplus(dt_raw + dt_bias)
    log_step = -jnp.exp(a_log) * dt_vals
    block_len = math.gcd(LEN, 256)
    block_count = LEN // block_len

    def split_blocks(values):
        return values.reshape((block_count, block_len) + values.shape[1:])
    start_state = jnp.zeros((HEADS, HEAD_DIM, STATE), jnp.float32)
    _, y_blocks = lax.scan(jax.checkpoint(scan_block), start_state, (split_blocks(x_heads), split_blocks(b_rows), split_blocks(c_rows), split_blocks(dt_vals), split_blocks(log_step)))
    y_heads = y_blocks.reshape(LEN, HEADS, HEAD_DIM) + d_skip[:, None] * x_heads
    gated_out = y_heads.reshape(LEN, INNER) * jax.nn.silu(gate_part)
    inv_gate = lax.rsqrt(lax.optimization_barrier(jnp.mean(gated_out * gated_out, axis=-1, keepdims=True)) + EPS)
    gate_normed = low(gated_out * inv_gate * gate_gain)
    return block_in + jnp.dot(gate_normed, out_weight, precision=HIGH, preferred_element_type=jnp.float32)

def add_pair(first, second):
    return first + second

def reference(block_input, cotangent, lengths, in_weight, out_weight, norm_gain, gate_gain, conv_weight, conv_bias, dt_bias, a_log, d_skip):
    params = (in_weight.astype(jnp.float32), out_weight.astype(jnp.float32), norm_gain.astype(jnp.float32), gate_gain.astype(jnp.float32), conv_weight.astype(jnp.float32), conv_bias.astype(jnp.float32), dt_bias, a_log, d_skip)
    positions = jnp.arange(LEN, dtype=jnp.int32)

    def one_slot(totals, item):
        slot_in, slot_cot, slot_len = item
        live = (positions < slot_len).astype(jnp.float32)[:, None]
        result, pull = jax.vjp(mixer_block, slot_in.astype(jnp.float32), *params)
        grads = pull(slot_cot.astype(jnp.float32) * live)
        totals = jax.tree.map(add_pair, totals, tuple(grads[1:]))
        return (totals, (result.astype(jnp.bfloat16), grads[0].astype(jnp.bfloat16)))
    zero_sums = tuple((jnp.zeros_like(param) for param in params))
    totals, (outputs, input_grads) = lax.scan(one_slot, zero_sums, (block_input, cotangent, lengths))
    return (outputs, input_grads, totals[0], totals[1], totals[2], totals[3], totals[4], totals[5], totals[6], totals[7], totals[8])
```

```python
import functools

import jax
import jax.numpy as jnp
from jax import lax
from jax.experimental import pallas as pl
from jax.experimental.pallas import tpu as pltpu
from jax.sharding import PartitionSpec as P

SLOTS_MB = 1


EPS = 1e-05
HIGH = lax.Precision.HIGHEST


def from_behind(value, axis, steps):
    count = lax.axis_size(axis)
    leading, last = (max(0, -steps), min(count, count - steps))
    return lax.ppermute(value, axis, [(source, source + steps) for source in range(leading, last)])


def carried_in(value, axis, join, neutral, backward):
    count = lax.axis_size(axis)
    place = lax.axis_index(axis)
    ahead = count - 1 - place if backward else place
    gathered = jax.tree.map(
        lambda a, kind: lax.all_gather(a.astype(kind), axis),
        value,
        jax.tree.map(lambda a: jnp.bfloat16 if a.dtype == jnp.float32 else a.dtype, value),
    )
    state = jax.tree.map(lambda a, e: jnp.zeros_like(a) + jnp.asarray(e, a.dtype), value, neutral)

    def one(lap, state):
        source = count - 1 - lap if backward else lap
        return join(
            state,
            jax.tree.map(
                lambda a, own: lax.dynamic_index_in_dim(a, source, 0, False).astype(own.dtype),
                gathered,
                value,
            ),
        )

    return lax.fori_loop(0, ahead, one, state)


def as_sent(value):

    def short(part):
        return part.astype(jnp.bfloat16) if part.dtype == jnp.float32 else part

    return jax.tree.map(short, value)


def link_states(earlier, later):
    return (earlier[0] * later[0], later[0][:, :, None, None] * earlier[1] + later[1])


def silu_slope(values):
    sigma = jax.nn.sigmoid(values)
    return sigma * (1.0 + values * (1.0 - sigma))


def rows_product(left, right):
    return lax.dot_general(
        left, right, (((0,), (0,)), ((), ())), preferred_element_type=jnp.float32
    )


def cols_product(left, right):
    return lax.dot_general(
        left, right, (((1,), (1,)), ((), ())), preferred_element_type=jnp.float32
    )


def add_pair(first, second):
    return first + second


def first_total(stacked):
    return jnp.sum(stacked, axis=0)


def owner_sums(grads):
    lifted = tuple((grad[None] for grad in grads))
    by_data = (
        lax.all_to_all(lifted[0], "dp", split_axis=1, concat_axis=0, tiled=True),
        lax.all_to_all(lifted[1], "dp", split_axis=1, concat_axis=0, tiled=True),
        lax.all_to_all(lifted[2], "dp", split_axis=1, concat_axis=0, tiled=True),
        lax.all_to_all(lifted[3], "dp", split_axis=1, concat_axis=0, tiled=True),
        lax.all_to_all(lifted[4], "dp", split_axis=1, concat_axis=0, tiled=True),
        lax.all_to_all(lifted[5], "dp", split_axis=1, concat_axis=0, tiled=True),
    )
    partial_value = tuple((first_total(stacked)[None] for stacked in by_data))
    by_piece = (
        lax.all_to_all(partial_value[0], "seq", split_axis=1, concat_axis=0, tiled=True),
        lax.all_to_all(partial_value[1], "seq", split_axis=1, concat_axis=0, tiled=True),
        lax.all_to_all(partial_value[2], "seq", split_axis=1, concat_axis=0, tiled=True),
        lax.all_to_all(partial_value[3], "seq", split_axis=1, concat_axis=0, tiled=True),
        lax.all_to_all(partial_value[4], "seq", split_axis=1, concat_axis=0, tiled=True),
        lax.all_to_all(partial_value[5], "seq", split_axis=1, concat_axis=0, tiled=True),
    )
    return tuple((first_total(stacked) for stacked in by_piece))


def forward_pass(slot_in, weights, head_params):
    in_full, out_full, norm_full, gate_full, conv_full, bias_full = weights
    dt_shift, log_rate, skip_gain = head_params
    slot_count, piece_len, model_width = slot_in.shape
    inner_width = out_full.shape[0]
    channels = conv_full.shape[1]
    kernel = conv_full.shape[0]
    head_count = dt_shift.shape[0]
    head_size = inner_width // head_count
    state_size = (channels - inner_width) // 2
    input_f = slot_in.astype(jnp.float32)
    inv_rms = lax.rsqrt(jnp.mean(input_f * input_f, axis=-1, keepdims=True) + EPS)
    normed = (input_f * inv_rms * norm_full.astype(jnp.float32)).astype(jnp.bfloat16)
    projected = jnp.dot(
        normed.reshape(-1, model_width), in_full, preferred_element_type=jnp.float32
    ).reshape(slot_count, piece_len, -1)
    gate_part = projected[..., :inner_width]
    conv_in = projected[..., inner_width : inner_width + channels]
    dt_arg = projected[..., inner_width + channels :] + dt_shift
    rim_rows = from_behind(
        conv_in[:, piece_len - kernel + 1 :].astype(jnp.bfloat16), "seq", 1
    ).astype(jnp.float32)
    extended = jnp.concatenate([rim_rows, conv_in], axis=1)
    conv_taps = conv_full.astype(jnp.float32)
    pre_act = bias_full.astype(jnp.float32) + sum(
        (
            conv_taps[tap_index] * extended[:, tap_index : tap_index + piece_len]
            for tap_index in range(kernel)
        )
    )
    activated = jax.nn.silu(pre_act)
    x_heads = activated[..., :inner_width].reshape(slot_count, piece_len, head_count, head_size)
    b_rows = activated[..., inner_width : inner_width + state_size]
    c_rows = activated[..., inner_width + state_size :]
    dt_vals = jax.nn.softplus(dt_arg)
    decay_rates = -jnp.exp(log_rate)
    log_cum = jnp.cumsum(dt_vals * decay_rates, axis=1)
    log_tot = log_cum[:, -1]
    weights_in = jnp.exp(log_tot[:, None] - log_cum) * dt_vals
    local_state = jnp.einsum(
        "sthp,stn->shpn", weights_in[..., None] * x_heads, b_rows, precision=HIGH
    )
    carry_decay = jnp.exp(log_tot)
    neutral = (jnp.ones_like(carry_decay), jnp.zeros_like(local_state))
    _, start_state = carried_in((carry_decay, local_state), "seq", link_states, neutral, False)
    spots = jnp.arange(piece_len)
    causal = spots[:, None] >= spots[None, :]
    cum_heads = jnp.swapaxes(log_cum, 1, 2)
    gap_vals = jnp.where(causal, cum_heads[..., :, None] - cum_heads[..., None, :], 0.0)
    decay_mat = jnp.where(causal, jnp.exp(gap_vals), 0.0)
    cb_mat = jnp.einsum("stn,sun->stu", c_rows, b_rows, precision=HIGH)
    dt_cols = jnp.swapaxes(dt_vals, 1, 2)[:, :, None, :]
    mixing = decay_mat * cb_mat[:, None] * dt_cols
    y_intra = jnp.einsum("shtu,suhp->sthp", mixing, x_heads, precision=HIGH)
    state_read = jnp.einsum("stn,shpn->sthp", c_rows, start_state, precision=HIGH)
    exp_cum = jnp.exp(log_cum)
    y_heads = y_intra + exp_cum[..., None] * state_read + skip_gain[:, None] * x_heads
    y_flat = y_heads.reshape(slot_count, piece_len, inner_width)
    gate_act = jax.nn.silu(gate_part)
    gated_out = y_flat * gate_act
    inv_gate = lax.rsqrt(jnp.mean(gated_out * gated_out, axis=-1, keepdims=True) + EPS)
    gate_normed = (gated_out * inv_gate * gate_full.astype(jnp.float32)).astype(jnp.bfloat16)
    mixed = jnp.dot(
        gate_normed.reshape(-1, inner_width), out_full, preferred_element_type=jnp.float32
    )
    output = (input_f + mixed.reshape(slot_count, piece_len, model_width)).astype(jnp.bfloat16)
    saved = dict(
        input_f=input_f,
        inv_rms=inv_rms,
        normed=normed,
        gate_part=gate_part,
        dt_arg=dt_arg,
        extended=extended,
        pre_act=pre_act,
        x_heads=x_heads,
        b_rows=b_rows,
        c_rows=c_rows,
        dt_vals=dt_vals,
        log_cum=log_cum,
        log_tot=log_tot,
        weights_in=weights_in,
        carry_decay=carry_decay,
        start_state=start_state,
        decay_mat=decay_mat,
        cb_mat=cb_mat,
        dt_cols=dt_cols,
        mixing=mixing,
        state_read=state_read,
        exp_cum=exp_cum,
        y_flat=y_flat,
        gate_act=gate_act,
        gated_out=gated_out,
        inv_gate=inv_gate,
        gate_normed=gate_normed,
    )
    return (output, saved)


def backward_pass(saved, slot_cot, live, weights, head_params):
    in_full, out_full, norm_full, gate_full, conv_full, bias_full = weights
    dt_shift, log_rate, skip_gain = head_params
    slot_count, piece_len, model_width = slot_cot.shape
    inner_width = out_full.shape[0]
    kernel = conv_full.shape[0]
    x_heads = saved["x_heads"]
    b_rows = saved["b_rows"]
    c_rows = saved["c_rows"]
    dt_vals = saved["dt_vals"]
    log_cum = saved["log_cum"]
    weights_in = saved["weights_in"]
    carry_decay = saved["carry_decay"]
    start_state = saved["start_state"]
    decay_mat = saved["decay_mat"]
    cb_mat = saved["cb_mat"]
    dt_cols = saved["dt_cols"]
    decay_rates = -jnp.exp(log_rate)
    masked_cot = slot_cot * live[..., None].astype(jnp.bfloat16)
    cot_rows = masked_cot.reshape(-1, model_width)
    d_gn = cols_product(cot_rows, out_full).reshape(slot_count, piece_len, inner_width)
    gate_hat = saved["gated_out"] * saved["inv_gate"]
    grad_ggain = jnp.sum(d_gn * gate_hat, axis=(0, 1))
    d_hat = d_gn * gate_full.astype(jnp.float32)
    d_gated = saved["inv_gate"] * (
        d_hat - gate_hat * jnp.mean(d_hat * gate_hat, axis=-1, keepdims=True)
    )
    d_gate_part = d_gated * saved["y_flat"] * silu_slope(saved["gate_part"])
    d_heads = (d_gated * saved["gate_act"]).reshape(x_heads.shape)
    grad_skip = jnp.sum(d_heads * x_heads, axis=(0, 1, 3))
    exp_cum = saved["exp_cum"]
    d_read = d_heads * exp_cum[..., None]
    d_cvals = jnp.einsum("sthp,shpn->stn", d_read, start_state, precision=HIGH)
    d_start = jnp.einsum("sthp,stn->shpn", d_read, c_rows, precision=HIGH)
    d_cum = jnp.sum(d_heads * saved["state_read"], axis=-1) * exp_cum
    d_mixing = jnp.einsum("sthp,suhp->shtu", d_heads, x_heads, precision=HIGH)
    d_x = skip_gain[:, None] * d_heads + jnp.einsum(
        "shtu,sthp->suhp", saved["mixing"], d_heads, precision=HIGH
    )
    d_decay = d_mixing * cb_mat[:, None] * dt_cols
    d_cb = jnp.sum(d_mixing * decay_mat * dt_cols, axis=1)
    d_dt = jnp.swapaxes(jnp.sum(d_mixing * decay_mat * cb_mat[:, None], axis=2), 1, 2)
    spread = d_decay * decay_mat
    d_cum = d_cum + jnp.swapaxes(jnp.sum(spread, axis=3) - jnp.sum(spread, axis=2), 1, 2)
    d_cvals = d_cvals + jnp.einsum("stu,sun->stn", d_cb, b_rows, precision=HIGH)
    d_bvals = jnp.einsum("stu,stn->sun", d_cb, c_rows, precision=HIGH)
    neutral = (jnp.ones_like(carry_decay), jnp.zeros_like(d_start))
    _, later_grad = carried_in((carry_decay, d_start), "seq", link_states, neutral, True)
    d_tot = jnp.sum(later_grad * start_state, axis=(2, 3)) * carry_decay
    grad_proj_b = jnp.einsum("shpn,stn->sthp", later_grad, b_rows, precision=HIGH)
    d_x = d_x + weights_in[..., None] * grad_proj_b
    d_weights = jnp.sum(grad_proj_b * x_heads, axis=-1)
    d_bvals = d_bvals + jnp.einsum(
        "sthp,shpn->stn", weights_in[..., None] * x_heads, later_grad, precision=HIGH
    )
    d_dt = d_dt + d_weights * jnp.exp(saved["log_tot"][:, None] - log_cum)
    through = d_weights * weights_in
    d_tot = d_tot + jnp.sum(through, axis=1)
    last_row = (jnp.arange(piece_len) == piece_len - 1).astype(jnp.float32)
    d_cum = d_cum - through + last_row[None, :, None] * d_tot[:, None, :]
    d_log = lax.cumsum(d_cum, axis=1, reverse=True)
    d_dt = d_dt + d_log * decay_rates
    grad_alog = jnp.sum(d_log * dt_vals, axis=(0, 1)) * decay_rates
    d_arg = d_dt * jax.nn.sigmoid(saved["dt_arg"])
    grad_dtb = jnp.sum(d_arg, axis=(0, 1))
    d_act = jnp.concatenate(
        [d_x.reshape(slot_count, piece_len, inner_width), d_bvals, d_cvals], axis=-1
    )
    d_pre = d_act * silu_slope(saved["pre_act"])
    grad_cbias = jnp.sum(d_pre, axis=(0, 1))
    extended = saved["extended"]
    grad_conv = jnp.stack(
        [
            jnp.sum(d_pre * extended[:, tap_index : tap_index + piece_len], axis=(0, 1))
            for tap_index in range(kernel)
        ]
    )
    conv_taps = conv_full.astype(jnp.float32)
    d_ext = sum(
        (
            jnp.pad(
                conv_taps[tap_index] * d_pre, ((0, 0), (tap_index, kernel - 1 - tap_index), (0, 0))
            )
            for tap_index in range(kernel)
        )
    )
    back_rim = from_behind(as_sent(d_ext[:, : kernel - 1]), "seq", -1)
    d_conv_in = d_ext[:, kernel - 1 :] + jnp.pad(
        back_rim, ((0, 0), (piece_len - kernel + 1, 0), (0, 0))
    )
    d_proj = jnp.concatenate([d_gate_part, d_conv_in, d_arg], axis=-1).astype(jnp.bfloat16)
    d_proj = d_proj.reshape(slot_count * piece_len, -1)
    d_normed = cols_product(d_proj, in_full).reshape(slot_count, piece_len, model_width)
    in_hat = saved["input_f"] * saved["inv_rms"]
    grad_ngain = jnp.sum(d_normed * in_hat, axis=(0, 1))
    d_norm_in = d_normed * norm_full.astype(jnp.float32)
    input_grad = saved["inv_rms"] * (
        d_norm_in - in_hat * jnp.mean(d_norm_in * in_hat, axis=-1, keepdims=True)
    )
    input_grad = input_grad + masked_cot.astype(jnp.float32)
    product_rows = (
        saved["normed"].reshape(-1, model_width),
        d_proj,
        saved["gate_normed"].reshape(-1, inner_width),
        cot_rows,
    )
    small_grads = (grad_ngain, grad_ggain, grad_conv, grad_cbias)
    return (
        input_grad.astype(jnp.bfloat16),
        product_rows,
        small_grads,
        (grad_dtb, grad_alog, grad_skip),
    )


def body(
    block_input,
    cotangent,
    lengths,
    in_weight,
    out_weight,
    norm_gain,
    gate_gain,
    conv_weight,
    conv_bias,
    dt_bias,
    a_log,
    d_skip,
):
    shards = (in_weight, out_weight, norm_gain, gate_gain, conv_weight, conv_bias)
    head_params = (dt_bias, a_log, d_skip)
    piece_len = block_input.shape[1]
    batches = block_input.shape[0] // SLOTS_MB
    positions = lax.axis_index("seq") * piece_len + jnp.arange(piece_len, dtype=jnp.int32)
    held = (
        lax.all_gather(shards[0], ("dp", "seq"), axis=0, tiled=True),
        lax.all_gather(shards[1], ("dp", "seq"), axis=0, tiled=True),
        lax.all_gather(shards[2], ("dp", "seq"), axis=0, tiled=True),
        lax.all_gather(shards[3], ("dp", "seq"), axis=0, tiled=True),
        lax.all_gather(shards[4], ("dp", "seq"), axis=1, tiled=True),
        lax.all_gather(shards[5], ("dp", "seq"), axis=0, tiled=True),
    )
    outputs = []
    input_grads = []
    kept_rows = []
    small_totals = None
    head_totals = None
    for batch_index in range(batches):
        first = batch_index * SLOTS_MB
        slot_in = block_input[first : first + SLOTS_MB]
        slot_cot = cotangent[first : first + SLOTS_MB]
        live = (positions[None, :] < lengths[first : first + SLOTS_MB, None]).astype(jnp.float32)
        output, saved = forward_pass(slot_in, held, head_params)
        input_grad, product_rows, small_grads, head_grads = backward_pass(
            saved, slot_cot, live, held, head_params
        )
        outputs.append(output)
        input_grads.append(input_grad)
        kept_rows.append(product_rows)
        small_totals = (
            small_grads
            if small_totals is None
            else jax.tree.map(add_pair, small_totals, small_grads)
        )
        head_totals = (
            head_grads if head_totals is None else jax.tree.map(add_pair, head_totals, head_grads)
        )
    normed_all = jnp.concatenate([rows[0] for rows in kept_rows], axis=0)
    dproj_all = jnp.concatenate([rows[1] for rows in kept_rows], axis=0)
    gnormed_all = jnp.concatenate([rows[2] for rows in kept_rows], axis=0)
    cot_all = jnp.concatenate([rows[3] for rows in kept_rows], axis=0)
    grad_win = rows_product(normed_all, dproj_all)
    grad_wout = rows_product(gnormed_all, cot_all)
    grad_ngain, grad_ggain, grad_conv, grad_cbias = small_totals
    owned = owner_sums((grad_win, grad_wout, grad_ngain, grad_ggain, grad_conv.T, grad_cbias))
    head_sums = lax.psum(head_totals, ("dp", "seq"))
    return (
        jnp.concatenate(outputs, axis=0),
        jnp.concatenate(input_grads, axis=0),
        owned[0],
        owned[1],
        owned[2],
        owned[3],
        owned[4].T,
        owned[5],
        head_sums[0],
        head_sums[1],
        head_sums[2],
    )


F32 = jnp.float32
BF16 = jnp.bfloat16
MESH_ID = pl.DeviceIdType.MESH
ANY = pl.BlockSpec(memory_space=pl.ANY)
INVMEM = pl.BlockSpec(memory_space=pltpu.VMEM)
VMEM_LIMIT = 60 * 1024 * 1024
CHUNK = 128


def flip(place, bit):
    return place + bit - 2 * bit * lax.rem(lax.div(place, bit), 2)


def flip_all(place, mask):
    for bit in (1, 2, 4):
        if mask & bit:
            place = flip(place, bit)
    return place


class Links:
    def __init__(self, sends, recvs):
        self.sends, self.recvs, self.used = sends, recvs, 0

    def copy(self, source, target, device):
        slot = self.used
        self.used += 1
        return pltpu.make_async_remote_copy(
            src_ref=source,
            dst_ref=target,
            send_sem=self.sends.at[slot],
            recv_sem=self.recvs.at[slot],
            device_id=device,
            device_id_type=MESH_ID,
        )


def greet(devices, conditions=()):
    barrier = pltpu.get_barrier_semaphore()
    for device in devices:
        pl.semaphore_signal(barrier, inc=1, device_id=device, device_id_type=MESH_ID)
    for condition, device in conditions:

        @pl.when(condition)
        def _():
            pl.semaphore_signal(barrier, inc=1, device_id=device, device_id_type=MESH_ID)

    count = len(devices)
    for condition, _ in conditions:
        count = count + jnp.where(condition, 1, 0)
    pl.semaphore_wait(barrier, count)


def spread_kernel(extent, own, everyone, sends, recvs, local):
    depth, width = extent
    row, place = lax.axis_index("dp"), lax.axis_index("seq")
    links = Links(sends, recvs)
    others = [
        (lax.rem(row + up, depth), lax.rem(place + right, width))
        for up in range(depth)
        for right in range(width)
        if up or right
    ]
    greet(others)
    mine = everyone.at[row, place]
    copies = [links.copy(own, mine, device) for device in others]
    for copy in copies:
        copy.start()
    kept = pltpu.make_async_copy(own, mine, local)
    kept.start()
    kept.wait()
    for copy in copies:
        copy.wait()


def spread(block, extent, collective):
    count = extent[0] * extent[1] - 1
    return pl.pallas_call(
        functools.partial(spread_kernel, extent),
        out_shape=jax.ShapeDtypeStruct(extent + block.shape, block.dtype),
        in_specs=[INVMEM],
        out_specs=INVMEM,
        scratch_shapes=[
            pltpu.SemaphoreType.DMA((count,)),
            pltpu.SemaphoreType.DMA((count,)),
            pltpu.SemaphoreType.DMA,
        ],
        compiler_params=pltpu.CompilerParams(collective_id=collective, has_side_effects=True),
        name="spread_small",
    )(block)


def plane_rows_kernel(parts, total, landed, sends, recvs):
    row, place = lax.axis_index("dp"), lax.axis_index("seq")
    links = Links(sends, recvs)
    peers = [(row, flip_all(place, mask)) for mask in range(1, 8)]
    greet(peers)
    copies = [
        links.copy(parts.at[peer[1]], landed.at[k], peer) for k, peer in enumerate(peers)
    ]
    for copy in copies:
        copy.start()
    for copy in copies:
        copy.wait()
    result = parts[place].astype(F32)
    for k in range(7):
        result = result + landed[k].astype(F32)
    total[...] = result


def plane_rows(parts, collective):
    return pl.pallas_call(
        plane_rows_kernel,
        out_shape=jax.ShapeDtypeStruct(parts.shape[1:], F32),
        in_specs=[INVMEM],
        out_specs=INVMEM,
        scratch_shapes=[
            pltpu.VMEM((7,) + parts.shape[1:], parts.dtype),
            pltpu.SemaphoreType.DMA((7,)),
            pltpu.SemaphoreType.DMA((7,)),
        ],
        compiler_params=pltpu.CompilerParams(collective_id=collective, has_side_effects=True),
        name="plane_rows",
    )(parts)


def add_rows(target, first, second, step=32):
    def one(number, carry):
        rows = pl.ds(pl.multiple_of(number * step, step), step)
        target[rows] = (first[rows].astype(F32) + second[rows].astype(F32)).astype(target.dtype)
        return carry

    lax.fori_loop(0, target.shape[0] // step, one, 0)


def cast_rows(target, source, step=32):
    def one(number, carry):
        rows = pl.ds(pl.multiple_of(number * step, step), step)
        target[rows] = source[rows].astype(target.dtype)
        return carry

    lax.fori_loop(0, target.shape[0] // step, one, 0)


class LineSum:
    def __init__(self, links, depth, row, place, own, valid, up_in, up_out, down_in, down_out):
        self.depth, self.row, self.own, self.valid = depth, row, own, valid
        self.up_in, self.up_out, self.down_in, self.down_out = up_in, up_out, down_in, down_out
        above, below = lax.min(row + 1, depth - 1), lax.max(row - 1, 0)
        self.ups = {
            q: links.copy(up_out.at[q - 1], up_in.at[q - 1], (above, place)) for q in range(1, depth)
        }
        self.downs = {
            q: links.copy(down_out.at[q], down_in.at[q], (below, place)) for q in range(depth - 1)
        }

    def up(self, q):
        row = self.row

        @pl.when(self.valid(q) & (row < q))
        def _():
            @pl.when(row == 0)
            def _():
                cast_rows(self.up_out.at[q - 1], self.own(q))

            @pl.when(row > 0)
            def _():
                self.ups[q].wait_recv()
                add_rows(self.up_out.at[q - 1], self.own(q), self.up_in.at[q - 1])

            self.ups[q].start()

    def down(self, q):
        row, depth = self.row, self.depth

        @pl.when(self.valid(q) & (row > q))
        def _():
            @pl.when(row == depth - 1)
            def _():
                cast_rows(self.down_out.at[q], self.own(q))

            @pl.when(row < depth - 1)
            def _():
                self.downs[q].wait_recv()
                add_rows(self.down_out.at[q], self.own(q), self.down_in.at[q])

            self.downs[q].start()

    def step(self, number):
        up_q, down_q = self.depth - 1 - number, number

        @pl.when(self.row < self.depth // 2)
        def _():
            self.up(up_q)
            self.down(down_q)

        @pl.when(self.row >= self.depth // 2)
        def _():
            self.down(down_q)
            self.up(up_q)

    def finish(self, total):
        depth, row = self.depth, self.row
        for q in range(depth):

            @pl.when(self.valid(q) & (row == q))
            def _():
                if q > 0:
                    self.ups[q].wait_recv()
                if q < depth - 1:
                    self.downs[q].wait_recv()
                if 0 < q < depth - 1:
                    add_rows(total, self.up_in.at[q - 1], self.down_in.at[q])
                    add_rows(total, total, self.own(q))
                elif q > 0:
                    add_rows(total, self.own(q), self.up_in.at[q - 1])
                else:
                    add_rows(total, self.own(q), self.down_in.at[q])

    def drain(self):
        for q, copy in self.ups.items():
            pl.when(self.valid(q) & (self.row < q))(copy.wait_send)
        for q, copy in self.downs.items():
            pl.when(self.valid(q) & (self.row > q))(copy.wait_send)


class PlaneSum:
    def __init__(self, links, row, place, parts, total, pair_in, sums, relay_in, last_in):
        self.place, self.parts, self.total = place, parts, total
        self.pair_in, self.sums, self.relay_in, self.last_in = pair_in, sums, relay_in, last_in
        peer = {mask: (row, flip_all(place, mask)) for mask in range(1, 8)}
        self.peer = peer
        rows = total.shape[0] // 2
        self.halves = (pl.ds(0, rows), pl.ds(rows, rows))
        self.pair = {
            mask: links.copy(parts.at[peer[mask ^ 1][1]], pair_in.at[mask // 2], peer[1])
            for mask in (6, 2, 4, 0)
        }
        top, low = self.halves
        self.relay4 = links.copy(sums.at[3, top], relay_in.at[0], peer[4])
        self.relay2 = links.copy(sums.at[3, low], relay_in.at[1], peer[2])
        self.last2 = links.copy(sums.at[1], last_in.at[0], peer[2])
        self.last4 = links.copy(sums.at[2], last_in.at[1], peer[4])

    def begin(self):
        for copy in self.pair.values():
            copy.start()

    def chip(self, mask):
        index = mask // 2
        self.pair[mask].wait_recv()
        mine = self.parts.at[self.peer[mask][1] if mask else self.place]
        add_rows(self.sums.at[index], mine, self.pair_in.at[index])

    def first(self):
        self.chip(6)
        self.relay4.start()
        self.relay2.start()
        self.chip(2)
        self.chip(4)
        self.chip(0)

    def second(self):
        top, low = self.halves
        self.relay4.wait_recv()
        add_rows(self.sums.at[1, top], self.sums.at[1, top], self.relay_in.at[0])
        self.last2.start()
        self.relay2.wait_recv()
        add_rows(self.sums.at[2, low], self.sums.at[2, low], self.relay_in.at[1])
        self.last4.start()

    def finish(self):
        self.last2.wait_recv()
        self.last4.wait_recv()
        add_rows(self.total, self.last_in.at[0], self.last_in.at[1])
        add_rows(self.total, self.total, self.sums.at[0])

    def drain(self):
        for copy in self.pair.values():
            copy.wait_send()
        for copy in (self.relay4, self.relay2, self.last2, self.last4):
            copy.wait_send()


def scatter_kernel(
    depth,
    d_parts,
    o_parts,
    g_in,
    g_out,
    d_total,
    o_total,
    in_total,
    out_total,
    d_pair,
    d_sums,
    d_relay,
    d_last,
    o_pair,
    o_sums,
    o_relay,
    o_last,
    in_up_in,
    in_up_out,
    in_down_in,
    in_down_out,
    in_sum,
    in_sent,
    out_up_in,
    out_up_out,
    out_down_in,
    out_down_out,
    out_sum,
    out_far,
    sends,
    recvs,
    local,
):
    row, place = lax.axis_index("dp"), lax.axis_index("seq")
    core = lax.rem(place, 2)
    half = depth // 2
    links = Links(sends, recvs)
    above, below = lax.min(row + 1, depth - 1), lax.max(row - 1, 0)
    peer = {mask: (row, flip_all(place, mask)) for mask in range(1, 8)}
    greet(
        [peer[mask] for mask in range(1, 8)],
        [(row < depth - 1, (above, place)), (row > 0, (below, place))],
    )
    always = row >= 0
    in_line = LineSum(
        links,
        depth,
        row,
        place,
        lambda q: g_in.at[q],
        lambda q: always,
        in_up_in,
        in_up_out,
        in_down_in,
        in_down_out,
    )
    out_line = LineSum(
        links,
        depth,
        row,
        place,
        lambda q: g_out.at[q % half],
        lambda q: core == q // half,
        out_up_in,
        out_up_out,
        out_down_in,
        out_down_out,
    )
    d_plane = PlaneSum(links, row, place, d_parts, d_total, d_pair, d_sums, d_relay, d_last)
    o_plane = PlaneSum(links, row, place, o_parts, o_total, o_pair, o_sums, o_relay, o_last)
    d_plane.begin()
    o_plane.begin()
    in_line.step(0)
    d_plane.first()
    o_plane.first()
    d_plane.second()
    for number in range(1, depth - 1):
        in_line.step(number)
    o_plane.second()
    for number in range(depth - 1):
        out_line.step(number)
    d_plane.finish()
    o_plane.finish()
    in_line.finish(in_sum)
    cast_rows(in_sent, in_sum)
    rows = in_sum.shape[0] // 8
    mine = in_total.at[place]
    back = []
    for mask in (6, 2, 4, 7, 3, 5, 1):
        target = peer[mask][1]
        block = in_sent.at[pl.ds(pl.multiple_of(target * rows, rows), rows)]
        back.append(links.copy(block, mine, peer[mask]))
        back[-1].start()
    kept = pltpu.make_async_copy(
        in_sent.at[pl.ds(pl.multiple_of(place * rows, rows), rows)], mine, local
    )
    kept.start()
    out_line.finish(out_sum)
    home = lax.div(row, half) == core
    rows_out = out_total.shape[0]
    far = links.copy(out_far, out_total, peer[1])
    for this in range(2):

        @pl.when(home & (core == this))
        def _():
            cast_rows(out_far, out_sum.at[pl.ds((1 - this) * rows_out, rows_out)])
            far.start()
            cast_rows(out_total, out_sum.at[pl.ds(this * rows_out, rows_out)])

    pl.when(jnp.logical_not(home))(far.wait_recv)
    pl.when(home)(far.wait_send)
    kept.wait()
    for copy in back:
        copy.wait()
    d_plane.drain()
    o_plane.drain()
    in_line.drain()
    out_line.drain()


def scatter(depth, d_parts, o_parts, g_in, g_out, collective):
    shape = jax.ShapeDtypeStruct
    width, rows, model = d_parts.shape
    in_piece, out_piece = g_in.shape[1:], g_out.shape[1:]
    plane = [
        pltpu.VMEM((4, rows, model), BF16),
        pltpu.VMEM((4, rows, model), BF16),
        pltpu.VMEM((2, rows // 2, model), BF16),
        pltpu.VMEM((2, rows, model), BF16),
    ]
    return pl.pallas_call(
        functools.partial(scatter_kernel, depth),
        out_shape=(
            shape((rows, model), F32),
            shape((rows, model), F32),
            shape((width, in_piece[0] // width, in_piece[1]), BF16),
            shape((out_piece[0] // 2, out_piece[1]), F32),
        ),
        in_specs=[INVMEM] * 4,
        out_specs=(INVMEM,) * 4,
        scratch_shapes=plane
        + plane
        + [pltpu.VMEM((depth - 1,) + in_piece, BF16)] * 4
        + [pltpu.VMEM(in_piece, F32), pltpu.VMEM(in_piece, BF16)]
        + [pltpu.VMEM((depth - 1,) + out_piece, BF16)] * 4
        + [
            pltpu.VMEM(out_piece, F32),
            pltpu.VMEM((out_piece[0] // 2, out_piece[1]), F32),
            pltpu.SemaphoreType.DMA((64,)),
            pltpu.SemaphoreType.DMA((64,)),
            pltpu.SemaphoreType.DMA,
        ],
        compiler_params=pltpu.CompilerParams(
            collective_id=collective, has_side_effects=True, vmem_limit_bytes=VMEM_LIMIT
        ),
        name="scatter_plane_and_line",
    )(d_parts, o_parts, g_in, g_out)


def dot(left, right, contract, precision=None):
    return lax.dot_general(
        left, right, (contract, ((), ())), precision=precision, preferred_element_type=F32
    )


def mm(left, right):
    return dot(left, right, ((1,), (0,)))


def mm_t(left, right):
    return dot(left, right, ((1,), (1,)))


def t_mm(left, right):
    return dot(left, right, ((0,), (0,)))


def widen(values, heads, head_size):
    rows = values.shape[0]
    lane = lax.broadcasted_iota(jnp.int32, (rows, 2 * head_size), 1)
    parts = []
    for pair in range(heads // 2):
        low = jnp.broadcast_to(values[:, 2 * pair : 2 * pair + 1], (rows, 2 * head_size))
        high = jnp.broadcast_to(values[:, 2 * pair + 1 : 2 * pair + 2], (rows, 2 * head_size))
        parts.append(jnp.where(lane < head_size, low, high))
    return jnp.concatenate(parts, axis=1)


def sigmoid(values):
    return 1.0 / (1.0 + jnp.exp(-values))


def softplus(values):
    return jnp.maximum(values, 0.0) + jnp.log1p(jnp.exp(-jnp.abs(values)))


def split_pair(values, head_size):
    lane = lax.broadcasted_iota(jnp.int32, values.shape, 1)
    zero = jnp.zeros_like(values)
    return jnp.where(lane < head_size, values, zero), jnp.where(lane < head_size, zero, values)


def triangles():
    rows = lax.broadcasted_iota(jnp.int32, (CHUNK, CHUNK), 0)
    cols = lax.broadcasted_iota(jnp.int32, (CHUNK, CHUNK), 1)
    return rows >= cols


def head_decays(cum, cum_t, head, causal):
    gap = cum[:, head : head + 1] - cum_t[head : head + 1, :]
    return jnp.exp(jnp.where(causal, gap, -1e30))


class Line:
    def __init__(self, links, depth, row, place, blocks, valid=None):
        self.depth, self.row = depth, row
        above, below = lax.min(row + 1, depth - 1), lax.max(row - 1, 0)
        self.steps = []
        for step in range(depth - 1):
            up_sent, up_got = row - step, row - 1 - step
            down_sent, down_got = row + step, row + 1 + step
            ways = []
            for sends, shard, gets, got, device in (
                ((row < depth - 1) & (up_sent >= 0), up_sent, (row > 0) & (up_got >= 0), up_got, above),
                ((row > 0) & (down_sent < depth), down_sent, (row < depth - 1) & (down_got < depth), down_got, below),
            ):
                shard = lax.clamp(0, shard, depth - 1)
                got = lax.clamp(0, got, depth - 1)
                if valid is not None:
                    sends, gets = sends & valid(shard), gets & valid(got)
                copies = [links.copy(block, block, (device, place)) for block in blocks(shard)]
                ways.append((sends, gets, copies))
            self.steps.append(ways)

    def send(self, number):
        for sends, _, copies in self.steps[number]:

            @pl.when(sends)
            def _():
                for copy in copies:
                    copy.start()

    def wait(self, number):
        for _, gets, copies in self.steps[number]:

            @pl.when(gets)
            def _():
                for copy in copies:
                    copy.wait_recv()

    def drain(self):
        for ways in self.steps:
            for sends, _, copies in ways:

                @pl.when(sends)
                def _():
                    for copy in copies:
                        copy.wait_send()


class Pass:
    def __init__(self, links, peer, place, own, everyone):
        rows = own.shape[0] // 2
        mine = everyone.at[place]
        from2, from4, far = (everyone.at[peer[mask][1]] for mask in (2, 4, 6))
        top, low = pl.ds(0, rows), pl.ds(rows, rows)
        self.kept = None
        self.to2 = links.copy(own, mine, peer[2])
        self.to4 = links.copy(own, mine, peer[4])
        self.to1 = links.copy(own, mine, peer[1])
        self.relay4 = links.copy(from2.at[top], from2.at[top], peer[4])
        self.relay2 = links.copy(from4.at[low], from4.at[low], peer[2])
        self.pair2 = links.copy(from2, from2, peer[1])
        self.pair4 = links.copy(from4, from4, peer[1])
        self.pair6 = links.copy(far.at[top], far.at[top], peer[1])
        self.pair7 = links.copy(far.at[low], far.at[low], peer[1])

    def first(self):
        self.to2.start()
        self.to4.start()
        self.to1.start()

    def relay(self):
        self.to2.wait_recv()
        self.relay4.start()
        self.to4.wait_recv()
        self.relay2.start()
        self.pair2.start()
        self.pair4.start()

    def last(self):
        self.relay4.wait_recv()
        self.pair6.start()
        self.relay2.wait_recv()
        self.pair7.start()

    def end(self):
        for copy in (self.to1, self.pair2, self.pair4, self.pair6, self.pair7):
            copy.wait_recv()

    def drain(self):
        for copy in (
            self.to2,
            self.to4,
            self.to1,
            self.relay4,
            self.relay2,
            self.pair2,
            self.pair4,
            self.pair6,
            self.pair7,
        ):
            copy.wait_send()


def lay_out(pieces, row, count):
    tiles = [None] * -(-count * len(pieces) // 128)
    for index, piece in enumerate(pieces):
        tile, shift = divmod(index * count, 128)
        moved = pltpu.roll(piece, shift, 1) if shift else piece
        lane = lax.broadcasted_iota(jnp.int32, piece.shape, 1)
        parts = [(tile, jnp.where((lane >= shift) & (lane < shift + count), moved, 0.0))]
        if shift + count > 128:
            parts.append((tile + 1, jnp.where(lane < shift + count - 128, moved, 0.0)))
        for at, part in parts:
            tiles[at] = part if tiles[at] is None else tiles[at] + part
    return tiles


def channel_windows(ref, place, plane, half, run):
    core, chip = lax.rem(place, 2), lax.div(place, 2)
    parts = []
    for j in range(half):
        start = ((core * half + j) * plane + chip) * run
        base = pl.multiple_of(lax.div(start, 128) * 128, 128)
        window = ref[:, pl.ds(base, run + 64)]
        moved = pltpu.roll(window, run, 1)
        parts.append(jnp.where(lax.rem(start, 128) == 0, window, moved)[:, :run])
    return jnp.concatenate(parts, axis=1)


def head_choice(place, plane, half, group, heads):
    core, chip = lax.rem(place, 2), lax.div(place, 2)
    head = lax.broadcasted_iota(jnp.int32, (128, 128), 0)
    lane = lax.broadcasted_iota(jnp.int32, (128, 128), 1)
    part = sum(((lane >= j * group).astype(jnp.int32) for j in range(1, half)), jnp.zeros_like(lane))
    chosen = ((core * half + part) * plane + chip) * group + lane - part * group
    return jnp.where((head == chosen) & (lane < heads), 1.0, 0.0)


def forward_kernel(
    dims,
    x_own,
    cot_own,
    wg_send,
    wx_send,
    wb_send,
    wo_own,
    pack,
    head_params,
    normed_out,
    cot_out,
    wg_out,
    wx_out,
    wb_out,
    wo_out,
    conv_out,
    pre_out,
    dt_out,
    gate_out,
    y_out,
    dgn_out,
    states_out,
    norms_out,
    taps_out,
    rows_out,
    w_dt_out,
    x_all,
    normed_all,
    cot_all,
    wg,
    wx,
    wb,
    wo,
    packs,
    conv_in,
    pre_all,
    dt_all,
    gate_all,
    y_all,
    dgn_all,
    states,
    ext,
    state,
    full,
    sums,
    sums_in,
    sends,
    recvs,
    locals_,
    stores,
):
    depth, width, heads, head_size, size, kernel, own_ch, inner_all = dims
    half, plane = depth // 2, width // 2
    inner = heads * head_size
    run = inner // half
    model = x_own.shape[1]
    piece = x_own.shape[0] // 2
    rows = 2 * piece
    slots = 2
    blocks = slots * width // 2
    row, place = lax.axis_index("dp"), lax.axis_index("seq")
    core = lax.rem(place, 2)
    links = Links(sends, recvs)
    peer = {mask: (row, flip_all(place, mask)) for mask in range(1, width)}
    line_peers = [(lax.rem(row + up, depth), place) for up in range(1, depth)]
    greet([peer[mask] for mask in range(1, width)] + line_peers)

    kept = [
        pltpu.make_async_copy(wx_send.at[place], wx.at[row, place], locals_.at[0]),
        pltpu.make_async_copy(wb_send.at[core], wb.at[core, row, place], locals_.at[1]),
        pltpu.make_async_copy(wg_send.at[place], wg.at[row, place], locals_.at[2]),
        pltpu.make_async_copy(x_own, x_all.at[place], locals_.at[3]),
        pltpu.make_async_copy(cot_own, cot_all.at[place], locals_.at[4]),
        pltpu.make_async_copy(pack, packs.at[row, place], locals_.at[5]),
    ]
    for copy in kept:
        copy.start()

    out_home = lax.div(row, half) == core
    out_block = wo.at[lax.rem(row, half), core]
    out_kept = pltpu.make_async_copy(wo_own, out_block, locals_.at[6])
    out_pair = links.copy(wo_own, out_block, peer[1])
    pl.when(out_home)(out_kept.start)
    pl.when(jnp.logical_not(out_home))(out_pair.start)

    order = (6, 2, 4, 7, 3, 5, 1)
    plane_x, plane_g = [], []
    for mask in order:
        target = peer[mask][1]
        its_core = lax.rem(target, 2)
        plane_x.append(links.copy(wx_send.at[target], wx.at[row, place], peer[mask]))
        plane_x.append(
            links.copy(wb_send.at[its_core], wb.at[its_core, row, place], peer[mask])
        )
        plane_g.append(links.copy(wg_send.at[target], wg.at[row, place], peer[mask]))
    for copy in plane_x:
        copy.start()
    pack_line = [links.copy(pack, packs.at[row, place], device) for device in line_peers]
    for copy in pack_line:
        copy.start()
    x_pass = Pass(links, peer, place, x_own, x_all)
    cot_pass = Pass(links, peer, place, cot_own, cot_all)
    x_pass.first()

    out_line = Line(
        links,
        depth,
        row,
        place,
        lambda shard: [wo.at[lax.rem(shard, half)]],
        lambda shard: lax.div(shard, half) == core,
    )
    x_line = Line(links, depth, row, place, lambda shard: [wx.at[shard], wb.at[core, shard]])
    gate_line = Line(links, depth, row, place, lambda shard: [wg.at[shard]])

    pl.when(out_home)(out_kept.wait)
    pl.when(out_home)(out_pair.wait_recv)
    out_line.send(0)
    kept[0].wait()
    kept[1].wait()
    for copy in plane_x:
        copy.wait_recv()
    x_line.send(0)
    kept[5].wait()
    for copy in pack_line:
        copy.wait_recv()
    mine = packs.at[:, place]
    pack_plane = [links.copy(mine, mine, peer[mask]) for mask in order]
    for copy in pack_plane:
        copy.start()
    for copy in plane_g:
        copy.start()
    x_pass.relay()
    x_line.wait(0)
    if depth > 2:
        x_line.send(1)
    for copy in pack_plane:
        copy.wait_recv()

    small = [
        packs[z, s, model // (depth * width) : model // (depth * width) + 16, :].astype(F32)[:8]
        for z in range(depth)
        for s in range(width)
    ]
    choice = head_choice(place, plane, half, run // head_size, heads)
    tap_tiles = lay_out(small, 0, own_ch)
    for at, tile in enumerate(tap_tiles):
        full[:, at * 128 : (at + 1) * 128] = tile
    taps_out[:, :inner] = channel_windows(full, place, plane, half, run)
    taps_out[:, inner:] = full[:, inner_all : inner_all + 2 * size]
    gate_tiles = lay_out(small, 5, inner_all // (depth * width))
    for at, tile in enumerate(gate_tiles):
        full[:, at * 128 : (at + 1) * 128] = tile
    gate_gain = channel_windows(full, place, plane, half, run)[5:6]
    norm_tiles = lay_out(small, 6, model // (depth * width))
    norm_gain = jnp.concatenate([tile[6:7] for tile in norm_tiles], axis=1)
    chosen = dot(head_params[...], choice, ((1,), (0,)), lax.Precision.HIGHEST)
    lane = lax.broadcasted_iota(jnp.int32, (1, 128), 1)
    rates = jnp.where(lane < heads, -jnp.exp(chosen[1:2]), 0.0)
    skip = widen(chosen[2:3], heads, head_size)
    dt_rows = packs[:, :, 0 : model // (depth * width), :].reshape(model, 128)
    w_dt_out[...] = mm(dt_rows, choice.astype(BF16)).astype(BF16)
    rows_out[...] = jnp.zeros_like(rows_out)
    rows_out[0:1, :] = norm_gain
    rows_out[1:2, :inner] = gate_gain
    rows_out[2:3, :inner] = skip
    rows_out[3:4, :128] = chosen[0:1]
    rows_out[4:5, :128] = rates

    x_pass.last()
    cot_pass.first()

    def normalise(index, carry):
        for part in range(2):
            held = x_all[index, part * piece : (part + 1) * piece, :].astype(F32)
            inv = lax.rsqrt(jnp.mean(held * held, axis=1, keepdims=True) + EPS)
            normed_all[index, part * piece : (part + 1) * piece, :] = (
                held * inv * rows_out[0:1, :]
            ).astype(BF16)
        return carry

    x_line.wait(1) if depth > 2 else None
    if depth > 3:
        x_line.send(2)
    for copy in plane_g:
        copy.wait_recv()
    kept[2].wait()
    x_pass.end()
    kept[3].wait()
    lax.fori_loop(0, width, normalise, 0)
    if depth > 3:
        x_line.wait(2)
    gate_line.send(0)
    mine_bc = wb.at[core]
    pair_bc = links.copy(mine_bc, mine_bc, peer[1])
    pair_bc.start()
    saves = [pltpu.make_async_copy(normed_all, normed_out, locals_.at[7])]
    saves[0].start()
    pair_bc.wait_recv()

    causal = triangles()
    ones = causal.astype(F32)

    def stored(index):
        at = pl.ds(pl.multiple_of(index * rows, rows), rows)
        pairs = [
            (conv_in.at[at], conv_out.at[at]),
            (pre_all.at[at], pre_out.at[at]),
            (dt_all.at[at], dt_out.at[at]),
            (y_all.at[at], y_out.at[at]),
            (
                states.at[pl.ds(index * (rows // CHUNK), rows // CHUNK)],
                states_out.at[pl.ds(index * (rows // CHUNK), rows // CHUNK)],
            ),
        ]
        return [
            pltpu.make_async_copy(source, target, stores.at[k, index])
            for k, (source, target) in enumerate(pairs)
        ]

    per_slot = blocks // slots

    def scan_block(index, carry):
        slot, block = lax.div(index, per_slot), lax.rem(index, per_slot)
        at = pl.multiple_of(index * rows, rows)

        @pl.when(block == 0)
        def _():
            ext[0:8, :] = jnp.zeros((8, ext.shape[1]), F32)
            state[...] = jnp.zeros_like(state)

        tokens = normed_all[
            pl.ds(2 * block, 2), pl.ds(pl.multiple_of(slot * piece, piece), piece), :
        ].reshape(rows, model)
        ext[8:, :inner] = mm(tokens, wx[...].reshape(model, inner))
        ext[8:, inner : inner + size] = mm(tokens, wb[0].reshape(model, size))
        ext[8:, inner + size :] = mm(tokens, wb[1].reshape(model, size))
        dt_arg = mm(tokens, w_dt_out[...]) + rows_out[3:4, :128]
        dt_all[pl.ds(at, rows), :] = dt_arg
        pre = taps_out[kernel : kernel + 1, :] + sum(
            taps_out[k : k + 1, :] * ext[9 - kernel + k : 9 - kernel + k + rows, :]
            for k in range(kernel)
        )
        conv_in[pl.ds(at, rows), :] = ext[8:, :inner]
        ext[0:8, :] = ext[rows : rows + 8, :]
        pre_all[pl.ds(at, rows), :] = pre
        act = pre * sigmoid(pre)
        dt_block = softplus(dt_arg)
        steps_block = dt_block * rows_out[4:5, :128]
        for sub in range(rows // CHUNK):
            part = slice(sub * CHUNK, (sub + 1) * CHUNK)
            x = act[part, :inner]
            b = act[part, inner : inner + size].astype(BF16)
            c = act[part, inner + size :].astype(BF16)
            cum = dot(ones, steps_block[part], ((1,), (0,)), lax.Precision.HIGHEST)
            cum_t = cum.T
            total = cum[CHUNK - 1 : CHUNK, :]
            x_dt = x * widen(dt_block[part], heads, head_size)
            x_dt16 = x_dt.astype(BF16)
            held = state[...]
            held16 = held.astype(BF16)
            states[index * (rows // CHUNK) + sub] = held16
            y = mm(c, held16) * widen(jnp.exp(cum), heads, head_size)
            y = y + rows_out[2:3, :inner] * x
            cb = mm_t(c, b)
            pieces = []
            for pair in range(heads // 2):
                lanes = slice(2 * pair * head_size, 2 * (pair + 1) * head_size)
                mixing = jnp.concatenate(
                    [
                        (head_decays(cum, cum_t, 2 * pair + k, causal) * cb).astype(BF16)
                        for k in range(2)
                    ],
                    axis=1,
                )
                pieces.append(
                    mm(mixing, jnp.concatenate(split_pair(x_dt16[:, lanes], head_size), axis=0))
                )
            y_all[pl.ds(pl.multiple_of(at + sub * CHUNK, CHUNK), CHUNK), :] = y + jnp.concatenate(
                pieces, axis=1
            )
            weighted = (x_dt * widen(jnp.exp(total - cum), heads, head_size)).astype(BF16)
            state[...] = held * widen(jnp.exp(total), heads, head_size) + t_mm(b, weighted)
        for copy in stored(index):
            copy.start()

        @pl.when(index == 1)
        def _():
            gate_line.wait(0)
            if depth > 2:
                gate_line.send(1)

        @pl.when(index == 2)
        def _():
            cot_pass.relay()

        if depth > 2:

            @pl.when(index == 4)
            def _():
                gate_line.wait(1)
                if depth > 3:
                    gate_line.send(2)

        @pl.when(index == 5)
        def _():
            cot_pass.last()
            out_line.wait(0)
            if depth <= 3 and depth > 2:
                out_line.send(1)

        if depth > 3:

            @pl.when(index == 6)
            def _():
                gate_line.wait(2)
                out_line.send(1)

        return carry

    lax.fori_loop(0, blocks, scan_block, 0)

    chunk_lane = lax.broadcasted_iota(jnp.int32, (CHUNK, 128), 1)
    sums[...] = jnp.zeros_like(sums)

    def gate_block(index, carry):
        slot, block = lax.div(index, per_slot), lax.rem(index, per_slot)
        at = pl.multiple_of(index * rows, rows)
        tokens = normed_all[
            pl.ds(2 * block, 2), pl.ds(pl.multiple_of(slot * piece, piece), piece), :
        ].reshape(rows, model)
        gate = mm(tokens, wg[...].reshape(model, inner))
        gate_all[pl.ds(at, rows), :] = gate
        gated = y_all[pl.ds(at, rows), :] * (gate * sigmoid(gate))
        for sub in range(rows // CHUNK):
            part = gated[sub * CHUNK : (sub + 1) * CHUNK]
            total = jnp.sum(part * part, axis=1, keepdims=True)
            sums[...] = jnp.where(chunk_lane == index * (rows // CHUNK) + sub, total, sums[...])
        if depth > 2:

            @pl.when(index == blocks // 2)
            def _():
                out_line.wait(1)
                if depth > 3:
                    out_line.send(2)

        return carry

    lax.fori_loop(0, blocks, gate_block, 0)
    save_gate = pltpu.make_async_copy(gate_all, gate_out, locals_.at[8])
    save_gate.start()
    cot_pass.end()
    kept[4].wait()
    save_cot = pltpu.make_async_copy(cot_all, cot_out, locals_.at[9])
    save_cot.start()
    if depth > 3:
        out_line.wait(2)
    save_weights = [
        pltpu.make_async_copy(source, target, locals_.at[10 + k])
        for k, (source, target) in enumerate(
            ((wg, wg_out), (wx, wx_out), (wb, wb_out), (wo, wo_out))
        )
    ]
    for copy in save_weights:
        copy.start()

    def cot_block(index, carry):
        slot, block = lax.div(index, per_slot), lax.rem(index, per_slot)
        at = pl.multiple_of(index * rows, rows)
        tokens = cot_all[
            pl.ds(2 * block, 2), pl.ds(pl.multiple_of(slot * piece, piece), piece), :
        ].reshape(rows, model)
        dgn = mm_t(tokens, wo[...].reshape(inner, model))
        dgn_all[pl.ds(at, rows), :] = dgn
        gate = gate_all[pl.ds(at, rows), :]
        gated = y_all[pl.ds(at, rows), :] * (gate * sigmoid(gate))
        cross = dgn * rows_out[1:2, :inner] * gated
        for sub in range(rows // CHUNK):
            part = cross[sub * CHUNK : (sub + 1) * CHUNK]
            total = jnp.sum(part, axis=1, keepdims=True)
            sums[...] = jnp.where(
                chunk_lane == 2 * blocks + index * (rows // CHUNK) + sub, total, sums[...]
            )
        return carry

    lax.fori_loop(0, blocks, cot_block, 0)
    save_dgn = pltpu.make_async_copy(dgn_all, dgn_out, locals_.at[14])
    save_dgn.start()
    count = 4 * blocks
    sums_in[0] = sums[...].T[:count]
    sum_copies = [
        links.copy(sums_in.at[0], sums_in.at[mask], peer[mask]) for mask in range(1, width)
    ]
    for copy in sum_copies:
        copy.start()
    for copy in sum_copies:
        copy.wait_recv()
    got = [sums_in[mask] for mask in range(width)]
    while len(got) > 1:
        got = [got[k] + got[k + 1] for k in range(0, len(got), 2)]
    squares, cross = got[0][: 2 * blocks], got[0][2 * blocks :]
    inv_gate = lax.rsqrt(squares / inner_all + EPS)
    mean = inv_gate * cross / inner_all
    norms = jnp.concatenate([inv_gate, mean, jnp.zeros((128 - count, 128), F32)], axis=0)
    norms_out[...] = norms.T

    for copies in (plane_x, plane_g, pack_line, pack_plane, sum_copies, [pair_bc]):
        for copy in copies:
            copy.wait_send()
    pl.when(jnp.logical_not(out_home))(out_pair.wait_send)
    for line in (out_line, x_line, gate_line):
        line.drain()
    x_pass.drain()
    cot_pass.drain()
    for copy in saves + [save_gate, save_cot, save_dgn] + save_weights:
        copy.wait()

    def stores_end(index, carry):
        for copy in stored(index):
            copy.wait()
        return carry

    lax.fori_loop(0, blocks, stores_end, 0)


def forward(dims, x_own, cot_own, wg_send, wx_send, wb_send, wo_own, pack, head_params, collective):
    depth, width, heads, head_size, size, kernel, own_ch, inner_all = dims
    inner = heads * head_size
    rows, model = x_own.shape
    tokens = rows * width
    wide = inner + 2 * size
    shape = jax.ShapeDtypeStruct
    chunks = tokens // CHUNK
    weights = [
        ((depth,) + wg_send.shape, BF16),
        ((depth,) + wx_send.shape, BF16),
        ((2, depth, width) + wb_send.shape[1:], BF16),
        ((depth // 2, 2) + wo_own.shape, BF16),
    ]
    kept = [
        ((tokens, inner), F32),
        ((tokens, wide), F32),
        ((tokens, 128), F32),
        ((tokens, inner), F32),
        ((tokens, inner), F32),
        ((tokens, inner), F32),
        ((chunks, size, inner), BF16),
    ]
    in_hbm = [((width, rows, model), BF16)] * 2 + weights + kept
    in_vmem = [((CHUNK, 128), F32), ((8, wide), F32), ((8, model), F32), ((model, 128), BF16)]
    return pl.pallas_call(
        functools.partial(forward_kernel, dims),
        out_shape=tuple(shape(*s) for s in in_hbm + in_vmem),
        in_specs=[INVMEM] * 8,
        out_specs=(ANY,) * len(in_hbm) + (INVMEM,) * len(in_vmem),
        scratch_shapes=[pltpu.VMEM((width, rows, model), BF16)] * 3
        + [pltpu.VMEM(*s) for s in weights]
        + [pltpu.VMEM((depth, width) + pack.shape, BF16)]
        + [pltpu.VMEM(*s) for s in kept]
        + [
            pltpu.VMEM((rows + 8, wide), F32),
            pltpu.VMEM((size, inner), F32),
            pltpu.VMEM((8, -(-own_ch * depth * width // 128) * 128), F32),
            pltpu.VMEM((CHUNK, 128), F32),
            pltpu.VMEM((width, 2 * chunks, 128), F32),
            pltpu.SemaphoreType.DMA((112,)),
            pltpu.SemaphoreType.DMA((112,)),
            pltpu.SemaphoreType.DMA((16,)),
            pltpu.SemaphoreType.DMA((5, tokens // rows)),
        ],
        compiler_params=pltpu.CompilerParams(
            collective_id=collective, has_side_effects=True, vmem_limit_bytes=VMEM_LIMIT
        ),
        name="forward_fused",
    )(x_own, cot_own, wg_send, wx_send, wb_send, wo_own, pack, head_params)


def backward_kernel(
    heads,
    head_size,
    blocks,
    cot,
    y_in,
    gate_in,
    dgn_in,
    pre_in,
    conv_in,
    dt_in,
    states,
    norms,
    w_out,
    taps,
    gains,
    head_rows,
    head_sum,
    o_parts,
    d_proj,
    d_bc,
    d_arg_out,
    g_out,
    channel_sums,
    head_sums,
    later,
    d_ext,
):
    inner = heads * head_size
    slot, step = pl.program_id(0), pl.program_id(1)
    rows = y_in.shape[0]
    size = (pre_in.shape[1] - inner) // 2

    @pl.when(step == 0)
    def _():
        later[...] = jnp.zeros_like(later)
        d_ext[rows:, :] = jnp.zeros((8, inner), F32)

    @pl.when((step == 0) & (slot == 0))
    def _():
        g_out[...] = jnp.zeros_like(g_out)
        channel_sums[...] = jnp.zeros_like(channel_sums)
        head_sums[...] = jnp.zeros_like(head_sums)

    gate = gate_in[...]
    gate_sig = sigmoid(gate)
    gate_act = gate * gate_sig
    y = y_in[...]
    inv = norms[:, 0:1]
    mean = norms[:, 1:2]
    hat = y * gate_act * inv
    gate_normed = (hat * gains[0:1, :]).astype(BF16)
    o_parts[...] = mm(gate_normed, w_out[...]).astype(BF16).reshape(o_parts.shape)
    cot_rows = cot[...].reshape(rows, cot.shape[2])
    g_out[...] += t_mm(gate_normed, cot_rows)
    d_gated = inv * (dgn_in[...] * gains[0:1, :] - hat * mean)
    d_y_all = d_gated * gate_act
    d_proj[:, :inner] = (d_gated * y * gate_sig * (1.0 + gate * (1.0 - gate_sig))).astype(BF16)

    pre = pre_in[...]
    pre_sig = sigmoid(pre)
    act = pre * pre_sig
    slope = pre_sig[:, :inner] * (1.0 + pre[:, :inner] * (1.0 - pre_sig[:, :inner]))
    dt_arg = dt_in[...]
    dt_all = softplus(dt_arg)
    steps_all = dt_all * head_rows[1:2, :]
    causal = triangles()
    ones = causal.astype(F32)
    before = 1.0 - ones.T

    def head_totals(values):
        return dot(values, head_sum[...], ((1,), (0,)), lax.Precision.HIGHEST)

    for sub in reversed(range(rows // CHUNK)):
        part = slice(sub * CHUNK, (sub + 1) * CHUNK)
        x = act[part, :inner]
        b = act[part, inner : inner + size].astype(BF16)
        c = act[part, inner + size :].astype(BF16)
        dt = dt_all[part]
        cum = dot(ones, steps_all[part], ((1,), (0,)), lax.Precision.HIGHEST)
        cum_t = cum.T
        total = cum[CHUNK - 1 : CHUNK, :]
        dt_wide = widen(dt, heads, head_size)
        x_dt = x * dt_wide
        x_dt16 = x_dt.astype(BF16)
        d_y = d_y_all[part]
        d_y16 = d_y.astype(BF16)
        cum_wide = widen(jnp.exp(cum), heads, head_size)
        d_read = (d_y * cum_wide).astype(BF16)
        out_wide = widen(jnp.exp(total - cum), heads, head_size)
        held16 = states[sub]
        read = mm(c, held16) * cum_wide
        grown = later[...]
        grown16 = grown.astype(BF16)
        d_x_later = out_wide * mm(b, grown16)
        d_b = mm_t(grown16, (x_dt * out_wide).astype(BF16))
        d_c = mm_t(held16, d_read)
        later[...] = grown * widen(jnp.exp(total), heads, head_size) + t_mm(c, d_read)
        cb = mm_t(c, b)
        d_cb = jnp.zeros((CHUNK, CHUNK), F32)
        pieces = []
        for pair in range(heads // 2):
            lanes = slice(2 * pair * head_size, 2 * (pair + 1) * head_size)
            d_y_split = split_pair(d_y16[:, lanes], head_size)
            mixing = []
            for k in range(2):
                decay = head_decays(cum, cum_t, 2 * pair + k, causal)
                mixing.append((decay * cb).astype(BF16))
                d_cb = d_cb + decay * mm_t(d_y_split[k], x_dt16[:, lanes])
            pieces.append(
                t_mm(jnp.concatenate(mixing, axis=0), jnp.concatenate(d_y_split, axis=0))
            )
        d_x_near = jnp.concatenate(pieces, axis=1)
        d_x_dt = d_x_later + d_x_near
        d_cb16 = d_cb.astype(BF16)
        d_b = d_b + t_mm(c, d_cb16)
        d_c = d_c + dot(b, d_cb16, ((0,), (1,)))
        d_bc[:size, part] = d_b.astype(BF16)
        d_bc[size:, part] = d_c.astype(BF16)
        skip = gains[1:2, :]
        d_x = d_x_dt * dt_wide + skip * d_y
        near = y[part] - skip * x - read
        cross_wide = (
            d_y * read + d_y16.astype(F32) * near - x_dt16.astype(F32) * d_x_near
        )
        d_dt_direct = head_totals(x * d_x_dt)
        d_cum = head_totals(cross_wide)
        through = head_totals(x_dt * d_x_later)
        over = head_totals(
            jnp.broadcast_to(jnp.sum(grown * held16.astype(F32), axis=0, keepdims=True), (8, inner))
        )
        d_log = (
            dot(ones, d_cum, ((0,), (0,)), lax.Precision.HIGHEST)
            + dot(before, through, ((1,), (0,)), lax.Precision.HIGHEST)
            + over[0:1, :] * jnp.exp(total)
        )
        d_dt = d_dt_direct + head_rows[1:2, :] * d_log
        d_arg = d_dt * sigmoid(dt_arg[part])
        d_arg_out[part, :] = d_arg.astype(BF16)
        head_sums[0:1, :] += jnp.sum(d_arg, axis=0, keepdims=True)
        head_sums[1:2, :] += jnp.sum(d_log * dt, axis=0, keepdims=True)
        channel_sums[5:6, :] += jnp.sum(d_y * x, axis=0, keepdims=True)
        d_ext[part, :] = d_x * slope[part]

    kernel = 4
    d_conv = jnp.zeros((rows, inner), F32)
    x_in = conv_in[...]
    for k in range(kernel):
        moved = d_ext[kernel - 1 - k : kernel - 1 - k + rows, :]
        d_conv = d_conv + taps[k : k + 1, :inner] * moved
        channel_sums[k : k + 1, :] += jnp.sum(moved * x_in, axis=0, keepdims=True)
    channel_sums[4:5, :] += jnp.sum(d_ext[0:rows, :], axis=0, keepdims=True)
    d_proj[:, inner:] = d_conv.astype(BF16)
    d_ext[rows:, :] = d_ext[0:8, :]


def weight_kernel(normed, d_proj, d_small, w_cat, d_parts, g_in):
    step = pl.program_id(0) * pl.num_programs(1) + pl.program_id(1)

    @pl.when(step == 0)
    def _():
        g_in[...] = jnp.zeros_like(g_in)

    rows = d_proj.shape[0]
    wide = d_proj.shape[1]
    tokens = normed[...].reshape(rows, normed.shape[2])
    g_in[:, :wide] += t_mm(tokens, d_proj[...])
    g_in[:, wide:] += t_mm(tokens, d_small[...])
    both = jnp.concatenate([d_proj[...], d_small[...]], axis=1)
    d_parts[...] = mm_t(both, w_cat[...]).astype(BF16).reshape(d_parts.shape)


def fast_body(
    depth,
    width,
    block_input,
    cotangent,
    lengths,
    in_weight,
    out_weight,
    norm_gain,
    gate_gain,
    conv_weight,
    conv_bias,
    dt_bias,
    a_log,
    d_skip,
):
    slots, piece, model = block_input.shape
    heads_all = dt_bias.shape[0]
    out_rows = out_weight.shape[0]
    in_rows = in_weight.shape[0]
    inner_all = out_rows * depth * width
    head_size = inner_all // heads_all
    taps_count = conv_weight.shape[0]
    channels = conv_weight.shape[1] * depth * width
    size = (channels - inner_all) // 2
    heads = heads_all // width
    inner = heads * head_size
    plane = width // 2
    half = depth // 2
    pair_rows = 2 * out_rows
    row, place = lax.axis_index("dp"), lax.axis_index("seq")
    core, chip = lax.rem(place, 2), lax.div(place, 2)
    slot_len = piece * width
    tokens = slots * slot_len

    def by_owner(values, axis):
        shape = values.shape
        return values.reshape(shape[:axis] + (2, half, plane, pair_rows) + shape[axis + 1 :])

    def mine(values):
        split = by_owner(values, values.ndim - 1)
        at = values.ndim - 1
        split = lax.dynamic_index_in_dim(split, core, at, False)
        split = lax.dynamic_index_in_dim(split, chip, at + 1, False)
        return split.reshape(values.shape[:-1] + (inner,))

    def my_heads(values):
        group = pair_rows // head_size
        at = values.ndim - 1
        split = values.reshape(values.shape[:-1] + (2, half, plane, group))
        split = lax.dynamic_index_in_dim(split, core, at, False)
        split = lax.dynamic_index_in_dim(split, chip, at + 1, False)
        return split.reshape(values.shape[:-1] + (heads,))

    gate_cols = inner_all
    conv_cols = gate_cols + inner_all
    bc_cols = conv_cols + 2 * size
    own_ch = conv_bias.shape[0]

    def padded(values, lanes=128):
        return jnp.pad(values, ((0, 0), (0, lanes - values.shape[1])))

    def placed(values, top):
        return jnp.pad(
            values, ((top, 16 + in_rows - top - values.shape[0]), (0, 128 - values.shape[1]))
        )

    pack = (
        placed(in_weight[:, bc_cols:], 0)
        + placed(conv_weight, in_rows)
        + placed(conv_bias[None], in_rows + taps_count)
        + placed(gate_gain[None], in_rows + 5)
        + placed(norm_gain[None], in_rows + 6)
    )
    head_params = jnp.pad(
        jnp.stack([dt_bias, a_log, d_skip]), ((0, 5), (0, 128 - heads_all))
    )
    input_f = block_input.astype(F32)
    inv_rms = lax.rsqrt(jnp.mean(input_f * input_f, axis=-1, keepdims=True) + EPS)
    positions = place * piece + jnp.arange(piece, dtype=jnp.int32)
    live = (positions[None, :] < lengths[:, None]).astype(BF16)
    masked = cotangent * live[..., None]

    def cols_for_all(values):
        split = by_owner(values, 1)
        return jnp.transpose(split, (3, 1, 0, 2, 4)).reshape(width, in_rows, inner)

    w_bc_send = jnp.swapaxes(in_weight[:, conv_cols:bc_cols].reshape(in_rows, 2, size), 0, 1)
    tokens_dev = slots * piece
    dims = (depth, width, heads, head_size, size, taps_count, own_ch, inner_all)
    (
        normed_all,
        cot_all,
        w_gate,
        w_x,
        w_bc,
        w_out,
        conv_in,
        pre,
        dt_arg,
        gate,
        y,
        dgn,
        states,
        norms,
        taps,
        param_rows,
        w_dt,
    ) = forward(
        dims,
        block_input.reshape(tokens_dev, model),
        masked.reshape(tokens_dev, model),
        cols_for_all(in_weight[:, :gate_cols]),
        cols_for_all(in_weight[:, gate_cols:conv_cols]),
        w_bc_send,
        out_weight,
        pack,
        head_params,
        2,
    )
    w_in = jnp.concatenate([w_gate.reshape(model, inner), w_x.reshape(model, inner)], axis=1)
    w_bc = w_bc.reshape(2, model, size)
    w_out = w_out.reshape(inner, model)
    norm_all = param_rows[0].reshape(1, 1, model)
    gains = jnp.pad(param_rows[1:3, :inner], ((0, 6), (0, 0)))
    rates = param_rows[4:5, :heads]
    head_rows = jnp.pad(param_rows[3:5, :128], ((0, 6), (0, 0)))
    head_sum = padded((jnp.arange(inner)[:, None] // head_size == jnp.arange(heads)).astype(F32))
    chunks = tokens // CHUNK
    norms = padded(jnp.stack([norms.T[:chunks].reshape(-1), norms.T[chunks : 2 * chunks].reshape(-1)], axis=1))

    rows = 2 * piece
    blocks = slot_len // rows
    shape = jax.ShapeDtypeStruct
    wide = inner + 2 * size

    def flat(cols, order):
        return pl.BlockSpec((rows, cols), lambda s, i: (s * blocks + order(i), 0))

    def by_piece(order):
        return pl.BlockSpec((2, piece, model), lambda s, i: (order(i), s, 0))

    def whole(values):
        return pl.BlockSpec(values.shape, lambda s, i: (0,) * values.ndim)

    def ahead(i):
        return i

    def behind(i):
        return blocks - 1 - i

    o_parts, d_proj, d_bc, d_arg, g_out, channel_sums, head_sums = pl.pallas_call(
        functools.partial(backward_kernel, heads, head_size, blocks),
        grid=(slots, blocks),
        out_shape=(
            shape(normed_all.shape, BF16),
            shape((tokens, 2 * inner), BF16),
            shape((2 * size, tokens), BF16),
            shape((tokens, 128), BF16),
            shape((inner, model), F32),
            shape((8, inner), F32),
            shape((8, 128), F32),
        ),
        in_specs=[
            by_piece(behind),
            flat(inner, behind),
            flat(inner, behind),
            flat(inner, behind),
            flat(wide, behind),
            flat(inner, behind),
            flat(128, behind),
            pl.BlockSpec((rows // CHUNK, size, inner), lambda s, i: (s * blocks + behind(i), 0, 0)),
            flat(128, behind),
        ]
        + [whole(v) for v in (w_out, taps, gains, head_rows, head_sum)],
        out_specs=(
            by_piece(behind),
            flat(2 * inner, behind),
            pl.BlockSpec((2 * size, rows), lambda s, i: (0, s * blocks + behind(i))),
            flat(128, behind),
            pl.BlockSpec((inner, model), lambda s, i: (0, 0)),
            pl.BlockSpec((8, inner), lambda s, i: (0, 0)),
            pl.BlockSpec((8, 128), lambda s, i: (0, 0)),
        ),
        scratch_shapes=[
            pltpu.VMEM((size, inner), F32),
            pltpu.VMEM((rows + 8, inner), F32),
        ],
        compiler_params=pltpu.CompilerParams(vmem_limit_bytes=VMEM_LIMIT),
        name="block_backward",
    )(
        cot_all,
        y,
        gate,
        dgn,
        pre,
        conv_in,
        dt_arg,
        states,
        norms,
        w_out,
        taps,
        gains,
        head_rows,
        head_sum,
    )

    bc_own = 2 * size // width
    d_bc_own = plane_rows(d_bc.reshape(width, bc_own, tokens), 4).T
    pre_own = lax.dynamic_slice_in_dim(pre, inner + place * bc_own, bc_own, 1)
    sig = jax.nn.sigmoid(pre_own)
    d_pre = (d_bc_own * sig * (1.0 + pre_own * (1.0 - sig))).reshape(slots, slot_len, bc_own)
    w_bc_own = lax.dynamic_slice_in_dim(
        jnp.swapaxes(w_bc, 0, 1).reshape(model, 2 * size), place * bc_own, bc_own, 1
    )
    bc_in = mm(
        jnp.transpose(normed_all.reshape(width, slots, piece, model), (1, 0, 2, 3)).reshape(
            tokens, model
        ),
        w_bc_own,
    ).reshape(slots, slot_len, bc_own)
    taps_own = lax.dynamic_slice_in_dim(taps, inner + place * bc_own, bc_own, 1)
    moved = [
        jnp.pad(d_pre[:, taps_count - 1 - k :], ((0, 0), (0, taps_count - 1 - k), (0, 0)))
        for k in range(taps_count)
    ]
    d_bc_in = sum(taps_own[k] * moved[k] for k in range(taps_count))
    bc_sums = jnp.stack(
        [jnp.sum(moved[k] * bc_in, axis=(0, 1)) for k in range(taps_count)]
        + [jnp.sum(d_pre, axis=(0, 1))]
    )
    d_small = padded(
        jnp.concatenate(
            [d_bc_in.reshape(tokens, bc_own).astype(BF16), d_arg[:, :heads]], axis=1
        )
    )
    w_cat = jnp.concatenate(
        [w_in, padded(jnp.concatenate([w_bc_own, w_dt[:, :heads]], axis=1))], axis=1
    )

    d_parts, g_in = pl.pallas_call(
        weight_kernel,
        grid=(slots, blocks),
        out_shape=(shape(normed_all.shape, BF16), shape((model, 2 * inner + 128), F32)),
        in_specs=[by_piece(ahead), flat(2 * inner, ahead), flat(128, ahead), whole(w_cat)],
        out_specs=(
            by_piece(ahead),
            pl.BlockSpec((model, 2 * inner + 128), lambda s, i: (0, 0)),
        ),
        compiler_params=pltpu.CompilerParams(vmem_limit_bytes=VMEM_LIMIT),
        name="weight_backward",
    )(normed_all, d_proj, d_small, w_cat)

    skip_sum = jnp.sum(channel_sums[5].reshape(heads, head_size), axis=1)
    head_part = jnp.stack([head_sums[0, :heads], head_sums[1, :heads] * rates[0], skip_sum])
    small = jnp.concatenate(
        [
            jnp.concatenate([channel_sums[:5], bc_sums], axis=1),
            jnp.pad(head_part, ((0, 0), (0, inner + bc_own - heads))),
        ],
        axis=0,
    )
    lanes = -(-small.shape[1] // 128) * 128
    smalls = jnp.sum(spread(padded(small, lanes), (depth, width), 5), axis=0)

    def to_whole(values, group):
        count = values.shape[1]
        split = values.reshape(plane, 2, count, half, group)
        return jnp.transpose(split, (2, 1, 3, 0, 4)).reshape(count, -1)

    conv_x = to_whole(smalls[:, :5, :inner], pair_rows)
    conv_bc = jnp.swapaxes(smalls[:, :5, inner : inner + bc_own], 0, 1).reshape(5, 2 * size)
    conv_grads = lax.dynamic_slice_in_dim(
        jnp.concatenate([conv_x, conv_bc], axis=1), (row * width + place) * own_ch, own_ch, 1
    )
    head_grads = to_whole(smalls[:, 5:8, :heads], pair_rows // head_size)

    d_total, o_total, in_total, out_grad = scatter(
        depth,
        d_parts,
        o_parts,
        g_in.reshape(depth, model // depth, 2 * inner + 128),
        g_out.reshape(half, pair_rows, model),
        6,
    )
    in_f = in_total.astype(F32)

    def cols_from_all(values):
        split = values.reshape(plane, 2, in_rows, half, pair_rows)
        return jnp.transpose(split, (2, 1, 3, 0, 4)).reshape(in_rows, inner_all)

    dt_cols = in_f[:, :, 2 * inner + bc_own : 2 * inner + bc_own + heads]
    dt_cols = jnp.swapaxes(to_whole(jnp.swapaxes(dt_cols, 1, 1), pair_rows // head_size), 0, 0)
    in_grad = jnp.concatenate(
        [
            cols_from_all(in_f[:, :, :inner]),
            cols_from_all(in_f[:, :, inner : 2 * inner]),
            jnp.swapaxes(in_f[:, :, 2 * inner : 2 * inner + bc_own], 0, 1).reshape(
                in_rows, 2 * size
            ),
            dt_cols,
        ],
        axis=1,
    )
    norm_grad = jnp.sum(in_grad * in_weight.astype(F32), axis=1) / norm_gain.astype(F32)
    gate_grad = jnp.sum(out_grad * out_weight.astype(F32), axis=1) / gate_gain.astype(F32)

    output = (input_f + o_total.reshape(slots, piece, model)).astype(BF16)
    in_hat = input_f * inv_rms
    d_h = d_total.reshape(slots, piece, model) * norm_all.astype(F32)
    input_grad = inv_rms * (d_h - in_hat * jnp.mean(d_h * in_hat, axis=-1, keepdims=True))
    input_grad = (input_grad + masked.astype(F32)).astype(BF16)
    return (
        output,
        input_grad,
        in_grad,
        out_grad,
        norm_grad,
        gate_grad,
        conv_grads[:4],
        conv_grads[4],
        head_grads[0],
        head_grads[1],
        head_grads[2],
    )


def heads_fit(depth, width, arrays):
    block_input, out_weight, dt_bias = arrays[0], arrays[4], arrays[9]
    pair_rows = 2 * out_weight.shape[0]
    head_size = out_weight.shape[0] * depth * width // dt_bias.shape[0]
    return (
        width == 8
        and depth % 2 == 0
        and pair_rows % head_size == 0
        and (depth // 2 * pair_rows) % 128 == 0
        and block_input.shape[1] % CHUNK == 0
        and 2 * head_size == CHUNK
    )


def solution(mesh):
    placed = (
        P("dp", "seq", None),
        P("dp", "seq", None),
        P("dp"),
        P(("dp", "seq"), None),
        P(("dp", "seq"), None),
        P(("dp", "seq")),
        P(("dp", "seq")),
        P(None, ("dp", "seq")),
        P(("dp", "seq")),
        P(),
        P(),
        P(),
    )
    depth, width = mesh.shape["dp"], mesh.shape["seq"]

    def either(*arrays):
        if heads_fit(depth, width, arrays):
            return fast_body(depth, width, *arrays)
        return body(*arrays)

    return jax.shard_map(
        either,
        mesh=mesh,
        in_specs=placed,
        out_specs=(
            P("dp", "seq", None),
            P("dp", "seq", None),
            P(("dp", "seq"), None),
            P(("dp", "seq"), None),
            P(("dp", "seq")),
            P(("dp", "seq")),
            P(None, ("dp", "seq")),
            P(("dp", "seq")),
            P(),
            P(),
            P(),
        ),
        check_vma=False,
    )
```

```python
import functools

import jax
import jax.numpy as jnp
from jax import lax
from jax.experimental import pallas as pl
from jax.experimental.pallas import tpu as pltpu
from jax.sharding import PartitionSpec as P

SLOTS_MB = 1


EPS = 1e-05
HIGH = lax.Precision.HIGHEST


def from_behind(value, axis, steps):
    count = lax.axis_size(axis)
    leading, last = (max(0, -steps), min(count, count - steps))
    return lax.ppermute(value, axis, [(source, source + steps) for source in range(leading, last)])


def carried_in(value, axis, join, neutral, backward):
    count = lax.axis_size(axis)
    place = lax.axis_index(axis)
    ahead = count - 1 - place if backward else place
    gathered = jax.tree.map(
        lambda a, kind: lax.all_gather(a.astype(kind), axis),
        value,
        jax.tree.map(lambda a: jnp.bfloat16 if a.dtype == jnp.float32 else a.dtype, value),
    )
    state = jax.tree.map(lambda a, e: jnp.zeros_like(a) + jnp.asarray(e, a.dtype), value, neutral)

    def one(lap, state):
        source = count - 1 - lap if backward else lap
        return join(
            state,
            jax.tree.map(
                lambda a, own: lax.dynamic_index_in_dim(a, source, 0, False).astype(own.dtype),
                gathered,
                value,
            ),
        )

    return lax.fori_loop(0, ahead, one, state)


def as_sent(value):

    def short(part):
        return part.astype(jnp.bfloat16) if part.dtype == jnp.float32 else part

    return jax.tree.map(short, value)


def link_states(earlier, later):
    return (earlier[0] * later[0], later[0][:, :, None, None] * earlier[1] + later[1])


def silu_slope(values):
    sigma = jax.nn.sigmoid(values)
    return sigma * (1.0 + values * (1.0 - sigma))


def rows_product(left, right):
    return lax.dot_general(
        left, right, (((0,), (0,)), ((), ())), preferred_element_type=jnp.float32
    )


def cols_product(left, right):
    return lax.dot_general(
        left, right, (((1,), (1,)), ((), ())), preferred_element_type=jnp.float32
    )


def add_pair(first, second):
    return first + second


def first_total(stacked):
    return jnp.sum(stacked, axis=0)


def owner_sums(grads):
    lifted = tuple((grad[None] for grad in grads))
    by_data = (
        lax.all_to_all(lifted[0], "dp", split_axis=1, concat_axis=0, tiled=True),
        lax.all_to_all(lifted[1], "dp", split_axis=1, concat_axis=0, tiled=True),
        lax.all_to_all(lifted[2], "dp", split_axis=1, concat_axis=0, tiled=True),
        lax.all_to_all(lifted[3], "dp", split_axis=1, concat_axis=0, tiled=True),
        lax.all_to_all(lifted[4], "dp", split_axis=1, concat_axis=0, tiled=True),
        lax.all_to_all(lifted[5], "dp", split_axis=1, concat_axis=0, tiled=True),
    )
    partial_value = tuple((first_total(stacked)[None] for stacked in by_data))
    by_piece = (
        lax.all_to_all(partial_value[0], "seq", split_axis=1, concat_axis=0, tiled=True),
        lax.all_to_all(partial_value[1], "seq", split_axis=1, concat_axis=0, tiled=True),
        lax.all_to_all(partial_value[2], "seq", split_axis=1, concat_axis=0, tiled=True),
        lax.all_to_all(partial_value[3], "seq", split_axis=1, concat_axis=0, tiled=True),
        lax.all_to_all(partial_value[4], "seq", split_axis=1, concat_axis=0, tiled=True),
        lax.all_to_all(partial_value[5], "seq", split_axis=1, concat_axis=0, tiled=True),
    )
    return tuple((first_total(stacked) for stacked in by_piece))


def forward_pass(slot_in, weights, head_params):
    in_full, out_full, norm_full, gate_full, conv_full, bias_full = weights
    dt_shift, log_rate, skip_gain = head_params
    slot_count, piece_len, model_width = slot_in.shape
    inner_width = out_full.shape[0]
    channels = conv_full.shape[1]
    kernel = conv_full.shape[0]
    head_count = dt_shift.shape[0]
    head_size = inner_width // head_count
    state_size = (channels - inner_width) // 2
    input_f = slot_in.astype(jnp.float32)
    inv_rms = lax.rsqrt(jnp.mean(input_f * input_f, axis=-1, keepdims=True) + EPS)
    normed = (input_f * inv_rms * norm_full.astype(jnp.float32)).astype(jnp.bfloat16)
    projected = jnp.dot(
        normed.reshape(-1, model_width), in_full, preferred_element_type=jnp.float32
    ).reshape(slot_count, piece_len, -1)
    gate_part = projected[..., :inner_width]
    conv_in = projected[..., inner_width : inner_width + channels]
    dt_arg = projected[..., inner_width + channels :] + dt_shift
    rim_rows = from_behind(
        conv_in[:, piece_len - kernel + 1 :].astype(jnp.bfloat16), "seq", 1
    ).astype(jnp.float32)
    extended = jnp.concatenate([rim_rows, conv_in], axis=1)
    conv_taps = conv_full.astype(jnp.float32)
    pre_act = bias_full.astype(jnp.float32) + sum(
        (
            conv_taps[tap_index] * extended[:, tap_index : tap_index + piece_len]
            for tap_index in range(kernel)
        )
    )
    activated = jax.nn.silu(pre_act)
    x_heads = activated[..., :inner_width].reshape(slot_count, piece_len, head_count, head_size)
    b_rows = activated[..., inner_width : inner_width + state_size]
    c_rows = activated[..., inner_width + state_size :]
    dt_vals = jax.nn.softplus(dt_arg)
    decay_rates = -jnp.exp(log_rate)
    log_cum = jnp.cumsum(dt_vals * decay_rates, axis=1)
    log_tot = log_cum[:, -1]
    weights_in = jnp.exp(log_tot[:, None] - log_cum) * dt_vals
    local_state = jnp.einsum(
        "sthp,stn->shpn", weights_in[..., None] * x_heads, b_rows, precision=HIGH
    )
    carry_decay = jnp.exp(log_tot)
    neutral = (jnp.ones_like(carry_decay), jnp.zeros_like(local_state))
    _, start_state = carried_in((carry_decay, local_state), "seq", link_states, neutral, False)
    spots = jnp.arange(piece_len)
    causal = spots[:, None] >= spots[None, :]
    cum_heads = jnp.swapaxes(log_cum, 1, 2)
    gap_vals = jnp.where(causal, cum_heads[..., :, None] - cum_heads[..., None, :], 0.0)
    decay_mat = jnp.where(causal, jnp.exp(gap_vals), 0.0)
    cb_mat = jnp.einsum("stn,sun->stu", c_rows, b_rows, precision=HIGH)
    dt_cols = jnp.swapaxes(dt_vals, 1, 2)[:, :, None, :]
    mixing = decay_mat * cb_mat[:, None] * dt_cols
    y_intra = jnp.einsum("shtu,suhp->sthp", mixing, x_heads, precision=HIGH)
    state_read = jnp.einsum("stn,shpn->sthp", c_rows, start_state, precision=HIGH)
    exp_cum = jnp.exp(log_cum)
    y_heads = y_intra + exp_cum[..., None] * state_read + skip_gain[:, None] * x_heads
    y_flat = y_heads.reshape(slot_count, piece_len, inner_width)
    gate_act = jax.nn.silu(gate_part)
    gated_out = y_flat * gate_act
    inv_gate = lax.rsqrt(jnp.mean(gated_out * gated_out, axis=-1, keepdims=True) + EPS)
    gate_normed = (gated_out * inv_gate * gate_full.astype(jnp.float32)).astype(jnp.bfloat16)
    mixed = jnp.dot(
        gate_normed.reshape(-1, inner_width), out_full, preferred_element_type=jnp.float32
    )
    output = (input_f + mixed.reshape(slot_count, piece_len, model_width)).astype(jnp.bfloat16)
    saved = dict(
        input_f=input_f,
        inv_rms=inv_rms,
        normed=normed,
        gate_part=gate_part,
        dt_arg=dt_arg,
        extended=extended,
        pre_act=pre_act,
        x_heads=x_heads,
        b_rows=b_rows,
        c_rows=c_rows,
        dt_vals=dt_vals,
        log_cum=log_cum,
        log_tot=log_tot,
        weights_in=weights_in,
        carry_decay=carry_decay,
        start_state=start_state,
        decay_mat=decay_mat,
        cb_mat=cb_mat,
        dt_cols=dt_cols,
        mixing=mixing,
        state_read=state_read,
        exp_cum=exp_cum,
        y_flat=y_flat,
        gate_act=gate_act,
        gated_out=gated_out,
        inv_gate=inv_gate,
        gate_normed=gate_normed,
    )
    return (output, saved)


def backward_pass(saved, slot_cot, live, weights, head_params):
    in_full, out_full, norm_full, gate_full, conv_full, bias_full = weights
    dt_shift, log_rate, skip_gain = head_params
    slot_count, piece_len, model_width = slot_cot.shape
    inner_width = out_full.shape[0]
    kernel = conv_full.shape[0]
    x_heads = saved["x_heads"]
    b_rows = saved["b_rows"]
    c_rows = saved["c_rows"]
    dt_vals = saved["dt_vals"]
    log_cum = saved["log_cum"]
    weights_in = saved["weights_in"]
    carry_decay = saved["carry_decay"]
    start_state = saved["start_state"]
    decay_mat = saved["decay_mat"]
    cb_mat = saved["cb_mat"]
    dt_cols = saved["dt_cols"]
    decay_rates = -jnp.exp(log_rate)
    masked_cot = slot_cot * live[..., None].astype(jnp.bfloat16)
    cot_rows = masked_cot.reshape(-1, model_width)
    d_gn = cols_product(cot_rows, out_full).reshape(slot_count, piece_len, inner_width)
    gate_hat = saved["gated_out"] * saved["inv_gate"]
    grad_ggain = jnp.sum(d_gn * gate_hat, axis=(0, 1))
    d_hat = d_gn * gate_full.astype(jnp.float32)
    d_gated = saved["inv_gate"] * (
        d_hat - gate_hat * jnp.mean(d_hat * gate_hat, axis=-1, keepdims=True)
    )
    d_gate_part = d_gated * saved["y_flat"] * silu_slope(saved["gate_part"])
    d_heads = (d_gated * saved["gate_act"]).reshape(x_heads.shape)
    grad_skip = jnp.sum(d_heads * x_heads, axis=(0, 1, 3))
    exp_cum = saved["exp_cum"]
    d_read = d_heads * exp_cum[..., None]
    d_cvals = jnp.einsum("sthp,shpn->stn", d_read, start_state, precision=HIGH)
    d_start = jnp.einsum("sthp,stn->shpn", d_read, c_rows, precision=HIGH)
    d_cum = jnp.sum(d_heads * saved["state_read"], axis=-1) * exp_cum
    d_mixing = jnp.einsum("sthp,suhp->shtu", d_heads, x_heads, precision=HIGH)
    d_x = skip_gain[:, None] * d_heads + jnp.einsum(
        "shtu,sthp->suhp", saved["mixing"], d_heads, precision=HIGH
    )
    d_decay = d_mixing * cb_mat[:, None] * dt_cols
    d_cb = jnp.sum(d_mixing * decay_mat * dt_cols, axis=1)
    d_dt = jnp.swapaxes(jnp.sum(d_mixing * decay_mat * cb_mat[:, None], axis=2), 1, 2)
    spread = d_decay * decay_mat
    d_cum = d_cum + jnp.swapaxes(jnp.sum(spread, axis=3) - jnp.sum(spread, axis=2), 1, 2)
    d_cvals = d_cvals + jnp.einsum("stu,sun->stn", d_cb, b_rows, precision=HIGH)
    d_bvals = jnp.einsum("stu,stn->sun", d_cb, c_rows, precision=HIGH)
    neutral = (jnp.ones_like(carry_decay), jnp.zeros_like(d_start))
    _, later_grad = carried_in((carry_decay, d_start), "seq", link_states, neutral, True)
    d_tot = jnp.sum(later_grad * start_state, axis=(2, 3)) * carry_decay
    grad_proj_b = jnp.einsum("shpn,stn->sthp", later_grad, b_rows, precision=HIGH)
    d_x = d_x + weights_in[..., None] * grad_proj_b
    d_weights = jnp.sum(grad_proj_b * x_heads, axis=-1)
    d_bvals = d_bvals + jnp.einsum(
        "sthp,shpn->stn", weights_in[..., None] * x_heads, later_grad, precision=HIGH
    )
    d_dt = d_dt + d_weights * jnp.exp(saved["log_tot"][:, None] - log_cum)
    through = d_weights * weights_in
    d_tot = d_tot + jnp.sum(through, axis=1)
    last_row = (jnp.arange(piece_len) == piece_len - 1).astype(jnp.float32)
    d_cum = d_cum - through + last_row[None, :, None] * d_tot[:, None, :]
    d_log = lax.cumsum(d_cum, axis=1, reverse=True)
    d_dt = d_dt + d_log * decay_rates
    grad_alog = jnp.sum(d_log * dt_vals, axis=(0, 1)) * decay_rates
    d_arg = d_dt * jax.nn.sigmoid(saved["dt_arg"])
    grad_dtb = jnp.sum(d_arg, axis=(0, 1))
    d_act = jnp.concatenate(
        [d_x.reshape(slot_count, piece_len, inner_width), d_bvals, d_cvals], axis=-1
    )
    d_pre = d_act * silu_slope(saved["pre_act"])
    grad_cbias = jnp.sum(d_pre, axis=(0, 1))
    extended = saved["extended"]
    grad_conv = jnp.stack(
        [
            jnp.sum(d_pre * extended[:, tap_index : tap_index + piece_len], axis=(0, 1))
            for tap_index in range(kernel)
        ]
    )
    conv_taps = conv_full.astype(jnp.float32)
    d_ext = sum(
        (
            jnp.pad(
                conv_taps[tap_index] * d_pre, ((0, 0), (tap_index, kernel - 1 - tap_index), (0, 0))
            )
            for tap_index in range(kernel)
        )
    )
    back_rim = from_behind(as_sent(d_ext[:, : kernel - 1]), "seq", -1)
    d_conv_in = d_ext[:, kernel - 1 :] + jnp.pad(
        back_rim, ((0, 0), (piece_len - kernel + 1, 0), (0, 0))
    )
    d_proj = jnp.concatenate([d_gate_part, d_conv_in, d_arg], axis=-1).astype(jnp.bfloat16)
    d_proj = d_proj.reshape(slot_count * piece_len, -1)
    d_normed = cols_product(d_proj, in_full).reshape(slot_count, piece_len, model_width)
    in_hat = saved["input_f"] * saved["inv_rms"]
    grad_ngain = jnp.sum(d_normed * in_hat, axis=(0, 1))
    d_norm_in = d_normed * norm_full.astype(jnp.float32)
    input_grad = saved["inv_rms"] * (
        d_norm_in - in_hat * jnp.mean(d_norm_in * in_hat, axis=-1, keepdims=True)
    )
    input_grad = input_grad + masked_cot.astype(jnp.float32)
    product_rows = (
        saved["normed"].reshape(-1, model_width),
        d_proj,
        saved["gate_normed"].reshape(-1, inner_width),
        cot_rows,
    )
    small_grads = (grad_ngain, grad_ggain, grad_conv, grad_cbias)
    return (
        input_grad.astype(jnp.bfloat16),
        product_rows,
        small_grads,
        (grad_dtb, grad_alog, grad_skip),
    )


def body(
    block_input,
    cotangent,
    lengths,
    in_weight,
    out_weight,
    norm_gain,
    gate_gain,
    conv_weight,
    conv_bias,
    dt_bias,
    a_log,
    d_skip,
):
    shards = (in_weight, out_weight, norm_gain, gate_gain, conv_weight, conv_bias)
    head_params = (dt_bias, a_log, d_skip)
    piece_len = block_input.shape[1]
    batches = block_input.shape[0] // SLOTS_MB
    positions = lax.axis_index("seq") * piece_len + jnp.arange(piece_len, dtype=jnp.int32)
    held = (
        lax.all_gather(shards[0], ("dp", "seq"), axis=0, tiled=True),
        lax.all_gather(shards[1], ("dp", "seq"), axis=0, tiled=True),
        lax.all_gather(shards[2], ("dp", "seq"), axis=0, tiled=True),
        lax.all_gather(shards[3], ("dp", "seq"), axis=0, tiled=True),
        lax.all_gather(shards[4], ("dp", "seq"), axis=1, tiled=True),
        lax.all_gather(shards[5], ("dp", "seq"), axis=0, tiled=True),
    )
    outputs = []
    input_grads = []
    kept_rows = []
    small_totals = None
    head_totals = None
    for batch_index in range(batches):
        first = batch_index * SLOTS_MB
        slot_in = block_input[first : first + SLOTS_MB]
        slot_cot = cotangent[first : first + SLOTS_MB]
        live = (positions[None, :] < lengths[first : first + SLOTS_MB, None]).astype(jnp.float32)
        output, saved = forward_pass(slot_in, held, head_params)
        input_grad, product_rows, small_grads, head_grads = backward_pass(
            saved, slot_cot, live, held, head_params
        )
        outputs.append(output)
        input_grads.append(input_grad)
        kept_rows.append(product_rows)
        small_totals = (
            small_grads
            if small_totals is None
            else jax.tree.map(add_pair, small_totals, small_grads)
        )
        head_totals = (
            head_grads if head_totals is None else jax.tree.map(add_pair, head_totals, head_grads)
        )
    normed_all = jnp.concatenate([rows[0] for rows in kept_rows], axis=0)
    dproj_all = jnp.concatenate([rows[1] for rows in kept_rows], axis=0)
    gnormed_all = jnp.concatenate([rows[2] for rows in kept_rows], axis=0)
    cot_all = jnp.concatenate([rows[3] for rows in kept_rows], axis=0)
    grad_win = rows_product(normed_all, dproj_all)
    grad_wout = rows_product(gnormed_all, cot_all)
    grad_ngain, grad_ggain, grad_conv, grad_cbias = small_totals
    owned = owner_sums((grad_win, grad_wout, grad_ngain, grad_ggain, grad_conv.T, grad_cbias))
    head_sums = lax.psum(head_totals, ("dp", "seq"))
    return (
        jnp.concatenate(outputs, axis=0),
        jnp.concatenate(input_grads, axis=0),
        owned[0],
        owned[1],
        owned[2],
        owned[3],
        owned[4].T,
        owned[5],
        head_sums[0],
        head_sums[1],
        head_sums[2],
    )


F32 = jnp.float32
BF16 = jnp.bfloat16
MESH_ID = pl.DeviceIdType.MESH
ANY = pl.BlockSpec(memory_space=pl.ANY)
INVMEM = pl.BlockSpec(memory_space=pltpu.VMEM)
VMEM_LIMIT = 63 * 1024 * 1024
CHUNK = 128


def flip(place, bit):
    return place + bit - 2 * bit * lax.rem(lax.div(place, bit), 2)


def flip_all(place, mask):
    for bit in (1, 2, 4):
        if mask & bit:
            place = flip(place, bit)
    return place


class Links:
    def __init__(self, sends, recvs):
        self.sends, self.recvs, self.used = sends, recvs, 0

    def copy(self, source, target, device):
        slot = self.used
        self.used += 1
        return pltpu.make_async_remote_copy(
            src_ref=source,
            dst_ref=target,
            send_sem=self.sends.at[slot],
            recv_sem=self.recvs.at[slot],
            device_id=device,
            device_id_type=MESH_ID,
        )


def greet(devices, conditions=()):
    barrier = pltpu.get_barrier_semaphore()
    for device in devices:
        pl.semaphore_signal(barrier, inc=1, device_id=device, device_id_type=MESH_ID)
    for condition, device in conditions:

        @pl.when(condition)
        def _():
            pl.semaphore_signal(barrier, inc=1, device_id=device, device_id_type=MESH_ID)

    count = len(devices)
    for condition, _ in conditions:
        count = count + jnp.where(condition, 1, 0)
    pl.semaphore_wait(barrier, count)


def add_rows(target, first, second, step=32):
    def one(number, carry):
        rows = pl.ds(pl.multiple_of(number * step, step), step)
        target[rows] = (first[rows].astype(F32) + second[rows].astype(F32)).astype(target.dtype)
        return carry

    lax.fori_loop(0, target.shape[0] // step, one, 0)


def cast_rows(target, source, step=32):
    def one(number, carry):
        rows = pl.ds(pl.multiple_of(number * step, step), step)
        target[rows] = source[rows].astype(target.dtype)
        return carry

    lax.fori_loop(0, target.shape[0] // step, one, 0)


class LineSum:
    def __init__(
        self, links, depth, row, place, own, valid, up_in, up_out, down_in, down_out, shared=None
    ):
        self.depth, self.row, self.own, self.valid = depth, row, own, valid
        above, below = lax.min(row + 1, depth - 1), lax.max(row - 1, 0)

        def slots(ref, shift):
            return {q: ref.at[q % shared if shared else q - shift] for q in range(shift, depth - 1 + shift)}

        self.up_in, self.up_out = slots(up_in, 1), slots(up_out, 1)
        self.down_in, self.down_out = slots(down_in, 0), slots(down_out, 0)
        self.ups = {
            q: links.copy(self.up_out[q], self.up_in[q], (above, place)) for q in self.up_in
        }
        self.downs = {
            q: links.copy(self.down_out[q], self.down_in[q], (below, place)) for q in self.down_in
        }

    def up(self, q):
        row = self.row

        @pl.when(self.valid(q) & (row < q))
        def _():
            @pl.when(row == 0)
            def _():
                cast_rows(self.up_out[q], self.own(q))

            @pl.when(row > 0)
            def _():
                self.ups[q].wait_recv()
                add_rows(self.up_out[q], self.own(q), self.up_in[q])

            self.ups[q].start()

    def down(self, q):
        row, depth = self.row, self.depth

        @pl.when(self.valid(q) & (row > q))
        def _():
            @pl.when(row == depth - 1)
            def _():
                cast_rows(self.down_out[q], self.own(q))

            @pl.when(row < depth - 1)
            def _():
                self.downs[q].wait_recv()
                add_rows(self.down_out[q], self.own(q), self.down_in[q])

            self.downs[q].start()

    def step(self, number):
        up_q, down_q = self.depth - 1 - number, number

        @pl.when(self.row < self.depth // 2)
        def _():
            self.up(up_q)
            self.down(down_q)

        @pl.when(self.row >= self.depth // 2)
        def _():
            self.down(down_q)
            self.up(up_q)

    def finish(self, total):
        depth, row = self.depth, self.row
        for q in range(depth):

            @pl.when(self.valid(q) & (row == q))
            def _():
                if q > 0:
                    self.ups[q].wait_recv()
                if q < depth - 1:
                    self.downs[q].wait_recv()
                if 0 < q < depth - 1:
                    add_rows(total, self.up_in[q], self.down_in[q])
                    add_rows(total, total, self.own(q))
                elif q > 0:
                    add_rows(total, self.own(q), self.up_in[q])
                else:
                    add_rows(total, self.own(q), self.down_in[q])

    def drain(self):
        for q, copy in self.ups.items():
            pl.when(self.valid(q) & (self.row < q))(copy.wait_send)
        for q, copy in self.downs.items():
            pl.when(self.valid(q) & (self.row > q))(copy.wait_send)


class PlaneSum:
    def __init__(self, links, row, place, parts, total, pair_in, sums, relay_in, last_in):
        self.place, self.parts, self.total = place, parts, total
        self.pair_in, self.sums, self.relay_in, self.last_in = pair_in, sums, relay_in, last_in
        peer = {mask: (row, flip_all(place, mask)) for mask in range(1, 8)}
        self.peer = peer
        rows = total.shape[0] // 2
        self.halves = (pl.ds(0, rows), pl.ds(rows, rows))
        self.pair = {
            mask: links.copy(parts.at[peer[mask ^ 1][1]], pair_in.at[mask // 2], peer[1])
            for mask in (6, 2, 4, 0)
        }
        top, low = self.halves
        self.relay4 = links.copy(sums.at[3, top], relay_in.at[0], peer[4])
        self.relay2 = links.copy(sums.at[3, low], relay_in.at[1], peer[2])
        self.last2 = links.copy(sums.at[1], last_in.at[0], peer[2])
        self.last4 = links.copy(sums.at[2], last_in.at[1], peer[4])

    def begin(self):
        for copy in self.pair.values():
            copy.start()

    def chip(self, mask):
        index = mask // 2
        self.pair[mask].wait_recv()
        mine = self.parts.at[self.peer[mask][1] if mask else self.place]
        add_rows(self.sums.at[index], mine, self.pair_in.at[index])

    def first(self):
        self.chip(6)
        self.relay4.start()
        self.relay2.start()
        self.chip(2)
        self.chip(4)
        self.chip(0)

    def second(self):
        top, low = self.halves
        self.relay4.wait_recv()
        add_rows(self.sums.at[1, top], self.sums.at[1, top], self.relay_in.at[0])
        self.last2.start()
        self.relay2.wait_recv()
        add_rows(self.sums.at[2, low], self.sums.at[2, low], self.relay_in.at[1])
        self.last4.start()

    def finish(self):
        self.last2.wait_recv()
        self.last4.wait_recv()
        add_rows(self.total, self.last_in.at[0], self.last_in.at[1])
        add_rows(self.total, self.total, self.sums.at[0])

    def drain(self):
        for copy in self.pair.values():
            copy.wait_send()
        for copy in (self.relay4, self.relay2, self.last2, self.last4):
            copy.wait_send()


def dot(left, right, contract, precision=None):
    return lax.dot_general(
        left, right, (contract, ((), ())), precision=precision, preferred_element_type=F32
    )


def mm(left, right):
    return dot(left, right, ((1,), (0,)))


def mm_t(left, right):
    return dot(left, right, ((1,), (1,)))


def t_mm(left, right):
    return dot(left, right, ((0,), (0,)))


def widen(values, heads, head_size):
    rows = values.shape[0]
    lane = lax.broadcasted_iota(jnp.int32, (rows, 2 * head_size), 1)
    parts = []
    for pair in range(heads // 2):
        low = jnp.broadcast_to(values[:, 2 * pair : 2 * pair + 1], (rows, 2 * head_size))
        high = jnp.broadcast_to(values[:, 2 * pair + 1 : 2 * pair + 2], (rows, 2 * head_size))
        parts.append(jnp.where(lane < head_size, low, high))
    return jnp.concatenate(parts, axis=1)


def sigmoid(values):
    return 1.0 / (1.0 + jnp.exp(-values))


def softplus(values):
    return jnp.maximum(values, 0.0) + jnp.log1p(jnp.exp(-jnp.abs(values)))


def split_pair(values, head_size):
    lane = lax.broadcasted_iota(jnp.int32, values.shape, 1)
    zero = jnp.zeros_like(values)
    return jnp.where(lane < head_size, values, zero), jnp.where(lane < head_size, zero, values)


def triangles():
    rows = lax.broadcasted_iota(jnp.int32, (CHUNK, CHUNK), 0)
    cols = lax.broadcasted_iota(jnp.int32, (CHUNK, CHUNK), 1)
    return rows >= cols


def head_decays(cum, cum_t, head, causal):
    gap = cum[:, head : head + 1] - cum_t[head : head + 1, :]
    return jnp.exp(jnp.where(causal, gap, -1e30))


class Line:
    def __init__(self, links, depth, row, place, blocks, valid=None):
        self.depth, self.row = depth, row
        above, below = lax.min(row + 1, depth - 1), lax.max(row - 1, 0)
        self.steps = []
        for step in range(depth - 1):
            up_sent, up_got = row - step, row - 1 - step
            down_sent, down_got = row + step, row + 1 + step
            ways = []
            for sends, shard, gets, got, device in (
                ((row < depth - 1) & (up_sent >= 0), up_sent, (row > 0) & (up_got >= 0), up_got, above),
                ((row > 0) & (down_sent < depth), down_sent, (row < depth - 1) & (down_got < depth), down_got, below),
            ):
                shard = lax.clamp(0, shard, depth - 1)
                got = lax.clamp(0, got, depth - 1)
                if valid is not None:
                    sends, gets = sends & valid(shard), gets & valid(got)
                copies = [links.copy(block, block, (device, place)) for block in blocks(shard)]
                ways.append((sends, gets, copies))
            self.steps.append(ways)

    def send(self, number):
        for sends, _, copies in self.steps[number]:

            @pl.when(sends)
            def _():
                for copy in copies:
                    copy.start()

    def wait(self, number):
        for _, gets, copies in self.steps[number]:

            @pl.when(gets)
            def _():
                for copy in copies:
                    copy.wait_recv()

    def drain(self):
        for ways in self.steps:
            for sends, _, copies in ways:

                @pl.when(sends)
                def _():
                    for copy in copies:
                        copy.wait_send()


class Pass:
    def __init__(self, links, peer, place, own, everyone):
        rows = own.shape[0] // 2
        mine = everyone.at[place]
        from2, from4, far = (everyone.at[peer[mask][1]] for mask in (2, 4, 6))
        top, low = pl.ds(0, rows), pl.ds(rows, rows)
        self.kept = None
        self.to2 = links.copy(own, mine, peer[2])
        self.to4 = links.copy(own, mine, peer[4])
        self.to1 = links.copy(own, mine, peer[1])
        self.relay4 = links.copy(from2.at[top], from2.at[top], peer[4])
        self.relay2 = links.copy(from4.at[low], from4.at[low], peer[2])
        self.pair2 = links.copy(from2, from2, peer[1])
        self.pair4 = links.copy(from4, from4, peer[1])
        self.pair6 = links.copy(far.at[top], far.at[top], peer[1])
        self.pair7 = links.copy(far.at[low], far.at[low], peer[1])

    def first(self):
        self.to2.start()
        self.to4.start()
        self.to1.start()

    def relay(self):
        self.to2.wait_recv()
        self.relay4.start()
        self.to4.wait_recv()
        self.relay2.start()
        self.pair2.start()
        self.pair4.start()

    def last(self):
        self.relay4.wait_recv()
        self.pair6.start()
        self.relay2.wait_recv()
        self.pair7.start()

    def end(self):
        for copy in (self.to1, self.pair2, self.pair4, self.pair6, self.pair7):
            copy.wait_recv()

    def drain(self):
        for copy in (
            self.to2,
            self.to4,
            self.to1,
            self.relay4,
            self.relay2,
            self.pair2,
            self.pair4,
            self.pair6,
            self.pair7,
        ):
            copy.wait_send()


def lay_out(pieces, row, count):
    tiles = [None] * -(-count * len(pieces) // 128)
    for index, piece in enumerate(pieces):
        tile, shift = divmod(index * count, 128)
        moved = pltpu.roll(piece, shift, 1) if shift else piece
        lane = lax.broadcasted_iota(jnp.int32, piece.shape, 1)
        parts = [(tile, jnp.where((lane >= shift) & (lane < shift + count), moved, 0.0))]
        if shift + count > 128:
            parts.append((tile + 1, jnp.where(lane < shift + count - 128, moved, 0.0)))
        for at, part in parts:
            tiles[at] = part if tiles[at] is None else tiles[at] + part
    return tiles


def channel_windows(ref, place, plane, half, run):
    core, chip = lax.rem(place, 2), lax.div(place, 2)
    parts = []
    for j in range(half):
        start = ((core * half + j) * plane + chip) * run
        base = pl.multiple_of(lax.div(start, 128) * 128, 128)
        window = ref[:, pl.ds(base, run + 64)]
        moved = pltpu.roll(window, run, 1)
        parts.append(jnp.where(lax.rem(start, 128) == 0, window, moved)[:, :run])
    return jnp.concatenate(parts, axis=1)


def head_choice(place, plane, half, group, heads):
    core, chip = lax.rem(place, 2), lax.div(place, 2)
    head = lax.broadcasted_iota(jnp.int32, (128, 128), 0)
    lane = lax.broadcasted_iota(jnp.int32, (128, 128), 1)
    part = sum(((lane >= j * group).astype(jnp.int32) for j in range(1, half)), jnp.zeros_like(lane))
    chosen = ((core * half + part) * plane + chip) * group + lane - part * group
    return jnp.where((head == chosen) & (lane < heads), 1.0, 0.0)


def forward_kernel(
    dims,
    x_own,
    cot_own,
    wg_send,
    wx_send,
    wb_send,
    wo_own,
    pack,
    head_params,
    normed_out,
    cot_out,
    wg_out,
    wx_out,
    wb_out,
    wo_out,
    conv_out,
    pre_out,
    dt_out,
    gate_out,
    y_out,
    dgn_out,
    states_out,
    norms_out,
    taps_out,
    rows_out,
    w_dt_out,
    x_all,
    normed_all,
    cot_all,
    wg,
    wx,
    wb,
    wo,
    packs,
    conv_in,
    pre_all,
    dt_all,
    gate_all,
    y_all,
    dgn_all,
    states,
    ext,
    state,
    full,
    sums,
    sums_in,
    sends,
    recvs,
    locals_,
    stores,
):
    depth, width, heads, head_size, size, kernel, own_ch, inner_all = dims
    half, plane = depth // 2, width // 2
    inner = heads * head_size
    run = inner // half
    model = x_own.shape[1]
    piece = x_own.shape[0] // 2
    rows = 2 * piece
    slots = 2
    blocks = slots * width // 2
    row, place = lax.axis_index("dp"), lax.axis_index("seq")
    core = lax.rem(place, 2)
    links = Links(sends, recvs)
    peer = {mask: (row, flip_all(place, mask)) for mask in range(1, width)}
    line_peers = [(lax.rem(row + up, depth), place) for up in range(1, depth)]
    greet([peer[mask] for mask in range(1, width)] + line_peers)

    kept = [
        pltpu.make_async_copy(wx_send.at[place], wx.at[row, place], locals_.at[0]),
        pltpu.make_async_copy(wb_send.at[core], wb.at[core, row, place], locals_.at[1]),
        pltpu.make_async_copy(wg_send.at[place], wg.at[row, place], locals_.at[2]),
        pltpu.make_async_copy(x_own, x_all.at[place], locals_.at[3]),
        pltpu.make_async_copy(cot_own, cot_all.at[place], locals_.at[4]),
        pltpu.make_async_copy(pack, packs.at[row, place], locals_.at[5]),
    ]
    for copy in kept:
        copy.start()

    out_home = lax.div(row, half) == core
    out_block = wo.at[lax.rem(row, half), core]
    out_kept = pltpu.make_async_copy(wo_own, out_block, locals_.at[6])
    out_pair = links.copy(wo_own, out_block, peer[1])
    pl.when(out_home)(out_kept.start)
    pl.when(jnp.logical_not(out_home))(out_pair.start)

    order = (6, 2, 4, 7, 3, 5, 1)
    plane_x, plane_g = [], []
    for mask in order:
        target = peer[mask][1]
        its_core = lax.rem(target, 2)
        plane_x.append(links.copy(wx_send.at[target], wx.at[row, place], peer[mask]))
        plane_x.append(
            links.copy(wb_send.at[its_core], wb.at[its_core, row, place], peer[mask])
        )
        plane_g.append(links.copy(wg_send.at[target], wg.at[row, place], peer[mask]))
    for copy in plane_x:
        copy.start()
    pack_line = [links.copy(pack, packs.at[row, place], device) for device in line_peers]
    for copy in pack_line:
        copy.start()
    x_pass = Pass(links, peer, place, x_own, x_all)
    cot_pass = Pass(links, peer, place, cot_own, cot_all)
    x_pass.first()

    out_line = Line(
        links,
        depth,
        row,
        place,
        lambda shard: [wo.at[lax.rem(shard, half)]],
        lambda shard: lax.div(shard, half) == core,
    )
    x_line = Line(links, depth, row, place, lambda shard: [wx.at[shard], wb.at[core, shard]])
    gate_line = Line(links, depth, row, place, lambda shard: [wg.at[shard]])

    pl.when(out_home)(out_kept.wait)
    pl.when(out_home)(out_pair.wait_recv)
    out_line.send(0)
    kept[0].wait()
    kept[1].wait()
    for copy in plane_x:
        copy.wait_recv()
    x_line.send(0)
    kept[5].wait()
    for copy in pack_line:
        copy.wait_recv()
    mine = packs.at[:, place]
    pack_plane = [links.copy(mine, mine, peer[mask]) for mask in order]
    for copy in pack_plane:
        copy.start()
    for copy in plane_g:
        copy.start()
    x_pass.relay()
    x_line.wait(0)
    if depth > 2:
        x_line.send(1)
    for copy in pack_plane:
        copy.wait_recv()

    small = [
        packs[z, s, model // (depth * width) : model // (depth * width) + 16, :].astype(F32)[:8]
        for z in range(depth)
        for s in range(width)
    ]
    choice = head_choice(place, plane, half, run // head_size, heads)
    tap_tiles = lay_out(small, 0, own_ch)
    for at, tile in enumerate(tap_tiles):
        full[:, at * 128 : (at + 1) * 128] = tile
    taps_out[:, :inner] = channel_windows(full, place, plane, half, run)
    taps_out[:, inner:] = full[:, inner_all : inner_all + 2 * size]
    gate_tiles = lay_out(small, 5, inner_all // (depth * width))
    for at, tile in enumerate(gate_tiles):
        full[:, at * 128 : (at + 1) * 128] = tile
    gate_gain = channel_windows(full, place, plane, half, run)[5:6]
    norm_tiles = lay_out(small, 6, model // (depth * width))
    norm_gain = jnp.concatenate([tile[6:7] for tile in norm_tiles], axis=1)
    chosen = dot(head_params[...], choice, ((1,), (0,)), lax.Precision.HIGHEST)
    lane = lax.broadcasted_iota(jnp.int32, (1, 128), 1)
    rates = jnp.where(lane < heads, -jnp.exp(chosen[1:2]), 0.0)
    skip = widen(chosen[2:3], heads, head_size)
    dt_rows = packs[:, :, 0 : model // (depth * width), :].reshape(model, 128)
    w_dt_out[...] = mm(dt_rows, choice.astype(BF16)).astype(BF16)
    rows_out[...] = jnp.zeros_like(rows_out)
    rows_out[0:1, :] = norm_gain
    rows_out[1:2, :inner] = gate_gain
    rows_out[2:3, :inner] = skip
    rows_out[3:4, :128] = chosen[0:1]
    rows_out[4:5, :128] = rates

    x_pass.last()
    cot_pass.first()

    def normalise(index, carry):
        for part in range(2):
            held = x_all[index, part * piece : (part + 1) * piece, :].astype(F32)
            inv = lax.rsqrt(jnp.mean(held * held, axis=1, keepdims=True) + EPS)
            normed_all[index, part * piece : (part + 1) * piece, :] = (
                held * inv * rows_out[0:1, :]
            ).astype(BF16)
        return carry

    x_line.wait(1) if depth > 2 else None
    if depth > 3:
        x_line.send(2)
    for copy in plane_g:
        copy.wait_recv()
    kept[2].wait()
    x_pass.end()
    kept[3].wait()
    lax.fori_loop(0, width, normalise, 0)
    if depth > 3:
        x_line.wait(2)
    gate_line.send(0)
    mine_bc = wb.at[core]
    pair_bc = links.copy(mine_bc, mine_bc, peer[1])
    pair_bc.start()
    saves = [pltpu.make_async_copy(normed_all, normed_out, locals_.at[7])]
    saves[0].start()
    pair_bc.wait_recv()

    causal = triangles()
    ones = causal.astype(F32)

    def stored(index):
        at = pl.ds(pl.multiple_of(index * rows, rows), rows)
        pairs = [
            (conv_in.at[at], conv_out.at[at]),
            (pre_all.at[at], pre_out.at[at]),
            (dt_all.at[at], dt_out.at[at]),
            (y_all.at[at], y_out.at[at]),
            (
                states.at[pl.ds(index * (rows // CHUNK), rows // CHUNK)],
                states_out.at[pl.ds(index * (rows // CHUNK), rows // CHUNK)],
            ),
        ]
        return [
            pltpu.make_async_copy(source, target, stores.at[k, index])
            for k, (source, target) in enumerate(pairs)
        ]

    per_slot = blocks // slots

    def scan_block(index, carry):
        slot, block = lax.div(index, per_slot), lax.rem(index, per_slot)
        at = pl.multiple_of(index * rows, rows)

        @pl.when(block == 0)
        def _():
            ext[0:8, :] = jnp.zeros((8, ext.shape[1]), F32)
            state[...] = jnp.zeros_like(state)

        tokens = normed_all[
            pl.ds(2 * block, 2), pl.ds(pl.multiple_of(slot * piece, piece), piece), :
        ].reshape(rows, model)
        ext[8:, :inner] = mm(tokens, wx[...].reshape(model, inner))
        ext[8:, inner : inner + size] = mm(tokens, wb[0].reshape(model, size))
        ext[8:, inner + size :] = mm(tokens, wb[1].reshape(model, size))
        dt_arg = mm(tokens, w_dt_out[...]) + rows_out[3:4, :128]
        dt_all[pl.ds(at, rows), :] = dt_arg
        pre = taps_out[kernel : kernel + 1, :] + sum(
            taps_out[k : k + 1, :] * ext[9 - kernel + k : 9 - kernel + k + rows, :]
            for k in range(kernel)
        )
        conv_in[pl.ds(at, rows), :] = ext[8:, :inner]
        ext[0:8, :] = ext[rows : rows + 8, :]
        pre_all[pl.ds(at, rows), :] = pre
        act = pre * sigmoid(pre)
        dt_block = softplus(dt_arg)
        steps_block = dt_block * rows_out[4:5, :128]
        for sub in range(rows // CHUNK):
            part = slice(sub * CHUNK, (sub + 1) * CHUNK)
            x = act[part, :inner]
            b = act[part, inner : inner + size].astype(BF16)
            c = act[part, inner + size :].astype(BF16)
            cum = dot(ones, steps_block[part], ((1,), (0,)), lax.Precision.HIGHEST)
            cum_t = cum.T
            total = cum[CHUNK - 1 : CHUNK, :]
            x_dt = x * widen(dt_block[part], heads, head_size)
            x_dt16 = x_dt.astype(BF16)
            held = state[...]
            held16 = held.astype(BF16)
            states[index * (rows // CHUNK) + sub] = held16
            y = mm(c, held16) * widen(jnp.exp(cum), heads, head_size)
            y = y + rows_out[2:3, :inner] * x
            cb = mm_t(c, b)
            pieces = []
            for pair in range(heads // 2):
                lanes = slice(2 * pair * head_size, 2 * (pair + 1) * head_size)
                mixing = jnp.concatenate(
                    [
                        (head_decays(cum, cum_t, 2 * pair + k, causal) * cb).astype(BF16)
                        for k in range(2)
                    ],
                    axis=1,
                )
                pieces.append(
                    mm(mixing, jnp.concatenate(split_pair(x_dt16[:, lanes], head_size), axis=0))
                )
            y_all[pl.ds(pl.multiple_of(at + sub * CHUNK, CHUNK), CHUNK), :] = y + jnp.concatenate(
                pieces, axis=1
            )
            weighted = (x_dt * widen(jnp.exp(total - cum), heads, head_size)).astype(BF16)
            state[...] = held * widen(jnp.exp(total), heads, head_size) + t_mm(b, weighted)
        for copy in stored(index):
            copy.start()

        @pl.when(index == 1)
        def _():
            gate_line.wait(0)
            if depth > 2:
                gate_line.send(1)

        @pl.when(index == 2)
        def _():
            cot_pass.relay()

        if depth > 2:

            @pl.when(index == 4)
            def _():
                gate_line.wait(1)
                if depth > 3:
                    gate_line.send(2)

        @pl.when(index == 5)
        def _():
            cot_pass.last()
            out_line.wait(0)
            if depth <= 3 and depth > 2:
                out_line.send(1)

        if depth > 3:

            @pl.when(index == 6)
            def _():
                gate_line.wait(2)
                out_line.send(1)

        return carry

    lax.fori_loop(0, blocks, scan_block, 0)

    chunk_lane = lax.broadcasted_iota(jnp.int32, (CHUNK, 128), 1)
    sums[...] = jnp.zeros_like(sums)

    def gate_block(index, carry):
        slot, block = lax.div(index, per_slot), lax.rem(index, per_slot)
        at = pl.multiple_of(index * rows, rows)
        tokens = normed_all[
            pl.ds(2 * block, 2), pl.ds(pl.multiple_of(slot * piece, piece), piece), :
        ].reshape(rows, model)
        gate = mm(tokens, wg[...].reshape(model, inner))
        gate_all[pl.ds(at, rows), :] = gate
        gated = y_all[pl.ds(at, rows), :] * (gate * sigmoid(gate))
        for sub in range(rows // CHUNK):
            part = gated[sub * CHUNK : (sub + 1) * CHUNK]
            total = jnp.sum(part * part, axis=1, keepdims=True)
            sums[...] = jnp.where(chunk_lane == index * (rows // CHUNK) + sub, total, sums[...])
        if depth > 2:

            @pl.when(index == blocks // 2)
            def _():
                out_line.wait(1)
                if depth > 3:
                    out_line.send(2)

        return carry

    lax.fori_loop(0, blocks, gate_block, 0)
    save_gate = pltpu.make_async_copy(gate_all, gate_out, locals_.at[8])
    save_gate.start()
    cot_pass.end()
    kept[4].wait()
    save_cot = pltpu.make_async_copy(cot_all, cot_out, locals_.at[9])
    save_cot.start()
    if depth > 3:
        out_line.wait(2)
    save_weights = [
        pltpu.make_async_copy(source, target, locals_.at[10 + k])
        for k, (source, target) in enumerate(
            ((wg, wg_out), (wx, wx_out), (wb, wb_out), (wo, wo_out))
        )
    ]
    for copy in save_weights:
        copy.start()

    def cot_block(index, carry):
        slot, block = lax.div(index, per_slot), lax.rem(index, per_slot)
        at = pl.multiple_of(index * rows, rows)
        tokens = cot_all[
            pl.ds(2 * block, 2), pl.ds(pl.multiple_of(slot * piece, piece), piece), :
        ].reshape(rows, model)
        dgn = mm_t(tokens, wo[...].reshape(inner, model))
        dgn_all[pl.ds(at, rows), :] = dgn
        gate = gate_all[pl.ds(at, rows), :]
        gated = y_all[pl.ds(at, rows), :] * (gate * sigmoid(gate))
        cross = dgn * rows_out[1:2, :inner] * gated
        for sub in range(rows // CHUNK):
            part = cross[sub * CHUNK : (sub + 1) * CHUNK]
            total = jnp.sum(part, axis=1, keepdims=True)
            sums[...] = jnp.where(
                chunk_lane == 2 * blocks + index * (rows // CHUNK) + sub, total, sums[...]
            )
        return carry

    lax.fori_loop(0, blocks, cot_block, 0)
    save_dgn = pltpu.make_async_copy(dgn_all, dgn_out, locals_.at[14])
    save_dgn.start()
    count = 4 * blocks
    sums_in[0] = sums[...].T[:count]
    sum_copies = [
        links.copy(sums_in.at[0], sums_in.at[mask], peer[mask]) for mask in range(1, width)
    ]
    for copy in sum_copies:
        copy.start()
    for copy in sum_copies:
        copy.wait_recv()
    got = [sums_in[mask] for mask in range(width)]
    while len(got) > 1:
        got = [got[k] + got[k + 1] for k in range(0, len(got), 2)]
    squares, cross = got[0][: 2 * blocks], got[0][2 * blocks :]
    inv_gate = lax.rsqrt(squares / inner_all + EPS)
    mean = inv_gate * cross / inner_all
    norms = jnp.concatenate([inv_gate, mean, jnp.zeros((128 - count, 128), F32)], axis=0)
    norms_out[...] = norms.T

    for copies in (plane_x, plane_g, pack_line, pack_plane, sum_copies, [pair_bc]):
        for copy in copies:
            copy.wait_send()
    pl.when(jnp.logical_not(out_home))(out_pair.wait_send)
    for line in (out_line, x_line, gate_line):
        line.drain()
    x_pass.drain()
    cot_pass.drain()
    for copy in saves + [save_gate, save_cot, save_dgn] + save_weights:
        copy.wait()

    def stores_end(index, carry):
        for copy in stored(index):
            copy.wait()
        return carry

    lax.fori_loop(0, blocks, stores_end, 0)


def forward(dims, x_own, cot_own, wg_send, wx_send, wb_send, wo_own, pack, head_params, collective):
    depth, width, heads, head_size, size, kernel, own_ch, inner_all = dims
    inner = heads * head_size
    rows, model = x_own.shape
    tokens = rows * width
    wide = inner + 2 * size
    shape = jax.ShapeDtypeStruct
    chunks = tokens // CHUNK
    weights = [
        ((depth,) + wg_send.shape, BF16),
        ((depth,) + wx_send.shape, BF16),
        ((2, depth, width) + wb_send.shape[1:], BF16),
        ((depth // 2, 2) + wo_own.shape, BF16),
    ]
    kept = [
        ((tokens, inner), F32),
        ((tokens, wide), F32),
        ((tokens, 128), F32),
        ((tokens, inner), F32),
        ((tokens, inner), F32),
        ((tokens, inner), F32),
        ((chunks, size, inner), BF16),
    ]
    in_hbm = [((width, rows, model), BF16)] * 2 + weights + kept
    in_vmem = [((CHUNK, 128), F32), ((8, wide), F32), ((8, model), F32), ((model, 128), BF16)]
    return pl.pallas_call(
        functools.partial(forward_kernel, dims),
        out_shape=tuple(shape(*s) for s in in_hbm + in_vmem),
        in_specs=[INVMEM] * 8,
        out_specs=(ANY,) * len(in_hbm) + (INVMEM,) * len(in_vmem),
        scratch_shapes=[pltpu.VMEM((width, rows, model), BF16)] * 3
        + [pltpu.VMEM(*s) for s in weights]
        + [pltpu.VMEM((depth, width) + pack.shape, BF16)]
        + [pltpu.VMEM(*s) for s in kept]
        + [
            pltpu.VMEM((rows + 8, wide), F32),
            pltpu.VMEM((size, inner), F32),
            pltpu.VMEM((8, -(-own_ch * depth * width // 128) * 128), F32),
            pltpu.VMEM((CHUNK, 128), F32),
            pltpu.VMEM((width, 2 * chunks, 128), F32),
            pltpu.SemaphoreType.DMA((112,)),
            pltpu.SemaphoreType.DMA((112,)),
            pltpu.SemaphoreType.DMA((16,)),
            pltpu.SemaphoreType.DMA((5, tokens // rows)),
        ],
        compiler_params=pltpu.CompilerParams(
            collective_id=collective, has_side_effects=True, vmem_limit_bytes=VMEM_LIMIT
        ),
        name="forward_fused",
    )(x_own, cot_own, wg_send, wx_send, wb_send, wo_own, pack, head_params)


class PlaneRows:
    def __init__(self, links, row, place, parts, landed):
        self.place, self.parts, self.landed = place, parts, landed
        peers = [(row, flip_all(place, mask)) for mask in (6, 7, 2, 3, 4, 5, 1)]
        self.copies = [
            links.copy(parts.at[peer[1]], landed.at[k], peer) for k, peer in enumerate(peers)
        ]

    def begin(self):
        for copy in self.copies:
            copy.start()

    def arrived(self):
        for copy in self.copies:
            copy.wait_recv()

    def drain(self):
        for copy in self.copies:
            copy.wait_send()


class SendBack:
    def __init__(self, links, row, place, sent, back, local):
        self.rows = back.shape[1]
        self.sent, self.back, self.place = sent, back, place
        mine = back.at[place]
        self.copies = [
            links.copy(self.block((row, flip_all(place, mask))[1]), mine, (row, flip_all(place, mask)))
            for mask in (6, 2, 4, 7, 3, 5, 1)
        ]
        self.kept = pltpu.make_async_copy(self.block(place), mine, local)

    def block(self, target):
        return self.sent.at[pl.ds(pl.multiple_of(target * self.rows, self.rows), self.rows)]

    def begin(self):
        for copy in self.copies:
            copy.start()
        self.kept.start()

    def end(self):
        self.kept.wait()
        for copy in self.copies:
            copy.wait()


def turn(target, source):
    for at in range(0, source.shape[0], 128):
        target[:, at : at + 128] = source[at : at + 128, :].T.astype(target.dtype)


def reverse_kernel(
    dims,
    cot_hbm,
    normed_hbm,
    gate_hbm,
    y_hbm,
    dgn_hbm,
    pre_hbm,
    conv_hbm,
    dt_hbm,
    states_hbm,
    wo_hbm,
    norms,
    taps,
    rows_in,
    head_sum,
    d_gate_hbm,
    d_x_hbm,
    d_bc_hbm,
    d_arg_hbm,
    o_total,
    gate_back,
    out_grad,
    channel_sums,
    head_sums,
    cot_all,
    normed_all,
    gate_all,
    y_all,
    d_y_all,
    wo,
    d_gate,
    d_x_all,
    d_bc,
    d_arg_all,
    g_out,
    g_gate,
    pre_two,
    conv_two,
    dt_two,
    states_two,
    later,
    d_ext,
    o_pair,
    o_sums,
    o_relay,
    o_last,
    out_up_in,
    out_up_out,
    out_down_in,
    out_down_out,
    gate_up_in,
    gate_up_out,
    gate_down_in,
    gate_down_out,
    out_sum,
    out_far,
    gate_sum,
    gate_sent,
    sends,
    recvs,
    locals_,
    streams,
):
    depth, width, heads, head_size, size, kernel, own_ch, inner_all = dims
    half = depth // 2
    inner = heads * head_size
    model = cot_all.shape[2]
    piece = cot_all.shape[1] // 2
    rows = 2 * piece
    slots = 2
    blocks = slots * width // 2
    per_slot = blocks // slots
    subs = rows // CHUNK
    row, place = lax.axis_index("dp"), lax.axis_index("seq")
    core = lax.rem(place, 2)
    links = Links(sends, recvs)
    above, below = lax.min(row + 1, depth - 1), lax.max(row - 1, 0)
    peer = {mask: (row, flip_all(place, mask)) for mask in range(1, width)}

    loads = [
        pltpu.make_async_copy(source, target, locals_.at[k])
        for k, (source, target) in enumerate(
            (
                (y_hbm, y_all),
                (gate_hbm, gate_all),
                (cot_hbm, cot_all),
                (wo_hbm, wo),
                (dgn_hbm, d_y_all),
                (normed_hbm, normed_all),
            )
        )
    ]
    for copy in loads:
        copy.start()

    def place_of(number):
        slot = lax.div(number, per_slot)
        return slot, per_slot - 1 - lax.rem(number, per_slot)

    def fetch(number):
        slot, block = place_of(number)
        index = slot * per_slot + block
        at = pl.ds(pl.multiple_of(index * rows, rows), rows)
        buffer = lax.rem(number, 2)
        pairs = (
            (pre_hbm.at[at], pre_two.at[buffer]),
            (conv_hbm.at[at], conv_two.at[buffer]),
            (dt_hbm.at[at], dt_two.at[buffer]),
            (states_hbm.at[pl.ds(index * subs, subs)], states_two.at[buffer]),
        )
        return [
            pltpu.make_async_copy(source, target, streams.at[buffer, k])
            for k, (source, target) in enumerate(pairs)
        ]

    for copy in fetch(0):
        copy.start()
    greet(
        [peer[mask] for mask in range(1, width)],
        [(row < depth - 1, (above, place)), (row > 0, (below, place))],
    )

    out_line = LineSum(
        links,
        depth,
        row,
        place,
        lambda q: g_out.at[pl.ds((q % half) * (inner // half), inner // half)],
        lambda q: core == q // half,
        out_up_in,
        out_up_out,
        out_down_in,
        out_down_out,
        half,
    )
    cols = model // depth
    gate_line = LineSum(
        links,
        depth,
        row,
        place,
        lambda q: g_gate.at[:, pl.ds(q * cols, cols)],
        lambda q: row >= 0,
        gate_up_in,
        gate_up_out,
        gate_down_in,
        gate_down_out,
    )
    o_plane = PlaneSum(links, row, place, cot_all, o_total, o_pair, o_sums, o_relay, o_last)
    send_gate = SendBack(links, row, place, gate_sent, gate_back, locals_.at[6])

    chunk_lane = lax.broadcasted_iota(jnp.int32, (CHUNK, 128), 1)

    def column(index, shift):
        parts = [
            jnp.sum(
                jnp.where(chunk_lane == shift + index * subs + sub, norms[...], 0.0),
                axis=1,
                keepdims=True,
            )
            for sub in range(subs)
        ]
        return jnp.concatenate(parts, axis=0)

    def tokens_of(ref, index):
        slot, block = lax.div(index, per_slot), lax.rem(index, per_slot)
        return ref.at[pl.ds(2 * block, 2), pl.ds(pl.multiple_of(slot * piece, piece), piece), :]

    gate_gain = rows_in[1:2, :inner]
    skip = rows_in[2:3, :inner]

    def normed_block(index, carry):
        at = pl.ds(pl.multiple_of(index * rows, rows), rows)
        gate = gate_all[at, :]
        hat = y_all[at, :] * (gate * sigmoid(gate)) * column(index, 0)
        tokens_of(d_gate, index)[...] = (
            (hat * gate_gain).astype(BF16).reshape(2, piece, inner)
        )
        return carry

    loads[0].wait()
    loads[1].wait()
    lax.fori_loop(0, blocks, normed_block, 0)

    everything = slots * width * piece

    def out_grad_tile(number, carry):
        at = pl.ds(pl.multiple_of(number * 128, 128), 128)
        left = d_gate[:, :, at].reshape(everything, 128)
        g_out[at, :] = t_mm(left, cot_all[...].reshape(everything, model))
        return carry

    loads[2].wait()
    lax.fori_loop(0, inner // 128, out_grad_tile, 0)
    out_line.step(0)

    def out_block(index, carry):
        cot_all[index] = mm(d_gate[index], wo[...].reshape(inner, model)).astype(BF16)
        return carry

    loads[3].wait()
    lax.fori_loop(0, width, out_block, 0)
    o_plane.begin()

    def gate_block(index, carry):
        at = pl.ds(pl.multiple_of(index * rows, rows), rows)
        gate = gate_all[at, :]
        sig = sigmoid(gate)
        gate_act = gate * sig
        y = y_all[at, :]
        inv = column(index, 0)
        hat = y * gate_act * inv
        d_gated = inv * (d_y_all[at, :] * gate_gain - hat * column(index, 2 * blocks))
        d_y_all[at, :] = d_gated * gate_act
        tokens_of(d_gate, index)[...] = (
            (d_gated * y * sig * (1.0 + gate * (1.0 - sig))).astype(BF16).reshape(2, piece, inner)
        )
        return carry

    loads[4].wait()
    lax.fori_loop(0, blocks, gate_block, 0)
    save_gate = pltpu.make_async_copy(d_gate, d_gate_hbm, locals_.at[7])
    save_gate.start()

    def gate_grad_tile(number, carry):
        at = pl.ds(pl.multiple_of(number * 128, 128), 128)
        left = d_gate[:, :, at].reshape(everything, 128)
        g_gate[at, :] = t_mm(left, normed_all[...].reshape(everything, model))
        return carry

    loads[5].wait()
    lax.fori_loop(0, inner // 128, gate_grad_tile, 0)
    gate_line.step(0)
    o_plane.first()

    channel_sums[...] = jnp.zeros_like(channel_sums)
    head_sums[...] = jnp.zeros_like(head_sums)
    causal = triangles()
    ones = causal.astype(F32)
    before = 1.0 - ones.T

    def head_totals(values):
        return dot(values, head_sum[...], ((1,), (0,)), lax.Precision.HIGHEST)

    def scan_block(number, carry):
        slot, block = place_of(number)
        index = slot * per_slot + block
        buffer = lax.rem(number, 2)
        for copy in fetch(number):
            copy.wait()

        @pl.when(number + 1 < blocks)
        def _():
            for copy in fetch(number + 1):
                copy.start()

        @pl.when(block == per_slot - 1)
        def _():
            later[...] = jnp.zeros_like(later)
            d_ext[rows:, :] = jnp.zeros((8, inner), F32)

        pre = pre_two[buffer]
        pre_sig = sigmoid(pre)
        act = pre * pre_sig
        slope = pre_sig[:, :inner] * (1.0 + pre[:, :inner] * (1.0 - pre_sig[:, :inner]))
        dt_arg = dt_two[buffer]
        dt_block = softplus(dt_arg)
        rates = rows_in[4:5, :128]
        steps_block = dt_block * rates
        for sub in reversed(range(subs)):
            part = slice(sub * CHUNK, (sub + 1) * CHUNK)
            at = pl.ds(pl.multiple_of(index * rows + sub * CHUNK, CHUNK), CHUNK)
            x = act[part, :inner]
            b = act[part, inner : inner + size].astype(BF16)
            c = act[part, inner + size :].astype(BF16)
            dt = dt_block[part]
            cum = dot(ones, steps_block[part], ((1,), (0,)), lax.Precision.HIGHEST)
            cum_t = cum.T
            total = cum[CHUNK - 1 : CHUNK, :]
            dt_wide = widen(dt, heads, head_size)
            x_dt = x * dt_wide
            x_dt16 = x_dt.astype(BF16)
            d_y = d_y_all[at, :]
            d_y16 = d_y.astype(BF16)
            cum_wide = widen(jnp.exp(cum), heads, head_size)
            d_read = (d_y * cum_wide).astype(BF16)
            out_wide = widen(jnp.exp(total - cum), heads, head_size)
            held16 = states_two[buffer, sub]
            read = mm(c, held16) * cum_wide
            grown = later[...]
            grown16 = grown.astype(BF16)
            d_x_later = out_wide * mm(b, grown16)
            d_b = mm_t(grown16, (x_dt * out_wide).astype(BF16))
            d_c = mm_t(held16, d_read)
            later[...] = grown * widen(jnp.exp(total), heads, head_size) + t_mm(c, d_read)
            cb = mm_t(c, b)
            d_cb = jnp.zeros((CHUNK, CHUNK), F32)
            pieces = []
            for pair in range(heads // 2):
                lanes = slice(2 * pair * head_size, 2 * (pair + 1) * head_size)
                d_y_split = split_pair(d_y16[:, lanes], head_size)
                mixing = []
                for k in range(2):
                    decay = head_decays(cum, cum_t, 2 * pair + k, causal)
                    mixing.append((decay * cb).astype(BF16))
                    d_cb = d_cb + decay * mm_t(d_y_split[k], x_dt16[:, lanes])
                pieces.append(
                    t_mm(jnp.concatenate(mixing, axis=0), jnp.concatenate(d_y_split, axis=0))
                )
            d_x_near = jnp.concatenate(pieces, axis=1)
            d_x_dt = d_x_later + d_x_near
            d_cb16 = d_cb.astype(BF16)
            d_b = d_b + t_mm(c, d_cb16)
            d_c = d_c + dot(b, d_cb16, ((0,), (1,)))
            d_bc[:size, at] = d_b.astype(BF16)
            d_bc[size:, at] = d_c.astype(BF16)
            d_x = d_x_dt * dt_wide + skip * d_y
            near = y_all[at, :] - skip * x - read
            cross_wide = d_y * read + d_y16.astype(F32) * near - x_dt16.astype(F32) * d_x_near
            d_dt_direct = head_totals(x * d_x_dt)
            d_cum = head_totals(cross_wide)
            through = head_totals(x_dt * d_x_later)
            over = head_totals(
                jnp.broadcast_to(
                    jnp.sum(grown * held16.astype(F32), axis=0, keepdims=True), (8, inner)
                )
            )
            d_log = (
                dot(ones, d_cum, ((0,), (0,)), lax.Precision.HIGHEST)
                + dot(before, through, ((1,), (0,)), lax.Precision.HIGHEST)
                + over[0:1, :] * jnp.exp(total)
            )
            d_dt = d_dt_direct + rates * d_log
            d_arg = d_dt * sigmoid(dt_arg[part])
            d_arg_all[2 * block + sub, pl.ds(pl.multiple_of(slot * piece, piece), piece), :] = (
                d_arg.astype(BF16)
            )
            head_sums[0:1, :] += jnp.sum(d_arg, axis=0, keepdims=True)
            head_sums[1:2, :] += jnp.sum(d_log * dt, axis=0, keepdims=True) * rates
            channel_sums[5:6, :] += jnp.sum(d_y * x, axis=0, keepdims=True)
            d_ext[part, :] = d_x * slope[part]

        d_conv = jnp.zeros((rows, inner), F32)
        x_in = conv_two[buffer]
        for k in range(kernel):
            moved = d_ext[kernel - 1 - k : kernel - 1 - k + rows, :]
            d_conv = d_conv + taps[k : k + 1, :inner] * moved
            channel_sums[k : k + 1, :] += jnp.sum(moved * x_in, axis=0, keepdims=True)
        channel_sums[4:5, :] += jnp.sum(d_ext[0:rows, :], axis=0, keepdims=True)
        d_x_all[
            pl.ds(2 * block, 2), pl.ds(pl.multiple_of(slot * piece, piece), piece), :
        ] = d_conv.astype(BF16).reshape(2, piece, inner)
        d_ext[rows:, :] = d_ext[0:8, :]

        @pl.when(number == 0)
        def _():
            if depth > 2:
                out_line.step(1)

        @pl.when(number == 1)
        def _():
            o_plane.second()
            if depth > 3:
                out_line.step(2)

        if depth > 2:

            @pl.when(number == 3)
            def _():
                gate_line.step(1)

        if depth > 3:

            @pl.when(number == 4)
            def _():
                gate_line.step(2)

        @pl.when(number == 6)
        def _():
            o_plane.finish()

        return carry

    lax.fori_loop(0, blocks, scan_block, 0)
    saves = [
        pltpu.make_async_copy(source, target, locals_.at[8 + k])
        for k, (source, target) in enumerate(
            ((d_x_all, d_x_hbm), (d_bc, d_bc_hbm), (d_arg_all, d_arg_hbm))
        )
    ]
    for copy in saves:
        copy.start()

    out_line.finish(out_sum)
    home = lax.div(row, half) == core
    rows_out = out_grad.shape[0]
    far = links.copy(out_far, out_grad, peer[1])
    for this in range(2):

        @pl.when(home & (core == this))
        def _():
            cast_rows(out_far, out_sum.at[pl.ds((1 - this) * rows_out, rows_out)])
            far.start()
            cast_rows(out_grad, out_sum.at[pl.ds(this * rows_out, rows_out)])

    gate_line.finish(gate_sum)
    turn(gate_sent, gate_sum)
    send_gate.begin()
    pl.when(jnp.logical_not(home))(far.wait_recv)
    pl.when(home)(far.wait_send)
    o_plane.drain()
    out_line.drain()
    gate_line.drain()
    send_gate.end()
    save_gate.wait()
    for copy in saves:
        copy.wait()


def line_buffers(count, extent):
    return [pltpu.VMEM((count,) + extent, BF16)] * 4


def plane_buffers(rows, model):
    return [
        pltpu.VMEM((4, rows, model), BF16),
        pltpu.VMEM((4, rows, model), BF16),
        pltpu.VMEM((2, rows // 2, model), BF16),
        pltpu.VMEM((2, rows, model), BF16),
    ]


def reverse(dims, hbm, vmem, collective):
    depth, width, heads, head_size, size, kernel, own_ch, inner_all = dims
    inner = heads * head_size
    _, rows, model = hbm[0].shape
    tokens = rows * width
    wide = inner + 2 * size
    shape = jax.ShapeDtypeStruct
    subs = rows // CHUNK
    half = depth // 2
    out_piece, in_piece = (inner // half, model), (inner, model // depth)
    saved = [
        ((width, rows, inner), BF16),
        ((width, rows, inner), BF16),
        ((2 * size, tokens), BF16),
        ((width, rows, 128), BF16),
    ]
    kept = [
        ((rows, model), F32),
        ((width, model // depth // width, inner), BF16),
        ((out_piece[0] // 2, model), F32),
        ((8, inner), F32),
        ((8, 128), F32),
    ]
    return pl.pallas_call(
        functools.partial(reverse_kernel, dims),
        out_shape=tuple(shape(*s) for s in saved + kept),
        in_specs=[ANY] * len(hbm) + [INVMEM] * len(vmem),
        out_specs=(ANY,) * len(saved) + (INVMEM,) * len(kept),
        scratch_shapes=[pltpu.VMEM((width, rows, model), BF16)] * 2
        + [pltpu.VMEM((tokens, inner), F32)] * 3
        + [pltpu.VMEM(hbm[-1].shape, BF16)]
        + [pltpu.VMEM(*s) for s in saved]
        + [
            pltpu.VMEM((inner, model), F32),
            pltpu.VMEM((inner, model), F32),
            pltpu.VMEM((2, rows, wide), F32),
            pltpu.VMEM((2, rows, inner), F32),
            pltpu.VMEM((2, rows, 128), F32),
            pltpu.VMEM((2, subs, size, inner), BF16),
            pltpu.VMEM((size, inner), F32),
            pltpu.VMEM((rows + 8, inner), F32),
        ]
        + plane_buffers(rows, model)
        + line_buffers(half, out_piece)
        + line_buffers(depth - 1, in_piece)
        + [
            pltpu.VMEM(out_piece, F32),
            pltpu.VMEM((out_piece[0] // 2, model), F32),
            pltpu.VMEM(in_piece, F32),
            pltpu.VMEM((in_piece[1], in_piece[0]), BF16),
            pltpu.SemaphoreType.DMA((48,)),
            pltpu.SemaphoreType.DMA((48,)),
            pltpu.SemaphoreType.DMA((12,)),
            pltpu.SemaphoreType.DMA((2, 4)),
        ],
        compiler_params=pltpu.CompilerParams(
            collective_id=collective, has_side_effects=True, vmem_limit_bytes=VMEM_LIMIT
        ),
        name="reverse_fused",
    )(*hbm, *vmem)


def weights_kernel(
    dims,
    normed_hbm,
    d_gate_hbm,
    d_x_hbm,
    d_arg_hbm,
    wg_hbm,
    wx_hbm,
    wb_hbm,
    w_dt_hbm,
    pre_hbm,
    d_bc,
    taps,
    channel_sums,
    head_sums,
    d_total,
    x_back,
    small_back,
    sums_all,
    normed_all,
    d_gate,
    d_x,
    d_arg,
    wg,
    wx,
    wb,
    w_dt,
    pre_own,
    bc_in,
    d_small,
    w_small,
    g_x,
    g_small,
    d_parts,
    d_ext,
    bc_landed,
    bc_sums,
    d_pair,
    d_sums,
    d_relay,
    d_last,
    x_up_in,
    x_up_out,
    x_down_in,
    x_down_out,
    small_up_in,
    small_up_out,
    small_down_in,
    small_down_out,
    x_sum,
    x_sent,
    small_sum,
    small_sent,
    sums_own,
    sums_line,
    sends,
    recvs,
    locals_,
):
    depth, width, heads, head_size, size, kernel, own_ch, inner_all = dims
    inner = heads * head_size
    model = normed_all.shape[2]
    piece = normed_all.shape[1] // 2
    rows = 2 * piece
    slots = 2
    blocks = slots * width // 2
    per_slot = blocks // slots
    everything = slots * width * piece
    own = 2 * size // width
    row, place = lax.axis_index("dp"), lax.axis_index("seq")
    links = Links(sends, recvs)
    above, below = lax.min(row + 1, depth - 1), lax.max(row - 1, 0)
    peer = {mask: (row, flip_all(place, mask)) for mask in range(1, width)}
    order = (6, 2, 4, 7, 3, 5, 1)
    per_block = 128 // own
    bc_block = lax.div(place, per_block)
    bc_turn = 128 - own * lax.rem(place, per_block)
    window = pl.ds(pl.multiple_of(inner + bc_block * 128, 128), 128)

    loads = [
        pltpu.make_async_copy(source, target, locals_.at[k])
        for k, (source, target) in enumerate(
            (
                (d_x_hbm, d_x),
                (normed_hbm, normed_all),
                (pre_hbm.at[:, window], pre_own),
                (wb_hbm, wb),
                (w_dt_hbm, w_dt),
                (d_arg_hbm, d_arg),
                (wg_hbm, wg),
                (wx_hbm, wx),
                (d_gate_hbm, d_gate),
            )
        )
    ]
    for copy in loads:
        copy.start()
    line_peers = [(lax.rem(row + up, depth), place) for up in range(1, depth)]
    greet([peer[mask] for mask in range(1, width)] + line_peers)

    bc_rows = PlaneRows(links, row, place, d_bc, bc_landed)
    bc_rows.begin()
    cols = model // depth

    def line(own_ref, buffers):
        return LineSum(
            links,
            depth,
            row,
            place,
            lambda q: own_ref.at[:, pl.ds(q * cols, cols)],
            lambda q: row >= 0,
            *buffers,
        )

    x_line = line(g_x, (x_up_in, x_up_out, x_down_in, x_down_out))
    small_line = line(g_small, (small_up_in, small_up_out, small_down_in, small_down_out))
    d_plane = PlaneSum(links, row, place, d_parts, d_total, d_pair, d_sums, d_relay, d_last)
    send_x = SendBack(links, row, place, x_sent, x_back, locals_.at[9])
    send_small = SendBack(links, row, place, small_sent, small_back, locals_.at[10])

    def x_grad_tile(number, carry):
        at = pl.ds(pl.multiple_of(number * 128, 128), 128)
        left = d_x[:, :, at].reshape(everything, 128)
        g_x[at, :] = t_mm(left, normed_all[...].reshape(everything, model))
        return carry

    loads[0].wait()
    loads[1].wait()
    lax.fori_loop(0, inner // 128, x_grad_tile, 0)
    x_line.step(0)

    lane = lax.broadcasted_iota(jnp.int32, (1, 128), 1)
    mine = lane < own

    def to_front(values):
        return pltpu.roll(values, bc_turn, 1)

    loads[3].wait()
    loads[4].wait()

    def small_weight(number, carry):
        at = pl.ds(pl.multiple_of(number * 128, 128), 128)
        bc = to_front(wb[bc_block, at, :].astype(F32))
        dt = pltpu.roll(w_dt[at, :].astype(F32), own, 1)
        w_small[at, :] = jnp.where(mine, bc, dt).astype(BF16)
        return carry

    lax.fori_loop(0, model // 128, small_weight, 0)
    own_taps = to_front(taps[:, window])

    def project(index, carry):
        bc_in[index] = mm(normed_all[index], w_small[...])
        return carry

    lax.fori_loop(0, width, project, 0)
    loads[2].wait()
    loads[5].wait()
    bc_rows.arrived()
    bc_sums[...] = jnp.zeros_like(bc_sums)
    d_ext[...] = jnp.zeros_like(d_ext)

    def small_block(number, carry):
        slot, block = lax.div(number, per_slot), per_slot - 1 - lax.rem(number, per_slot)
        at = pl.ds(pl.multiple_of((slot * per_slot + block) * rows, rows), rows)

        @pl.when(block == per_slot - 1)
        def _():
            d_ext[rows:, :] = jnp.zeros((8, 128), F32)

        total = d_bc[place, :, at].astype(F32)
        for k in range(width - 1):
            total = total + bc_landed[k, :, at].astype(F32)
        total = jnp.concatenate([total, jnp.zeros((128 - own, rows), F32)], axis=0)
        pre = to_front(pre_own[at, :])
        sig = sigmoid(pre)
        d_pre = jnp.where(mine, total.T * (sig * (1.0 + pre * (1.0 - sig))), 0.0)
        d_ext[0:rows, :] = d_pre
        where = (pl.ds(2 * block, 2), pl.ds(pl.multiple_of(slot * piece, piece), piece))
        conv_in = bc_in[where[0], where[1], :].reshape(rows, 128)
        d_conv = jnp.zeros((rows, 128), F32)
        for k in range(kernel):
            moved = d_ext[kernel - 1 - k : kernel - 1 - k + rows, :]
            d_conv = d_conv + own_taps[k : k + 1, :] * moved
            bc_sums[k : k + 1, :] += jnp.sum(moved * conv_in, axis=0, keepdims=True)
        bc_sums[4:5, :] += jnp.sum(d_pre, axis=0, keepdims=True)
        d_ext[rows:, :] = d_ext[0:8, :]
        d_dt = pltpu.roll(
            d_arg[where[0], where[1], :].astype(F32).reshape(rows, 128), own, 1
        )
        both = jnp.where(mine, d_conv, jnp.where(lane < own + heads, d_dt, 0.0))
        d_small[where[0], where[1], :] = both.astype(BF16).reshape(2, piece, 128)
        return carry

    lax.fori_loop(0, blocks, small_block, 0)
    g_small[...] = t_mm(
        d_small[...].reshape(everything, 128), normed_all[...].reshape(everything, model)
    )
    small_line.step(0)
    for copy in loads[6:]:
        copy.wait()

    def token_grads(index, carry):
        total = (
            mm_t(d_gate[index], wg[...])
            + mm_t(d_x[index], wx[...])
            + mm_t(d_small[index], w_small[...])
        )
        d_parts[index] = total.astype(BF16)
        return carry

    lax.fori_loop(0, width, token_grads, 0)
    d_plane.begin()

    sums_own[:, :inner] = channel_sums[...]
    sums_own[:, inner : inner + 128] = bc_sums[...]
    sums_own[:, inner + 128 :] = head_sums[...]
    sums_copies = [
        links.copy(sums_own, sums_line.at[k], device) for k, device in enumerate(line_peers)
    ]
    for copy in sums_copies:
        copy.start()
    if depth > 2:
        x_line.step(1)
        small_line.step(1)
    d_plane.first()
    for copy in sums_copies:
        copy.wait()
    total = jnp.zeros(sums_own.shape, F32)
    for q in range(depth):
        term = jnp.zeros(sums_own.shape, F32)
        for up in range(1, depth):
            term = jnp.where(lax.rem(row + depth - up, depth) == q, sums_line[up - 1], term)
        total = total + jnp.where(row == q, sums_own[...], term)
    sums_all[place] = total
    mine_all = sums_all.at[place]
    spread_sums = [links.copy(mine_all, mine_all, peer[mask]) for mask in order]
    for copy in spread_sums:
        copy.start()
    if depth > 3:
        x_line.step(2)
        small_line.step(2)
    d_plane.second()
    x_line.finish(x_sum)
    turn(x_sent, x_sum)
    send_x.begin()
    small_line.finish(small_sum)
    turn(small_sent, small_sum)
    send_small.begin()
    d_plane.finish()
    d_plane.drain()
    x_line.drain()
    small_line.drain()
    send_x.end()
    send_small.end()
    bc_rows.drain()
    for copy in spread_sums:
        copy.wait()


def weights(dims, hbm, vmem, collective):
    depth, width, heads, head_size, size, kernel, own_ch, inner_all = dims
    inner = heads * head_size
    _, rows, model = hbm[0].shape
    tokens = rows * width
    shape = jax.ShapeDtypeStruct
    cols = model // depth
    kept = [
        ((rows, model), F32),
        ((width, cols // width, inner), BF16),
        ((width, cols // width, 128), BF16),
        ((width, 8, inner + 256), F32),
    ]
    return pl.pallas_call(
        functools.partial(weights_kernel, dims),
        out_shape=tuple(shape(*s) for s in kept),
        in_specs=[ANY] * len(hbm) + [INVMEM] * len(vmem),
        out_specs=(INVMEM,) * len(kept),
        scratch_shapes=[pltpu.VMEM(v.shape, v.dtype) for v in hbm[:-1]]
        + [
            pltpu.VMEM((tokens, 128), F32),
            pltpu.VMEM((width, rows, 128), F32),
            pltpu.VMEM((width, rows, 128), BF16),
            pltpu.VMEM((model, 128), BF16),
            pltpu.VMEM((inner, model), F32),
            pltpu.VMEM((128, model), F32),
            pltpu.VMEM((width, rows, model), BF16),
            pltpu.VMEM((rows + 8, 128), F32),
            pltpu.VMEM((width - 1, 2 * size // width, tokens), BF16),
            pltpu.VMEM((8, 128), F32),
        ]
        + plane_buffers(rows, model)
        + line_buffers(depth - 1, (inner, cols))
        + line_buffers(depth - 1, (128, cols))
        + [
            pltpu.VMEM((inner, cols), F32),
            pltpu.VMEM((cols, inner), BF16),
            pltpu.VMEM((128, cols), F32),
            pltpu.VMEM((cols, 128), BF16),
            pltpu.VMEM((8, inner + 256), F32),
            pltpu.VMEM((depth - 1, 8, inner + 256), F32),
            pltpu.SemaphoreType.DMA((80,)),
            pltpu.SemaphoreType.DMA((80,)),
            pltpu.SemaphoreType.DMA((12,)),
        ],
        compiler_params=pltpu.CompilerParams(
            collective_id=collective, has_side_effects=True, vmem_limit_bytes=VMEM_LIMIT
        ),
        name="weights_fused",
    )(*hbm, *vmem)


def fast_body(
    depth,
    width,
    block_input,
    cotangent,
    lengths,
    in_weight,
    out_weight,
    norm_gain,
    gate_gain,
    conv_weight,
    conv_bias,
    dt_bias,
    a_log,
    d_skip,
):
    slots, piece, model = block_input.shape
    heads_all = dt_bias.shape[0]
    out_rows = out_weight.shape[0]
    in_rows = in_weight.shape[0]
    inner_all = out_rows * depth * width
    head_size = inner_all // heads_all
    taps_count = conv_weight.shape[0]
    channels = conv_weight.shape[1] * depth * width
    size = (channels - inner_all) // 2
    heads = heads_all // width
    inner = heads * head_size
    plane = width // 2
    half = depth // 2
    pair_rows = 2 * out_rows
    row, place = lax.axis_index("dp"), lax.axis_index("seq")
    core, chip = lax.rem(place, 2), lax.div(place, 2)
    slot_len = piece * width
    tokens = slots * slot_len

    def by_owner(values, axis):
        shape = values.shape
        return values.reshape(shape[:axis] + (2, half, plane, pair_rows) + shape[axis + 1 :])

    gate_cols = inner_all
    conv_cols = gate_cols + inner_all
    bc_cols = conv_cols + 2 * size
    own_ch = conv_bias.shape[0]

    def padded(values, lanes=128):
        return jnp.pad(values, ((0, 0), (0, lanes - values.shape[1])))

    def placed(values, top):
        return jnp.pad(
            values, ((top, 16 + in_rows - top - values.shape[0]), (0, 128 - values.shape[1]))
        )

    pack = (
        placed(in_weight[:, bc_cols:], 0)
        + placed(conv_weight, in_rows)
        + placed(conv_bias[None], in_rows + taps_count)
        + placed(gate_gain[None], in_rows + 5)
        + placed(norm_gain[None], in_rows + 6)
    )
    head_params = jnp.pad(
        jnp.stack([dt_bias, a_log, d_skip]), ((0, 5), (0, 128 - heads_all))
    )
    input_f = block_input.astype(F32)
    inv_rms = lax.rsqrt(jnp.mean(input_f * input_f, axis=-1, keepdims=True) + EPS)
    positions = place * piece + jnp.arange(piece, dtype=jnp.int32)
    live = (positions[None, :] < lengths[:, None]).astype(BF16)
    masked = cotangent * live[..., None]

    def cols_for_all(values):
        split = by_owner(values, 1)
        return jnp.transpose(split, (3, 1, 0, 2, 4)).reshape(width, in_rows, inner)

    w_bc_send = jnp.swapaxes(in_weight[:, conv_cols:bc_cols].reshape(in_rows, 2, size), 0, 1)
    tokens_dev = slots * piece
    dims = (depth, width, heads, head_size, size, taps_count, own_ch, inner_all)
    (
        normed_all,
        cot_all,
        w_gate,
        w_x,
        w_bc,
        w_out,
        conv_in,
        pre,
        dt_arg,
        gate,
        y,
        dgn,
        states,
        norms,
        taps,
        param_rows,
        w_dt,
    ) = forward(
        dims,
        block_input.reshape(tokens_dev, model),
        masked.reshape(tokens_dev, model),
        cols_for_all(in_weight[:, :gate_cols]),
        cols_for_all(in_weight[:, gate_cols:conv_cols]),
        w_bc_send,
        out_weight,
        pack,
        head_params,
        2,
    )
    norm_all = param_rows[0].reshape(1, 1, model)
    head_sum = padded((jnp.arange(inner)[:, None] // head_size == jnp.arange(heads)).astype(F32))
    (
        d_gate,
        d_x,
        d_bc,
        d_arg,
        o_total,
        gate_back,
        out_grad,
        channel_sums,
        head_sums,
    ) = reverse(
        dims,
        (cot_all, normed_all, gate, y, dgn, pre, conv_in, dt_arg, states, w_out),
        (norms, taps, param_rows, head_sum),
        3,
    )
    bc_own = 2 * size // width
    d_total, x_back, small_back, smalls = weights(
        dims,
        (
            normed_all,
            d_gate,
            d_x,
            d_arg,
            w_gate.reshape(model, inner),
            w_x.reshape(model, inner),
            w_bc.reshape(2, model, size),
            w_dt,
            pre,
        ),
        (d_bc.reshape(width, bc_own, tokens), taps, channel_sums, head_sums),
        4,
    )

    def to_whole(values, group):
        count = values.shape[1]
        split = values.reshape(plane, 2, count, half, group)
        return jnp.transpose(split, (2, 1, 3, 0, 4)).reshape(count, -1)

    conv_x = to_whole(smalls[:, :5, :inner], pair_rows)
    conv_bc = jnp.swapaxes(smalls[:, :5, inner : inner + bc_own], 0, 1).reshape(5, 2 * size)
    conv_grads = lax.dynamic_slice_in_dim(
        jnp.concatenate([conv_x, conv_bc], axis=1), (row * width + place) * own_ch, own_ch, 1
    )
    skip_sum = jnp.sum(smalls[:, 5:6, :inner].reshape(width, 1, heads, head_size), axis=3)
    head_grads = to_whole(
        jnp.concatenate([smalls[:, :2, inner + 128 : inner + 128 + heads], skip_sum], axis=1),
        pair_rows // head_size,
    )
    small_f = small_back.astype(F32)
    in_grad = jnp.concatenate(
        [
            to_whole(gate_back.astype(F32), pair_rows),
            to_whole(x_back.astype(F32), pair_rows),
            jnp.swapaxes(small_f[:, :, :bc_own], 0, 1).reshape(in_rows, 2 * size),
            to_whole(small_f[:, :, bc_own : bc_own + heads], pair_rows // head_size),
        ],
        axis=1,
    )
    norm_grad = jnp.sum(in_grad * in_weight.astype(F32), axis=1) / norm_gain.astype(F32)
    gate_grad = jnp.sum(out_grad * out_weight.astype(F32), axis=1) / gate_gain.astype(F32)

    output = (input_f + o_total.reshape(slots, piece, model)).astype(BF16)
    in_hat = input_f * inv_rms
    d_h = d_total.reshape(slots, piece, model) * norm_all.astype(F32)
    input_grad = inv_rms * (d_h - in_hat * jnp.mean(d_h * in_hat, axis=-1, keepdims=True))
    input_grad = (input_grad + masked.astype(F32)).astype(BF16)
    return (
        output,
        input_grad,
        in_grad,
        out_grad,
        norm_grad,
        gate_grad,
        conv_grads[:4],
        conv_grads[4],
        head_grads[0],
        head_grads[1],
        head_grads[2],
    )


def heads_fit(depth, width, arrays):
    block_input, out_weight, dt_bias = arrays[0], arrays[4], arrays[9]
    pair_rows = 2 * out_weight.shape[0]
    head_size = out_weight.shape[0] * depth * width // dt_bias.shape[0]
    return (
        width == 8
        and depth % 2 == 0
        and pair_rows % head_size == 0
        and (depth // 2 * pair_rows) % 128 == 0
        and block_input.shape[1] % CHUNK == 0
        and 2 * head_size == CHUNK
    )


def solution(mesh):
    placed = (
        P("dp", "seq", None),
        P("dp", "seq", None),
        P("dp"),
        P(("dp", "seq"), None),
        P(("dp", "seq"), None),
        P(("dp", "seq")),
        P(("dp", "seq")),
        P(None, ("dp", "seq")),
        P(("dp", "seq")),
        P(),
        P(),
        P(),
    )
    depth, width = mesh.shape["dp"], mesh.shape["seq"]

    def either(*arrays):
        if heads_fit(depth, width, arrays):
            return fast_body(depth, width, *arrays)
        return body(*arrays)

    return jax.shard_map(
        either,
        mesh=mesh,
        in_specs=placed,
        out_specs=(
            P("dp", "seq", None),
            P("dp", "seq", None),
            P(("dp", "seq"), None),
            P(("dp", "seq"), None),
            P(("dp", "seq")),
            P(("dp", "seq")),
            P(None, ("dp", "seq")),
            P(("dp", "seq")),
            P(),
            P(),
            P(),
        ),
        check_vma=False,
    )
```

```python
import functools

import jax
import jax.numpy as jnp
from jax import lax
from jax.experimental import pallas as pl
from jax.experimental.pallas import tpu as pltpu
from jax.sharding import PartitionSpec as P

SLOTS_MB = 1


EPS = 1e-05
HIGH = lax.Precision.HIGHEST


def from_behind(value, axis, steps):
    count = lax.axis_size(axis)
    leading, last = (max(0, -steps), min(count, count - steps))
    return lax.ppermute(value, axis, [(source, source + steps) for source in range(leading, last)])


def carried_in(value, axis, join, neutral, backward):
    count = lax.axis_size(axis)
    place = lax.axis_index(axis)
    ahead = count - 1 - place if backward else place
    gathered = jax.tree.map(
        lambda a, kind: lax.all_gather(a.astype(kind), axis),
        value,
        jax.tree.map(lambda a: jnp.bfloat16 if a.dtype == jnp.float32 else a.dtype, value),
    )
    state = jax.tree.map(lambda a, e: jnp.zeros_like(a) + jnp.asarray(e, a.dtype), value, neutral)

    def one(lap, state):
        source = count - 1 - lap if backward else lap
        return join(
            state,
            jax.tree.map(
                lambda a, own: lax.dynamic_index_in_dim(a, source, 0, False).astype(own.dtype),
                gathered,
                value,
            ),
        )

    return lax.fori_loop(0, ahead, one, state)


def as_sent(value):

    def short(part):
        return part.astype(jnp.bfloat16) if part.dtype == jnp.float32 else part

    return jax.tree.map(short, value)


def link_states(earlier, later):
    return (earlier[0] * later[0], later[0][:, :, None, None] * earlier[1] + later[1])


def silu_slope(values):
    sigma = jax.nn.sigmoid(values)
    return sigma * (1.0 + values * (1.0 - sigma))


def rows_product(left, right):
    return lax.dot_general(
        left, right, (((0,), (0,)), ((), ())), preferred_element_type=jnp.float32
    )


def cols_product(left, right):
    return lax.dot_general(
        left, right, (((1,), (1,)), ((), ())), preferred_element_type=jnp.float32
    )


def add_pair(first, second):
    return first + second


def first_total(stacked):
    return jnp.sum(stacked, axis=0)


def owner_sums(grads):
    lifted = tuple((grad[None] for grad in grads))
    by_data = (
        lax.all_to_all(lifted[0], "dp", split_axis=1, concat_axis=0, tiled=True),
        lax.all_to_all(lifted[1], "dp", split_axis=1, concat_axis=0, tiled=True),
        lax.all_to_all(lifted[2], "dp", split_axis=1, concat_axis=0, tiled=True),
        lax.all_to_all(lifted[3], "dp", split_axis=1, concat_axis=0, tiled=True),
        lax.all_to_all(lifted[4], "dp", split_axis=1, concat_axis=0, tiled=True),
        lax.all_to_all(lifted[5], "dp", split_axis=1, concat_axis=0, tiled=True),
    )
    partial_value = tuple((first_total(stacked)[None] for stacked in by_data))
    by_piece = (
        lax.all_to_all(partial_value[0], "seq", split_axis=1, concat_axis=0, tiled=True),
        lax.all_to_all(partial_value[1], "seq", split_axis=1, concat_axis=0, tiled=True),
        lax.all_to_all(partial_value[2], "seq", split_axis=1, concat_axis=0, tiled=True),
        lax.all_to_all(partial_value[3], "seq", split_axis=1, concat_axis=0, tiled=True),
        lax.all_to_all(partial_value[4], "seq", split_axis=1, concat_axis=0, tiled=True),
        lax.all_to_all(partial_value[5], "seq", split_axis=1, concat_axis=0, tiled=True),
    )
    return tuple((first_total(stacked) for stacked in by_piece))


def forward_pass(slot_in, weights, head_params):
    in_full, out_full, norm_full, gate_full, conv_full, bias_full = weights
    dt_shift, log_rate, skip_gain = head_params
    slot_count, piece_len, model_width = slot_in.shape
    inner_width = out_full.shape[0]
    channels = conv_full.shape[1]
    kernel = conv_full.shape[0]
    head_count = dt_shift.shape[0]
    head_size = inner_width // head_count
    state_size = (channels - inner_width) // 2
    input_f = slot_in.astype(jnp.float32)
    inv_rms = lax.rsqrt(jnp.mean(input_f * input_f, axis=-1, keepdims=True) + EPS)
    normed = (input_f * inv_rms * norm_full.astype(jnp.float32)).astype(jnp.bfloat16)
    projected = jnp.dot(
        normed.reshape(-1, model_width), in_full, preferred_element_type=jnp.float32
    ).reshape(slot_count, piece_len, -1)
    gate_part = projected[..., :inner_width]
    conv_in = projected[..., inner_width : inner_width + channels]
    dt_arg = projected[..., inner_width + channels :] + dt_shift
    rim_rows = from_behind(
        conv_in[:, piece_len - kernel + 1 :].astype(jnp.bfloat16), "seq", 1
    ).astype(jnp.float32)
    extended = jnp.concatenate([rim_rows, conv_in], axis=1)
    conv_taps = conv_full.astype(jnp.float32)
    pre_act = bias_full.astype(jnp.float32) + sum(
        (
            conv_taps[tap_index] * extended[:, tap_index : tap_index + piece_len]
            for tap_index in range(kernel)
        )
    )
    activated = jax.nn.silu(pre_act)
    x_heads = activated[..., :inner_width].reshape(slot_count, piece_len, head_count, head_size)
    b_rows = activated[..., inner_width : inner_width + state_size]
    c_rows = activated[..., inner_width + state_size :]
    dt_vals = jax.nn.softplus(dt_arg)
    decay_rates = -jnp.exp(log_rate)
    log_cum = jnp.cumsum(dt_vals * decay_rates, axis=1)
    log_tot = log_cum[:, -1]
    weights_in = jnp.exp(log_tot[:, None] - log_cum) * dt_vals
    local_state = jnp.einsum(
        "sthp,stn->shpn", weights_in[..., None] * x_heads, b_rows, precision=HIGH
    )
    carry_decay = jnp.exp(log_tot)
    neutral = (jnp.ones_like(carry_decay), jnp.zeros_like(local_state))
    _, start_state = carried_in((carry_decay, local_state), "seq", link_states, neutral, False)
    spots = jnp.arange(piece_len)
    causal = spots[:, None] >= spots[None, :]
    cum_heads = jnp.swapaxes(log_cum, 1, 2)
    gap_vals = jnp.where(causal, cum_heads[..., :, None] - cum_heads[..., None, :], 0.0)
    decay_mat = jnp.where(causal, jnp.exp(gap_vals), 0.0)
    cb_mat = jnp.einsum("stn,sun->stu", c_rows, b_rows, precision=HIGH)
    dt_cols = jnp.swapaxes(dt_vals, 1, 2)[:, :, None, :]
    mixing = decay_mat * cb_mat[:, None] * dt_cols
    y_intra = jnp.einsum("shtu,suhp->sthp", mixing, x_heads, precision=HIGH)
    state_read = jnp.einsum("stn,shpn->sthp", c_rows, start_state, precision=HIGH)
    exp_cum = jnp.exp(log_cum)
    y_heads = y_intra + exp_cum[..., None] * state_read + skip_gain[:, None] * x_heads
    y_flat = y_heads.reshape(slot_count, piece_len, inner_width)
    gate_act = jax.nn.silu(gate_part)
    gated_out = y_flat * gate_act
    inv_gate = lax.rsqrt(jnp.mean(gated_out * gated_out, axis=-1, keepdims=True) + EPS)
    gate_normed = (gated_out * inv_gate * gate_full.astype(jnp.float32)).astype(jnp.bfloat16)
    mixed = jnp.dot(
        gate_normed.reshape(-1, inner_width), out_full, preferred_element_type=jnp.float32
    )
    output = (input_f + mixed.reshape(slot_count, piece_len, model_width)).astype(jnp.bfloat16)
    saved = dict(
        input_f=input_f,
        inv_rms=inv_rms,
        normed=normed,
        gate_part=gate_part,
        dt_arg=dt_arg,
        extended=extended,
        pre_act=pre_act,
        x_heads=x_heads,
        b_rows=b_rows,
        c_rows=c_rows,
        dt_vals=dt_vals,
        log_cum=log_cum,
        log_tot=log_tot,
        weights_in=weights_in,
        carry_decay=carry_decay,
        start_state=start_state,
        decay_mat=decay_mat,
        cb_mat=cb_mat,
        dt_cols=dt_cols,
        mixing=mixing,
        state_read=state_read,
        exp_cum=exp_cum,
        y_flat=y_flat,
        gate_act=gate_act,
        gated_out=gated_out,
        inv_gate=inv_gate,
        gate_normed=gate_normed,
    )
    return (output, saved)


def backward_pass(saved, slot_cot, live, weights, head_params):
    in_full, out_full, norm_full, gate_full, conv_full, bias_full = weights
    dt_shift, log_rate, skip_gain = head_params
    slot_count, piece_len, model_width = slot_cot.shape
    inner_width = out_full.shape[0]
    kernel = conv_full.shape[0]
    x_heads = saved["x_heads"]
    b_rows = saved["b_rows"]
    c_rows = saved["c_rows"]
    dt_vals = saved["dt_vals"]
    log_cum = saved["log_cum"]
    weights_in = saved["weights_in"]
    carry_decay = saved["carry_decay"]
    start_state = saved["start_state"]
    decay_mat = saved["decay_mat"]
    cb_mat = saved["cb_mat"]
    dt_cols = saved["dt_cols"]
    decay_rates = -jnp.exp(log_rate)
    masked_cot = slot_cot * live[..., None].astype(jnp.bfloat16)
    cot_rows = masked_cot.reshape(-1, model_width)
    d_gn = cols_product(cot_rows, out_full).reshape(slot_count, piece_len, inner_width)
    gate_hat = saved["gated_out"] * saved["inv_gate"]
    grad_ggain = jnp.sum(d_gn * gate_hat, axis=(0, 1))
    d_hat = d_gn * gate_full.astype(jnp.float32)
    d_gated = saved["inv_gate"] * (
        d_hat - gate_hat * jnp.mean(d_hat * gate_hat, axis=-1, keepdims=True)
    )
    d_gate_part = d_gated * saved["y_flat"] * silu_slope(saved["gate_part"])
    d_heads = (d_gated * saved["gate_act"]).reshape(x_heads.shape)
    grad_skip = jnp.sum(d_heads * x_heads, axis=(0, 1, 3))
    exp_cum = saved["exp_cum"]
    d_read = d_heads * exp_cum[..., None]
    d_cvals = jnp.einsum("sthp,shpn->stn", d_read, start_state, precision=HIGH)
    d_start = jnp.einsum("sthp,stn->shpn", d_read, c_rows, precision=HIGH)
    d_cum = jnp.sum(d_heads * saved["state_read"], axis=-1) * exp_cum
    d_mixing = jnp.einsum("sthp,suhp->shtu", d_heads, x_heads, precision=HIGH)
    d_x = skip_gain[:, None] * d_heads + jnp.einsum(
        "shtu,sthp->suhp", saved["mixing"], d_heads, precision=HIGH
    )
    d_decay = d_mixing * cb_mat[:, None] * dt_cols
    d_cb = jnp.sum(d_mixing * decay_mat * dt_cols, axis=1)
    d_dt = jnp.swapaxes(jnp.sum(d_mixing * decay_mat * cb_mat[:, None], axis=2), 1, 2)
    spread = d_decay * decay_mat
    d_cum = d_cum + jnp.swapaxes(jnp.sum(spread, axis=3) - jnp.sum(spread, axis=2), 1, 2)
    d_cvals = d_cvals + jnp.einsum("stu,sun->stn", d_cb, b_rows, precision=HIGH)
    d_bvals = jnp.einsum("stu,stn->sun", d_cb, c_rows, precision=HIGH)
    neutral = (jnp.ones_like(carry_decay), jnp.zeros_like(d_start))
    _, later_grad = carried_in((carry_decay, d_start), "seq", link_states, neutral, True)
    d_tot = jnp.sum(later_grad * start_state, axis=(2, 3)) * carry_decay
    grad_proj_b = jnp.einsum("shpn,stn->sthp", later_grad, b_rows, precision=HIGH)
    d_x = d_x + weights_in[..., None] * grad_proj_b
    d_weights = jnp.sum(grad_proj_b * x_heads, axis=-1)
    d_bvals = d_bvals + jnp.einsum(
        "sthp,shpn->stn", weights_in[..., None] * x_heads, later_grad, precision=HIGH
    )
    d_dt = d_dt + d_weights * jnp.exp(saved["log_tot"][:, None] - log_cum)
    through = d_weights * weights_in
    d_tot = d_tot + jnp.sum(through, axis=1)
    last_row = (jnp.arange(piece_len) == piece_len - 1).astype(jnp.float32)
    d_cum = d_cum - through + last_row[None, :, None] * d_tot[:, None, :]
    d_log = lax.cumsum(d_cum, axis=1, reverse=True)
    d_dt = d_dt + d_log * decay_rates
    grad_alog = jnp.sum(d_log * dt_vals, axis=(0, 1)) * decay_rates
    d_arg = d_dt * jax.nn.sigmoid(saved["dt_arg"])
    grad_dtb = jnp.sum(d_arg, axis=(0, 1))
    d_act = jnp.concatenate(
        [d_x.reshape(slot_count, piece_len, inner_width), d_bvals, d_cvals], axis=-1
    )
    d_pre = d_act * silu_slope(saved["pre_act"])
    grad_cbias = jnp.sum(d_pre, axis=(0, 1))
    extended = saved["extended"]
    grad_conv = jnp.stack(
        [
            jnp.sum(d_pre * extended[:, tap_index : tap_index + piece_len], axis=(0, 1))
            for tap_index in range(kernel)
        ]
    )
    conv_taps = conv_full.astype(jnp.float32)
    d_ext = sum(
        (
            jnp.pad(
                conv_taps[tap_index] * d_pre, ((0, 0), (tap_index, kernel - 1 - tap_index), (0, 0))
            )
            for tap_index in range(kernel)
        )
    )
    back_rim = from_behind(as_sent(d_ext[:, : kernel - 1]), "seq", -1)
    d_conv_in = d_ext[:, kernel - 1 :] + jnp.pad(
        back_rim, ((0, 0), (piece_len - kernel + 1, 0), (0, 0))
    )
    d_proj = jnp.concatenate([d_gate_part, d_conv_in, d_arg], axis=-1).astype(jnp.bfloat16)
    d_proj = d_proj.reshape(slot_count * piece_len, -1)
    d_normed = cols_product(d_proj, in_full).reshape(slot_count, piece_len, model_width)
    in_hat = saved["input_f"] * saved["inv_rms"]
    grad_ngain = jnp.sum(d_normed * in_hat, axis=(0, 1))
    d_norm_in = d_normed * norm_full.astype(jnp.float32)
    input_grad = saved["inv_rms"] * (
        d_norm_in - in_hat * jnp.mean(d_norm_in * in_hat, axis=-1, keepdims=True)
    )
    input_grad = input_grad + masked_cot.astype(jnp.float32)
    product_rows = (
        saved["normed"].reshape(-1, model_width),
        d_proj,
        saved["gate_normed"].reshape(-1, inner_width),
        cot_rows,
    )
    small_grads = (grad_ngain, grad_ggain, grad_conv, grad_cbias)
    return (
        input_grad.astype(jnp.bfloat16),
        product_rows,
        small_grads,
        (grad_dtb, grad_alog, grad_skip),
    )


def body(
    block_input,
    cotangent,
    lengths,
    in_weight,
    out_weight,
    norm_gain,
    gate_gain,
    conv_weight,
    conv_bias,
    dt_bias,
    a_log,
    d_skip,
):
    shards = (in_weight, out_weight, norm_gain, gate_gain, conv_weight, conv_bias)
    head_params = (dt_bias, a_log, d_skip)
    piece_len = block_input.shape[1]
    batches = block_input.shape[0] // SLOTS_MB
    positions = lax.axis_index("seq") * piece_len + jnp.arange(piece_len, dtype=jnp.int32)
    held = (
        lax.all_gather(shards[0], ("dp", "seq"), axis=0, tiled=True),
        lax.all_gather(shards[1], ("dp", "seq"), axis=0, tiled=True),
        lax.all_gather(shards[2], ("dp", "seq"), axis=0, tiled=True),
        lax.all_gather(shards[3], ("dp", "seq"), axis=0, tiled=True),
        lax.all_gather(shards[4], ("dp", "seq"), axis=1, tiled=True),
        lax.all_gather(shards[5], ("dp", "seq"), axis=0, tiled=True),
    )
    outputs = []
    input_grads = []
    kept_rows = []
    small_totals = None
    head_totals = None
    for batch_index in range(batches):
        first = batch_index * SLOTS_MB
        slot_in = block_input[first : first + SLOTS_MB]
        slot_cot = cotangent[first : first + SLOTS_MB]
        live = (positions[None, :] < lengths[first : first + SLOTS_MB, None]).astype(jnp.float32)
        output, saved = forward_pass(slot_in, held, head_params)
        input_grad, product_rows, small_grads, head_grads = backward_pass(
            saved, slot_cot, live, held, head_params
        )
        outputs.append(output)
        input_grads.append(input_grad)
        kept_rows.append(product_rows)
        small_totals = (
            small_grads
            if small_totals is None
            else jax.tree.map(add_pair, small_totals, small_grads)
        )
        head_totals = (
            head_grads if head_totals is None else jax.tree.map(add_pair, head_totals, head_grads)
        )
    normed_all = jnp.concatenate([rows[0] for rows in kept_rows], axis=0)
    dproj_all = jnp.concatenate([rows[1] for rows in kept_rows], axis=0)
    gnormed_all = jnp.concatenate([rows[2] for rows in kept_rows], axis=0)
    cot_all = jnp.concatenate([rows[3] for rows in kept_rows], axis=0)
    grad_win = rows_product(normed_all, dproj_all)
    grad_wout = rows_product(gnormed_all, cot_all)
    grad_ngain, grad_ggain, grad_conv, grad_cbias = small_totals
    owned = owner_sums((grad_win, grad_wout, grad_ngain, grad_ggain, grad_conv.T, grad_cbias))
    head_sums = lax.psum(head_totals, ("dp", "seq"))
    return (
        jnp.concatenate(outputs, axis=0),
        jnp.concatenate(input_grads, axis=0),
        owned[0],
        owned[1],
        owned[2],
        owned[3],
        owned[4].T,
        owned[5],
        head_sums[0],
        head_sums[1],
        head_sums[2],
    )


F32 = jnp.float32
BF16 = jnp.bfloat16
MESH_ID = pl.DeviceIdType.MESH
ANY = pl.BlockSpec(memory_space=pl.ANY)
INVMEM = pl.BlockSpec(memory_space=pltpu.VMEM)
VMEM_LIMIT = 63 * 1024 * 1024
CHUNK = 128


def flip(place, bit):
    return place + bit - 2 * bit * lax.rem(lax.div(place, bit), 2)


def flip_all(place, mask):
    for bit in (1, 2, 4):
        if mask & bit:
            place = flip(place, bit)
    return place


class Links:
    def __init__(self, sends, recvs):
        self.sends, self.recvs, self.used = sends, recvs, 0

    def copy(self, source, target, device):
        slot = self.used
        self.used += 1
        return pltpu.make_async_remote_copy(
            src_ref=source,
            dst_ref=target,
            send_sem=self.sends.at[slot],
            recv_sem=self.recvs.at[slot],
            device_id=device,
            device_id_type=MESH_ID,
        )


def greet(devices, conditions=()):
    barrier = pltpu.get_barrier_semaphore()
    for device in devices:
        pl.semaphore_signal(barrier, inc=1, device_id=device, device_id_type=MESH_ID)
    for condition, device in conditions:

        @pl.when(condition)
        def _():
            pl.semaphore_signal(barrier, inc=1, device_id=device, device_id_type=MESH_ID)

    count = len(devices)
    for condition, _ in conditions:
        count = count + jnp.where(condition, 1, 0)
    pl.semaphore_wait(barrier, count)


def add_rows(target, first, second, step=32):
    def one(number, carry):
        rows = pl.ds(pl.multiple_of(number * step, step), step)
        target[rows] = (first[rows].astype(F32) + second[rows].astype(F32)).astype(target.dtype)
        return carry

    lax.fori_loop(0, target.shape[0] // step, one, 0)


def cast_rows(target, source, step=32):
    def one(number, carry):
        rows = pl.ds(pl.multiple_of(number * step, step), step)
        target[rows] = source[rows].astype(target.dtype)
        return carry

    lax.fori_loop(0, target.shape[0] // step, one, 0)


class LineSum:
    def __init__(
        self, links, depth, row, place, own, valid, up_in, up_out, down_in, down_out, shared=None
    ):
        self.depth, self.row, self.own, self.valid = depth, row, own, valid
        above, below = lax.min(row + 1, depth - 1), lax.max(row - 1, 0)

        def slots(ref, shift):
            return {q: ref.at[q % shared if shared else q - shift] for q in range(shift, depth - 1 + shift)}

        self.up_in, self.up_out = slots(up_in, 1), slots(up_out, 1)
        self.down_in, self.down_out = slots(down_in, 0), slots(down_out, 0)
        self.ups = {
            q: links.copy(self.up_out[q], self.up_in[q], (above, place)) for q in self.up_in
        }
        self.downs = {
            q: links.copy(self.down_out[q], self.down_in[q], (below, place)) for q in self.down_in
        }

    def up(self, q, row):
        @pl.when(self.valid(q) & (self.row == row))
        def _():
            if row == 0:
                cast_rows(self.up_out[q], self.own(q))
            else:
                self.ups[q].wait_recv()
                add_rows(self.up_out[q], self.own(q), self.up_in[q])
            self.ups[q].start()

    def down(self, q, row):
        @pl.when(self.valid(q) & (self.row == row))
        def _():
            if row == self.depth - 1:
                cast_rows(self.down_out[q], self.own(q))
            else:
                self.downs[q].wait_recv()
                add_rows(self.down_out[q], self.own(q), self.down_in[q])
            self.downs[q].start()

    def phase(self, number):
        for row in range(self.depth):
            up_q = self.depth - 1 + row - number
            if row < up_q < self.depth:
                self.up(up_q, row)
            down_q = number - (self.depth - 1 - row)
            if 0 <= down_q < row:
                self.down(down_q, row)

    def finish(self, total):
        depth, row = self.depth, self.row
        for q in range(depth):

            @pl.when(self.valid(q) & (row == q))
            def _():
                if q > 0:
                    self.ups[q].wait_recv()
                if q < depth - 1:
                    self.downs[q].wait_recv()
                if 0 < q < depth - 1:
                    add_rows(total, self.up_in[q], self.down_in[q])
                    add_rows(total, total, self.own(q))
                elif q > 0:
                    add_rows(total, self.own(q), self.up_in[q])
                else:
                    add_rows(total, self.own(q), self.down_in[q])

    def drain(self):
        for q, copy in self.ups.items():
            pl.when(self.valid(q) & (self.row < q))(copy.wait_send)
        for q, copy in self.downs.items():
            pl.when(self.valid(q) & (self.row > q))(copy.wait_send)


class PlaneSum:
    def __init__(self, links, row, place, parts, pair_in, sums, relay_in, last_in):
        self.place, self.parts = place, parts
        self.pair_in, self.sums, self.relay_in, self.last_in = pair_in, sums, relay_in, last_in
        peer = {mask: (row, flip_all(place, mask)) for mask in range(1, 8)}
        self.peer = peer
        rows = last_in.shape[1] // 2
        self.halves = (pl.ds(0, rows), pl.ds(rows, rows))
        self.pair = {
            mask: links.copy(parts.at[peer[mask ^ 1][1]], pair_in.at[mask // 2], peer[1])
            for mask in (6, 2, 4, 0)
        }
        top, low = self.halves
        self.relay4 = links.copy(sums.at[3, top], relay_in.at[0], peer[4])
        self.relay2 = links.copy(sums.at[3, low], relay_in.at[1], peer[2])
        self.last2 = [
            links.copy(sums.at[1, half], last_in.at[0, half], peer[2]) for half in self.halves
        ]
        self.last4 = [
            links.copy(sums.at[2, half], last_in.at[1, half], peer[4]) for half in self.halves
        ]

    def begin(self):
        for copy in self.pair.values():
            copy.start()

    def chip(self, mask):
        index = mask // 2
        self.pair[mask].wait_recv()
        mine = self.parts.at[self.peer[mask][1] if mask else self.place]
        add_rows(self.sums.at[index], mine, self.pair_in.at[index])

    def far(self):
        self.chip(6)
        self.relay4.start()
        self.relay2.start()

    def near(self, mask):
        self.chip(mask)
        if mask:
            (self.last2[1] if mask == 2 else self.last4[0]).start()

    def first(self):
        self.far()
        for mask in (2, 4, 0):
            self.near(mask)

    def second(self):
        top, low = self.halves
        self.relay4.wait_recv()
        add_rows(self.sums.at[1, top], self.sums.at[1, top], self.relay_in.at[0])
        self.last2[0].start()
        self.relay2.wait_recv()
        add_rows(self.sums.at[2, low], self.sums.at[2, low], self.relay_in.at[1])
        self.last4[1].start()

    def finish(self, store):
        for copy in self.last2 + self.last4:
            copy.wait_recv()

        def one(number, carry):
            at = pl.ds(pl.multiple_of(number * 32, 32), 32)
            total = self.last_in[0, at].astype(F32) + self.last_in[1, at].astype(F32)
            store(at, total + self.sums[0, at].astype(F32))
            return carry

        lax.fori_loop(0, self.last_in.shape[1] // 32, one, 0)

    def drain(self):
        for copy in self.pair.values():
            copy.wait_send()
        for copy in [self.relay4, self.relay2] + self.last2 + self.last4:
            copy.wait_send()


def dot(left, right, contract, precision=None):
    return lax.dot_general(
        left, right, (contract, ((), ())), precision=precision, preferred_element_type=F32
    )


def mm(left, right):
    return dot(left, right, ((1,), (0,)))


def mm_t(left, right):
    return dot(left, right, ((1,), (1,)))


def t_mm(left, right):
    return dot(left, right, ((0,), (0,)))


def widen(values, heads, head_size):
    rows = values.shape[0]
    lane = lax.broadcasted_iota(jnp.int32, (rows, 2 * head_size), 1)
    parts = []
    for pair in range(heads // 2):
        low = jnp.broadcast_to(values[:, 2 * pair : 2 * pair + 1], (rows, 2 * head_size))
        high = jnp.broadcast_to(values[:, 2 * pair + 1 : 2 * pair + 2], (rows, 2 * head_size))
        parts.append(jnp.where(lane < head_size, low, high))
    return jnp.concatenate(parts, axis=1)


def sigmoid(values):
    return 1.0 / (1.0 + jnp.exp(-values))


def softplus(values):
    return jnp.maximum(values, 0.0) + jnp.log1p(jnp.exp(-jnp.abs(values)))


def split_pair(values, head_size):
    lane = lax.broadcasted_iota(jnp.int32, values.shape, 1)
    zero = jnp.zeros_like(values)
    return jnp.where(lane < head_size, values, zero), jnp.where(lane < head_size, zero, values)


def triangles():
    rows = lax.broadcasted_iota(jnp.int32, (CHUNK, CHUNK), 0)
    cols = lax.broadcasted_iota(jnp.int32, (CHUNK, CHUNK), 1)
    return rows >= cols


def head_decays(cum, cum_t, head, causal):
    gap = cum[:, head : head + 1] - cum_t[head : head + 1, :]
    return jnp.exp(jnp.where(causal, gap, -1e30))


def plane_total(links, sums, landed, peer, count):
    landed[0] = sums[...].T[:count]
    copies = [links.copy(landed.at[0], landed.at[mask], peer[mask]) for mask in peer]
    for copy in copies:
        copy.start()

    def end():
        for copy in copies:
            copy.wait()
        got = [landed[mask] for mask in range(len(peer) + 1)]
        while len(got) > 1:
            got = [got[k] + got[k + 1] for k in range(0, len(got), 2)]
        return got[0]

    return end


def by_column(values):
    return jnp.concatenate([values, jnp.zeros((128 - values.shape[0], CHUNK), F32)], axis=0).T


class Line:
    def __init__(self, links, depth, row, place, blocks, valid=None):
        self.depth, self.row = depth, row
        above, below = lax.min(row + 1, depth - 1), lax.max(row - 1, 0)
        self.steps = []
        for step in range(depth - 1):
            up_sent, up_got = row - step, row - 1 - step
            down_sent, down_got = row + step, row + 1 + step
            ways = []
            for sends, shard, gets, got, device in (
                ((row < depth - 1) & (up_sent >= 0), up_sent, (row > 0) & (up_got >= 0), up_got, above),
                ((row > 0) & (down_sent < depth), down_sent, (row < depth - 1) & (down_got < depth), down_got, below),
            ):
                shard = lax.clamp(0, shard, depth - 1)
                got = lax.clamp(0, got, depth - 1)
                if valid is not None:
                    sends, gets = sends & valid(shard), gets & valid(got)
                copies = [links.copy(block, block, (device, place)) for block in blocks(shard)]
                ways.append((sends, gets, copies))
            self.steps.append(ways)

    def send(self, number):
        for sends, _, copies in self.steps[number]:

            @pl.when(sends)
            def _():
                for copy in copies:
                    copy.start()

    def wait(self, number):
        for _, gets, copies in self.steps[number]:

            @pl.when(gets)
            def _():
                for copy in copies:
                    copy.wait_recv()

    def drain(self):
        for ways in self.steps:
            for sends, _, copies in ways:

                @pl.when(sends)
                def _():
                    for copy in copies:
                        copy.wait_send()


class Pass:
    def __init__(self, links, peer, place, own, everyone):
        rows = own.shape[0] // 2
        mine = everyone.at[place]
        from2, from4, far = (everyone.at[peer[mask][1]] for mask in (2, 4, 6))
        top, low = pl.ds(0, rows), pl.ds(rows, rows)
        self.kept = None
        self.to2 = links.copy(own, mine, peer[2])
        self.to4 = links.copy(own, mine, peer[4])
        self.to1 = links.copy(own, mine, peer[1])
        self.relay4 = links.copy(from2.at[top], from2.at[top], peer[4])
        self.relay2 = links.copy(from4.at[low], from4.at[low], peer[2])
        self.pair2 = links.copy(from2, from2, peer[1])
        self.pair4 = links.copy(from4, from4, peer[1])
        self.pair6 = links.copy(far.at[top], far.at[top], peer[1])
        self.pair7 = links.copy(far.at[low], far.at[low], peer[1])

    def first(self):
        self.to2.start()
        self.to4.start()
        self.to1.start()

    def relay(self):
        self.to2.wait_recv()
        self.relay4.start()
        self.to4.wait_recv()
        self.relay2.start()
        self.pair2.start()
        self.pair4.start()

    def last(self):
        self.relay4.wait_recv()
        self.pair6.start()
        self.relay2.wait_recv()
        self.pair7.start()

    def end(self):
        for copy in (self.to1, self.pair2, self.pair4, self.pair6, self.pair7):
            copy.wait_recv()

    def drain(self):
        for copy in (
            self.to2,
            self.to4,
            self.to1,
            self.relay4,
            self.relay2,
            self.pair2,
            self.pair4,
            self.pair6,
            self.pair7,
        ):
            copy.wait_send()


def lay_out(pieces, row, count):
    tiles = [None] * -(-count * len(pieces) // 128)
    for index, piece in enumerate(pieces):
        tile, shift = divmod(index * count, 128)
        moved = pltpu.roll(piece, shift, 1) if shift else piece
        lane = lax.broadcasted_iota(jnp.int32, piece.shape, 1)
        parts = [(tile, jnp.where((lane >= shift) & (lane < shift + count), moved, 0.0))]
        if shift + count > 128:
            parts.append((tile + 1, jnp.where(lane < shift + count - 128, moved, 0.0)))
        for at, part in parts:
            tiles[at] = part if tiles[at] is None else tiles[at] + part
    return tiles


def channel_windows(ref, place, plane, half, run):
    core, chip = lax.rem(place, 2), lax.div(place, 2)
    parts = []
    for j in range(half):
        start = ((core * half + j) * plane + chip) * run
        base = pl.multiple_of(lax.div(start, 128) * 128, 128)
        window = ref[:, pl.ds(base, run + 64)]
        moved = pltpu.roll(window, run, 1)
        parts.append(jnp.where(lax.rem(start, 128) == 0, window, moved)[:, :run])
    return jnp.concatenate(parts, axis=1)


def head_choice(place, plane, half, group, heads):
    core, chip = lax.rem(place, 2), lax.div(place, 2)
    head = lax.broadcasted_iota(jnp.int32, (128, 128), 0)
    lane = lax.broadcasted_iota(jnp.int32, (128, 128), 1)
    part = sum(((lane >= j * group).astype(jnp.int32) for j in range(1, half)), jnp.zeros_like(lane))
    chosen = ((core * half + part) * plane + chip) * group + lane - part * group
    return jnp.where((head == chosen) & (lane < heads), 1.0, 0.0)


def forward_kernel(
    dims,
    x_own,
    cot_own,
    wg_send,
    wx_send,
    wb_send,
    wo_own,
    pack,
    head_params,
    normed_out,
    cot_out,
    wg_out,
    wx_out,
    wb_out,
    wo_out,
    conv_out,
    pre_out,
    dt_out,
    gate_out,
    y_out,
    states_out,
    norms_out,
    taps_out,
    rows_out,
    w_dt_out,
    w_dt_all_out,
    x_all,
    normed_all,
    cot_all,
    wg,
    wx,
    wb,
    wo,
    packs,
    conv_in,
    pre_all,
    dt_all,
    gate_all,
    y_all,
    states,
    ext,
    state,
    full,
    sums,
    sums_in,
    sends,
    recvs,
    locals_,
    stores,
):
    depth, width, heads, head_size, size, kernel, own_ch, inner_all = dims
    half, plane = depth // 2, width // 2
    inner = heads * head_size
    run = inner // half
    model = x_own.shape[1]
    piece = x_own.shape[0] // 2
    rows = 2 * piece
    slots = 2
    blocks = slots * width // 2
    row, place = lax.axis_index("dp"), lax.axis_index("seq")
    core = lax.rem(place, 2)
    links = Links(sends, recvs)
    peer = {mask: (row, flip_all(place, mask)) for mask in range(1, width)}
    line_peers = [(lax.rem(row + up, depth), place) for up in range(1, depth)]
    greet([peer[mask] for mask in range(1, width)] + line_peers)

    kept = [
        pltpu.make_async_copy(wx_send.at[place], wx.at[row, place], locals_.at[0]),
        pltpu.make_async_copy(wb_send.at[core], wb.at[core, row, place], locals_.at[1]),
        pltpu.make_async_copy(wg_send.at[place], wg.at[row, place], locals_.at[2]),
        pltpu.make_async_copy(x_own, x_all.at[place], locals_.at[3]),
        pltpu.make_async_copy(cot_own, cot_all.at[place], locals_.at[4]),
        pltpu.make_async_copy(pack, packs.at[row, place], locals_.at[5]),
    ]
    for copy in kept:
        copy.start()

    out_home = lax.div(row, half) == core
    out_block = wo.at[lax.rem(row, half), core]
    out_kept = pltpu.make_async_copy(wo_own, out_block, locals_.at[6])
    out_pair = links.copy(wo_own, out_block, peer[1])
    pl.when(out_home)(out_kept.start)
    pl.when(jnp.logical_not(out_home))(out_pair.start)

    order = (6, 2, 4, 7, 3, 5, 1)
    plane_x, plane_g = [], []
    for mask in order:
        target = peer[mask][1]
        its_core = lax.rem(target, 2)
        plane_x.append(links.copy(wx_send.at[target], wx.at[row, place], peer[mask]))
        plane_x.append(
            links.copy(wb_send.at[its_core], wb.at[its_core, row, place], peer[mask])
        )
        plane_g.append(links.copy(wg_send.at[target], wg.at[row, place], peer[mask]))
    for copy in plane_x:
        copy.start()
    pack_line = [links.copy(pack, packs.at[row, place], device) for device in line_peers]
    for copy in pack_line:
        copy.start()
    x_pass = Pass(links, peer, place, x_own, x_all)
    cot_pass = Pass(links, peer, place, cot_own, cot_all)
    x_pass.first()

    out_line = Line(
        links,
        depth,
        row,
        place,
        lambda shard: [wo.at[lax.rem(shard, half)]],
        lambda shard: lax.div(shard, half) == core,
    )
    x_line = Line(links, depth, row, place, lambda shard: [wx.at[shard], wb.at[core, shard]])
    gate_line = Line(links, depth, row, place, lambda shard: [wg.at[shard]])

    pl.when(out_home)(out_kept.wait)
    pl.when(out_home)(out_pair.wait_recv)
    out_line.send(0)
    kept[0].wait()
    kept[1].wait()
    for copy in plane_x:
        copy.wait_recv()
    x_line.send(0)
    kept[5].wait()
    for copy in pack_line:
        copy.wait_recv()
    mine = packs.at[:, place]
    pack_plane = [links.copy(mine, mine, peer[mask]) for mask in order]
    for copy in pack_plane:
        copy.start()
    for copy in plane_g:
        copy.start()
    x_pass.relay()
    x_line.wait(0)
    if depth > 2:
        x_line.send(1)
    for copy in pack_plane:
        copy.wait_recv()

    small = [
        packs[z, s, model // (depth * width) : model // (depth * width) + 16, :].astype(F32)[:8]
        for z in range(depth)
        for s in range(width)
    ]
    choice = head_choice(place, plane, half, run // head_size, heads)
    tap_tiles = lay_out(small, 0, own_ch)
    for at, tile in enumerate(tap_tiles):
        full[:, at * 128 : (at + 1) * 128] = tile
    taps_out[:, :inner] = channel_windows(full, place, plane, half, run)
    taps_out[:, inner:] = full[:, inner_all : inner_all + 2 * size]
    gate_tiles = lay_out(small, 5, inner_all // (depth * width))
    for at, tile in enumerate(gate_tiles):
        full[:, at * 128 : (at + 1) * 128] = tile
    gate_gain = channel_windows(full, place, plane, half, run)[5:6]
    norm_tiles = lay_out(small, 6, model // (depth * width))
    norm_gain = jnp.concatenate([tile[6:7] for tile in norm_tiles], axis=1)
    chosen = dot(head_params[...], choice, ((1,), (0,)), lax.Precision.HIGHEST)
    lane = lax.broadcasted_iota(jnp.int32, (1, 128), 1)
    rates = jnp.where(lane < heads, -jnp.exp(chosen[1:2]), 0.0)
    skip = widen(chosen[2:3], heads, head_size)
    dt_rows = packs[:, :, 0 : model // (depth * width), :].reshape(model, 128)
    w_dt_all_out[...] = dt_rows
    w_dt_out[...] = mm(dt_rows, choice.astype(BF16)).astype(BF16)
    rows_out[...] = jnp.zeros_like(rows_out)
    rows_out[0:1, :] = norm_gain
    rows_out[1:2, :inner] = gate_gain
    rows_out[2:3, :inner] = skip
    rows_out[3:4, :128] = chosen[0:1]
    rows_out[4:5, :128] = rates

    x_pass.last()
    cot_pass.first()

    def normalise(index, carry):
        for part in range(2):
            held = x_all[index, part * piece : (part + 1) * piece, :].astype(F32)
            inv = lax.rsqrt(jnp.mean(held * held, axis=1, keepdims=True) + EPS)
            normed_all[index, part * piece : (part + 1) * piece, :] = (
                held * inv * rows_out[0:1, :]
            ).astype(BF16)
        return carry

    x_line.wait(1) if depth > 2 else None
    if depth > 3:
        x_line.send(2)
    for copy in plane_g:
        copy.wait_recv()
    kept[2].wait()
    x_pass.end()
    kept[3].wait()
    lax.fori_loop(0, width, normalise, 0)
    if depth > 3:
        x_line.wait(2)
    gate_line.send(0)
    mine_bc = wb.at[core]
    pair_bc = links.copy(mine_bc, mine_bc, peer[1])
    pair_bc.start()
    saves = [pltpu.make_async_copy(normed_all, normed_out, locals_.at[7])]
    saves[0].start()
    pair_bc.wait_recv()

    causal = triangles()
    ones = causal.astype(F32)

    def stored(index):
        at = pl.ds(pl.multiple_of(index * rows, rows), rows)
        pairs = [
            (conv_in.at[at], conv_out.at[at]),
            (pre_all.at[at], pre_out.at[at]),
            (dt_all.at[at], dt_out.at[at]),
            (y_all.at[at], y_out.at[at]),
            (
                states.at[pl.ds(index * (rows // CHUNK), rows // CHUNK)],
                states_out.at[pl.ds(index * (rows // CHUNK), rows // CHUNK)],
            ),
        ]
        return [
            pltpu.make_async_copy(source, target, stores.at[k, index])
            for k, (source, target) in enumerate(pairs)
        ]

    per_slot = blocks // slots

    def scan_block(index, carry):
        slot, block = lax.div(index, per_slot), lax.rem(index, per_slot)
        at = pl.multiple_of(index * rows, rows)

        @pl.when(block == 0)
        def _():
            ext[0:8, :] = jnp.zeros((8, ext.shape[1]), F32)
            state[...] = jnp.zeros_like(state)

        tokens = normed_all[
            pl.ds(2 * block, 2), pl.ds(pl.multiple_of(slot * piece, piece), piece), :
        ].reshape(rows, model)
        ext[8:, :inner] = mm(tokens, wx[...].reshape(model, inner))
        ext[8:, inner : inner + size] = mm(tokens, wb[0].reshape(model, size))
        ext[8:, inner + size :] = mm(tokens, wb[1].reshape(model, size))
        dt_arg = mm(tokens, w_dt_out[...]) + rows_out[3:4, :128]
        dt_all[pl.ds(at, rows), :] = dt_arg
        pre = taps_out[kernel : kernel + 1, :] + sum(
            taps_out[k : k + 1, :] * ext[9 - kernel + k : 9 - kernel + k + rows, :]
            for k in range(kernel)
        )
        conv_in[pl.ds(at, rows), :] = ext[8:, :]
        ext[0:8, :] = ext[rows : rows + 8, :]
        pre_all[pl.ds(at, rows), :] = pre
        act = pre * sigmoid(pre)
        dt_block = softplus(dt_arg)
        steps_block = dt_block * rows_out[4:5, :128]
        for sub in range(rows // CHUNK):
            part = slice(sub * CHUNK, (sub + 1) * CHUNK)
            x = act[part, :inner]
            b = act[part, inner : inner + size].astype(BF16)
            c = act[part, inner + size :].astype(BF16)
            cum = dot(ones, steps_block[part], ((1,), (0,)), lax.Precision.HIGHEST)
            cum_t = cum.T
            total = cum[CHUNK - 1 : CHUNK, :]
            x_dt = x * widen(dt_block[part], heads, head_size)
            x_dt16 = x_dt.astype(BF16)
            held = state[...]
            held16 = held.astype(BF16)
            states[index * (rows // CHUNK) + sub] = held16
            y = mm(c, held16) * widen(jnp.exp(cum), heads, head_size)
            y = y + rows_out[2:3, :inner] * x
            cb = mm_t(c, b)
            pieces = []
            for pair in range(heads // 2):
                lanes = slice(2 * pair * head_size, 2 * (pair + 1) * head_size)
                mixing = jnp.concatenate(
                    [
                        (head_decays(cum, cum_t, 2 * pair + k, causal) * cb).astype(BF16)
                        for k in range(2)
                    ],
                    axis=1,
                )
                pieces.append(
                    mm(mixing, jnp.concatenate(split_pair(x_dt16[:, lanes], head_size), axis=0))
                )
            y_all[pl.ds(pl.multiple_of(at + sub * CHUNK, CHUNK), CHUNK), :] = y + jnp.concatenate(
                pieces, axis=1
            )
            weighted = (x_dt * widen(jnp.exp(total - cum), heads, head_size)).astype(BF16)
            state[...] = held * widen(jnp.exp(total), heads, head_size) + t_mm(b, weighted)
        for copy in stored(index):
            copy.start()

        @pl.when(index == 1)
        def _():
            gate_line.wait(0)
            if depth > 2:
                gate_line.send(1)

        @pl.when(index == 2)
        def _():
            cot_pass.relay()

        if depth > 2:

            @pl.when(index == 4)
            def _():
                gate_line.wait(1)
                if depth > 3:
                    gate_line.send(2)

        @pl.when(index == 5)
        def _():
            cot_pass.last()
            out_line.wait(0)
            if depth <= 3 and depth > 2:
                out_line.send(1)

        if depth > 3:

            @pl.when(index == 6)
            def _():
                gate_line.wait(2)
                out_line.send(1)

        return carry

    lax.fori_loop(0, blocks, scan_block, 0)

    chunk_lane = lax.broadcasted_iota(jnp.int32, (CHUNK, 128), 1)
    sums[...] = jnp.zeros_like(sums)

    def gate_block(index, carry):
        slot, block = lax.div(index, per_slot), lax.rem(index, per_slot)
        at = pl.multiple_of(index * rows, rows)
        tokens = normed_all[
            pl.ds(2 * block, 2), pl.ds(pl.multiple_of(slot * piece, piece), piece), :
        ].reshape(rows, model)
        gate = mm(tokens, wg[...].reshape(model, inner))
        gate_all[pl.ds(at, rows), :] = gate
        gated = y_all[pl.ds(at, rows), :] * (gate * sigmoid(gate))
        for sub in range(rows // CHUNK):
            part = gated[sub * CHUNK : (sub + 1) * CHUNK]
            total = jnp.sum(part * part, axis=1, keepdims=True)
            sums[...] = jnp.where(chunk_lane == index * (rows // CHUNK) + sub, total, sums[...])
        if depth > 2:

            @pl.when(index == blocks // 2)
            def _():
                out_line.wait(1)
                if depth > 3:
                    out_line.send(2)

        return carry

    lax.fori_loop(0, blocks, gate_block, 0)
    save_gate = pltpu.make_async_copy(gate_all, gate_out, locals_.at[8])
    save_gate.start()
    cot_pass.end()
    kept[4].wait()
    save_cot = pltpu.make_async_copy(cot_all, cot_out, locals_.at[9])
    save_cot.start()
    if depth > 3:
        out_line.wait(2)
    save_weights = [
        pltpu.make_async_copy(source, target, locals_.at[10 + k])
        for k, (source, target) in enumerate(
            ((wg, wg_out), (wx, wx_out), (wb, wb_out), (wo, wo_out))
        )
    ]
    for copy in save_weights:
        copy.start()

    squares = plane_total(links, sums, sums_in, peer, 2 * blocks)
    inv_gate = lax.rsqrt(squares() / inner_all + EPS)
    norms_out[...] = by_column(inv_gate)

    for copies in (plane_x, plane_g, pack_line, pack_plane, [pair_bc]):
        for copy in copies:
            copy.wait_send()
    pl.when(jnp.logical_not(out_home))(out_pair.wait_send)
    for line in (out_line, x_line, gate_line):
        line.drain()
    x_pass.drain()
    cot_pass.drain()
    for copy in saves + [save_gate, save_cot] + save_weights:
        copy.wait()

    def stores_end(index, carry):
        for copy in stored(index):
            copy.wait()
        return carry

    lax.fori_loop(0, blocks, stores_end, 0)


def forward(dims, x_own, cot_own, wg_send, wx_send, wb_send, wo_own, pack, head_params, collective):
    depth, width, heads, head_size, size, kernel, own_ch, inner_all = dims
    inner = heads * head_size
    rows, model = x_own.shape
    tokens = rows * width
    wide = inner + 2 * size
    shape = jax.ShapeDtypeStruct
    chunks = tokens // CHUNK
    weights = [
        ((depth,) + wg_send.shape, BF16),
        ((depth,) + wx_send.shape, BF16),
        ((2, depth, width) + wb_send.shape[1:], BF16),
        ((depth // 2, 2) + wo_own.shape, BF16),
    ]
    kept = [
        ((tokens, wide), F32),
        ((tokens, wide), F32),
        ((tokens, 128), F32),
        ((tokens, inner), F32),
        ((tokens, inner), F32),
        ((chunks, size, inner), BF16),
    ]
    in_hbm = [((width, rows, model), BF16)] * 2 + weights + kept
    in_vmem = [((CHUNK, 128), F32), ((8, wide), F32), ((8, model), F32)] + [((model, 128), BF16)] * 2
    return pl.pallas_call(
        functools.partial(forward_kernel, dims),
        out_shape=tuple(shape(*s) for s in in_hbm + in_vmem),
        in_specs=[INVMEM] * 8,
        out_specs=(ANY,) * len(in_hbm) + (INVMEM,) * len(in_vmem),
        scratch_shapes=[pltpu.VMEM((width, rows, model), BF16)] * 3
        + [pltpu.VMEM(*s) for s in weights]
        + [pltpu.VMEM((depth, width) + pack.shape, BF16)]
        + [pltpu.VMEM(*s) for s in kept]
        + [
            pltpu.VMEM((rows + 8, wide), F32),
            pltpu.VMEM((size, inner), F32),
            pltpu.VMEM((8, -(-own_ch * depth * width // 128) * 128), F32),
            pltpu.VMEM((CHUNK, 128), F32),
            pltpu.VMEM((width, chunks, 128), F32),
            pltpu.SemaphoreType.DMA((112,)),
            pltpu.SemaphoreType.DMA((112,)),
            pltpu.SemaphoreType.DMA((16,)),
            pltpu.SemaphoreType.DMA((5, tokens // rows)),
        ],
        compiler_params=pltpu.CompilerParams(
            collective_id=collective, has_side_effects=True, vmem_limit_bytes=VMEM_LIMIT
        ),
        name="forward_fused",
    )(x_own, cot_own, wg_send, wx_send, wb_send, wo_own, pack, head_params)


class PlaneRows:
    def __init__(self, links, row, place, parts, landed, local):
        mine = landed.at[place]
        peers = [(row, flip_all(place, mask)) for mask in (6, 7, 2, 3, 4, 5, 1)]
        self.copies = [links.copy(parts.at[peer[1]], mine, peer) for peer in peers]
        self.kept = pltpu.make_async_copy(parts.at[place], mine, local)

    def begin(self):
        for copy in self.copies:
            copy.start()
        self.kept.start()

    def arrived(self):
        self.kept.wait()
        for copy in self.copies:
            copy.wait_recv()

    def drain(self):
        for copy in self.copies:
            copy.wait_send()


class SendBack:
    def __init__(self, links, row, place, sent, back, local):
        self.rows = back.shape[1]
        self.sent, self.back, self.place = sent, back, place
        mine = back.at[place]
        self.copies = [
            links.copy(self.block((row, flip_all(place, mask))[1]), mine, (row, flip_all(place, mask)))
            for mask in (6, 2, 4, 7, 3, 5, 1)
        ]
        self.kept = pltpu.make_async_copy(self.block(place), mine, local)

    def block(self, target):
        return self.sent.at[pl.ds(pl.multiple_of(target * self.rows, self.rows), self.rows)]

    def begin(self):
        for copy in self.copies:
            copy.start()
        self.kept.start()

    def end(self):
        self.kept.wait()
        for copy in self.copies:
            copy.wait()


def turn(target, source):
    for at in range(0, source.shape[0], 128):
        target[:, at : at + 128] = source[at : at + 128, :].T.astype(target.dtype)


def reverse_kernel(
    dims,
    cot_hbm,
    normed_hbm,
    gate_hbm,
    y_hbm,
    pre_hbm,
    conv_hbm,
    dt_hbm,
    states_hbm,
    wo_hbm,
    norms,
    taps,
    rows_in,
    head_sum,
    x_own,
    d_gate_hbm,
    d_x_hbm,
    d_bc_hbm,
    d_arg_hbm,
    output,
    gate_back,
    out_grad,
    channel_sums,
    head_sums,
    cot_all,
    normed_all,
    gate_all,
    y_all,
    d_y_all,
    wo,
    d_gate,
    d_x_all,
    d_bc,
    d_arg_all,
    g_out,
    g_gate,
    pre_two,
    conv_two,
    dt_two,
    states_two,
    later,
    d_ext,
    o_pair,
    o_sums,
    o_relay,
    o_last,
    out_up_in,
    out_up_out,
    out_down_in,
    out_down_out,
    gate_up_in,
    gate_up_out,
    gate_down_in,
    gate_down_out,
    out_sum,
    out_far,
    gate_sum,
    gate_sent,
    means,
    sums_in,
    sends,
    recvs,
    locals_,
    streams,
):
    depth, width, heads, head_size, size, kernel, own_ch, inner_all = dims
    half = depth // 2
    inner = heads * head_size
    model = cot_all.shape[2]
    piece = cot_all.shape[1] // 2
    rows = 2 * piece
    slots = 2
    blocks = slots * width // 2
    per_slot = blocks // slots
    subs = rows // CHUNK
    row, place = lax.axis_index("dp"), lax.axis_index("seq")
    core = lax.rem(place, 2)
    links = Links(sends, recvs)
    above, below = lax.min(row + 1, depth - 1), lax.max(row - 1, 0)
    peer = {mask: (row, flip_all(place, mask)) for mask in range(1, width)}

    loads = [
        pltpu.make_async_copy(source, target, locals_.at[k])
        for k, (source, target) in enumerate(
            (
                (y_hbm, y_all),
                (gate_hbm, gate_all),
                (cot_hbm, cot_all),
                (wo_hbm, wo),
                (normed_hbm, normed_all),
            )
        )
    ]
    for copy in loads:
        copy.start()

    def place_of(number):
        slot = lax.div(number, per_slot)
        return slot, per_slot - 1 - lax.rem(number, per_slot)

    def fetch(number):
        slot, block = place_of(number)
        index = slot * per_slot + block
        at = pl.ds(pl.multiple_of(index * rows, rows), rows)
        buffer = lax.rem(number, 2)
        pairs = (
            (pre_hbm.at[at], pre_two.at[buffer]),
            (conv_hbm.at[at, pl.ds(0, inner)], conv_two.at[buffer]),
            (dt_hbm.at[at], dt_two.at[buffer]),
            (states_hbm.at[pl.ds(index * subs, subs)], states_two.at[buffer]),
        )
        return [
            pltpu.make_async_copy(source, target, streams.at[buffer, k])
            for k, (source, target) in enumerate(pairs)
        ]

    for copy in fetch(0):
        copy.start()
    greet(
        [peer[mask] for mask in range(1, width)],
        [(row < depth - 1, (above, place)), (row > 0, (below, place))],
    )

    out_line = LineSum(
        links,
        depth,
        row,
        place,
        lambda q: g_out.at[pl.ds((q % half) * (inner // half), inner // half)],
        lambda q: core == q // half,
        out_up_in,
        out_up_out,
        out_down_in,
        out_down_out,
        half,
    )
    cols = model // depth
    gate_line = LineSum(
        links,
        depth,
        row,
        place,
        lambda q: g_gate.at[:, pl.ds(q * cols, cols)],
        lambda q: row >= 0,
        gate_up_in,
        gate_up_out,
        gate_down_in,
        gate_down_out,
    )
    o_plane = PlaneSum(links, row, place, cot_all, o_pair, o_sums, o_relay, o_last)
    send_gate = SendBack(links, row, place, gate_sent, gate_back, locals_.at[6])

    chunk_lane = lax.broadcasted_iota(jnp.int32, (CHUNK, 128), 1)

    def column(ref, index):
        parts = [
            jnp.sum(
                jnp.where(chunk_lane == index * subs + sub, ref[...], 0.0),
                axis=1,
                keepdims=True,
            )
            for sub in range(subs)
        ]
        return jnp.concatenate(parts, axis=0)

    def tokens_of(ref, index):
        slot, block = lax.div(index, per_slot), lax.rem(index, per_slot)
        return ref.at[pl.ds(2 * block, 2), pl.ds(pl.multiple_of(slot * piece, piece), piece), :]

    gate_gain = rows_in[1:2, :inner]
    skip = rows_in[2:3, :inner]

    def normed_block(index, carry):
        at = pl.ds(pl.multiple_of(index * rows, rows), rows)
        gate = gate_all[at, :]
        hat = y_all[at, :] * (gate * sigmoid(gate)) * column(norms, index)
        tokens_of(d_gate, index)[...] = (
            (hat * gate_gain).astype(BF16).reshape(2, piece, inner)
        )
        return carry

    loads[0].wait()
    loads[1].wait()
    lax.fori_loop(0, blocks, normed_block, 0)

    everything = slots * width * piece

    def out_grad_tile(number, carry):
        at = pl.ds(pl.multiple_of(number * 128, 128), 128)
        left = d_gate[:, :, at].reshape(everything, 128)
        g_out[at, :] = t_mm(left, cot_all[...].reshape(everything, model))
        return carry

    loads[2].wait()
    lax.fori_loop(0, inner // 128, out_grad_tile, 0)
    out_line.phase(0)

    def cot_block(index, carry):
        at = pl.ds(pl.multiple_of(index * rows, rows), rows)
        tokens = tokens_of(cot_all, index)[...].reshape(rows, model)
        dgn = mm_t(tokens, wo[...].reshape(inner, model))
        d_y_all[at, :] = dgn
        gate = gate_all[at, :]
        cross = dgn * gate_gain * y_all[at, :] * (gate * sigmoid(gate))
        for sub in range(subs):
            part = cross[sub * CHUNK : (sub + 1) * CHUNK]
            total = jnp.sum(part, axis=1, keepdims=True)
            means[...] = jnp.where(chunk_lane == index * subs + sub, total, means[...])
        return carry

    loads[3].wait()
    means[...] = jnp.zeros_like(means)
    lax.fori_loop(0, blocks, cot_block, 0)
    crosses = plane_total(links, means, sums_in, peer, 2 * blocks)

    def out_block(index, carry):
        cot_all[index] = mm(d_gate[index], wo[...].reshape(inner, model)).astype(BF16)
        return carry

    lax.fori_loop(0, width, out_block, 0)
    o_plane.begin()
    means[...] = norms[...] * by_column(crosses() / inner_all)

    def gate_block(index, carry):
        at = pl.ds(pl.multiple_of(index * rows, rows), rows)
        gate = gate_all[at, :]
        sig = sigmoid(gate)
        gate_act = gate * sig
        y = y_all[at, :]
        inv = column(norms, index)
        hat = y * gate_act * inv
        d_gated = inv * (d_y_all[at, :] * gate_gain - hat * column(means, index))
        d_y_all[at, :] = d_gated * gate_act
        tokens_of(d_gate, index)[...] = (
            (d_gated * y * sig * (1.0 + gate * (1.0 - sig))).astype(BF16).reshape(2, piece, inner)
        )
        return carry

    lax.fori_loop(0, blocks, gate_block, 0)
    save_gate = pltpu.make_async_copy(d_gate, d_gate_hbm, locals_.at[7])
    save_gate.start()

    def gate_grad_tile(number, carry):
        at = pl.ds(pl.multiple_of(number * 128, 128), 128)
        left = d_gate[:, :, at].reshape(everything, 128)
        g_gate[at, :] = t_mm(left, normed_all[...].reshape(everything, model))
        return carry

    loads[4].wait()
    lax.fori_loop(0, inner // 128, gate_grad_tile, 0)
    gate_line.phase(0)
    o_plane.first()

    channel_sums[...] = jnp.zeros_like(channel_sums)
    head_sums[...] = jnp.zeros_like(head_sums)
    causal = triangles()
    ones = causal.astype(F32)
    before = 1.0 - ones.T

    def head_totals(values):
        return dot(values, head_sum[...], ((1,), (0,)), lax.Precision.HIGHEST)

    def pump_first():
        if depth > 2:
            out_line.phase(1)

    def pump_second():
        o_plane.second()
        if depth > 3:
            out_line.phase(2)

    def pump_gate():
        if depth > 2:
            gate_line.phase(1)

    def pump_gate_last():
        if depth > 3:
            gate_line.phase(2)

    pumps = {
        0: pump_first,
        2: pump_second,
        4: pump_gate,
        5: lambda: o_plane.finish(store_output),
        6: pump_gate_last,
    }

    def store_output(at, total):
        output[at] = (x_own[at].astype(F32) + total).astype(BF16)

    def scan_block(number, carry):
        slot, block = place_of(number)
        index = slot * per_slot + block
        buffer = lax.rem(number, 2)
        for copy in fetch(number):
            copy.wait()

        @pl.when(number + 1 < blocks)
        def _():
            for copy in fetch(number + 1):
                copy.start()

        @pl.when(block == per_slot - 1)
        def _():
            later[...] = jnp.zeros_like(later)
            d_ext[rows:, :] = jnp.zeros((8, inner), F32)

        pre = pre_two[buffer]
        pre_sig = sigmoid(pre)
        act = pre * pre_sig
        slope = pre_sig[:, :inner] * (1.0 + pre[:, :inner] * (1.0 - pre_sig[:, :inner]))
        dt_arg = dt_two[buffer]
        dt_block = softplus(dt_arg)
        rates = rows_in[4:5, :128]
        steps_block = dt_block * rates
        for sub in reversed(range(subs)):
            part = slice(sub * CHUNK, (sub + 1) * CHUNK)
            at = pl.ds(pl.multiple_of(index * rows + sub * CHUNK, CHUNK), CHUNK)
            x = act[part, :inner]
            b = act[part, inner : inner + size].astype(BF16)
            c = act[part, inner + size :].astype(BF16)
            dt = dt_block[part]
            cum = dot(ones, steps_block[part], ((1,), (0,)), lax.Precision.HIGHEST)
            cum_t = cum.T
            total = cum[CHUNK - 1 : CHUNK, :]
            dt_wide = widen(dt, heads, head_size)
            x_dt = x * dt_wide
            x_dt16 = x_dt.astype(BF16)
            d_y = d_y_all[at, :]
            d_y16 = d_y.astype(BF16)
            cum_wide = widen(jnp.exp(cum), heads, head_size)
            d_read = (d_y * cum_wide).astype(BF16)
            out_wide = widen(jnp.exp(total - cum), heads, head_size)
            held16 = states_two[buffer, sub]
            read = mm(c, held16) * cum_wide
            grown = later[...]
            grown16 = grown.astype(BF16)
            d_x_later = out_wide * mm(b, grown16)
            d_b = mm_t(grown16, (x_dt * out_wide).astype(BF16))
            d_c = mm_t(held16, d_read)
            later[...] = grown * widen(jnp.exp(total), heads, head_size) + t_mm(c, d_read)
            cb = mm_t(c, b)
            d_cb = jnp.zeros((CHUNK, CHUNK), F32)
            pieces = []
            for pair in range(heads // 2):
                lanes = slice(2 * pair * head_size, 2 * (pair + 1) * head_size)
                d_y_split = split_pair(d_y16[:, lanes], head_size)
                mixing = []
                for k in range(2):
                    decay = head_decays(cum, cum_t, 2 * pair + k, causal)
                    mixing.append((decay * cb).astype(BF16))
                    d_cb = d_cb + decay * mm_t(d_y_split[k], x_dt16[:, lanes])
                pieces.append(
                    t_mm(jnp.concatenate(mixing, axis=0), jnp.concatenate(d_y_split, axis=0))
                )
            d_x_near = jnp.concatenate(pieces, axis=1)
            d_x_dt = d_x_later + d_x_near
            d_cb16 = d_cb.astype(BF16)
            d_b = d_b + t_mm(c, d_cb16)
            d_c = d_c + dot(b, d_cb16, ((0,), (1,)))
            d_bc[:size, at] = d_b.astype(BF16)
            d_bc[size:, at] = d_c.astype(BF16)
            d_x = d_x_dt * dt_wide + skip * d_y
            near = y_all[at, :] - skip * x - read
            cross_wide = d_y * read + d_y16.astype(F32) * near - x_dt16.astype(F32) * d_x_near
            d_dt_direct = head_totals(x * d_x_dt)
            d_cum = head_totals(cross_wide)
            through = head_totals(x_dt * d_x_later)
            over = head_totals(
                jnp.broadcast_to(
                    jnp.sum(grown * held16.astype(F32), axis=0, keepdims=True), (8, inner)
                )
            )
            d_log = (
                dot(ones, d_cum, ((0,), (0,)), lax.Precision.HIGHEST)
                + dot(before, through, ((1,), (0,)), lax.Precision.HIGHEST)
                + over[0:1, :] * jnp.exp(total)
            )
            d_dt = d_dt_direct + rates * d_log
            d_arg = d_dt * sigmoid(dt_arg[part])
            d_arg_all[2 * block + sub, pl.ds(pl.multiple_of(slot * piece, piece), piece), :] = (
                d_arg.astype(BF16)
            )
            head_sums[0:1, :] += jnp.sum(d_arg, axis=0, keepdims=True)
            head_sums[1:2, :] += jnp.sum(d_log * dt, axis=0, keepdims=True) * rates
            channel_sums[5:6, :] += jnp.sum(d_y * x, axis=0, keepdims=True)
            d_ext[part, :] = d_x * slope[part]

        d_conv = jnp.zeros((rows, inner), F32)
        x_in = conv_two[buffer]
        for k in range(kernel):
            moved = d_ext[kernel - 1 - k : kernel - 1 - k + rows, :]
            d_conv = d_conv + taps[k : k + 1, :inner] * moved
            channel_sums[k : k + 1, :] += jnp.sum(moved * x_in, axis=0, keepdims=True)
        channel_sums[4:5, :] += jnp.sum(d_ext[0:rows, :], axis=0, keepdims=True)
        d_x_all[
            pl.ds(2 * block, 2), pl.ds(pl.multiple_of(slot * piece, piece), piece), :
        ] = d_conv.astype(BF16).reshape(2, piece, inner)
        d_ext[rows:, :] = d_ext[0:8, :]

        for at_step, action in pumps.items():
            pl.when(number == at_step)(action)

        return carry

    lax.fori_loop(0, blocks, scan_block, 0)
    saves = [
        pltpu.make_async_copy(source, target, locals_.at[8 + k])
        for k, (source, target) in enumerate(
            ((d_x_all, d_x_hbm), (d_bc, d_bc_hbm), (d_arg_all, d_arg_hbm))
        )
    ]
    for copy in saves:
        copy.start()

    out_line.finish(out_sum)
    home = lax.div(row, half) == core
    rows_out = out_grad.shape[0]
    far = links.copy(out_far, out_grad, peer[1])
    for this in range(2):

        @pl.when(home & (core == this))
        def _():
            cast_rows(out_far, out_sum.at[pl.ds((1 - this) * rows_out, rows_out)])
            far.start()
            cast_rows(out_grad, out_sum.at[pl.ds(this * rows_out, rows_out)])

    gate_line.finish(gate_sum)
    turn(gate_sent, gate_sum)
    send_gate.begin()
    pl.when(jnp.logical_not(home))(far.wait_recv)
    pl.when(home)(far.wait_send)
    o_plane.drain()
    out_line.drain()
    gate_line.drain()
    send_gate.end()
    save_gate.wait()
    for copy in saves:
        copy.wait()


def line_buffers(count, extent):
    return [pltpu.VMEM((count,) + extent, BF16)] * 4


def plane_buffers(rows, model):
    return [
        pltpu.VMEM((4, rows, model), BF16),
        pltpu.VMEM((4, rows, model), BF16),
        pltpu.VMEM((2, rows // 2, model), BF16),
        pltpu.VMEM((2, rows, model), BF16),
    ]


def reverse(dims, hbm, vmem, collective):
    depth, width, heads, head_size, size, kernel, own_ch, inner_all = dims
    inner = heads * head_size
    _, rows, model = hbm[0].shape
    tokens = rows * width
    wide = inner + 2 * size
    shape = jax.ShapeDtypeStruct
    subs = rows // CHUNK
    half = depth // 2
    out_piece, in_piece = (inner // half, model), (inner, model // depth)
    saved = [
        ((width, rows, inner), BF16),
        ((width, rows, inner), BF16),
        ((2 * size, tokens), BF16),
        ((width, rows, 128), BF16),
    ]
    kept = [
        ((rows, model), BF16),
        ((width, model // depth // width, inner), BF16),
        ((out_piece[0] // 2, model), F32),
        ((8, inner), F32),
        ((8, 128), F32),
    ]
    return pl.pallas_call(
        functools.partial(reverse_kernel, dims),
        out_shape=tuple(shape(*s) for s in saved + kept),
        in_specs=[ANY] * len(hbm) + [INVMEM] * len(vmem),
        out_specs=(ANY,) * len(saved) + (INVMEM,) * len(kept),
        scratch_shapes=[pltpu.VMEM((width, rows, model), BF16)] * 2
        + [pltpu.VMEM((tokens, inner), F32)] * 3
        + [pltpu.VMEM(hbm[-1].shape, BF16)]
        + [pltpu.VMEM(*s) for s in saved]
        + [
            pltpu.VMEM((inner, model), F32),
            pltpu.VMEM((inner, model), F32),
            pltpu.VMEM((2, rows, wide), F32),
            pltpu.VMEM((2, rows, inner), F32),
            pltpu.VMEM((2, rows, 128), F32),
            pltpu.VMEM((2, subs, size, inner), BF16),
            pltpu.VMEM((size, inner), F32),
            pltpu.VMEM((rows + 8, inner), F32),
        ]
        + plane_buffers(rows, model)
        + line_buffers(half, out_piece)
        + line_buffers(depth - 1, in_piece)
        + [
            pltpu.VMEM(out_piece, F32),
            pltpu.VMEM((out_piece[0] // 2, model), F32),
            pltpu.VMEM(in_piece, F32),
            pltpu.VMEM((in_piece[1], in_piece[0]), BF16),
            pltpu.VMEM((CHUNK, 128), F32),
            pltpu.VMEM((width, tokens // CHUNK, 128), F32),
            pltpu.SemaphoreType.DMA((48,)),
            pltpu.SemaphoreType.DMA((48,)),
            pltpu.SemaphoreType.DMA((12,)),
            pltpu.SemaphoreType.DMA((2, 4)),
        ],
        compiler_params=pltpu.CompilerParams(
            collective_id=collective, has_side_effects=True, vmem_limit_bytes=VMEM_LIMIT
        ),
        name="reverse_fused",
    )(*hbm, *vmem)


def runs_of(width, half, run):
    plane = width // 2
    for place in range(width):
        for j in range(half):
            yield place, j * run, (((place % 2) * half + j) * plane + place // 2) * run


def head_places(place, half, plane, group, heads, shift):
    lane = lax.broadcasted_iota(jnp.int32, (128, 128), 0) - shift
    head = lax.broadcasted_iota(jnp.int32, (128, 128), 1)
    part = sum(((lane >= j * group).astype(jnp.int32) for j in range(1, half)), jnp.zeros_like(lane))
    chosen = ((place % 2 * half + part) * plane + place // 2) * group + lane - part * group
    return jnp.where((head == chosen) & (lane >= 0) & (lane < heads), 1.0, 0.0)


def weights_kernel(
    dims,
    d_x_hbm,
    normed_hbm,
    wg_hbm,
    wx_hbm,
    d_gate_hbm,
    pre_hbm,
    conv_hbm,
    d_arg_hbm,
    wb_hbm,
    cot_hbm,
    d_bc,
    taps,
    channel_sums,
    head_sums,
    head_sum,
    rows_in,
    x_own,
    w_dt_all,
    gate_back,
    input_grad,
    in_grad,
    smalls,
    d_x,
    normed_all,
    wg,
    wx,
    d_gate,
    pre_own,
    conv_own,
    d_arg,
    wb,
    cot_own,
    w_turned,
    d_small,
    small_in,
    g_x,
    g_small,
    d_parts,
    d_extra,
    d_ext,
    bc_landed,
    bc_sums,
    d_pair,
    d_sums,
    d_relay,
    d_last,
    x_up_in,
    x_up_out,
    x_down_in,
    x_down_out,
    small_up_in,
    small_up_out,
    small_down_in,
    small_down_out,
    x_sum,
    x_sent,
    small_sum,
    small_sent,
    x_back,
    small_back,
    sums_own,
    sums_line,
    sums_all,
    full,
    sends,
    recvs,
    locals_,
):
    depth, width, heads, head_size, size, kernel, own_ch, inner_all = dims
    half, plane = depth // 2, width // 2
    inner = heads * head_size
    run = inner // half
    group = run // head_size
    model = normed_all.shape[2]
    piece = normed_all.shape[1] // 2
    rows = 2 * piece
    slots = 2
    blocks = slots * width // 2
    per_slot = blocks // slots
    everything = slots * width * piece
    own = 2 * size // width
    row, place = lax.axis_index("dp"), lax.axis_index("seq")
    links = Links(sends, recvs)
    peer = {mask: (row, flip_all(place, mask)) for mask in range(1, width)}
    order = (6, 2, 4, 7, 3, 5, 1)
    per_block = 128 // own
    bc_turn = 128 - own * lax.rem(place, per_block)
    window = pl.ds(pl.multiple_of(inner + lax.div(place, per_block) * 128, 128), 128)

    loads = [
        pltpu.make_async_copy(source, target, locals_.at[k])
        for k, (source, target) in enumerate(
            (
                (d_x_hbm, d_x),
                (normed_hbm, normed_all),
                (wg_hbm, wg),
                (wx_hbm, wx),
                (d_gate_hbm, d_gate),
                (pre_hbm.at[:, window], pre_own),
                (conv_hbm.at[:, window], conv_own),
                (d_arg_hbm, d_arg),
                (wb_hbm, wb),
                (cot_hbm.at[place], cot_own),
            )
        )
    ]
    for copy in loads:
        copy.start()
    line_peers = [(lax.rem(row + up, depth), place) for up in range(1, depth)]
    greet([peer[mask] for mask in range(1, width)] + line_peers)

    bc_rows = PlaneRows(links, row, place, d_bc, bc_landed, locals_.at[10])
    bc_rows.begin()
    small_rows = PlaneRows(links, row, place, d_small, small_in, locals_.at[11])
    cols = model // depth

    def line(own_ref, buffers):
        return LineSum(
            links,
            depth,
            row,
            place,
            lambda q: own_ref.at[:, pl.ds(q * cols, cols)],
            lambda q: row >= 0,
            *buffers,
        )

    x_line = line(g_x, (x_up_in, x_up_out, x_down_in, x_down_out))
    small_line = line(g_small, (small_up_in, small_up_out, small_down_in, small_down_out))
    d_plane = PlaneSum(links, row, place, d_parts, d_pair, d_sums, d_relay, d_last)
    send_x = SendBack(links, row, place, x_sent, x_back, locals_.at[12])
    send_small = SendBack(links, row, place, small_sent, small_back, locals_.at[13])

    def x_grad_tile(number, carry):
        at = pl.ds(pl.multiple_of(number * 128, 128), 128)
        left = d_x[:, :, at].reshape(everything, 128)
        g_x[at, :] = t_mm(left, normed_all[...].reshape(everything, model))
        return carry

    loads[0].wait()
    loads[1].wait()
    lax.fori_loop(0, inner // 128, x_grad_tile, 0)
    x_line.phase(0)

    for copy in loads[2:5]:
        copy.wait()

    def turn_weights(number, carry):
        at = pl.ds(pl.multiple_of(number * 128, 128), 128)
        w_turned[:inner, at] = wg[at, :].T
        w_turned[inner:, at] = wx[at, :].T
        return carry

    lax.fori_loop(0, model // 128, turn_weights, 0)

    def token_grads(index):
        both = jnp.concatenate([d_gate[index], d_x[index]], axis=1)
        d_parts[index] = mm(both, w_turned[...]).astype(BF16)

    for mask in (6, 2, 4, 0):
        token_grads(peer[mask ^ 1][1])
        d_plane.pair[mask].start()
    token_grads(peer[6][1])
    d_plane.far()
    token_grads(peer[2][1])
    d_plane.near(2)
    token_grads(peer[4][1])
    d_plane.near(4)
    if depth > 2:
        x_line.phase(1)
    token_grads(place)
    d_plane.near(0)

    lane = lax.broadcasted_iota(jnp.int32, (1, 128), 1)
    mine = lane < own

    def to_front(values):
        return pltpu.roll(values, bc_turn, 1)

    own_taps = to_front(taps[:, window])
    for copy in loads[5:8]:
        copy.wait()
    bc_rows.arrived()
    bc_sums[...] = jnp.zeros_like(bc_sums)

    def small_block(number, carry):
        slot, block = lax.div(number, per_slot), per_slot - 1 - lax.rem(number, per_slot)
        at = pl.ds(pl.multiple_of((slot * per_slot + block) * rows, rows), rows)

        @pl.when(block == per_slot - 1)
        def _():
            d_ext[rows:, :] = jnp.zeros((8, 128), F32)

        total = sum(bc_landed[k, :, at].astype(F32) for k in range(width))
        total = jnp.concatenate([total, jnp.zeros((128 - own, rows), F32)], axis=0)
        pre = to_front(pre_own[at, :])
        sig = sigmoid(pre)
        d_pre = jnp.where(mine, total.T * (sig * (1.0 + pre * (1.0 - sig))), 0.0)
        d_ext[0:rows, :] = d_pre
        where = (pl.ds(2 * block, 2), pl.ds(pl.multiple_of(slot * piece, piece), piece))
        conv_in = to_front(conv_own[at, :])
        d_conv = jnp.zeros((rows, 128), F32)
        for k in range(kernel):
            moved = d_ext[kernel - 1 - k : kernel - 1 - k + rows, :]
            d_conv = d_conv + own_taps[k : k + 1, :] * moved
            bc_sums[k : k + 1, :] += jnp.sum(moved * conv_in, axis=0, keepdims=True)
        bc_sums[4:5, :] += jnp.sum(d_pre, axis=0, keepdims=True)
        d_ext[rows:, :] = d_ext[0:8, :]
        d_dt = pltpu.roll(
            d_arg[where[0], where[1], :].astype(F32).reshape(rows, 128), own, 1
        )
        both = jnp.where(mine, d_conv, jnp.where(lane < own + heads, d_dt, 0.0))
        d_small[where[0], where[1], :] = both.astype(BF16).reshape(2, piece, 128)
        return carry

    lax.fori_loop(0, blocks, small_block, 0)
    small_rows.begin()
    g_small[...] = t_mm(
        d_small[...].reshape(everything, 128), normed_all[...].reshape(everything, model)
    )
    small_line.phase(0)
    sums_own[:, :inner] = channel_sums[...]
    sums_own[:, inner : inner + 128] = bc_sums[...]
    sums_own[:, inner + 128 :] = head_sums[...]
    sums_own[2:3, inner + 128 :] = dot(
        channel_sums[...], head_sum[...], ((1,), (0,)), lax.Precision.HIGHEST
    )[5:6]
    sums_copies = [
        links.copy(sums_own, sums_line.at[k], device) for k, device in enumerate(line_peers)
    ]
    for copy in sums_copies:
        copy.start()
    d_plane.second()
    if depth > 3:
        x_line.phase(2)
    if depth > 2:
        small_line.phase(1)
    for copy in sums_copies:
        copy.wait()
    total = jnp.zeros(sums_own.shape, F32)
    for q in range(depth):
        term = jnp.zeros(sums_own.shape, F32)
        for up in range(1, depth):
            term = jnp.where(lax.rem(row + depth - up, depth) == q, sums_line[up - 1], term)
        total = total + jnp.where(row == q, sums_own[...], term)
    sums_all[place] = total
    mine_all = sums_all.at[place]
    spread_sums = [links.copy(mine_all, mine_all, peer[mask]) for mask in order]
    for copy in spread_sums:
        copy.start()

    small_rows.arrived()
    for copy in loads[8:]:
        copy.wait()
    bc_tiles = [jnp.zeros((rows, 128), F32)] * (2 * size // 128)
    d_dt_all = jnp.zeros((rows, 128), F32)
    for source in range(width):
        got = small_in[source]
        moved = jnp.where(mine, got.astype(F32), 0.0)
        turn_by = own * (source % per_block)
        if turn_by:
            moved = pltpu.roll(moved, turn_by, 1)
        bc_tiles[source // per_block] = bc_tiles[source // per_block] + moved
        places = head_places(source, half, plane, group, heads, own).astype(BF16)
        d_dt_all = d_dt_all + mm(got, places)
    extra = mm_t(d_dt_all.astype(BF16), w_dt_all[...])
    for k, tile in enumerate(bc_tiles):
        extra = extra + mm_t(tile.astype(BF16), wb[k])
    d_extra[...] = extra
    x_line.finish(x_sum)
    turn(x_sent, x_sum)
    send_x.begin()
    if depth > 3:
        small_line.phase(2)

    for source, at, to in runs_of(width, half, run):
        in_grad[:, to : to + run] = gate_back[source, :, at : at + run].astype(F32)
    small_line.finish(small_sum)
    turn(small_sent, small_sum)
    send_small.begin()
    for copy in spread_sums:
        copy.wait()
    for source, at, to in runs_of(width, half, run):
        full[:, to : to + run] = sums_all[source, :, at : at + run]
    for source in range(width):
        to = inner_all + source * own
        full[:, to : to + own] = sums_all[source, :, inner : inner + own]
    first = (row * width + place) * own_ch
    base = pl.multiple_of(lax.div(first, 128) * 128, 128)
    view = pltpu.roll(full[:, pl.ds(base, 256)], 256 - lax.rem(first, 128), 1)
    smalls[0:8, :] = view[:, :128]
    smalls[8:16, :] = sum(
        dot(
            sums_all[source, :, inner + 128 :],
            head_places(source, half, plane, group, heads, 0),
            ((1,), (0,)),
            lax.Precision.HIGHEST,
        )
        for source in range(width)
    )
    send_x.end()
    for source, at, to in runs_of(width, half, run):
        in_grad[:, inner_all + to : inner_all + to + run] = x_back[
            source, :, at : at + run
        ].astype(F32)
    send_small.end()
    for source in range(width):
        to = 2 * inner_all + source * own
        in_grad[:, to : to + own] = small_back[source, :, :own].astype(F32)
    for source, at, to in runs_of(width, half, group):
        to = 2 * inner_all + 2 * size + to
        in_grad[:, to : to + group] = small_back[
            source, :, own + at : own + at + group
        ].astype(F32)

    norm_gain = rows_in[0:1, :]

    def store_grad(at, total):
        held = x_own[at].astype(F32)
        inv = lax.rsqrt(jnp.mean(held * held, axis=1, keepdims=True) + EPS)
        hat = held * inv
        d_h = (total + d_extra[at]) * norm_gain
        grad = inv * (d_h - hat * jnp.mean(d_h * hat, axis=1, keepdims=True))
        input_grad[at] = (grad + cot_own[at].astype(F32)).astype(BF16)

    d_plane.finish(store_grad)
    d_plane.drain()
    x_line.drain()
    small_line.drain()
    bc_rows.drain()
    small_rows.drain()


def weights(dims, hbm, vmem, collective):
    depth, width, heads, head_size, size, kernel, own_ch, inner_all = dims
    inner = heads * head_size
    _, rows, model = hbm[1].shape
    tokens = rows * width
    shape = jax.ShapeDtypeStruct
    cols = model // depth
    owned = cols // width
    own = 2 * size // width
    kept = [
        ((rows, model), BF16),
        ((owned, 2 * inner_all + 2 * size + heads * width), F32),
        ((16, 128), F32),
    ]
    return pl.pallas_call(
        functools.partial(weights_kernel, dims),
        out_shape=tuple(shape(*s) for s in kept),
        in_specs=[ANY] * len(hbm) + [INVMEM] * len(vmem),
        out_specs=(INVMEM,) * len(kept),
        scratch_shapes=[pltpu.VMEM(v.shape, v.dtype) for v in hbm[:5]]
        + [
            pltpu.VMEM((tokens, 128), F32),
            pltpu.VMEM((tokens, 128), F32),
            pltpu.VMEM(hbm[7].shape, BF16),
            pltpu.VMEM(hbm[8].shape, BF16),
            pltpu.VMEM((rows, model), BF16),
            pltpu.VMEM((2 * inner, model), BF16),
            pltpu.VMEM((width, rows, 128), BF16),
            pltpu.VMEM((width, rows, 128), BF16),
            pltpu.VMEM((inner, model), F32),
            pltpu.VMEM((128, model), F32),
            pltpu.VMEM((width, rows, model), BF16),
            pltpu.VMEM((rows, model), F32),
            pltpu.VMEM((rows + 8, 128), F32),
            pltpu.VMEM((width, own, tokens), BF16),
            pltpu.VMEM((8, 128), F32),
        ]
        + plane_buffers(rows, model)
        + line_buffers(depth - 1, (inner, cols))
        + line_buffers(depth - 1, (128, cols))
        + [
            pltpu.VMEM((inner, cols), F32),
            pltpu.VMEM((cols, inner), BF16),
            pltpu.VMEM((128, cols), F32),
            pltpu.VMEM((cols, 128), BF16),
            pltpu.VMEM((width, owned, inner), BF16),
            pltpu.VMEM((width, owned, 128), BF16),
            pltpu.VMEM((8, inner + 256), F32),
            pltpu.VMEM((depth - 1, 8, inner + 256), F32),
            pltpu.VMEM((width, 8, inner + 256), F32),
            pltpu.VMEM((8, inner_all + 2 * size + 256), F32),
            pltpu.SemaphoreType.DMA((88,)),
            pltpu.SemaphoreType.DMA((88,)),
            pltpu.SemaphoreType.DMA((14,)),
        ],
        compiler_params=pltpu.CompilerParams(
            collective_id=collective, has_side_effects=True, vmem_limit_bytes=VMEM_LIMIT
        ),
        name="weights_fused",
    )(*hbm, *vmem)


def fast_body(
    depth,
    width,
    block_input,
    cotangent,
    lengths,
    in_weight,
    out_weight,
    norm_gain,
    gate_gain,
    conv_weight,
    conv_bias,
    dt_bias,
    a_log,
    d_skip,
):
    slots, piece, model = block_input.shape
    heads_all = dt_bias.shape[0]
    out_rows = out_weight.shape[0]
    in_rows = in_weight.shape[0]
    inner_all = out_rows * depth * width
    head_size = inner_all // heads_all
    taps_count = conv_weight.shape[0]
    channels = conv_weight.shape[1] * depth * width
    size = (channels - inner_all) // 2
    heads = heads_all // width
    inner = heads * head_size
    plane = width // 2
    half = depth // 2
    pair_rows = 2 * out_rows
    row, place = lax.axis_index("dp"), lax.axis_index("seq")
    core, chip = lax.rem(place, 2), lax.div(place, 2)
    slot_len = piece * width
    tokens = slots * slot_len

    def by_owner(values, axis):
        shape = values.shape
        return values.reshape(shape[:axis] + (2, half, plane, pair_rows) + shape[axis + 1 :])

    gate_cols = inner_all
    conv_cols = gate_cols + inner_all
    bc_cols = conv_cols + 2 * size
    own_ch = conv_bias.shape[0]

    def padded(values, lanes=128):
        return jnp.pad(values, ((0, 0), (0, lanes - values.shape[1])))

    def placed(values, top):
        return jnp.pad(
            values, ((top, 16 + in_rows - top - values.shape[0]), (0, 128 - values.shape[1]))
        )

    pack = (
        placed(in_weight[:, bc_cols:], 0)
        + placed(conv_weight, in_rows)
        + placed(conv_bias[None], in_rows + taps_count)
        + placed(gate_gain[None], in_rows + 5)
        + placed(norm_gain[None], in_rows + 6)
    )
    head_params = jnp.pad(
        jnp.stack([dt_bias, a_log, d_skip]), ((0, 5), (0, 128 - heads_all))
    )
    positions = place * piece + jnp.arange(piece, dtype=jnp.int32)
    live = (positions[None, :] < lengths[:, None]).astype(BF16)
    masked = cotangent * live[..., None]

    def cols_for_all(values):
        split = by_owner(values, 1)
        return jnp.transpose(split, (3, 1, 0, 2, 4)).reshape(width, in_rows, inner)

    w_bc_send = jnp.swapaxes(in_weight[:, conv_cols:bc_cols].reshape(in_rows, 2, size), 0, 1)
    tokens_dev = slots * piece
    dims = (depth, width, heads, head_size, size, taps_count, own_ch, inner_all)
    (
        normed_all,
        cot_all,
        w_gate,
        w_x,
        w_bc,
        w_out,
        conv_in,
        pre,
        dt_arg,
        gate,
        y,
        states,
        norms,
        taps,
        param_rows,
        w_dt,
        w_dt_all,
    ) = forward(
        dims,
        block_input.reshape(tokens_dev, model),
        masked.reshape(tokens_dev, model),
        cols_for_all(in_weight[:, :gate_cols]),
        cols_for_all(in_weight[:, gate_cols:conv_cols]),
        w_bc_send,
        out_weight,
        pack,
        head_params,
        2,
    )
    x_own = block_input.reshape(tokens_dev, model)
    head_sum = padded((jnp.arange(inner)[:, None] // head_size == jnp.arange(heads)).astype(F32))
    (
        d_gate,
        d_x,
        d_bc,
        d_arg,
        output,
        gate_back,
        out_grad,
        channel_sums,
        head_sums,
    ) = reverse(
        dims,
        (cot_all, normed_all, gate, y, pre, conv_in, dt_arg, states, w_out),
        (norms, taps, param_rows, head_sum, x_own),
        3,
    )
    bc_own = 2 * size // width
    input_grad, in_grad, smalls = weights(
        dims,
        (
            d_x,
            normed_all,
            w_gate.reshape(model, inner),
            w_x.reshape(model, inner),
            d_gate,
            pre,
            conv_in,
            d_arg,
            w_bc.reshape(2, model, size),
            cot_all,
        ),
        (
            d_bc.reshape(width, bc_own, tokens),
            taps,
            channel_sums,
            head_sums,
            head_sum,
            param_rows,
            x_own,
            w_dt_all,
            gate_back,
        ),
        4,
    )
    norm_grad = jnp.sum(in_grad * in_weight.astype(F32), axis=1) / norm_gain.astype(F32)
    gate_grad = jnp.sum(out_grad * out_weight.astype(F32), axis=1) / gate_gain.astype(F32)
    return (
        output.reshape(slots, piece, model),
        input_grad.reshape(slots, piece, model),
        in_grad,
        out_grad,
        norm_grad,
        gate_grad,
        smalls[:4, :own_ch],
        smalls[4, :own_ch],
        smalls[8, :heads_all],
        smalls[9, :heads_all],
        smalls[10, :heads_all],
    )


def heads_fit(depth, width, arrays):
    block_input, out_weight, dt_bias = arrays[0], arrays[4], arrays[9]
    pair_rows = 2 * out_weight.shape[0]
    head_size = out_weight.shape[0] * depth * width // dt_bias.shape[0]
    return (
        width == 8
        and depth % 2 == 0
        and pair_rows % head_size == 0
        and (depth // 2 * pair_rows) % 128 == 0
        and block_input.shape[1] % CHUNK == 0
        and 2 * head_size == CHUNK
    )


def solution(mesh):
    placed = (
        P("dp", "seq", None),
        P("dp", "seq", None),
        P("dp"),
        P(("dp", "seq"), None),
        P(("dp", "seq"), None),
        P(("dp", "seq")),
        P(("dp", "seq")),
        P(None, ("dp", "seq")),
        P(("dp", "seq")),
        P(),
        P(),
        P(),
    )
    depth, width = mesh.shape["dp"], mesh.shape["seq"]

    def either(*arrays):
        if heads_fit(depth, width, arrays):
            return fast_body(depth, width, *arrays)
        return body(*arrays)

    return jax.shard_map(
        either,
        mesh=mesh,
        in_specs=placed,
        out_specs=(
            P("dp", "seq", None),
            P("dp", "seq", None),
            P(("dp", "seq"), None),
            P(("dp", "seq"), None),
            P(("dp", "seq")),
            P(("dp", "seq")),
            P(None, ("dp", "seq")),
            P(("dp", "seq")),
            P(),
            P(),
            P(),
        ),
        check_vma=False,
    )
```

```python
import functools

import jax
import jax.numpy as jnp
from jax import lax
from jax.experimental import pallas as pl
from jax.experimental.pallas import tpu as pltpu
from jax.sharding import PartitionSpec as P

SLOTS_MB = 1


EPS = 1e-05
HIGH = lax.Precision.HIGHEST


def from_behind(value, axis, steps):
    count = lax.axis_size(axis)
    leading, last = (max(0, -steps), min(count, count - steps))
    return lax.ppermute(value, axis, [(source, source + steps) for source in range(leading, last)])


def carried_in(value, axis, join, neutral, backward):
    count = lax.axis_size(axis)
    place = lax.axis_index(axis)
    ahead = count - 1 - place if backward else place
    gathered = jax.tree.map(
        lambda a, kind: lax.all_gather(a.astype(kind), axis),
        value,
        jax.tree.map(lambda a: jnp.bfloat16 if a.dtype == jnp.float32 else a.dtype, value),
    )
    state = jax.tree.map(lambda a, e: jnp.zeros_like(a) + jnp.asarray(e, a.dtype), value, neutral)

    def one(lap, state):
        source = count - 1 - lap if backward else lap
        return join(
            state,
            jax.tree.map(
                lambda a, own: lax.dynamic_index_in_dim(a, source, 0, False).astype(own.dtype),
                gathered,
                value,
            ),
        )

    return lax.fori_loop(0, ahead, one, state)


def as_sent(value):

    def short(part):
        return part.astype(jnp.bfloat16) if part.dtype == jnp.float32 else part

    return jax.tree.map(short, value)


def link_states(earlier, later):
    return (earlier[0] * later[0], later[0][:, :, None, None] * earlier[1] + later[1])


def silu_slope(values):
    sigma = jax.nn.sigmoid(values)
    return sigma * (1.0 + values * (1.0 - sigma))


def rows_product(left, right):
    return lax.dot_general(
        left, right, (((0,), (0,)), ((), ())), preferred_element_type=jnp.float32
    )


def cols_product(left, right):
    return lax.dot_general(
        left, right, (((1,), (1,)), ((), ())), preferred_element_type=jnp.float32
    )


def add_pair(first, second):
    return first + second


def first_total(stacked):
    return jnp.sum(stacked, axis=0)


def owner_sums(grads):
    lifted = tuple((grad[None] for grad in grads))
    by_data = (
        lax.all_to_all(lifted[0], "dp", split_axis=1, concat_axis=0, tiled=True),
        lax.all_to_all(lifted[1], "dp", split_axis=1, concat_axis=0, tiled=True),
        lax.all_to_all(lifted[2], "dp", split_axis=1, concat_axis=0, tiled=True),
        lax.all_to_all(lifted[3], "dp", split_axis=1, concat_axis=0, tiled=True),
        lax.all_to_all(lifted[4], "dp", split_axis=1, concat_axis=0, tiled=True),
        lax.all_to_all(lifted[5], "dp", split_axis=1, concat_axis=0, tiled=True),
    )
    partial_value = tuple((first_total(stacked)[None] for stacked in by_data))
    by_piece = (
        lax.all_to_all(partial_value[0], "seq", split_axis=1, concat_axis=0, tiled=True),
        lax.all_to_all(partial_value[1], "seq", split_axis=1, concat_axis=0, tiled=True),
        lax.all_to_all(partial_value[2], "seq", split_axis=1, concat_axis=0, tiled=True),
        lax.all_to_all(partial_value[3], "seq", split_axis=1, concat_axis=0, tiled=True),
        lax.all_to_all(partial_value[4], "seq", split_axis=1, concat_axis=0, tiled=True),
        lax.all_to_all(partial_value[5], "seq", split_axis=1, concat_axis=0, tiled=True),
    )
    return tuple((first_total(stacked) for stacked in by_piece))


def forward_pass(slot_in, weights, head_params):
    in_full, out_full, norm_full, gate_full, conv_full, bias_full = weights
    dt_shift, log_rate, skip_gain = head_params
    slot_count, piece_len, model_width = slot_in.shape
    inner_width = out_full.shape[0]
    channels = conv_full.shape[1]
    kernel = conv_full.shape[0]
    head_count = dt_shift.shape[0]
    head_size = inner_width // head_count
    state_size = (channels - inner_width) // 2
    input_f = slot_in.astype(jnp.float32)
    inv_rms = lax.rsqrt(jnp.mean(input_f * input_f, axis=-1, keepdims=True) + EPS)
    normed = (input_f * inv_rms * norm_full.astype(jnp.float32)).astype(jnp.bfloat16)
    projected = jnp.dot(
        normed.reshape(-1, model_width), in_full, preferred_element_type=jnp.float32
    ).reshape(slot_count, piece_len, -1)
    gate_part = projected[..., :inner_width]
    conv_in = projected[..., inner_width : inner_width + channels]
    dt_arg = projected[..., inner_width + channels :] + dt_shift
    rim_rows = from_behind(
        conv_in[:, piece_len - kernel + 1 :].astype(jnp.bfloat16), "seq", 1
    ).astype(jnp.float32)
    extended = jnp.concatenate([rim_rows, conv_in], axis=1)
    conv_taps = conv_full.astype(jnp.float32)
    pre_act = bias_full.astype(jnp.float32) + sum(
        (
            conv_taps[tap_index] * extended[:, tap_index : tap_index + piece_len]
            for tap_index in range(kernel)
        )
    )
    activated = jax.nn.silu(pre_act)
    x_heads = activated[..., :inner_width].reshape(slot_count, piece_len, head_count, head_size)
    b_rows = activated[..., inner_width : inner_width + state_size]
    c_rows = activated[..., inner_width + state_size :]
    dt_vals = jax.nn.softplus(dt_arg)
    decay_rates = -jnp.exp(log_rate)
    log_cum = jnp.cumsum(dt_vals * decay_rates, axis=1)
    log_tot = log_cum[:, -1]
    weights_in = jnp.exp(log_tot[:, None] - log_cum) * dt_vals
    local_state = jnp.einsum(
        "sthp,stn->shpn", weights_in[..., None] * x_heads, b_rows, precision=HIGH
    )
    carry_decay = jnp.exp(log_tot)
    neutral = (jnp.ones_like(carry_decay), jnp.zeros_like(local_state))
    _, start_state = carried_in((carry_decay, local_state), "seq", link_states, neutral, False)
    spots = jnp.arange(piece_len)
    causal = spots[:, None] >= spots[None, :]
    cum_heads = jnp.swapaxes(log_cum, 1, 2)
    gap_vals = jnp.where(causal, cum_heads[..., :, None] - cum_heads[..., None, :], 0.0)
    decay_mat = jnp.where(causal, jnp.exp(gap_vals), 0.0)
    cb_mat = jnp.einsum("stn,sun->stu", c_rows, b_rows, precision=HIGH)
    dt_cols = jnp.swapaxes(dt_vals, 1, 2)[:, :, None, :]
    mixing = decay_mat * cb_mat[:, None] * dt_cols
    y_intra = jnp.einsum("shtu,suhp->sthp", mixing, x_heads, precision=HIGH)
    state_read = jnp.einsum("stn,shpn->sthp", c_rows, start_state, precision=HIGH)
    exp_cum = jnp.exp(log_cum)
    y_heads = y_intra + exp_cum[..., None] * state_read + skip_gain[:, None] * x_heads
    y_flat = y_heads.reshape(slot_count, piece_len, inner_width)
    gate_act = jax.nn.silu(gate_part)
    gated_out = y_flat * gate_act
    inv_gate = lax.rsqrt(jnp.mean(gated_out * gated_out, axis=-1, keepdims=True) + EPS)
    gate_normed = (gated_out * inv_gate * gate_full.astype(jnp.float32)).astype(jnp.bfloat16)
    mixed = jnp.dot(
        gate_normed.reshape(-1, inner_width), out_full, preferred_element_type=jnp.float32
    )
    output = (input_f + mixed.reshape(slot_count, piece_len, model_width)).astype(jnp.bfloat16)
    saved = dict(
        input_f=input_f,
        inv_rms=inv_rms,
        normed=normed,
        gate_part=gate_part,
        dt_arg=dt_arg,
        extended=extended,
        pre_act=pre_act,
        x_heads=x_heads,
        b_rows=b_rows,
        c_rows=c_rows,
        dt_vals=dt_vals,
        log_cum=log_cum,
        log_tot=log_tot,
        weights_in=weights_in,
        carry_decay=carry_decay,
        start_state=start_state,
        decay_mat=decay_mat,
        cb_mat=cb_mat,
        dt_cols=dt_cols,
        mixing=mixing,
        state_read=state_read,
        exp_cum=exp_cum,
        y_flat=y_flat,
        gate_act=gate_act,
        gated_out=gated_out,
        inv_gate=inv_gate,
        gate_normed=gate_normed,
    )
    return (output, saved)


def backward_pass(saved, slot_cot, live, weights, head_params):
    in_full, out_full, norm_full, gate_full, conv_full, bias_full = weights
    dt_shift, log_rate, skip_gain = head_params
    slot_count, piece_len, model_width = slot_cot.shape
    inner_width = out_full.shape[0]
    kernel = conv_full.shape[0]
    x_heads = saved["x_heads"]
    b_rows = saved["b_rows"]
    c_rows = saved["c_rows"]
    dt_vals = saved["dt_vals"]
    log_cum = saved["log_cum"]
    weights_in = saved["weights_in"]
    carry_decay = saved["carry_decay"]
    start_state = saved["start_state"]
    decay_mat = saved["decay_mat"]
    cb_mat = saved["cb_mat"]
    dt_cols = saved["dt_cols"]
    decay_rates = -jnp.exp(log_rate)
    masked_cot = slot_cot * live[..., None].astype(jnp.bfloat16)
    cot_rows = masked_cot.reshape(-1, model_width)
    d_gn = cols_product(cot_rows, out_full).reshape(slot_count, piece_len, inner_width)
    gate_hat = saved["gated_out"] * saved["inv_gate"]
    grad_ggain = jnp.sum(d_gn * gate_hat, axis=(0, 1))
    d_hat = d_gn * gate_full.astype(jnp.float32)
    d_gated = saved["inv_gate"] * (
        d_hat - gate_hat * jnp.mean(d_hat * gate_hat, axis=-1, keepdims=True)
    )
    d_gate_part = d_gated * saved["y_flat"] * silu_slope(saved["gate_part"])
    d_heads = (d_gated * saved["gate_act"]).reshape(x_heads.shape)
    grad_skip = jnp.sum(d_heads * x_heads, axis=(0, 1, 3))
    exp_cum = saved["exp_cum"]
    d_read = d_heads * exp_cum[..., None]
    d_cvals = jnp.einsum("sthp,shpn->stn", d_read, start_state, precision=HIGH)
    d_start = jnp.einsum("sthp,stn->shpn", d_read, c_rows, precision=HIGH)
    d_cum = jnp.sum(d_heads * saved["state_read"], axis=-1) * exp_cum
    d_mixing = jnp.einsum("sthp,suhp->shtu", d_heads, x_heads, precision=HIGH)
    d_x = skip_gain[:, None] * d_heads + jnp.einsum(
        "shtu,sthp->suhp", saved["mixing"], d_heads, precision=HIGH
    )
    d_decay = d_mixing * cb_mat[:, None] * dt_cols
    d_cb = jnp.sum(d_mixing * decay_mat * dt_cols, axis=1)
    d_dt = jnp.swapaxes(jnp.sum(d_mixing * decay_mat * cb_mat[:, None], axis=2), 1, 2)
    spread = d_decay * decay_mat
    d_cum = d_cum + jnp.swapaxes(jnp.sum(spread, axis=3) - jnp.sum(spread, axis=2), 1, 2)
    d_cvals = d_cvals + jnp.einsum("stu,sun->stn", d_cb, b_rows, precision=HIGH)
    d_bvals = jnp.einsum("stu,stn->sun", d_cb, c_rows, precision=HIGH)
    neutral = (jnp.ones_like(carry_decay), jnp.zeros_like(d_start))
    _, later_grad = carried_in((carry_decay, d_start), "seq", link_states, neutral, True)
    d_tot = jnp.sum(later_grad * start_state, axis=(2, 3)) * carry_decay
    grad_proj_b = jnp.einsum("shpn,stn->sthp", later_grad, b_rows, precision=HIGH)
    d_x = d_x + weights_in[..., None] * grad_proj_b
    d_weights = jnp.sum(grad_proj_b * x_heads, axis=-1)
    d_bvals = d_bvals + jnp.einsum(
        "sthp,shpn->stn", weights_in[..., None] * x_heads, later_grad, precision=HIGH
    )
    d_dt = d_dt + d_weights * jnp.exp(saved["log_tot"][:, None] - log_cum)
    through = d_weights * weights_in
    d_tot = d_tot + jnp.sum(through, axis=1)
    last_row = (jnp.arange(piece_len) == piece_len - 1).astype(jnp.float32)
    d_cum = d_cum - through + last_row[None, :, None] * d_tot[:, None, :]
    d_log = lax.cumsum(d_cum, axis=1, reverse=True)
    d_dt = d_dt + d_log * decay_rates
    grad_alog = jnp.sum(d_log * dt_vals, axis=(0, 1)) * decay_rates
    d_arg = d_dt * jax.nn.sigmoid(saved["dt_arg"])
    grad_dtb = jnp.sum(d_arg, axis=(0, 1))
    d_act = jnp.concatenate(
        [d_x.reshape(slot_count, piece_len, inner_width), d_bvals, d_cvals], axis=-1
    )
    d_pre = d_act * silu_slope(saved["pre_act"])
    grad_cbias = jnp.sum(d_pre, axis=(0, 1))
    extended = saved["extended"]
    grad_conv = jnp.stack(
        [
            jnp.sum(d_pre * extended[:, tap_index : tap_index + piece_len], axis=(0, 1))
            for tap_index in range(kernel)
        ]
    )
    conv_taps = conv_full.astype(jnp.float32)
    d_ext = sum(
        (
            jnp.pad(
                conv_taps[tap_index] * d_pre, ((0, 0), (tap_index, kernel - 1 - tap_index), (0, 0))
            )
            for tap_index in range(kernel)
        )
    )
    back_rim = from_behind(as_sent(d_ext[:, : kernel - 1]), "seq", -1)
    d_conv_in = d_ext[:, kernel - 1 :] + jnp.pad(
        back_rim, ((0, 0), (piece_len - kernel + 1, 0), (0, 0))
    )
    d_proj = jnp.concatenate([d_gate_part, d_conv_in, d_arg], axis=-1).astype(jnp.bfloat16)
    d_proj = d_proj.reshape(slot_count * piece_len, -1)
    d_normed = cols_product(d_proj, in_full).reshape(slot_count, piece_len, model_width)
    in_hat = saved["input_f"] * saved["inv_rms"]
    grad_ngain = jnp.sum(d_normed * in_hat, axis=(0, 1))
    d_norm_in = d_normed * norm_full.astype(jnp.float32)
    input_grad = saved["inv_rms"] * (
        d_norm_in - in_hat * jnp.mean(d_norm_in * in_hat, axis=-1, keepdims=True)
    )
    input_grad = input_grad + masked_cot.astype(jnp.float32)
    product_rows = (
        saved["normed"].reshape(-1, model_width),
        d_proj,
        saved["gate_normed"].reshape(-1, inner_width),
        cot_rows,
    )
    small_grads = (grad_ngain, grad_ggain, grad_conv, grad_cbias)
    return (
        input_grad.astype(jnp.bfloat16),
        product_rows,
        small_grads,
        (grad_dtb, grad_alog, grad_skip),
    )


def body(
    block_input,
    cotangent,
    lengths,
    in_weight,
    out_weight,
    norm_gain,
    gate_gain,
    conv_weight,
    conv_bias,
    dt_bias,
    a_log,
    d_skip,
):
    shards = (in_weight, out_weight, norm_gain, gate_gain, conv_weight, conv_bias)
    head_params = (dt_bias, a_log, d_skip)
    piece_len = block_input.shape[1]
    batches = block_input.shape[0] // SLOTS_MB
    positions = lax.axis_index("seq") * piece_len + jnp.arange(piece_len, dtype=jnp.int32)
    held = (
        lax.all_gather(shards[0], ("dp", "seq"), axis=0, tiled=True),
        lax.all_gather(shards[1], ("dp", "seq"), axis=0, tiled=True),
        lax.all_gather(shards[2], ("dp", "seq"), axis=0, tiled=True),
        lax.all_gather(shards[3], ("dp", "seq"), axis=0, tiled=True),
        lax.all_gather(shards[4], ("dp", "seq"), axis=1, tiled=True),
        lax.all_gather(shards[5], ("dp", "seq"), axis=0, tiled=True),
    )
    outputs = []
    input_grads = []
    kept_rows = []
    small_totals = None
    head_totals = None
    for batch_index in range(batches):
        first = batch_index * SLOTS_MB
        slot_in = block_input[first : first + SLOTS_MB]
        slot_cot = cotangent[first : first + SLOTS_MB]
        live = (positions[None, :] < lengths[first : first + SLOTS_MB, None]).astype(jnp.float32)
        output, saved = forward_pass(slot_in, held, head_params)
        input_grad, product_rows, small_grads, head_grads = backward_pass(
            saved, slot_cot, live, held, head_params
        )
        outputs.append(output)
        input_grads.append(input_grad)
        kept_rows.append(product_rows)
        small_totals = (
            small_grads
            if small_totals is None
            else jax.tree.map(add_pair, small_totals, small_grads)
        )
        head_totals = (
            head_grads if head_totals is None else jax.tree.map(add_pair, head_totals, head_grads)
        )
    normed_all = jnp.concatenate([rows[0] for rows in kept_rows], axis=0)
    dproj_all = jnp.concatenate([rows[1] for rows in kept_rows], axis=0)
    gnormed_all = jnp.concatenate([rows[2] for rows in kept_rows], axis=0)
    cot_all = jnp.concatenate([rows[3] for rows in kept_rows], axis=0)
    grad_win = rows_product(normed_all, dproj_all)
    grad_wout = rows_product(gnormed_all, cot_all)
    grad_ngain, grad_ggain, grad_conv, grad_cbias = small_totals
    owned = owner_sums((grad_win, grad_wout, grad_ngain, grad_ggain, grad_conv.T, grad_cbias))
    head_sums = lax.psum(head_totals, ("dp", "seq"))
    return (
        jnp.concatenate(outputs, axis=0),
        jnp.concatenate(input_grads, axis=0),
        owned[0],
        owned[1],
        owned[2],
        owned[3],
        owned[4].T,
        owned[5],
        head_sums[0],
        head_sums[1],
        head_sums[2],
    )


F32 = jnp.float32
BF16 = jnp.bfloat16
MESH_ID = pl.DeviceIdType.MESH
ANY = pl.BlockSpec(memory_space=pl.ANY)
INVMEM = pl.BlockSpec(memory_space=pltpu.VMEM)
VMEM_LIMIT = 63 * 1024 * 1024
CHUNK = 128


def flip(place, bit):
    return place + bit - 2 * bit * lax.rem(lax.div(place, bit), 2)


def flip_all(place, mask):
    for bit in (1, 2, 4):
        if mask & bit:
            place = flip(place, bit)
    return place


class Links:
    def __init__(self, sends, recvs):
        self.sends, self.recvs, self.used = sends, recvs, 0

    def copy(self, source, target, device):
        slot = self.used
        self.used += 1
        return pltpu.make_async_remote_copy(
            src_ref=source,
            dst_ref=target,
            send_sem=self.sends.at[slot],
            recv_sem=self.recvs.at[slot],
            device_id=device,
            device_id_type=MESH_ID,
        )


def greet(devices, conditions=(), between=None):
    barrier = pltpu.get_barrier_semaphore()
    for device in devices:
        pl.semaphore_signal(barrier, inc=1, device_id=device, device_id_type=MESH_ID)
    for condition, device in conditions:

        @pl.when(condition)
        def _():
            pl.semaphore_signal(barrier, inc=1, device_id=device, device_id_type=MESH_ID)

    count = len(devices)
    for condition, _ in conditions:
        count = count + jnp.where(condition, 1, 0)
    if between is not None:
        between()
    pl.semaphore_wait(barrier, count)


def add_rows(target, first, second, step=32):
    def one(number, carry):
        rows = pl.ds(pl.multiple_of(number * step, step), step)
        target[rows] = (first[rows].astype(F32) + second[rows].astype(F32)).astype(target.dtype)
        return carry

    lax.fori_loop(0, target.shape[0] // step, one, 0)


def cast_rows(target, source, step=32):
    def one(number, carry):
        rows = pl.ds(pl.multiple_of(number * step, step), step)
        target[rows] = source[rows].astype(target.dtype)
        return carry

    lax.fori_loop(0, target.shape[0] // step, one, 0)


class LineSum:
    def __init__(
        self, links, depth, row, place, own, valid, up_in, up_out, down_in, down_out, shared=None
    ):
        self.depth, self.row, self.own, self.valid = depth, row, own, valid
        above, below = lax.min(row + 1, depth - 1), lax.max(row - 1, 0)

        def slots(ref, shift):
            return {q: ref.at[q % shared if shared else q - shift] for q in range(shift, depth - 1 + shift)}

        self.up_in, self.up_out = slots(up_in, 1), slots(up_out, 1)
        self.down_in, self.down_out = slots(down_in, 0), slots(down_out, 0)
        self.ups = {
            q: links.copy(self.up_out[q], self.up_in[q], (above, place)) for q in self.up_in
        }
        self.downs = {
            q: links.copy(self.down_out[q], self.down_in[q], (below, place)) for q in self.down_in
        }

    def up(self, q, row):
        @pl.when(self.valid(q) & (self.row == row))
        def _():
            if row == 0:
                cast_rows(self.up_out[q], self.own(q))
            else:
                self.ups[q].wait_recv()
                add_rows(self.up_out[q], self.own(q), self.up_in[q])
            self.ups[q].start()

    def down(self, q, row):
        @pl.when(self.valid(q) & (self.row == row))
        def _():
            if row == self.depth - 1:
                cast_rows(self.down_out[q], self.own(q))
            else:
                self.downs[q].wait_recv()
                add_rows(self.down_out[q], self.own(q), self.down_in[q])
            self.downs[q].start()

    def phase(self, number):
        for row in range(self.depth):
            up_q = self.depth - 1 + row - number
            if row < up_q < self.depth:
                self.up(up_q, row)
            down_q = number - (self.depth - 1 - row)
            if 0 <= down_q < row:
                self.down(down_q, row)

    def finish(self, total):
        depth, row = self.depth, self.row
        for q in range(depth):

            @pl.when(self.valid(q) & (row == q))
            def _():
                if q > 0:
                    self.ups[q].wait_recv()
                if q < depth - 1:
                    self.downs[q].wait_recv()
                if 0 < q < depth - 1:
                    add_rows(total, self.up_in[q], self.down_in[q])
                    add_rows(total, total, self.own(q))
                elif q > 0:
                    add_rows(total, self.own(q), self.up_in[q])
                else:
                    add_rows(total, self.own(q), self.down_in[q])

    def drain(self):
        for q, copy in self.ups.items():
            pl.when(self.valid(q) & (self.row < q))(copy.wait_send)
        for q, copy in self.downs.items():
            pl.when(self.valid(q) & (self.row > q))(copy.wait_send)


class PlaneSum:
    def __init__(self, links, row, place, parts, pair_in, sums, relay_in, last_in):
        self.place, self.parts = place, parts
        self.pair_in, self.sums, self.relay_in, self.last_in = pair_in, sums, relay_in, last_in
        peer = {mask: (row, flip_all(place, mask)) for mask in range(1, 8)}
        self.peer = peer
        rows = last_in.shape[1] // 2
        self.halves = (pl.ds(0, rows), pl.ds(rows, rows))
        self.pair = {
            mask: links.copy(parts.at[peer[mask ^ 1][1]], pair_in.at[mask // 2], peer[1])
            for mask in (6, 2, 4, 0)
        }
        top, low = self.halves
        self.relay4 = links.copy(sums.at[3, top], relay_in.at[0], peer[4])
        self.relay2 = links.copy(sums.at[3, low], relay_in.at[1], peer[2])
        self.last2 = [
            links.copy(sums.at[1, half], last_in.at[0, half], peer[2]) for half in self.halves
        ]
        self.last4 = [
            links.copy(sums.at[2, half], last_in.at[1, half], peer[4]) for half in self.halves
        ]

    def begin(self):
        for copy in self.pair.values():
            copy.start()

    def chip(self, mask):
        index = mask // 2
        self.pair[mask].wait_recv()
        mine = self.parts.at[self.peer[mask][1] if mask else self.place]
        add_rows(self.sums.at[index], mine, self.pair_in.at[index])

    def far(self):
        self.chip(6)
        self.relay4.start()
        self.relay2.start()

    def near(self, mask):
        self.chip(mask)
        if mask:
            (self.last2[1] if mask == 2 else self.last4[0]).start()

    def first(self):
        self.far()
        for mask in (2, 4, 0):
            self.near(mask)

    def second(self):
        top, low = self.halves
        self.relay4.wait_recv()
        add_rows(self.sums.at[1, top], self.sums.at[1, top], self.relay_in.at[0])
        self.last2[0].start()
        self.relay2.wait_recv()
        add_rows(self.sums.at[2, low], self.sums.at[2, low], self.relay_in.at[1])
        self.last4[1].start()

    def finish(self, store):
        for copy in self.last2 + self.last4:
            copy.wait_recv()

        def one(number, carry):
            at = pl.ds(pl.multiple_of(number * 32, 32), 32)
            total = self.last_in[0, at].astype(F32) + self.last_in[1, at].astype(F32)
            store(at, total + self.sums[0, at].astype(F32))
            return carry

        lax.fori_loop(0, self.last_in.shape[1] // 32, one, 0)

    def drain(self):
        for copy in self.pair.values():
            copy.wait_send()
        for copy in [self.relay4, self.relay2] + self.last2 + self.last4:
            copy.wait_send()


def dot(left, right, contract, precision=None):
    return lax.dot_general(
        left, right, (contract, ((), ())), precision=precision, preferred_element_type=F32
    )


def mm(left, right):
    return dot(left, right, ((1,), (0,)))


def mm_t(left, right):
    return dot(left, right, ((1,), (1,)))


def t_mm(left, right):
    return dot(left, right, ((0,), (0,)))


def widen(values, heads, head_size):
    rows = values.shape[0]
    lane = lax.broadcasted_iota(jnp.int32, (rows, 2 * head_size), 1)
    parts = []
    for pair in range(heads // 2):
        low = jnp.broadcast_to(values[:, 2 * pair : 2 * pair + 1], (rows, 2 * head_size))
        high = jnp.broadcast_to(values[:, 2 * pair + 1 : 2 * pair + 2], (rows, 2 * head_size))
        parts.append(jnp.where(lane < head_size, low, high))
    return jnp.concatenate(parts, axis=1)


def head_of_channel(inner, head_size):
    channel = lax.broadcasted_iota(jnp.int32, (inner, 128), 0)
    first = lax.broadcasted_iota(jnp.int32, (inner, 128), 1) * head_size
    return jnp.where((channel >= first) & (channel < first + head_size), 1.0, 0.0)


def sigmoid(values):
    return 0.5 * jnp.tanh(0.5 * values) + 0.5


def in_parts(values, count):
    parts = []
    for _ in range(count):
        parts.append(values.astype(BF16))
        values = values - parts[-1].astype(F32)
    return parts


def softplus(values):
    return jnp.maximum(values, 0.0) + jnp.log1p(jnp.exp(-jnp.abs(values)))


def split_pair(values, head_size):
    lane = lax.broadcasted_iota(jnp.int32, values.shape, 1)
    zero = jnp.zeros_like(values)
    return jnp.where(lane < head_size, values, zero), jnp.where(lane < head_size, zero, values)


def triangles():
    rows = lax.broadcasted_iota(jnp.int32, (CHUNK, CHUNK), 0)
    cols = lax.broadcasted_iota(jnp.int32, (CHUNK, CHUNK), 1)
    return rows >= cols


def triangles_up():
    rows = lax.broadcasted_iota(jnp.int32, (CHUNK, CHUNK), 0)
    cols = lax.broadcasted_iota(jnp.int32, (CHUNK, CHUNK), 1)
    return cols >= rows


def head_decays(cum, cum_t, head, causal):
    gap = cum[:, head : head + 1] - cum_t[head : head + 1, :]
    return jnp.exp(jnp.where(causal, gap, -1e30))


def plane_total(links, sums, landed, peer, count):
    landed[0] = sums[...].T[:count]
    copies = [links.copy(landed.at[0], landed.at[mask], peer[mask]) for mask in peer]
    for copy in copies:
        copy.start()

    def end():
        for copy in copies:
            copy.wait()
        got = [landed[mask] for mask in range(len(peer) + 1)]
        while len(got) > 1:
            got = [got[k] + got[k + 1] for k in range(0, len(got), 2)]
        return got[0]

    return end


def by_column(values):
    return jnp.concatenate([values, jnp.zeros((128 - values.shape[0], CHUNK), F32)], axis=0).T


class Line:
    def __init__(self, links, depth, row, place, blocks, valid=None):
        self.depth, self.row = depth, row
        above, below = lax.min(row + 1, depth - 1), lax.max(row - 1, 0)
        self.steps = []
        for step in range(depth - 1):
            up_sent, up_got = row - step, row - 1 - step
            down_sent, down_got = row + step, row + 1 + step
            ways = []
            for sends, shard, gets, got, device in (
                ((row < depth - 1) & (up_sent >= 0), up_sent, (row > 0) & (up_got >= 0), up_got, above),
                ((row > 0) & (down_sent < depth), down_sent, (row < depth - 1) & (down_got < depth), down_got, below),
            ):
                shard = lax.clamp(0, shard, depth - 1)
                got = lax.clamp(0, got, depth - 1)
                if valid is not None:
                    sends, gets = sends & valid(shard), gets & valid(got)
                copies = [links.copy(block, block, (device, place)) for block in blocks(shard)]
                ways.append((sends, gets, copies))
            self.steps.append(ways)

    def send(self, number):
        for sends, _, copies in self.steps[number]:

            @pl.when(sends)
            def _():
                for copy in copies:
                    copy.start()

    def wait(self, number):
        for _, gets, copies in self.steps[number]:

            @pl.when(gets)
            def _():
                for copy in copies:
                    copy.wait_recv()

    def drain(self):
        for ways in self.steps:
            for sends, _, copies in ways:

                @pl.when(sends)
                def _():
                    for copy in copies:
                        copy.wait_send()


class Pass:
    def __init__(self, links, peer, place, own, everyone):
        rows = own.shape[0] // 2
        mine = everyone.at[place]
        from2, from4, far = (everyone.at[peer[mask][1]] for mask in (2, 4, 6))
        top, low = pl.ds(0, rows), pl.ds(rows, rows)
        self.kept = None
        self.to2 = links.copy(own, mine, peer[2])
        self.to4 = links.copy(own, mine, peer[4])
        self.to1 = links.copy(own, mine, peer[1])
        self.relay4 = links.copy(from2.at[top], from2.at[top], peer[4])
        self.relay2 = links.copy(from4.at[low], from4.at[low], peer[2])
        self.pair2 = links.copy(from2, from2, peer[1])
        self.pair4 = links.copy(from4, from4, peer[1])
        self.pair6 = links.copy(far.at[top], far.at[top], peer[1])
        self.pair7 = links.copy(far.at[low], far.at[low], peer[1])

    def first(self):
        self.to2.start()
        self.to4.start()
        self.to1.start()

    def relay(self):
        self.to2.wait_recv()
        self.relay4.start()
        self.to4.wait_recv()
        self.relay2.start()
        self.pair2.start()
        self.pair4.start()

    def last(self):
        self.relay4.wait_recv()
        self.pair6.start()
        self.relay2.wait_recv()
        self.pair7.start()

    def end(self):
        for copy in (self.to1, self.pair2, self.pair4, self.pair6, self.pair7):
            copy.wait_recv()

    def drain(self):
        for copy in (
            self.to2,
            self.to4,
            self.to1,
            self.relay4,
            self.relay2,
            self.pair2,
            self.pair4,
            self.pair6,
            self.pair7,
        ):
            copy.wait_send()


def lay_out(pieces, row, count):
    tiles = [None] * -(-count * len(pieces) // 128)
    for index, piece in enumerate(pieces):
        tile, shift = divmod(index * count, 128)
        moved = pltpu.roll(piece, shift, 1) if shift else piece
        lane = lax.broadcasted_iota(jnp.int32, piece.shape, 1)
        parts = [(tile, jnp.where((lane >= shift) & (lane < shift + count), moved, 0.0))]
        if shift + count > 128:
            parts.append((tile + 1, jnp.where(lane < shift + count - 128, moved, 0.0)))
        for at, part in parts:
            tiles[at] = part if tiles[at] is None else tiles[at] + part
    return tiles


def channel_windows(ref, place, plane, half, run):
    core, chip = lax.rem(place, 2), lax.div(place, 2)
    parts = []
    for j in range(half):
        start = ((core * half + j) * plane + chip) * run
        base = pl.multiple_of(lax.div(start, 128) * 128, 128)
        window = ref[:, pl.ds(base, run + 64)]
        moved = pltpu.roll(window, run, 1)
        parts.append(jnp.where(lax.rem(start, 128) == 0, window, moved)[:, :run])
    return jnp.concatenate(parts, axis=1)


def head_choice(place, plane, half, group, heads):
    core, chip = lax.rem(place, 2), lax.div(place, 2)
    head = lax.broadcasted_iota(jnp.int32, (128, 128), 0)
    lane = lax.broadcasted_iota(jnp.int32, (128, 128), 1)
    part = sum(((lane >= j * group).astype(jnp.int32) for j in range(1, half)), jnp.zeros_like(lane))
    chosen = ((core * half + part) * plane + chip) * group + lane - part * group
    return jnp.where((head == chosen) & (lane < heads), 1.0, 0.0)


def forward_kernel(
    dims,
    x_own,
    cot_in,
    lengths,
    in_weight,
    wo_own,
    norm_in,
    gate_in,
    conv_w_in,
    conv_b_in,
    dt_bias_in,
    a_log_in,
    d_skip_in,
    normed_out,
    cot_out,
    turned_out,
    wb_out,
    wo_out,
    conv_out,
    pre_out,
    dt_out,
    gate_out,
    y_out,
    states_out,
    norms_out,
    taps_out,
    rows_out,
    w_dt_out,
    x_all,
    normed_all,
    cot_all,
    wg,
    wx,
    wb_far,
    wo,
    packs,
    dt_got,
    turned,
    conv_in,
    pre_all,
    dt_all,
    gate_all,
    y_all,
    states,
    ext,
    state,
    full,
    sums,
    sums_in,
    cot_own,
    wg_send,
    wx_send,
    pack,
    dt_own,
    dt_pack,
    dt_send,
    head_params,
    sends,
    recvs,
    locals_,
    stores,
):
    depth, width, heads, head_size, size, kernel, own_ch, inner_all = dims
    half, plane = depth // 2, width // 2
    inner = heads * head_size
    run = inner // half
    model = x_own.shape[1]
    piece = x_own.shape[0] // 2
    rows = 2 * piece
    slots = 2
    blocks = slots * width // 2
    row, place = lax.axis_index("dp"), lax.axis_index("seq")
    core = lax.rem(place, 2)
    links = Links(sends, recvs)
    peer = {mask: (row, flip_all(place, mask)) for mask in range(1, width)}
    line_peers = [(lax.rem(row + up, depth), place) for up in range(1, depth)]
    in_rows = in_weight.shape[0]
    bc_cols = 2 * inner_all

    def prepare():
        for target, at, to in runs_of(width, half, run):
            wx_send[target, :, at : at + run] = in_weight[:, inner_all + to : inner_all + to + run]
        for target in range(width):
            first = bc_cols + target % 2 * size
            wx_send[target, :, inner:] = in_weight[:, first : first + size]

    greet([peer[mask] for mask in range(1, width)] + line_peers, between=prepare)
    kept = [
        pltpu.make_async_copy(wx_send.at[place], wx.at[row, place], locals_.at[0]),
        pltpu.make_async_copy(dt_send.at[place], dt_got.at[place], locals_.at[1]),
        pltpu.make_async_copy(wg_send.at[place], wg.at[row, place], locals_.at[2]),
        pltpu.make_async_copy(x_own, x_all.at[place], locals_.at[3]),
        pltpu.make_async_copy(cot_own, cot_all.at[place], locals_.at[4]),
        pltpu.make_async_copy(pack, packs.at[row, place], locals_.at[5]),
    ]
    for number in (0, 3):
        kept[number].start()

    out_home = lax.div(row, half) == core
    out_block = wo.at[lax.rem(row, half), core]
    out_kept = pltpu.make_async_copy(wo_own, out_block, locals_.at[6])
    out_pair = links.copy(wo_own, out_block, peer[1])
    order = (6, 2, 4, 7, 3, 5, 1)
    plane_x, plane_g = [], []
    for mask in order:
        target = peer[mask][1]
        plane_x.append(links.copy(wx_send.at[target], wx.at[row, place], peer[mask]))
        plane_g.append(links.copy(wg_send.at[target], wg.at[row, place], peer[mask]))
    for copy in plane_x:
        copy.start()
    pl.when(out_home)(out_kept.start)
    pl.when(jnp.logical_not(out_home))(out_pair.start)
    x_pass = Pass(links, peer, place, x_own, x_all)
    cot_pass = Pass(links, peer, place, cot_own, cot_all)
    x_pass.first()

    dt_own[...] = jnp.zeros_like(dt_own)
    last = in_weight.shape[1]
    dt_own[:, 0 : last - bc_cols - 2 * size] = in_weight[:, bc_cols + 2 * size : last]
    dt_pack[row] = dt_own[...]
    lines = [conv_w_in[...], conv_b_in[...], gate_in[...], norm_in[...]]
    small_rows = jnp.concatenate(
        [jnp.pad(v.astype(F32), ((0, 0), (0, 128 - v.shape[1]))) for v in lines]
        + [jnp.zeros((16 - sum(v.shape[0] for v in lines), 128), F32)],
        axis=0,
    )
    pack[...] = small_rows.astype(BF16)
    pack_line = [links.copy(pack, packs.at[row, place], device) for device in line_peers]
    pack_line += [
        links.copy(dt_own, dt_pack.at[row], device) for device in line_peers
    ]
    for copy in pack_line:
        copy.start()
    kept[5].start()
    head_params[...] = jnp.zeros_like(head_params)
    for k, v in enumerate((dt_bias_in, a_log_in, d_skip_in)):
        head_params[k : k + 1, 0 : v.shape[1]] = v[...]
    for target, at, to in runs_of(width, half, run):
        wg_send[target, :, at : at + run] = in_weight[:, to : to + run]
    kept[2].start()
    token = lax.broadcasted_iota(jnp.int32, (piece, model), 0) + place * piece
    for slot in range(slots):
        live = token < lengths[0:1, slot : slot + 1]
        part = slice(slot * piece, (slot + 1) * piece)
        cot_own[part, :] = jnp.where(live, cot_in[part, :].astype(F32), 0.0).astype(BF16)
    kept[4].start()
    out_line = Line(
        links,
        depth,
        row,
        place,
        lambda shard: [wo.at[lax.rem(shard, half)]],
        lambda shard: lax.div(shard, half) == core,
    )
    x_line = Line(links, depth, row, place, lambda shard: [wx.at[shard]])
    gate_line = Line(links, depth, row, place, lambda shard: [wg.at[shard]])

    pl.when(out_home)(out_kept.wait)
    pl.when(out_home)(out_pair.wait_recv)
    out_line.send(0)
    kept[0].wait()
    for copy in plane_x:
        copy.wait_recv()
    x_line.send(0)
    for copy in plane_g:
        copy.start()
    kept[5].wait()
    for copy in pack_line:
        copy.wait_recv()
    targets = jnp.concatenate(
        [head_choice(target, plane, half, run // head_size, heads)[:, :16] for target in range(width)],
        axis=1,
    ).astype(BF16)
    dt_rows = dot(targets, dt_pack[...].reshape(depth * in_rows, 128), ((0,), (1,)))
    dt_send[...] = jnp.zeros_like(dt_send)
    dt_send[:, :, 0 : depth * in_rows] = dt_rows.astype(BF16).reshape(width, 16, depth * in_rows)
    kept[1].start()
    mine = packs.at[:, place]
    pack_plane = [links.copy(mine, mine, peer[mask]) for mask in order]
    pack_plane += [
        links.copy(dt_send.at[peer[mask][1]], dt_got.at[place], peer[mask]) for mask in order
    ]
    for copy in pack_plane:
        copy.start()
    x_pass.relay()
    cot_pass.first()
    x_line.wait(0)
    if depth > 2:
        x_line.send(1)
    kept[1].wait()
    for copy in pack_plane:
        copy.wait_recv()

    small = [
        packs[z, s].astype(F32)[:8]
        for z in range(depth)
        for s in range(width)
    ]
    choice = head_choice(place, plane, half, run // head_size, heads)
    tap_tiles = lay_out(small, 0, own_ch)
    for at, tile in enumerate(tap_tiles):
        full[:, at * 128 : (at + 1) * 128] = tile
    taps_out[:, :inner] = channel_windows(full, place, plane, half, run)
    taps_out[:, inner:] = full[:, inner_all : inner_all + 2 * size]
    gate_tiles = lay_out(small, 5, inner_all // (depth * width))
    for at, tile in enumerate(gate_tiles):
        full[:, at * 128 : (at + 1) * 128] = tile
    gate_gain = channel_windows(full, place, plane, half, run)[5:6]
    norm_tiles = lay_out(small, 6, model // (depth * width))
    norm_gain = jnp.concatenate([tile[6:7] for tile in norm_tiles], axis=1)
    chosen = dot(head_params[...], choice, ((1,), (0,)), lax.Precision.HIGHEST)
    lane = lax.broadcasted_iota(jnp.int32, (1, 128), 1)
    rates = jnp.where(lane < heads, -jnp.exp(chosen[1:2]), 0.0)
    skip = widen(chosen[2:3], heads, head_size)
    dt_tiles = lay_out(
        [
            pltpu.roll(dt_got[s].astype(F32), 256 - z * in_rows, 1)[:, :128]
            if z
            else dt_got[s].astype(F32)[:, :128]
            for z in range(depth)
            for s in range(width)
        ],
        0,
        in_rows,
    )
    w_dt_out[...] = jnp.zeros_like(w_dt_out)
    w_dt_out[0:16, :] = jnp.concatenate(dt_tiles, axis=1).astype(BF16)
    rows_out[...] = jnp.zeros_like(rows_out)
    rows_out[0:1, :] = norm_gain
    rows_out[1:2, :inner] = gate_gain
    rows_out[2:3, :inner] = skip
    rows_out[3:4, :128] = chosen[0:1]
    rows_out[4:5, :128] = rates

    x_pass.last()

    def normalise(index, carry):
        for part in range(2):
            held = x_all[index, part * piece : (part + 1) * piece, :].astype(F32)
            inv = lax.rsqrt(jnp.mean(held * held, axis=1, keepdims=True) + EPS)
            normed_all[index, part * piece : (part + 1) * piece, :] = (
                held * inv * rows_out[0:1, :]
            ).astype(BF16)
        return carry

    x_line.wait(1) if depth > 2 else None
    if depth > 3:
        x_line.send(2)
    for copy in plane_g:
        copy.wait_recv()
    kept[2].wait()
    x_pass.end()
    kept[3].wait()
    lax.fori_loop(0, width, normalise, 0)
    if depth > 3:
        x_line.wait(2)
    gate_line.send(0)
    near_bc = wx.at[:, :, :, pl.ds(inner, size)]
    pair_bc = links.copy(near_bc, wb_far, peer[1])
    pair_bc.start()
    saves = [pltpu.make_async_copy(normed_all, normed_out, locals_.at[7])]
    saves[0].start()
    pair_bc.wait_recv()

    causal = triangles()
    ones_three = jnp.concatenate([causal.astype(BF16)] * 3, axis=1)

    def stored(index):
        at = pl.ds(pl.multiple_of(index * rows, rows), rows)
        pairs = [
            (conv_in.at[at], conv_out.at[at]),
            (pre_all.at[at], pre_out.at[at]),
            (dt_all.at[at], dt_out.at[at]),
            (y_all.at[at], y_out.at[at]),
            (
                states.at[pl.ds(index * (rows // CHUNK), rows // CHUNK)],
                states_out.at[pl.ds(index * (rows // CHUNK), rows // CHUNK)],
            ),
        ]
        return [
            pltpu.make_async_copy(source, target, stores.at[k, index])
            for k, (source, target) in enumerate(pairs)
        ]

    per_slot = blocks // slots

    def scan_block(index, carry):
        slot, block = lax.div(index, per_slot), lax.rem(index, per_slot)
        at = pl.multiple_of(index * rows, rows)

        @pl.when(block == 0)
        def _():
            ext[0:8, :] = jnp.zeros((8, ext.shape[1]), F32)
            state[...] = jnp.zeros_like(state)

        tokens = normed_all[
            pl.ds(2 * block, 2), pl.ds(pl.multiple_of(slot * piece, piece), piece), :
        ].reshape(rows, model)
        mine = mm(tokens, wx[...].reshape(model, inner + size))
        ext[8:, :inner] = mine[:, :inner]
        ext[8:, pl.ds(pl.multiple_of(inner + core * size, 128), size)] = mine[:, inner:]
        ext[8:, pl.ds(pl.multiple_of(inner + (1 - core) * size, 128), size)] = mm(
            tokens, wb_far[...].reshape(model, size)
        )
        dt_arg = mm_t(tokens, w_dt_out[...]) + rows_out[3:4, :128]
        dt_all[pl.ds(at, rows), :] = dt_arg
        pre = taps_out[kernel : kernel + 1, :] + sum(
            taps_out[k : k + 1, :] * ext[9 - kernel + k : 9 - kernel + k + rows, :]
            for k in range(kernel)
        )
        conv_in[pl.ds(at, rows), :] = ext[8:, :]
        ext[0:8, :] = ext[rows : rows + 8, :]
        pre_all[pl.ds(at, rows), :] = pre
        act = pre * sigmoid(pre)
        dt_block = softplus(dt_arg)
        steps_block = dt_block * rows_out[4:5, :128]
        subs = rows // CHUNK
        parts = [slice(sub * CHUNK, (sub + 1) * CHUNK) for sub in range(subs)]
        x = act[:, :inner]
        b = act[:, inner : inner + size].astype(BF16)
        c = act[:, inner + size :].astype(BF16)
        cums = [
            mm(ones_three, jnp.concatenate(in_parts(steps_block[part], 3), axis=0))
            for part in parts
        ]
        lasts = [cum[CHUNK - 1 : CHUNK, :] for cum in cums]
        x_dt = x * widen(dt_block, heads, head_size)
        x_dt16 = x_dt.astype(BF16)
        cum_wide = widen(jnp.exp(jnp.concatenate(cums, axis=0)), heads, head_size)
        out_wide = widen(
            jnp.exp(jnp.concatenate([last - cum for last, cum in zip(lasts, cums)], axis=0)),
            heads,
            head_size,
        )
        weighted = (x_dt * out_wide).astype(BF16)
        near, read = [], []
        for sub, part in enumerate(parts):
            cum_t = cums[sub].T
            cb = mm_t(c[part], b[part])
            pieces = []
            for pair in range(heads // 2):
                lanes = slice(2 * pair * head_size, 2 * (pair + 1) * head_size)
                mixing = jnp.concatenate(
                    [
                        (head_decays(cums[sub], cum_t, 2 * pair + k, causal) * cb).astype(BF16)
                        for k in range(2)
                    ],
                    axis=1,
                )
                pieces.append(
                    mm(
                        mixing,
                        jnp.concatenate(split_pair(x_dt16[part, lanes], head_size), axis=0),
                    )
                )
            near.append(jnp.concatenate(pieces, axis=1))
        for sub, part in enumerate(parts):
            held = state[...]
            held16 = held.astype(BF16)
            states[index * subs + sub] = held16
            read.append(mm(c[part], held16))
            state[...] = held * widen(jnp.exp(lasts[sub]), heads, head_size) + t_mm(
                b[part], weighted[part]
            )
        y_all[pl.ds(at, rows), :] = (
            jnp.concatenate(near, axis=0)
            + jnp.concatenate(read, axis=0) * cum_wide
            + rows_out[2:3, :inner] * x
        )
        for copy in stored(index):
            copy.start()

        @pl.when(index == 1)
        def _():
            gate_line.wait(0)
            if depth > 2:
                gate_line.send(1)

        @pl.when(index == 2)
        def _():
            cot_pass.relay()

        if depth > 2:

            @pl.when(index == 4)
            def _():
                gate_line.wait(1)
                if depth > 3:
                    gate_line.send(2)

        @pl.when(index == 5)
        def _():
            cot_pass.last()
            out_line.wait(0)
            if depth <= 3 and depth > 2:
                out_line.send(1)

        if depth > 3:

            @pl.when(index == 6)
            def _():
                gate_line.wait(2)
                out_line.send(1)

        return carry

    lax.fori_loop(0, blocks, scan_block, 0)

    chunk_lane = lax.broadcasted_iota(jnp.int32, (CHUNK, 128), 1)
    sums[...] = jnp.zeros_like(sums)

    def gate_block(index, carry):
        slot, block = lax.div(index, per_slot), lax.rem(index, per_slot)
        at = pl.multiple_of(index * rows, rows)
        tokens = normed_all[
            pl.ds(2 * block, 2), pl.ds(pl.multiple_of(slot * piece, piece), piece), :
        ].reshape(rows, model)
        gate = mm(tokens, wg[...].reshape(model, inner))
        gate_all[pl.ds(at, rows), :] = gate
        gated = y_all[pl.ds(at, rows), :] * (gate * sigmoid(gate))
        for sub in range(rows // CHUNK):
            part = gated[sub * CHUNK : (sub + 1) * CHUNK]
            total = jnp.sum(part * part, axis=1, keepdims=True)
            sums[...] = jnp.where(chunk_lane == index * (rows // CHUNK) + sub, total, sums[...])
        if depth > 2:

            @pl.when(index == blocks // 2)
            def _():
                out_line.wait(1)
                if depth > 3:
                    out_line.send(2)

        return carry

    lax.fori_loop(0, blocks, gate_block, 0)
    squares = plane_total(links, sums, sums_in, peer, 2 * blocks)
    save_gate = pltpu.make_async_copy(gate_all, gate_out, locals_.at[8])
    save_gate.start()
    wg_flat, wx_flat = wg[...].reshape(model, inner), wx[...].reshape(model, inner + size)
    for at in range(0, model, 128):
        turned[:inner, at : at + 128] = wg_flat[at : at + 128, :].T
        turned[inner:, at : at + 128] = wx_flat[at : at + 128, :inner].T
    save_weights = [
        pltpu.make_async_copy(source, target, locals_.at[10 + k])
        for k, (source, target) in enumerate(
            (
                (turned, turned_out),
                (near_bc, wb_out.at[core]),
                (wb_far, wb_out.at[1 - core]),
                (wo, wo_out),
            )
        )
    ]
    for copy in save_weights[:3]:
        copy.start()
    cot_pass.end()
    kept[4].wait()
    save_cot = pltpu.make_async_copy(cot_all, cot_out, locals_.at[9])
    save_cot.start()
    if depth > 3:
        out_line.wait(2)
    save_weights[3].start()
    inv_gate = lax.rsqrt(squares() / inner_all + EPS)
    norms_out[...] = by_column(inv_gate)

    for copies in (plane_x, plane_g, pack_line, pack_plane, [pair_bc]):
        for copy in copies:
            copy.wait_send()
    pl.when(jnp.logical_not(out_home))(out_pair.wait_send)
    for line in (out_line, x_line, gate_line):
        line.drain()
    x_pass.drain()
    cot_pass.drain()
    for copy in saves + [save_gate, save_cot] + save_weights:
        copy.wait()

    def stores_end(index, carry):
        for copy in stored(index):
            copy.wait()
        return carry

    lax.fori_loop(0, blocks, stores_end, 0)


def forward(dims, arrays, collective):
    depth, width, heads, head_size, size, kernel, own_ch, inner_all = dims
    inner = heads * head_size
    x_own, _, _, in_weight, wo_own = arrays[:5]
    rows, model = x_own.shape
    in_rows = in_weight.shape[0]
    tokens = rows * width
    wide = inner + 2 * size
    shape = jax.ShapeDtypeStruct
    chunks = tokens // CHUNK
    weights = [
        ((depth, width, in_rows, inner), BF16),
        ((depth, width, in_rows, inner + size), BF16),
        ((depth, width, in_rows, size), BF16),
        ((depth // 2, 2) + wo_own.shape, BF16),
    ]
    passed = [
        ((2 * inner, model), BF16),
        ((2, depth, width, in_rows, size), BF16),
        ((depth // 2, 2) + wo_own.shape, BF16),
    ]
    kept = [
        ((tokens, wide), F32),
        ((tokens, wide), F32),
        ((tokens, 128), F32),
        ((tokens, inner), F32),
        ((tokens, inner), F32),
        ((chunks, size, inner), BF16),
    ]
    in_hbm = [((width, rows, model), BF16)] * 2 + passed + kept
    in_vmem = [((CHUNK, 128), F32), ((8, wide), F32), ((8, model), F32), ((128, model), BF16)]
    return pl.pallas_call(
        functools.partial(forward_kernel, dims),
        out_shape=tuple(shape(*s) for s in in_hbm + in_vmem),
        in_specs=[INVMEM] * len(arrays),
        out_specs=(ANY,) * len(in_hbm) + (INVMEM,) * len(in_vmem),
        scratch_shapes=[pltpu.VMEM((width, rows, model), BF16)] * 3
        + [pltpu.VMEM(*s) for s in weights]
        + [
            pltpu.VMEM((depth, width, 16, 128), BF16),
            pltpu.VMEM((width, 16, 256), BF16),
            pltpu.VMEM((2 * inner, model), BF16),
        ]
        + [pltpu.VMEM(*s) for s in kept]
        + [
            pltpu.VMEM((rows + 8, wide), F32),
            pltpu.VMEM((size, inner), F32),
            pltpu.VMEM((8, -(-own_ch * depth * width // 128) * 128), F32),
            pltpu.VMEM((CHUNK, 128), F32),
            pltpu.VMEM((width, chunks, 128), F32),
            pltpu.VMEM((rows, model), BF16),
            pltpu.VMEM((width, in_rows, inner), BF16),
            pltpu.VMEM((width, in_rows, inner + size), BF16),
            pltpu.VMEM((16, 128), BF16),
            pltpu.VMEM((in_rows, 128), BF16),
            pltpu.VMEM((depth, in_rows, 128), BF16),
            pltpu.VMEM((width, 16, 256), BF16),
            pltpu.VMEM((8, 128), F32),
            pltpu.SemaphoreType.DMA((112,)),
            pltpu.SemaphoreType.DMA((112,)),
            pltpu.SemaphoreType.DMA((16,)),
            pltpu.SemaphoreType.DMA((5, tokens // rows)),
        ],
        compiler_params=pltpu.CompilerParams(
            collective_id=collective, has_side_effects=True, vmem_limit_bytes=VMEM_LIMIT
        ),
        name="forward_fused",
    )(*arrays)


class PlaneRows:
    def __init__(self, links, row, place, parts, landed, at, local):
        mine = landed.at[place, :, at]
        peers = [(row, flip_all(place, mask)) for mask in (6, 7, 2, 3, 4, 5, 1)]
        self.copies = [links.copy(parts.at[peer[1], :, at], mine, peer) for peer in peers]
        self.kept = pltpu.make_async_copy(parts.at[place, :, at], mine, local)

    def begin(self):
        for copy in self.copies:
            copy.start()
        self.kept.start()

    def end(self):
        self.kept.wait()
        for copy in self.copies:
            copy.wait()


class SendBack:
    def __init__(self, links, row, place, sent, back, local):
        self.rows = back.shape[1]
        self.sent, self.back, self.place = sent, back, place
        mine = back.at[place]
        self.copies = [
            links.copy(self.block((row, flip_all(place, mask))[1]), mine, (row, flip_all(place, mask)))
            for mask in (6, 2, 4, 7, 3, 5, 1)
        ]
        self.kept = pltpu.make_async_copy(self.block(place), mine, local)

    def block(self, target):
        return self.sent.at[pl.ds(pl.multiple_of(target * self.rows, self.rows), self.rows)]

    def begin(self):
        for copy in self.copies:
            copy.start()
        self.kept.start()

    def end(self):
        self.kept.wait()
        for copy in self.copies:
            copy.wait()


def turn(target, source):
    for at in range(0, source.shape[0], 128):
        target[:, at : at + 128] = source[at : at + 128, :].T.astype(target.dtype)


def reverse_kernel(
    dims,
    cot_hbm,
    normed_hbm,
    gate_hbm,
    y_hbm,
    pre_hbm,
    conv_hbm,
    dt_hbm,
    states_hbm,
    wo_hbm,
    norms,
    taps,
    rows_in,
    x_own,
    d_gate_hbm,
    d_x_hbm,
    d_arg_hbm,
    output,
    gate_back,
    out_grad,
    channel_sums,
    head_sums,
    bc_landed,
    cot_all,
    normed_all,
    gate_all,
    y_all,
    d_y_all,
    wo,
    d_gate,
    d_x_all,
    d_arg_all,
    d_bc,
    g_out,
    g_gate,
    pre_two,
    conv_two,
    dt_two,
    states_two,
    later,
    d_ext,
    o_pair,
    o_sums,
    o_relay,
    o_last,
    out_up_in,
    out_up_out,
    out_down_in,
    out_down_out,
    gate_up_in,
    gate_up_out,
    gate_down_in,
    gate_down_out,
    out_sum,
    out_far,
    gate_sum,
    gate_sent,
    means,
    sums_in,
    sends,
    recvs,
    locals_,
    streams,
):
    depth, width, heads, head_size, size, kernel, own_ch, inner_all = dims
    half = depth // 2
    inner = heads * head_size
    model = cot_all.shape[2]
    piece = cot_all.shape[1] // 2
    rows = 2 * piece
    slots = 2
    blocks = slots * width // 2
    per_slot = blocks // slots
    subs = rows // CHUNK
    row, place = lax.axis_index("dp"), lax.axis_index("seq")
    core = lax.rem(place, 2)
    links = Links(sends, recvs)
    above, below = lax.min(row + 1, depth - 1), lax.max(row - 1, 0)
    peer = {mask: (row, flip_all(place, mask)) for mask in range(1, width)}

    loads = [
        pltpu.make_async_copy(source, target, locals_.at[k])
        for k, (source, target) in enumerate(
            (
                (y_hbm, y_all),
                (gate_hbm, gate_all),
                (cot_hbm, cot_all),
                (wo_hbm, wo),
                (normed_hbm, normed_all),
            )
        )
    ]
    for copy in loads:
        copy.start()

    def place_of(number):
        slot = lax.div(number, per_slot)
        return slot, per_slot - 1 - lax.rem(number, per_slot)

    def fetch(number):
        slot, block = place_of(number)
        index = slot * per_slot + block
        at = pl.ds(pl.multiple_of(index * rows, rows), rows)
        buffer = lax.rem(number, 2)
        pairs = (
            (pre_hbm.at[at], pre_two.at[buffer]),
            (conv_hbm.at[at, pl.ds(0, inner)], conv_two.at[buffer]),
            (dt_hbm.at[at], dt_two.at[buffer]),
            (states_hbm.at[pl.ds(index * subs, subs)], states_two.at[buffer]),
        )
        return [
            pltpu.make_async_copy(source, target, streams.at[buffer, k])
            for k, (source, target) in enumerate(pairs)
        ]

    for copy in fetch(0):
        copy.start()
    greet(
        [peer[mask] for mask in range(1, width)],
        [(row < depth - 1, (above, place)), (row > 0, (below, place))],
    )

    out_line = LineSum(
        links,
        depth,
        row,
        place,
        lambda q: g_out.at[pl.ds((q % half) * (inner // half), inner // half)],
        lambda q: core == q // half,
        out_up_in,
        out_up_out,
        out_down_in,
        out_down_out,
        half,
    )
    cols = model // depth
    gate_line = LineSum(
        links,
        depth,
        row,
        place,
        lambda q: g_gate.at[:, pl.ds(q * cols, cols)],
        lambda q: row >= 0,
        gate_up_in,
        gate_up_out,
        gate_down_in,
        gate_down_out,
    )
    o_plane = PlaneSum(links, row, place, cot_all, o_pair, o_sums, o_relay, o_last)
    send_gate = SendBack(links, row, place, gate_sent, gate_back, locals_.at[6])

    chunk_lane = lax.broadcasted_iota(jnp.int32, (CHUNK, 128), 1)

    def column(ref, index):
        parts = [
            jnp.sum(
                jnp.where(chunk_lane == index * subs + sub, ref[...], 0.0),
                axis=1,
                keepdims=True,
            )
            for sub in range(subs)
        ]
        return jnp.concatenate(parts, axis=0)

    def tokens_of(ref, index):
        slot, block = lax.div(index, per_slot), lax.rem(index, per_slot)
        return ref.at[pl.ds(2 * block, 2), pl.ds(pl.multiple_of(slot * piece, piece), piece), :]

    gate_gain = rows_in[1:2, :inner]
    skip = rows_in[2:3, :inner]

    def normed_block(index, carry):
        at = pl.ds(pl.multiple_of(index * rows, rows), rows)
        gate = gate_all[at, :]
        hat = y_all[at, :] * (gate * sigmoid(gate)) * column(norms, index)
        tokens_of(d_gate, index)[...] = (
            (hat * gate_gain).astype(BF16).reshape(2, piece, inner)
        )
        return carry

    loads[0].wait()
    loads[1].wait()
    lax.fori_loop(0, blocks, normed_block, 0)

    everything = slots * width * piece

    def out_grad_tile(number, carry):
        at = pl.ds(pl.multiple_of(number * 128, 128), 128)
        left = d_gate[:, :, at].reshape(everything, 128)
        g_out[at, :] = t_mm(left, cot_all[...].reshape(everything, model))
        return carry

    loads[2].wait()
    lax.fori_loop(0, inner // 128, out_grad_tile, 0)
    out_line.phase(0)

    def cot_block(index, carry):
        at = pl.ds(pl.multiple_of(index * rows, rows), rows)
        tokens = tokens_of(cot_all, index)[...].reshape(rows, model)
        dgn = mm_t(tokens, wo[...].reshape(inner, model))
        d_y_all[at, :] = dgn
        gate = gate_all[at, :]
        cross = dgn * gate_gain * y_all[at, :] * (gate * sigmoid(gate))
        for sub in range(subs):
            part = cross[sub * CHUNK : (sub + 1) * CHUNK]
            total = jnp.sum(part, axis=1, keepdims=True)
            means[...] = jnp.where(chunk_lane == index * subs + sub, total, means[...])
        return carry

    loads[3].wait()
    means[...] = jnp.zeros_like(means)
    lax.fori_loop(0, blocks, cot_block, 0)
    crosses = plane_total(links, means, sums_in, peer, 2 * blocks)

    def out_block(index, carry):
        cot_all[index] = mm(d_gate[index], wo[...].reshape(inner, model)).astype(BF16)
        return carry

    lax.fori_loop(0, width, out_block, 0)
    o_plane.begin()
    if depth > 2:
        out_line.phase(1)
    means[...] = norms[...] * by_column(crosses() / inner_all)

    def gate_block(index, carry):
        at = pl.ds(pl.multiple_of(index * rows, rows), rows)
        gate = gate_all[at, :]
        sig = sigmoid(gate)
        gate_act = gate * sig
        y = y_all[at, :]
        inv = column(norms, index)
        hat = y * gate_act * inv
        d_gated = inv * (d_y_all[at, :] * gate_gain - hat * column(means, index))
        d_y_all[at, :] = d_gated * gate_act
        tokens_of(d_gate, index)[...] = (
            (d_gated * y * sig * (1.0 + gate * (1.0 - sig))).astype(BF16).reshape(2, piece, inner)
        )
        return carry

    lax.fori_loop(0, blocks, gate_block, 0)
    save_gate = pltpu.make_async_copy(d_gate, d_gate_hbm, locals_.at[7])
    save_gate.start()

    def gate_grad_tile(number, carry):
        at = pl.ds(pl.multiple_of(number * 128, 128), 128)
        left = d_gate[:, :, at].reshape(everything, 128)
        g_gate[at, :] = t_mm(left, normed_all[...].reshape(everything, model))
        return carry

    loads[4].wait()
    lax.fori_loop(0, inner // 128, gate_grad_tile, 0)
    gate_line.phase(0)
    o_plane.first()

    channel_sums[...] = jnp.zeros_like(channel_sums)
    head_sums[...] = jnp.zeros_like(head_sums)
    causal = triangles()
    ones = causal.astype(BF16)
    ones_three = jnp.concatenate([ones] * 3, axis=1)
    after = jnp.where(triangles_up(), 1.0, 0.0).astype(BF16)
    before = jnp.where(triangles_up(), 0.0, 1.0).astype(BF16)
    both_ways = jnp.concatenate([after, before] * 2, axis=1)
    of_head = head_of_channel(inner, head_size).astype(BF16)

    def head_totals(values):
        high, low = in_parts(values, 2)
        return mm(high, of_head) + mm(low, of_head)

    home = lax.div(row, half) == core
    rows_out = out_grad.shape[0]
    far = links.copy(out_far, out_grad, peer[1])

    def pump_gate():
        if depth > 2:
            gate_line.phase(1)

    def pump_gate_last():
        if depth > 3:
            gate_line.phase(2)

    def pump_out():
        out_line.finish(out_sum)
        for this in range(2):

            @pl.when(home & (core == this))
            def _():
                cast_rows(out_far, out_sum.at[pl.ds((1 - this) * rows_out, rows_out)])
                far.start()
                cast_rows(out_grad, out_sum.at[pl.ds(this * rows_out, rows_out)])

    def pump_back():
        gate_line.finish(gate_sum)
        turn(gate_sent, gate_sum)
        send_gate.begin()

    quarter = everything // 4
    bc_rows = [
        PlaneRows(
            links,
            row,
            place,
            d_bc,
            bc_landed,
            pl.ds((2 * (k // 2) + 1 - k % 2) * quarter, quarter),
            locals_.at[10 + k],
        )
        for k in range(4)
    ]

    def pump_out_last():
        if depth > 3:
            out_line.phase(2)

    pumps = {
        0: [pump_out_last],
        1: [bc_rows[0].begin],
        2: [pump_gate, o_plane.second],
        3: [bc_rows[1].begin],
        4: [pump_gate_last],
        5: [bc_rows[2].begin, pump_out],
        6: [lambda: o_plane.finish(store_output)],
    }

    def store_output(at, total):
        output[at] = (x_own[at].astype(F32) + total).astype(BF16)

    def scan_block(number, carry):
        slot, block = place_of(number)
        index = slot * per_slot + block
        buffer = lax.rem(number, 2)
        for copy in fetch(number):
            copy.wait()

        @pl.when(number + 1 < blocks)
        def _():
            for copy in fetch(number + 1):
                copy.start()

        @pl.when(block == per_slot - 1)
        def _():
            later[...] = jnp.zeros_like(later)
            d_ext[rows:, :] = jnp.zeros((8, inner), F32)

        pre = pre_two[buffer]
        pre_sig = sigmoid(pre)
        act = pre * pre_sig
        slope = pre_sig[:, :inner] * (1.0 + pre[:, :inner] * (1.0 - pre_sig[:, :inner]))
        dt_arg = dt_two[buffer]
        dt_block = softplus(dt_arg)
        rates = rows_in[4:5, :128]
        steps_block = dt_block * rates
        parts = [slice(sub * CHUNK, (sub + 1) * CHUNK) for sub in range(subs)]
        at = pl.ds(pl.multiple_of(index * rows, rows), rows)
        x = act[:, :inner]
        b = act[:, inner : inner + size].astype(BF16)
        c = act[:, inner + size :].astype(BF16)
        cums = [
            mm(ones_three, jnp.concatenate(in_parts(steps_block[part], 3), axis=0))
            for part in parts
        ]
        lasts = [cum[CHUNK - 1 : CHUNK, :] for cum in cums]
        dt_wide = widen(dt_block, heads, head_size)
        cum_wide = widen(jnp.exp(jnp.concatenate(cums, axis=0)), heads, head_size)
        out_wide = widen(
            jnp.exp(jnp.concatenate([last - cum for last, cum in zip(lasts, cums)], axis=0)),
            heads,
            head_size,
        )
        x_dt = x * dt_wide
        x_dt16 = x_dt.astype(BF16)
        d_y = d_y_all[at, :]
        d_y16 = d_y.astype(BF16)
        d_read = (d_y * cum_wide).astype(BF16)
        sent = (x_dt * out_wide).astype(BF16)
        near, d_cbs = [], []
        for sub, part in enumerate(parts):
            cum_t = cums[sub].T
            cb = mm_t(c[part], b[part])
            d_cb = jnp.zeros((CHUNK, CHUNK), F32)
            pieces = []
            for pair in range(heads // 2):
                lanes = slice(2 * pair * head_size, 2 * (pair + 1) * head_size)
                d_y_split = split_pair(d_y16[part, lanes], head_size)
                mixing = []
                for k in range(2):
                    decay = head_decays(cums[sub], cum_t, 2 * pair + k, causal)
                    mixing.append((decay * cb).astype(BF16))
                    d_cb = d_cb + decay * mm_t(d_y_split[k], x_dt16[part, lanes])
                pieces.append(
                    t_mm(jnp.concatenate(mixing, axis=0), jnp.concatenate(d_y_split, axis=0))
                )
            near.append(jnp.concatenate(pieces, axis=1))
            d_cbs.append(d_cb.astype(BF16))
        later_rows, overs = [None] * subs, [None] * subs
        for sub in reversed(range(subs)):
            part = parts[sub]
            held16 = states_two[buffer, sub]
            grown = later[...]
            grown16 = grown.astype(BF16)
            later_rows[sub] = mm(b[part], grown16)
            column_at = pl.ds(pl.multiple_of(index * rows + sub * CHUNK, CHUNK), CHUNK)
            d_b = mm_t(grown16, sent[part]) + t_mm(c[part], d_cbs[sub])
            d_c = mm_t(held16, d_read[part]) + dot(b[part], d_cbs[sub], ((0,), (1,)))
            for first, value in ((0, d_b), (width // 2, d_c)):
                d_bc[first : first + width // 2, :, column_at] = value.astype(BF16).reshape(
                    width // 2, 2 * size // width, CHUNK
                )
            overs[sub] = jnp.sum(grown * held16.astype(F32), axis=0, keepdims=True)
            later[...] = grown * widen(jnp.exp(lasts[sub]), heads, head_size) + t_mm(
                c[part], d_read[part]
            )
        d_x_near = jnp.concatenate(near, axis=0)
        d_x_later = out_wide * jnp.concatenate(later_rows, axis=0)
        d_x_dt = d_x_later + d_x_near
        d_x = d_x_dt * dt_wide + skip * d_y
        d_ext[0:rows, :] = d_x * slope
        channel_sums[5:6, :] += jnp.sum(d_y * x, axis=0, keepdims=True)
        cross_wide = d_y16.astype(F32) * (y_all[at, :] - skip * x) - x_dt16.astype(F32) * d_x_near
        over_wide = jnp.concatenate(overs + [jnp.zeros((8 - subs, inner), F32)], axis=0)
        d_dt_direct = mm((x * d_x_dt).astype(BF16), of_head)
        d_cum = head_totals(cross_wide)
        through = mm((x_dt * d_x_later).astype(BF16), of_head)
        over = head_totals(over_wide)
        d_log = jnp.concatenate(
            [
                mm(
                    both_ways,
                    jnp.concatenate(
                        in_parts(jnp.concatenate([d_cum[part], through[part]], axis=0), 2), axis=0
                    ),
                )
                + over[sub : sub + 1] * jnp.exp(lasts[sub])
                for sub, part in enumerate(parts)
            ],
            axis=0,
        )
        d_arg = (d_dt_direct + rates * d_log) * sigmoid(dt_arg)
        d_arg_all[
            pl.ds(2 * block, 2), pl.ds(pl.multiple_of(slot * piece, piece), piece), :
        ] = d_arg.astype(BF16).reshape(2, piece, 128)
        head_sums[0:1, :] += jnp.sum(d_arg, axis=0, keepdims=True)
        head_sums[1:2, :] += jnp.sum(d_log * dt_block, axis=0, keepdims=True) * rates

        d_conv = jnp.zeros((rows, inner), F32)
        x_in = conv_two[buffer]
        for k in range(kernel):
            moved = d_ext[kernel - 1 - k : kernel - 1 - k + rows, :]
            d_conv = d_conv + taps[k : k + 1, :inner] * moved
            channel_sums[k : k + 1, :] += jnp.sum(moved * x_in, axis=0, keepdims=True)
        channel_sums[4:5, :] += jnp.sum(d_ext[0:rows, :], axis=0, keepdims=True)
        d_x_all[
            pl.ds(2 * block, 2), pl.ds(pl.multiple_of(slot * piece, piece), piece), :
        ] = d_conv.astype(BF16).reshape(2, piece, inner)
        d_ext[rows:, :] = d_ext[0:8, :]

        for at_step, actions in pumps.items():

            @pl.when(number == at_step)
            def _():
                for action in actions:
                    action()

        return carry

    lax.fori_loop(0, blocks, scan_block, 0)
    bc_rows[3].begin()
    pump_back()
    saves = [
        pltpu.make_async_copy(source, target, locals_.at[8 + k])
        for k, (source, target) in enumerate(
            ((d_x_all, d_x_hbm), (d_arg_all, d_arg_hbm))
        )
    ]
    for copy in saves:
        copy.start()

    pl.when(jnp.logical_not(home))(far.wait_recv)
    pl.when(home)(far.wait_send)
    o_plane.drain()
    out_line.drain()
    gate_line.drain()
    send_gate.end()
    save_gate.wait()
    for copy in saves:
        copy.wait()
    for rows_ in bc_rows:
        rows_.end()


def line_buffers(count, extent):
    return [pltpu.VMEM((count,) + extent, BF16)] * 4


def plane_buffers(rows, model):
    return [
        pltpu.VMEM((4, rows, model), BF16),
        pltpu.VMEM((4, rows, model), BF16),
        pltpu.VMEM((2, rows // 2, model), BF16),
        pltpu.VMEM((2, rows, model), BF16),
    ]


def reverse(dims, hbm, vmem, collective):
    depth, width, heads, head_size, size, kernel, own_ch, inner_all = dims
    inner = heads * head_size
    _, rows, model = hbm[0].shape
    tokens = rows * width
    wide = inner + 2 * size
    shape = jax.ShapeDtypeStruct
    subs = rows // CHUNK
    half = depth // 2
    out_piece, in_piece = (inner // half, model), (inner, model // depth)
    saved = [
        ((width, rows, inner), BF16),
        ((width, rows, inner), BF16),
        ((width, rows, 128), BF16),
    ]
    bc = ((width, 2 * size // width, tokens), BF16)
    kept = [
        ((rows, model), BF16),
        ((width, model // depth // width, inner), BF16),
        ((out_piece[0] // 2, model), F32),
        ((8, inner), F32),
        ((8, 128), F32),
        bc,
    ]
    return pl.pallas_call(
        functools.partial(reverse_kernel, dims),
        out_shape=tuple(shape(*s) for s in saved + kept),
        in_specs=[ANY] * len(hbm) + [INVMEM] * len(vmem),
        out_specs=(ANY,) * len(saved) + (INVMEM,) * len(kept),
        scratch_shapes=[pltpu.VMEM((width, rows, model), BF16)] * 2
        + [pltpu.VMEM((tokens, inner), F32)] * 3
        + [pltpu.VMEM(hbm[-1].shape, BF16)]
        + [pltpu.VMEM(*s) for s in saved]
        + [
            pltpu.VMEM(*bc),
            pltpu.VMEM((inner, model), F32),
            pltpu.VMEM((inner, model), F32),
            pltpu.VMEM((2, rows, wide), F32),
            pltpu.VMEM((2, rows, inner), F32),
            pltpu.VMEM((2, rows, 128), F32),
            pltpu.VMEM((2, subs, size, inner), BF16),
            pltpu.VMEM((size, inner), F32),
            pltpu.VMEM((rows + 8, inner), F32),
        ]
        + plane_buffers(rows, model)
        + line_buffers(half, out_piece)
        + line_buffers(depth - 1, in_piece)
        + [
            pltpu.VMEM(out_piece, F32),
            pltpu.VMEM((out_piece[0] // 2, model), F32),
            pltpu.VMEM(in_piece, F32),
            pltpu.VMEM((in_piece[1], in_piece[0]), BF16),
            pltpu.VMEM((CHUNK, 128), F32),
            pltpu.VMEM((width, tokens // CHUNK, 128), F32),
            pltpu.SemaphoreType.DMA((80,)),
            pltpu.SemaphoreType.DMA((80,)),
            pltpu.SemaphoreType.DMA((14,)),
            pltpu.SemaphoreType.DMA((2, 4)),
        ],
        compiler_params=pltpu.CompilerParams(
            collective_id=collective, has_side_effects=True, vmem_limit_bytes=VMEM_LIMIT
        ),
        name="reverse_fused",
    )(*hbm, *vmem)


def runs_of(width, half, run):
    plane = width // 2
    for place in range(width):
        for j in range(half):
            yield place, j * run, (((place % 2) * half + j) * plane + place // 2) * run


def head_places(place, half, plane, group, heads, shift):
    lane = lax.broadcasted_iota(jnp.int32, (128, 128), 0) - shift
    head = lax.broadcasted_iota(jnp.int32, (128, 128), 1)
    part = sum(((lane >= j * group).astype(jnp.int32) for j in range(1, half)), jnp.zeros_like(lane))
    chosen = ((place % 2 * half + part) * plane + place // 2) * group + lane - part * group
    return jnp.where((head == chosen) & (lane >= 0) & (lane < heads), 1.0, 0.0)


def weights_kernel(
    dims,
    d_x_hbm,
    normed_hbm,
    turned_hbm,
    d_gate_hbm,
    pre_hbm,
    conv_hbm,
    d_arg_hbm,
    wb_hbm,
    cot_hbm,
    bc_landed,
    taps,
    channel_sums,
    head_sums,
    rows_in,
    x_own,
    w_dt,
    gate_back,
    input_grad,
    in_grad,
    smalls,
    d_x,
    normed_all,
    d_gate,
    pre_own,
    conv_own,
    d_arg,
    wb,
    cot_own,
    w_turned,
    d_small,
    g_x,
    g_small,
    d_parts,
    d_ext,
    bc_sums,
    d_pair,
    d_sums,
    d_relay,
    d_last,
    x_up_in,
    x_up_out,
    x_down_in,
    x_down_out,
    small_up_in,
    small_up_out,
    small_down_in,
    small_down_out,
    x_sum,
    x_sent,
    small_sum,
    small_sent,
    x_back,
    small_back,
    sums_own,
    sums_line,
    sums_all,
    full,
    sends,
    recvs,
    locals_,
):
    depth, width, heads, head_size, size, kernel, own_ch, inner_all = dims
    half, plane = depth // 2, width // 2
    inner = heads * head_size
    run = inner // half
    group = run // head_size
    model = normed_all.shape[2]
    piece = normed_all.shape[1] // 2
    rows = 2 * piece
    slots = 2
    blocks = slots * width // 2
    per_slot = blocks // slots
    everything = slots * width * piece
    own = 2 * size // width
    row, place = lax.axis_index("dp"), lax.axis_index("seq")
    links = Links(sends, recvs)
    peer = {mask: (row, flip_all(place, mask)) for mask in range(1, width)}
    order = (6, 2, 4, 7, 3, 5, 1)
    per_block = 128 // own
    bc_turn = 128 - own * lax.rem(place, per_block)
    window = pl.ds(pl.multiple_of(inner + lax.div(place, per_block) * 128, 128), 128)

    loads = [
        pltpu.make_async_copy(source, target, locals_.at[k])
        for k, (source, target) in enumerate(
            (
                (d_x_hbm, d_x),
                (normed_hbm, normed_all),
                (turned_hbm, w_turned.at[pl.ds(0, 2 * inner)]),
                (d_gate_hbm, d_gate),
                (pre_hbm.at[:, window], pre_own),
                (conv_hbm.at[:, window], conv_own),
                (d_arg_hbm, d_arg),
                (wb_hbm, wb),
                (cot_hbm.at[place], cot_own),
            )
        )
    ]
    for copy in loads:
        copy.start()
    line_peers = [(lax.rem(row + up, depth), place) for up in range(1, depth)]
    greet([peer[mask] for mask in range(1, width)] + line_peers)

    cols = model // depth

    def line(own_ref, buffers):
        return LineSum(
            links,
            depth,
            row,
            place,
            lambda q: own_ref.at[:, pl.ds(q * cols, cols)],
            lambda q: row >= 0,
            *buffers,
        )

    x_line = line(g_x, (x_up_in, x_up_out, x_down_in, x_down_out))
    small_line = line(g_small, (small_up_in, small_up_out, small_down_in, small_down_out))
    d_plane = PlaneSum(links, row, place, d_parts, d_pair, d_sums, d_relay, d_last)
    send_x = SendBack(links, row, place, x_sent, x_back, locals_.at[12])
    send_small = SendBack(links, row, place, small_sent, small_back, locals_.at[13])

    def x_grad_tile(number, carry):
        at = pl.ds(pl.multiple_of(number * 128, 128), 128)
        left = d_x[:, :, at].reshape(everything, 128)
        g_x[at, :] = t_mm(left, normed_all[...].reshape(everything, model))
        return carry

    loads[0].wait()
    loads[1].wait()
    lax.fori_loop(0, inner // 128, x_grad_tile, 0)
    x_line.phase(0)

    lane = lax.broadcasted_iota(jnp.int32, (1, 128), 1)
    mine = lane < own

    def to_front(values):
        return pltpu.roll(values, bc_turn, 1)

    own_taps = to_front(taps[:, window])
    for copy in loads[4:8]:
        copy.wait()
    bc_sums[...] = jnp.zeros_like(bc_sums)

    def small_block(number, carry):
        slot, block = lax.div(number, per_slot), per_slot - 1 - lax.rem(number, per_slot)
        at = pl.ds(pl.multiple_of((slot * per_slot + block) * rows, rows), rows)

        @pl.when(block == per_slot - 1)
        def _():
            d_ext[rows:, :] = jnp.zeros((8, 128), F32)

        total = sum(bc_landed[k, :, at].astype(F32) for k in range(width))
        total = jnp.concatenate([total, jnp.zeros((128 - own, rows), F32)], axis=0)
        pre = to_front(pre_own[at, :])
        sig = sigmoid(pre)
        d_pre = jnp.where(mine, total.T * (sig * (1.0 + pre * (1.0 - sig))), 0.0)
        d_ext[0:rows, :] = d_pre
        where = (pl.ds(2 * block, 2), pl.ds(pl.multiple_of(slot * piece, piece), piece))
        conv_in = to_front(conv_own[at, :])
        d_conv = jnp.zeros((rows, 128), F32)
        for k in range(kernel):
            moved = d_ext[kernel - 1 - k : kernel - 1 - k + rows, :]
            d_conv = d_conv + own_taps[k : k + 1, :] * moved
            bc_sums[k : k + 1, :] += jnp.sum(moved * conv_in, axis=0, keepdims=True)
        bc_sums[4:5, :] += jnp.sum(d_pre, axis=0, keepdims=True)
        d_ext[rows:, :] = d_ext[0:8, :]
        d_dt = pltpu.roll(
            d_arg[where[0], where[1], :].astype(F32).reshape(rows, 128), own, 1
        )
        both = jnp.where(mine, d_conv, jnp.where(lane < own + heads, d_dt, 0.0))
        d_small[where[0], where[1], :] = both.astype(BF16).reshape(2, piece, 128)
        return carry

    lax.fori_loop(0, blocks, small_block, 0)
    g_small[...] = t_mm(
        d_small[...].reshape(everything, 128), normed_all[...].reshape(everything, model)
    )
    small_line.phase(0)
    for copy in loads[2:4]:
        copy.wait()

    def turn_weights(number, carry):
        at = pl.ds(pl.multiple_of(number * 128, 128), 128)
        bc = to_front(wb[lax.div(place, per_block), at, :].astype(F32))
        w_turned[2 * inner :, at] = jnp.where(mine, bc, 0.0).T.astype(BF16)
        return carry

    lax.fori_loop(0, model // 128, turn_weights, 0)
    w_turned[2 * inner + own : 2 * inner + own + 16, :] = w_dt[0:16, :]

    def token_grads(index):
        both = jnp.concatenate([d_gate[index], d_x[index], d_small[index]], axis=1)
        d_parts[index] = mm(both, w_turned[...]).astype(BF16)

    for mask in (6, 2, 4, 0):
        token_grads(peer[mask ^ 1][1])
        d_plane.pair[mask].start()
    token_grads(peer[6][1])
    d_plane.far()
    token_grads(peer[2][1])
    d_plane.near(2)
    token_grads(peer[4][1])
    d_plane.near(4)
    if depth > 2:
        x_line.phase(1)
    token_grads(place)
    d_plane.near(0)

    sums_own[:, :inner] = channel_sums[...]
    sums_own[:, inner : inner + 128] = bc_sums[...]
    sums_own[:, inner + 128 :] = head_sums[...]
    sums_own[2:3, inner + 128 :] = dot(
        channel_sums[...],
        head_of_channel(inner, head_size),
        ((1,), (0,)),
        lax.Precision.HIGHEST,
    )[5:6]
    sums_copies = [
        links.copy(sums_own, sums_line.at[k], device) for k, device in enumerate(line_peers)
    ]
    for copy in sums_copies:
        copy.start()
    d_plane.second()
    if depth > 3:
        x_line.phase(2)
    if depth > 2:
        small_line.phase(1)
    for copy in sums_copies:
        copy.wait()
    total = jnp.zeros(sums_own.shape, F32)
    for q in range(depth):
        term = jnp.zeros(sums_own.shape, F32)
        for up in range(1, depth):
            term = jnp.where(lax.rem(row + depth - up, depth) == q, sums_line[up - 1], term)
        total = total + jnp.where(row == q, sums_own[...], term)
    sums_all[place] = total
    mine_all = sums_all.at[place]
    spread_sums = [links.copy(mine_all, mine_all, peer[mask]) for mask in order]
    for copy in spread_sums:
        copy.start()

    x_line.finish(x_sum)
    turn(x_sent, x_sum)
    send_x.begin()
    if depth > 3:
        small_line.phase(2)

    for source, at, to in runs_of(width, half, run):
        in_grad[:, to : to + run] = gate_back[source, :, at : at + run].astype(F32)
    small_line.finish(small_sum)
    turn(small_sent, small_sum)
    send_small.begin()
    for copy in spread_sums:
        copy.wait()
    for source, at, to in runs_of(width, half, run):
        full[:, to : to + run] = sums_all[source, :, at : at + run]
    for source in range(width):
        to = inner_all + source * own
        full[:, to : to + own] = sums_all[source, :, inner : inner + own]
    first = (row * width + place) * own_ch
    base = pl.multiple_of(lax.div(first, 128) * 128, 128)
    view = pltpu.roll(full[:, pl.ds(base, 256)], 256 - lax.rem(first, 128), 1)
    smalls[0:8, :] = view[:, :128]
    smalls[8:16, :] = sum(
        dot(
            sums_all[source, :, inner + 128 :],
            head_places(source, half, plane, group, heads, 0),
            ((1,), (0,)),
            lax.Precision.HIGHEST,
        )
        for source in range(width)
    )
    send_x.end()
    for source, at, to in runs_of(width, half, run):
        in_grad[:, inner_all + to : inner_all + to + run] = x_back[
            source, :, at : at + run
        ].astype(F32)
    send_small.end()
    for source in range(width):
        to = 2 * inner_all + source * own
        in_grad[:, to : to + own] = small_back[source, :, :own].astype(F32)
    for source, at, to in runs_of(width, half, group):
        to = 2 * inner_all + 2 * size + to
        in_grad[:, to : to + group] = small_back[
            source, :, own + at : own + at + group
        ].astype(F32)

    norm_gain = rows_in[0:1, :]

    def store_grad(at, total):
        held = x_own[at].astype(F32)
        inv = lax.rsqrt(jnp.mean(held * held, axis=1, keepdims=True) + EPS)
        hat = held * inv
        d_h = total * norm_gain
        grad = inv * (d_h - hat * jnp.mean(d_h * hat, axis=1, keepdims=True))
        input_grad[at] = (grad + cot_own[at].astype(F32)).astype(BF16)

    loads[8].wait()
    d_plane.finish(store_grad)
    d_plane.drain()
    x_line.drain()
    small_line.drain()


def weights(dims, hbm, vmem, collective):
    depth, width, heads, head_size, size, kernel, own_ch, inner_all = dims
    inner = heads * head_size
    _, rows, model = hbm[1].shape
    tokens = rows * width
    shape = jax.ShapeDtypeStruct
    cols = model // depth
    owned = cols // width
    own = 2 * size // width
    kept = [
        ((rows, model), BF16),
        ((owned, 2 * inner_all + 2 * size + heads * width), F32),
        ((16, 128), F32),
    ]
    return pl.pallas_call(
        functools.partial(weights_kernel, dims),
        out_shape=tuple(shape(*s) for s in kept),
        in_specs=[ANY] * len(hbm) + [INVMEM] * len(vmem),
        out_specs=(INVMEM,) * len(kept),
        scratch_shapes=[pltpu.VMEM(v.shape, v.dtype) for v in (hbm[0], hbm[1], hbm[3])]
        + [
            pltpu.VMEM((tokens, 128), F32),
            pltpu.VMEM((tokens, 128), F32),
            pltpu.VMEM(hbm[6].shape, BF16),
            pltpu.VMEM(hbm[7].shape, BF16),
            pltpu.VMEM((rows, model), BF16),
            pltpu.VMEM((2 * inner + 128, model), BF16),
            pltpu.VMEM((width, rows, 128), BF16),
            pltpu.VMEM((inner, model), F32),
            pltpu.VMEM((128, model), F32),
            pltpu.VMEM((width, rows, model), BF16),
            pltpu.VMEM((rows + 8, 128), F32),
            pltpu.VMEM((8, 128), F32),
        ]
        + plane_buffers(rows, model)
        + line_buffers(depth - 1, (inner, cols))
        + line_buffers(depth - 1, (128, cols))
        + [
            pltpu.VMEM((inner, cols), F32),
            pltpu.VMEM((cols, inner), BF16),
            pltpu.VMEM((128, cols), F32),
            pltpu.VMEM((cols, 128), BF16),
            pltpu.VMEM((width, owned, inner), BF16),
            pltpu.VMEM((width, owned, 128), BF16),
            pltpu.VMEM((8, inner + 256), F32),
            pltpu.VMEM((depth - 1, 8, inner + 256), F32),
            pltpu.VMEM((width, 8, inner + 256), F32),
            pltpu.VMEM((8, inner_all + 2 * size + 256), F32),
            pltpu.SemaphoreType.DMA((88,)),
            pltpu.SemaphoreType.DMA((88,)),
            pltpu.SemaphoreType.DMA((14,)),
        ],
        compiler_params=pltpu.CompilerParams(
            collective_id=collective, has_side_effects=True, vmem_limit_bytes=VMEM_LIMIT
        ),
        name="weights_fused",
    )(*hbm, *vmem)


def fast_body(
    depth,
    width,
    block_input,
    cotangent,
    lengths,
    in_weight,
    out_weight,
    norm_gain,
    gate_gain,
    conv_weight,
    conv_bias,
    dt_bias,
    a_log,
    d_skip,
):
    slots, piece, model = block_input.shape
    heads_all = dt_bias.shape[0]
    out_rows = out_weight.shape[0]
    in_rows = in_weight.shape[0]
    inner_all = out_rows * depth * width
    head_size = inner_all // heads_all
    taps_count = conv_weight.shape[0]
    channels = conv_weight.shape[1] * depth * width
    size = (channels - inner_all) // 2
    heads = heads_all // width
    inner = heads * head_size
    plane = width // 2
    half = depth // 2
    pair_rows = 2 * out_rows
    row, place = lax.axis_index("dp"), lax.axis_index("seq")
    core, chip = lax.rem(place, 2), lax.div(place, 2)
    slot_len = piece * width
    tokens = slots * slot_len

    own_ch = conv_bias.shape[0]
    tokens_dev = slots * piece
    dims = (depth, width, heads, head_size, size, taps_count, own_ch, inner_all)
    (
        normed_all,
        cot_all,
        w_turned,
        w_bc,
        w_out,
        conv_in,
        pre,
        dt_arg,
        gate,
        y,
        states,
        norms,
        taps,
        param_rows,
        w_dt,
    ) = forward(
        dims,
        (
            block_input.reshape(tokens_dev, model),
            cotangent.reshape(tokens_dev, model),
            lengths[None],
            in_weight,
            out_weight,
            norm_gain[None],
            gate_gain[None],
            conv_weight,
            conv_bias[None],
            dt_bias[None],
            a_log[None],
            d_skip[None],
        ),
        2,
    )
    x_own = block_input.reshape(tokens_dev, model)
    (
        d_gate,
        d_x,
        d_arg,
        output,
        gate_back,
        out_grad,
        channel_sums,
        head_sums,
        d_bc,
    ) = reverse(
        dims,
        (cot_all, normed_all, gate, y, pre, conv_in, dt_arg, states, w_out),
        (norms, taps, param_rows, x_own),
        3,
    )
    input_grad, in_grad, smalls = weights(
        dims,
        (
            d_x,
            normed_all,
            w_turned,
            d_gate,
            pre,
            conv_in,
            d_arg,
            w_bc.reshape(2, model, size),
            cot_all,
        ),
        (
            d_bc,
            taps,
            channel_sums,
            head_sums,
            param_rows,
            x_own,
            w_dt,
            gate_back,
        ),
        4,
    )
    norm_grad = jnp.sum(in_grad * in_weight.astype(F32), axis=1) / norm_gain.astype(F32)
    gate_grad = jnp.sum(out_grad * out_weight.astype(F32), axis=1) / gate_gain.astype(F32)
    return (
        output.reshape(slots, piece, model),
        input_grad.reshape(slots, piece, model),
        in_grad,
        out_grad,
        norm_grad,
        gate_grad,
        smalls[:4, :own_ch],
        smalls[4, :own_ch],
        smalls[8, :heads_all],
        smalls[9, :heads_all],
        smalls[10, :heads_all],
    )


def heads_fit(depth, width, arrays):
    block_input, out_weight, dt_bias = arrays[0], arrays[4], arrays[9]
    pair_rows = 2 * out_weight.shape[0]
    head_size = out_weight.shape[0] * depth * width // dt_bias.shape[0]
    return (
        width == 8
        and depth % 2 == 0
        and pair_rows % head_size == 0
        and (depth // 2 * pair_rows) % 128 == 0
        and block_input.shape[1] % CHUNK == 0
        and 2 * head_size == CHUNK
    )


def solution(mesh):
    placed = (
        P("dp", "seq", None),
        P("dp", "seq", None),
        P("dp"),
        P(("dp", "seq"), None),
        P(("dp", "seq"), None),
        P(("dp", "seq")),
        P(("dp", "seq")),
        P(None, ("dp", "seq")),
        P(("dp", "seq")),
        P(),
        P(),
        P(),
    )
    depth, width = mesh.shape["dp"], mesh.shape["seq"]

    def either(*arrays):
        if heads_fit(depth, width, arrays):
            return fast_body(depth, width, *arrays)
        return body(*arrays)

    return jax.shard_map(
        either,
        mesh=mesh,
        in_specs=placed,
        out_specs=(
            P("dp", "seq", None),
            P("dp", "seq", None),
            P(("dp", "seq"), None),
            P(("dp", "seq"), None),
            P(("dp", "seq")),
            P(("dp", "seq")),
            P(None, ("dp", "seq")),
            P(("dp", "seq")),
            P(),
            P(),
            P(),
        ),
        check_vma=False,
    )
```

```python
import functools

import jax
import jax.numpy as jnp
from jax import lax
from jax.experimental import pallas as pl
from jax.experimental.pallas import tpu as pltpu
from jax.sharding import PartitionSpec as P

SLOTS_MB = 1


EPS = 1e-05
HIGH = lax.Precision.HIGHEST


def from_behind(value, axis, steps):
    count = lax.axis_size(axis)
    leading, last = (max(0, -steps), min(count, count - steps))
    return lax.ppermute(value, axis, [(source, source + steps) for source in range(leading, last)])


def carried_in(value, axis, join, neutral, backward):
    count = lax.axis_size(axis)
    place = lax.axis_index(axis)
    ahead = count - 1 - place if backward else place
    gathered = jax.tree.map(
        lambda a, kind: lax.all_gather(a.astype(kind), axis),
        value,
        jax.tree.map(lambda a: jnp.bfloat16 if a.dtype == jnp.float32 else a.dtype, value),
    )
    state = jax.tree.map(lambda a, e: jnp.zeros_like(a) + jnp.asarray(e, a.dtype), value, neutral)

    def one(lap, state):
        source = count - 1 - lap if backward else lap
        return join(
            state,
            jax.tree.map(
                lambda a, own: lax.dynamic_index_in_dim(a, source, 0, False).astype(own.dtype),
                gathered,
                value,
            ),
        )

    return lax.fori_loop(0, ahead, one, state)


def as_sent(value):

    def short(part):
        return part.astype(jnp.bfloat16) if part.dtype == jnp.float32 else part

    return jax.tree.map(short, value)


def link_states(earlier, later):
    return (earlier[0] * later[0], later[0][:, :, None, None] * earlier[1] + later[1])


def silu_slope(values):
    sigma = jax.nn.sigmoid(values)
    return sigma * (1.0 + values * (1.0 - sigma))


def rows_product(left, right):
    return lax.dot_general(
        left, right, (((0,), (0,)), ((), ())), preferred_element_type=jnp.float32
    )


def cols_product(left, right):
    return lax.dot_general(
        left, right, (((1,), (1,)), ((), ())), preferred_element_type=jnp.float32
    )


def add_pair(first, second):
    return first + second


def first_total(stacked):
    return jnp.sum(stacked, axis=0)


def owner_sums(grads):
    lifted = tuple((grad[None] for grad in grads))
    by_data = (
        lax.all_to_all(lifted[0], "dp", split_axis=1, concat_axis=0, tiled=True),
        lax.all_to_all(lifted[1], "dp", split_axis=1, concat_axis=0, tiled=True),
        lax.all_to_all(lifted[2], "dp", split_axis=1, concat_axis=0, tiled=True),
        lax.all_to_all(lifted[3], "dp", split_axis=1, concat_axis=0, tiled=True),
        lax.all_to_all(lifted[4], "dp", split_axis=1, concat_axis=0, tiled=True),
        lax.all_to_all(lifted[5], "dp", split_axis=1, concat_axis=0, tiled=True),
    )
    partial_value = tuple((first_total(stacked)[None] for stacked in by_data))
    by_piece = (
        lax.all_to_all(partial_value[0], "seq", split_axis=1, concat_axis=0, tiled=True),
        lax.all_to_all(partial_value[1], "seq", split_axis=1, concat_axis=0, tiled=True),
        lax.all_to_all(partial_value[2], "seq", split_axis=1, concat_axis=0, tiled=True),
        lax.all_to_all(partial_value[3], "seq", split_axis=1, concat_axis=0, tiled=True),
        lax.all_to_all(partial_value[4], "seq", split_axis=1, concat_axis=0, tiled=True),
        lax.all_to_all(partial_value[5], "seq", split_axis=1, concat_axis=0, tiled=True),
    )
    return tuple((first_total(stacked) for stacked in by_piece))


def forward_pass(slot_in, weights, head_params):
    in_full, out_full, norm_full, gate_full, conv_full, bias_full = weights
    dt_shift, log_rate, skip_gain = head_params
    slot_count, piece_len, model_width = slot_in.shape
    inner_width = out_full.shape[0]
    channels = conv_full.shape[1]
    kernel = conv_full.shape[0]
    head_count = dt_shift.shape[0]
    head_size = inner_width // head_count
    state_size = (channels - inner_width) // 2
    input_f = slot_in.astype(jnp.float32)
    inv_rms = lax.rsqrt(jnp.mean(input_f * input_f, axis=-1, keepdims=True) + EPS)
    normed = (input_f * inv_rms * norm_full.astype(jnp.float32)).astype(jnp.bfloat16)
    projected = jnp.dot(
        normed.reshape(-1, model_width), in_full, preferred_element_type=jnp.float32
    ).reshape(slot_count, piece_len, -1)
    gate_part = projected[..., :inner_width]
    conv_in = projected[..., inner_width : inner_width + channels]
    dt_arg = projected[..., inner_width + channels :] + dt_shift
    rim_rows = from_behind(
        conv_in[:, piece_len - kernel + 1 :].astype(jnp.bfloat16), "seq", 1
    ).astype(jnp.float32)
    extended = jnp.concatenate([rim_rows, conv_in], axis=1)
    conv_taps = conv_full.astype(jnp.float32)
    pre_act = bias_full.astype(jnp.float32) + sum(
        (
            conv_taps[tap_index] * extended[:, tap_index : tap_index + piece_len]
            for tap_index in range(kernel)
        )
    )
    activated = jax.nn.silu(pre_act)
    x_heads = activated[..., :inner_width].reshape(slot_count, piece_len, head_count, head_size)
    b_rows = activated[..., inner_width : inner_width + state_size]
    c_rows = activated[..., inner_width + state_size :]
    dt_vals = jax.nn.softplus(dt_arg)
    decay_rates = -jnp.exp(log_rate)
    log_cum = jnp.cumsum(dt_vals * decay_rates, axis=1)
    log_tot = log_cum[:, -1]
    weights_in = jnp.exp(log_tot[:, None] - log_cum) * dt_vals
    local_state = jnp.einsum(
        "sthp,stn->shpn", weights_in[..., None] * x_heads, b_rows, precision=HIGH
    )
    carry_decay = jnp.exp(log_tot)
    neutral = (jnp.ones_like(carry_decay), jnp.zeros_like(local_state))
    _, start_state = carried_in((carry_decay, local_state), "seq", link_states, neutral, False)
    spots = jnp.arange(piece_len)
    causal = spots[:, None] >= spots[None, :]
    cum_heads = jnp.swapaxes(log_cum, 1, 2)
    gap_vals = jnp.where(causal, cum_heads[..., :, None] - cum_heads[..., None, :], 0.0)
    decay_mat = jnp.where(causal, jnp.exp(gap_vals), 0.0)
    cb_mat = jnp.einsum("stn,sun->stu", c_rows, b_rows, precision=HIGH)
    dt_cols = jnp.swapaxes(dt_vals, 1, 2)[:, :, None, :]
    mixing = decay_mat * cb_mat[:, None] * dt_cols
    y_intra = jnp.einsum("shtu,suhp->sthp", mixing, x_heads, precision=HIGH)
    state_read = jnp.einsum("stn,shpn->sthp", c_rows, start_state, precision=HIGH)
    exp_cum = jnp.exp(log_cum)
    y_heads = y_intra + exp_cum[..., None] * state_read + skip_gain[:, None] * x_heads
    y_flat = y_heads.reshape(slot_count, piece_len, inner_width)
    gate_act = jax.nn.silu(gate_part)
    gated_out = y_flat * gate_act
    inv_gate = lax.rsqrt(jnp.mean(gated_out * gated_out, axis=-1, keepdims=True) + EPS)
    gate_normed = (gated_out * inv_gate * gate_full.astype(jnp.float32)).astype(jnp.bfloat16)
    mixed = jnp.dot(
        gate_normed.reshape(-1, inner_width), out_full, preferred_element_type=jnp.float32
    )
    output = (input_f + mixed.reshape(slot_count, piece_len, model_width)).astype(jnp.bfloat16)
    saved = dict(
        input_f=input_f,
        inv_rms=inv_rms,
        normed=normed,
        gate_part=gate_part,
        dt_arg=dt_arg,
        extended=extended,
        pre_act=pre_act,
        x_heads=x_heads,
        b_rows=b_rows,
        c_rows=c_rows,
        dt_vals=dt_vals,
        log_cum=log_cum,
        log_tot=log_tot,
        weights_in=weights_in,
        carry_decay=carry_decay,
        start_state=start_state,
        decay_mat=decay_mat,
        cb_mat=cb_mat,
        dt_cols=dt_cols,
        mixing=mixing,
        state_read=state_read,
        exp_cum=exp_cum,
        y_flat=y_flat,
        gate_act=gate_act,
        gated_out=gated_out,
        inv_gate=inv_gate,
        gate_normed=gate_normed,
    )
    return (output, saved)


def backward_pass(saved, slot_cot, live, weights, head_params):
    in_full, out_full, norm_full, gate_full, conv_full, bias_full = weights
    dt_shift, log_rate, skip_gain = head_params
    slot_count, piece_len, model_width = slot_cot.shape
    inner_width = out_full.shape[0]
    kernel = conv_full.shape[0]
    x_heads = saved["x_heads"]
    b_rows = saved["b_rows"]
    c_rows = saved["c_rows"]
    dt_vals = saved["dt_vals"]
    log_cum = saved["log_cum"]
    weights_in = saved["weights_in"]
    carry_decay = saved["carry_decay"]
    start_state = saved["start_state"]
    decay_mat = saved["decay_mat"]
    cb_mat = saved["cb_mat"]
    dt_cols = saved["dt_cols"]
    decay_rates = -jnp.exp(log_rate)
    masked_cot = slot_cot * live[..., None].astype(jnp.bfloat16)
    cot_rows = masked_cot.reshape(-1, model_width)
    d_gn = cols_product(cot_rows, out_full).reshape(slot_count, piece_len, inner_width)
    gate_hat = saved["gated_out"] * saved["inv_gate"]
    grad_ggain = jnp.sum(d_gn * gate_hat, axis=(0, 1))
    d_hat = d_gn * gate_full.astype(jnp.float32)
    d_gated = saved["inv_gate"] * (
        d_hat - gate_hat * jnp.mean(d_hat * gate_hat, axis=-1, keepdims=True)
    )
    d_gate_part = d_gated * saved["y_flat"] * silu_slope(saved["gate_part"])
    d_heads = (d_gated * saved["gate_act"]).reshape(x_heads.shape)
    grad_skip = jnp.sum(d_heads * x_heads, axis=(0, 1, 3))
    exp_cum = saved["exp_cum"]
    d_read = d_heads * exp_cum[..., None]
    d_cvals = jnp.einsum("sthp,shpn->stn", d_read, start_state, precision=HIGH)
    d_start = jnp.einsum("sthp,stn->shpn", d_read, c_rows, precision=HIGH)
    d_cum = jnp.sum(d_heads * saved["state_read"], axis=-1) * exp_cum
    d_mixing = jnp.einsum("sthp,suhp->shtu", d_heads, x_heads, precision=HIGH)
    d_x = skip_gain[:, None] * d_heads + jnp.einsum(
        "shtu,sthp->suhp", saved["mixing"], d_heads, precision=HIGH
    )
    d_decay = d_mixing * cb_mat[:, None] * dt_cols
    d_cb = jnp.sum(d_mixing * decay_mat * dt_cols, axis=1)
    d_dt = jnp.swapaxes(jnp.sum(d_mixing * decay_mat * cb_mat[:, None], axis=2), 1, 2)
    spread = d_decay * decay_mat
    d_cum = d_cum + jnp.swapaxes(jnp.sum(spread, axis=3) - jnp.sum(spread, axis=2), 1, 2)
    d_cvals = d_cvals + jnp.einsum("stu,sun->stn", d_cb, b_rows, precision=HIGH)
    d_bvals = jnp.einsum("stu,stn->sun", d_cb, c_rows, precision=HIGH)
    neutral = (jnp.ones_like(carry_decay), jnp.zeros_like(d_start))
    _, later_grad = carried_in((carry_decay, d_start), "seq", link_states, neutral, True)
    d_tot = jnp.sum(later_grad * start_state, axis=(2, 3)) * carry_decay
    grad_proj_b = jnp.einsum("shpn,stn->sthp", later_grad, b_rows, precision=HIGH)
    d_x = d_x + weights_in[..., None] * grad_proj_b
    d_weights = jnp.sum(grad_proj_b * x_heads, axis=-1)
    d_bvals = d_bvals + jnp.einsum(
        "sthp,shpn->stn", weights_in[..., None] * x_heads, later_grad, precision=HIGH
    )
    d_dt = d_dt + d_weights * jnp.exp(saved["log_tot"][:, None] - log_cum)
    through = d_weights * weights_in
    d_tot = d_tot + jnp.sum(through, axis=1)
    last_row = (jnp.arange(piece_len) == piece_len - 1).astype(jnp.float32)
    d_cum = d_cum - through + last_row[None, :, None] * d_tot[:, None, :]
    d_log = lax.cumsum(d_cum, axis=1, reverse=True)
    d_dt = d_dt + d_log * decay_rates
    grad_alog = jnp.sum(d_log * dt_vals, axis=(0, 1)) * decay_rates
    d_arg = d_dt * jax.nn.sigmoid(saved["dt_arg"])
    grad_dtb = jnp.sum(d_arg, axis=(0, 1))
    d_act = jnp.concatenate(
        [d_x.reshape(slot_count, piece_len, inner_width), d_bvals, d_cvals], axis=-1
    )
    d_pre = d_act * silu_slope(saved["pre_act"])
    grad_cbias = jnp.sum(d_pre, axis=(0, 1))
    extended = saved["extended"]
    grad_conv = jnp.stack(
        [
            jnp.sum(d_pre * extended[:, tap_index : tap_index + piece_len], axis=(0, 1))
            for tap_index in range(kernel)
        ]
    )
    conv_taps = conv_full.astype(jnp.float32)
    d_ext = sum(
        (
            jnp.pad(
                conv_taps[tap_index] * d_pre, ((0, 0), (tap_index, kernel - 1 - tap_index), (0, 0))
            )
            for tap_index in range(kernel)
        )
    )
    back_rim = from_behind(as_sent(d_ext[:, : kernel - 1]), "seq", -1)
    d_conv_in = d_ext[:, kernel - 1 :] + jnp.pad(
        back_rim, ((0, 0), (piece_len - kernel + 1, 0), (0, 0))
    )
    d_proj = jnp.concatenate([d_gate_part, d_conv_in, d_arg], axis=-1).astype(jnp.bfloat16)
    d_proj = d_proj.reshape(slot_count * piece_len, -1)
    d_normed = cols_product(d_proj, in_full).reshape(slot_count, piece_len, model_width)
    in_hat = saved["input_f"] * saved["inv_rms"]
    grad_ngain = jnp.sum(d_normed * in_hat, axis=(0, 1))
    d_norm_in = d_normed * norm_full.astype(jnp.float32)
    input_grad = saved["inv_rms"] * (
        d_norm_in - in_hat * jnp.mean(d_norm_in * in_hat, axis=-1, keepdims=True)
    )
    input_grad = input_grad + masked_cot.astype(jnp.float32)
    product_rows = (
        saved["normed"].reshape(-1, model_width),
        d_proj,
        saved["gate_normed"].reshape(-1, inner_width),
        cot_rows,
    )
    small_grads = (grad_ngain, grad_ggain, grad_conv, grad_cbias)
    return (
        input_grad.astype(jnp.bfloat16),
        product_rows,
        small_grads,
        (grad_dtb, grad_alog, grad_skip),
    )


def body(
    block_input,
    cotangent,
    lengths,
    in_weight,
    out_weight,
    norm_gain,
    gate_gain,
    conv_weight,
    conv_bias,
    dt_bias,
    a_log,
    d_skip,
):
    shards = (in_weight, out_weight, norm_gain, gate_gain, conv_weight, conv_bias)
    head_params = (dt_bias, a_log, d_skip)
    piece_len = block_input.shape[1]
    batches = block_input.shape[0] // SLOTS_MB
    positions = lax.axis_index("seq") * piece_len + jnp.arange(piece_len, dtype=jnp.int32)
    held = (
        lax.all_gather(shards[0], ("dp", "seq"), axis=0, tiled=True),
        lax.all_gather(shards[1], ("dp", "seq"), axis=0, tiled=True),
        lax.all_gather(shards[2], ("dp", "seq"), axis=0, tiled=True),
        lax.all_gather(shards[3], ("dp", "seq"), axis=0, tiled=True),
        lax.all_gather(shards[4], ("dp", "seq"), axis=1, tiled=True),
        lax.all_gather(shards[5], ("dp", "seq"), axis=0, tiled=True),
    )
    outputs = []
    input_grads = []
    kept_rows = []
    small_totals = None
    head_totals = None
    for batch_index in range(batches):
        first = batch_index * SLOTS_MB
        slot_in = block_input[first : first + SLOTS_MB]
        slot_cot = cotangent[first : first + SLOTS_MB]
        live = (positions[None, :] < lengths[first : first + SLOTS_MB, None]).astype(jnp.float32)
        output, saved = forward_pass(slot_in, held, head_params)
        input_grad, product_rows, small_grads, head_grads = backward_pass(
            saved, slot_cot, live, held, head_params
        )
        outputs.append(output)
        input_grads.append(input_grad)
        kept_rows.append(product_rows)
        small_totals = (
            small_grads
            if small_totals is None
            else jax.tree.map(add_pair, small_totals, small_grads)
        )
        head_totals = (
            head_grads if head_totals is None else jax.tree.map(add_pair, head_totals, head_grads)
        )
    normed_all = jnp.concatenate([rows[0] for rows in kept_rows], axis=0)
    dproj_all = jnp.concatenate([rows[1] for rows in kept_rows], axis=0)
    gnormed_all = jnp.concatenate([rows[2] for rows in kept_rows], axis=0)
    cot_all = jnp.concatenate([rows[3] for rows in kept_rows], axis=0)
    grad_win = rows_product(normed_all, dproj_all)
    grad_wout = rows_product(gnormed_all, cot_all)
    grad_ngain, grad_ggain, grad_conv, grad_cbias = small_totals
    owned = owner_sums((grad_win, grad_wout, grad_ngain, grad_ggain, grad_conv.T, grad_cbias))
    head_sums = lax.psum(head_totals, ("dp", "seq"))
    return (
        jnp.concatenate(outputs, axis=0),
        jnp.concatenate(input_grads, axis=0),
        owned[0],
        owned[1],
        owned[2],
        owned[3],
        owned[4].T,
        owned[5],
        head_sums[0],
        head_sums[1],
        head_sums[2],
    )


F32 = jnp.float32
BF16 = jnp.bfloat16
MESH_ID = pl.DeviceIdType.MESH
ANY = pl.BlockSpec(memory_space=pl.ANY)
INVMEM = pl.BlockSpec(memory_space=pltpu.VMEM)
VMEM_LIMIT = 63 * 1024 * 1024
CHUNK = 128


def flip(place, bit):
    return place + bit - 2 * bit * lax.rem(lax.div(place, bit), 2)


def flip_all(place, mask):
    for bit in (1, 2, 4):
        if mask & bit:
            place = flip(place, bit)
    return place


class Links:
    def __init__(self, sends, recvs):
        self.sends, self.recvs, self.used = sends, recvs, 0

    def copy(self, source, target, device):
        slot = self.used
        self.used += 1
        return pltpu.make_async_remote_copy(
            src_ref=source,
            dst_ref=target,
            send_sem=self.sends.at[slot],
            recv_sem=self.recvs.at[slot],
            device_id=device,
            device_id_type=MESH_ID,
        )


def greet(devices, conditions=(), between=None):
    barrier = pltpu.get_barrier_semaphore()
    for device in devices:
        pl.semaphore_signal(barrier, inc=1, device_id=device, device_id_type=MESH_ID)
    for condition, device in conditions:

        @pl.when(condition)
        def _():
            pl.semaphore_signal(barrier, inc=1, device_id=device, device_id_type=MESH_ID)

    count = len(devices)
    for condition, _ in conditions:
        count = count + jnp.where(condition, 1, 0)
    if between is not None:
        between()
    pl.semaphore_wait(barrier, count)


def add_rows(target, first, second, step=32):
    def one(number, carry):
        rows = pl.ds(pl.multiple_of(number * step, step), step)
        target[rows] = (first[rows].astype(F32) + second[rows].astype(F32)).astype(target.dtype)
        return carry

    lax.fori_loop(0, target.shape[0] // step, one, 0)


def cast_rows(target, source, step=32):
    def one(number, carry):
        rows = pl.ds(pl.multiple_of(number * step, step), step)
        target[rows] = source[rows].astype(target.dtype)
        return carry

    lax.fori_loop(0, target.shape[0] // step, one, 0)


class LineSum:
    def __init__(
        self, links, depth, row, place, own, valid, up_in, up_out, down_in, down_out, shared=None
    ):
        self.depth, self.row, self.own, self.valid = depth, row, own, valid
        above, below = lax.min(row + 1, depth - 1), lax.max(row - 1, 0)

        def slots(ref, shift):
            return {q: ref.at[q % shared if shared else q - shift] for q in range(shift, depth - 1 + shift)}

        self.up_in, self.up_out = slots(up_in, 1), slots(up_out, 1)
        self.down_in, self.down_out = slots(down_in, 0), slots(down_out, 0)
        self.ups = {
            q: links.copy(self.up_out[q], self.up_in[q], (above, place)) for q in self.up_in
        }
        self.downs = {
            q: links.copy(self.down_out[q], self.down_in[q], (below, place)) for q in self.down_in
        }

    def up(self, q, row):
        @pl.when(self.valid(q) & (self.row == row))
        def _():
            if row == 0:
                cast_rows(self.up_out[q], self.own(q))
            else:
                self.ups[q].wait_recv()
                add_rows(self.up_out[q], self.own(q), self.up_in[q])
            self.ups[q].start()

    def down(self, q, row):
        @pl.when(self.valid(q) & (self.row == row))
        def _():
            if row == self.depth - 1:
                cast_rows(self.down_out[q], self.own(q))
            else:
                self.downs[q].wait_recv()
                add_rows(self.down_out[q], self.own(q), self.down_in[q])
            self.downs[q].start()

    def phase(self, number):
        for row in range(self.depth):
            up_q = self.depth - 1 + row - number
            if row < up_q < self.depth:
                self.up(up_q, row)
            down_q = number - (self.depth - 1 - row)
            if 0 <= down_q < row:
                self.down(down_q, row)

    def finish(self, total):
        depth, row = self.depth, self.row
        for q in range(depth):

            @pl.when(self.valid(q) & (row == q))
            def _():
                if q > 0:
                    self.ups[q].wait_recv()
                if q < depth - 1:
                    self.downs[q].wait_recv()
                if 0 < q < depth - 1:
                    add_rows(total, self.up_in[q], self.down_in[q])
                    add_rows(total, total, self.own(q))
                elif q > 0:
                    add_rows(total, self.own(q), self.up_in[q])
                else:
                    add_rows(total, self.own(q), self.down_in[q])

    def drain(self):
        for q, copy in self.ups.items():
            pl.when(self.valid(q) & (self.row < q))(copy.wait_send)
        for q, copy in self.downs.items():
            pl.when(self.valid(q) & (self.row > q))(copy.wait_send)


class PlaneSum:
    def __init__(self, links, row, place, parts, pair_in, sums, relay_in, last_in):
        self.place, self.parts = place, parts
        self.pair_in, self.sums, self.relay_in, self.last_in = pair_in, sums, relay_in, last_in
        peer = {mask: (row, flip_all(place, mask)) for mask in range(1, 8)}
        self.peer = peer
        rows = last_in.shape[1] // 2
        self.halves = (pl.ds(0, rows), pl.ds(rows, rows))
        self.pair = {
            mask: links.copy(parts.at[peer[mask ^ 1][1]], pair_in.at[mask // 2], peer[1])
            for mask in (6, 2, 4, 0)
        }
        top, low = self.halves
        self.relay4 = links.copy(sums.at[3, top], relay_in.at[0], peer[4])
        self.relay2 = links.copy(sums.at[3, low], relay_in.at[1], peer[2])
        self.last2 = [
            links.copy(sums.at[1, half], last_in.at[0, half], peer[2]) for half in self.halves
        ]
        self.last4 = [
            links.copy(sums.at[2, half], last_in.at[1, half], peer[4]) for half in self.halves
        ]

    def begin(self):
        for copy in self.pair.values():
            copy.start()

    def chip(self, mask):
        index = mask // 2
        self.pair[mask].wait_recv()
        mine = self.parts.at[self.peer[mask][1] if mask else self.place]
        add_rows(self.sums.at[index], mine, self.pair_in.at[index])

    def far(self):
        self.chip(6)
        self.relay4.start()
        self.relay2.start()

    def near(self, mask):
        self.chip(mask)
        if mask:
            (self.last2[1] if mask == 2 else self.last4[0]).start()

    def first(self):
        self.far()
        for mask in (2, 4, 0):
            self.near(mask)

    def second(self):
        top, low = self.halves
        self.relay4.wait_recv()
        add_rows(self.sums.at[1, top], self.sums.at[1, top], self.relay_in.at[0])
        self.last2[0].start()
        self.relay2.wait_recv()
        add_rows(self.sums.at[2, low], self.sums.at[2, low], self.relay_in.at[1])
        self.last4[1].start()

    def finish(self, store):
        for copy in self.last2 + self.last4:
            copy.wait_recv()

        def one(number, carry):
            at = pl.ds(pl.multiple_of(number * 32, 32), 32)
            total = self.last_in[0, at].astype(F32) + self.last_in[1, at].astype(F32)
            store(at, total + self.sums[0, at].astype(F32))
            return carry

        lax.fori_loop(0, self.last_in.shape[1] // 32, one, 0)

    def drain(self):
        for copy in self.pair.values():
            copy.wait_send()
        for copy in [self.relay4, self.relay2] + self.last2 + self.last4:
            copy.wait_send()


def dot(left, right, contract, precision=None):
    return lax.dot_general(
        left, right, (contract, ((), ())), precision=precision, preferred_element_type=F32
    )


def mm(left, right):
    return dot(left, right, ((1,), (0,)))


def mm_t(left, right):
    return dot(left, right, ((1,), (1,)))


def t_mm(left, right):
    return dot(left, right, ((0,), (0,)))


def widen(values, heads, head_size):
    rows = values.shape[0]
    lane = lax.broadcasted_iota(jnp.int32, (rows, 2 * head_size), 1)
    parts = []
    for pair in range(heads // 2):
        low = jnp.broadcast_to(values[:, 2 * pair : 2 * pair + 1], (rows, 2 * head_size))
        high = jnp.broadcast_to(values[:, 2 * pair + 1 : 2 * pair + 2], (rows, 2 * head_size))
        parts.append(jnp.where(lane < head_size, low, high))
    return jnp.concatenate(parts, axis=1)


def head_of_channel(inner, head_size):
    channel = lax.broadcasted_iota(jnp.int32, (inner, 128), 0)
    first = lax.broadcasted_iota(jnp.int32, (inner, 128), 1) * head_size
    return jnp.where((channel >= first) & (channel < first + head_size), 1.0, 0.0)


def sigmoid(values):
    return 0.5 * jnp.tanh(0.5 * values) + 0.5


def in_parts(values, count):
    parts = []
    for _ in range(count):
        parts.append(values.astype(BF16))
        values = values - parts[-1].astype(F32)
    return parts


def softplus(values):
    return jnp.maximum(values, 0.0) + jnp.log1p(jnp.exp(-jnp.abs(values)))


def split_pair(values, head_size):
    lane = lax.broadcasted_iota(jnp.int32, values.shape, 1)
    zero = jnp.zeros_like(values)
    return jnp.where(lane < head_size, values, zero), jnp.where(lane < head_size, zero, values)


def triangles():
    rows = lax.broadcasted_iota(jnp.int32, (CHUNK, CHUNK), 0)
    cols = lax.broadcasted_iota(jnp.int32, (CHUNK, CHUNK), 1)
    return rows >= cols


def triangles_up():
    rows = lax.broadcasted_iota(jnp.int32, (CHUNK, CHUNK), 0)
    cols = lax.broadcasted_iota(jnp.int32, (CHUNK, CHUNK), 1)
    return cols >= rows


def head_decays(cum, cum_t, head, causal):
    gap = cum[:, head : head + 1] - cum_t[head : head + 1, :]
    return jnp.exp(jnp.where(causal, gap, -1e30))


def plane_total(links, sums, landed, peer, count):
    landed[0] = sums[...].T[:count]
    copies = [links.copy(landed.at[0], landed.at[mask], peer[mask]) for mask in peer]
    for copy in copies:
        copy.start()

    def end():
        for copy in copies:
            copy.wait()
        got = [landed[mask] for mask in range(len(peer) + 1)]
        while len(got) > 1:
            got = [got[k] + got[k + 1] for k in range(0, len(got), 2)]
        return got[0]

    return end


def by_column(values):
    return jnp.concatenate([values, jnp.zeros((128 - values.shape[0], CHUNK), F32)], axis=0).T


class Line:
    def __init__(self, links, depth, row, place, blocks, valid=None):
        self.depth, self.row = depth, row
        above, below = lax.min(row + 1, depth - 1), lax.max(row - 1, 0)
        self.steps = []
        for step in range(depth - 1):
            up_sent, up_got = row - step, row - 1 - step
            down_sent, down_got = row + step, row + 1 + step
            ways = []
            for sends, shard, gets, got, device in (
                ((row < depth - 1) & (up_sent >= 0), up_sent, (row > 0) & (up_got >= 0), up_got, above),
                ((row > 0) & (down_sent < depth), down_sent, (row < depth - 1) & (down_got < depth), down_got, below),
            ):
                shard = lax.clamp(0, shard, depth - 1)
                got = lax.clamp(0, got, depth - 1)
                if valid is not None:
                    sends, gets = sends & valid(shard), gets & valid(got)
                copies = [links.copy(block, block, (device, place)) for block in blocks(shard)]
                ways.append((sends, gets, copies))
            self.steps.append(ways)

    def send(self, number):
        for sends, _, copies in self.steps[number]:

            @pl.when(sends)
            def _():
                for copy in copies:
                    copy.start()

    def wait(self, number):
        for _, gets, copies in self.steps[number]:

            @pl.when(gets)
            def _():
                for copy in copies:
                    copy.wait_recv()

    def drain(self):
        for ways in self.steps:
            for sends, _, copies in ways:

                @pl.when(sends)
                def _():
                    for copy in copies:
                        copy.wait_send()


class Pass:
    def __init__(self, links, peer, place, own, everyone, at):
        own = own.at[at]
        rows = own.shape[0] // 2
        mine = everyone.at[place, at]
        from2, from4, far = (everyone.at[peer[mask][1], at] for mask in (2, 4, 6))
        top, low = pl.ds(0, rows), pl.ds(rows, rows)
        self.kept = None
        self.to2 = links.copy(own, mine, peer[2])
        self.to4 = links.copy(own, mine, peer[4])
        self.to1 = links.copy(own, mine, peer[1])
        self.relay4 = links.copy(from2.at[top], from2.at[top], peer[4])
        self.relay2 = links.copy(from4.at[low], from4.at[low], peer[2])
        self.pair2 = links.copy(from2, from2, peer[1])
        self.pair4 = links.copy(from4, from4, peer[1])
        self.pair6 = links.copy(far.at[top], far.at[top], peer[1])
        self.pair7 = links.copy(far.at[low], far.at[low], peer[1])

    def first(self):
        self.to2.start()
        self.to4.start()
        self.to1.start()

    def relay(self):
        self.to2.wait_recv()
        self.relay4.start()
        self.to4.wait_recv()
        self.relay2.start()
        self.pair2.start()
        self.pair4.start()

    def last(self):
        self.relay4.wait_recv()
        self.pair6.start()
        self.relay2.wait_recv()
        self.pair7.start()

    def end(self):
        for copy in (self.to1, self.pair2, self.pair4, self.pair6, self.pair7):
            copy.wait_recv()

    def drain(self):
        for copy in (
            self.to2,
            self.to4,
            self.to1,
            self.relay4,
            self.relay2,
            self.pair2,
            self.pair4,
            self.pair6,
            self.pair7,
        ):
            copy.wait_send()


def lay_out(pieces, row, count):
    tiles = [None] * -(-count * len(pieces) // 128)
    for index, piece in enumerate(pieces):
        tile, shift = divmod(index * count, 128)
        moved = pltpu.roll(piece, shift, 1) if shift else piece
        lane = lax.broadcasted_iota(jnp.int32, piece.shape, 1)
        parts = [(tile, jnp.where((lane >= shift) & (lane < shift + count), moved, 0.0))]
        if shift + count > 128:
            parts.append((tile + 1, jnp.where(lane < shift + count - 128, moved, 0.0)))
        for at, part in parts:
            tiles[at] = part if tiles[at] is None else tiles[at] + part
    return tiles


def channel_windows(ref, place, plane, half, run):
    core, chip = lax.rem(place, 2), lax.div(place, 2)
    parts = []
    for j in range(half):
        start = ((core * half + j) * plane + chip) * run
        base = pl.multiple_of(lax.div(start, 128) * 128, 128)
        window = ref[:, pl.ds(base, run + 64)]
        moved = pltpu.roll(window, run, 1)
        parts.append(jnp.where(lax.rem(start, 128) == 0, window, moved)[:, :run])
    return jnp.concatenate(parts, axis=1)


def head_choice(place, plane, half, group, heads):
    core, chip = lax.rem(place, 2), lax.div(place, 2)
    head = lax.broadcasted_iota(jnp.int32, (128, 128), 0)
    lane = lax.broadcasted_iota(jnp.int32, (128, 128), 1)
    part = sum(((lane >= j * group).astype(jnp.int32) for j in range(1, half)), jnp.zeros_like(lane))
    chosen = ((core * half + part) * plane + chip) * group + lane - part * group
    return jnp.where((head == chosen) & (lane < heads), 1.0, 0.0)


def forward_kernel(
    dims,
    x_own,
    cot_in,
    lengths,
    in_weight,
    wo_own,
    norm_in,
    gate_in,
    conv_w_in,
    conv_b_in,
    dt_bias_in,
    a_log_in,
    d_skip_in,
    normed_out,
    cot_out,
    turned_out,
    wb_out,
    wo_out,
    conv_out,
    pre_out,
    dt_out,
    gate_out,
    y_out,
    states_out,
    norms_out,
    taps_out,
    rows_out,
    w_dt_out,
    x_all,
    normed_all,
    cot_all,
    wg,
    wx,
    wb_far,
    wo,
    packs,
    dt_got,
    turned,
    conv_in,
    pre_all,
    dt_all,
    gate_all,
    y_all,
    states,
    ext,
    state,
    full,
    sums,
    sums_in,
    cot_own,
    wg_send,
    wx_send,
    pack,
    dt_own,
    dt_pack,
    dt_send,
    head_params,
    sends,
    recvs,
    locals_,
    stores,
):
    depth, width, heads, head_size, size, kernel, own_ch, inner_all = dims
    half, plane = depth // 2, width // 2
    inner = heads * head_size
    run = inner // half
    model = x_own.shape[1]
    piece = x_own.shape[0] // 2
    rows = 2 * piece
    slots = 2
    blocks = slots * width // 2
    row, place = lax.axis_index("dp"), lax.axis_index("seq")
    core = lax.rem(place, 2)
    links = Links(sends, recvs)
    peer = {mask: (row, flip_all(place, mask)) for mask in range(1, width)}
    line_peers = [(lax.rem(row + up, depth), place) for up in range(1, depth)]
    in_rows = in_weight.shape[0]
    bc_cols = 2 * inner_all

    def prepare():
        for target, at, to in runs_of(width, half, run):
            wx_send[target, :, at : at + run] = in_weight[:, inner_all + to : inner_all + to + run]
        for target in range(width):
            first = bc_cols + target % 2 * size
            wx_send[target, :, inner:] = in_weight[:, first : first + size]

    greet([peer[mask] for mask in range(1, width)] + line_peers, between=prepare)
    kept = [
        pltpu.make_async_copy(wx_send.at[place], wx.at[row, place], locals_.at[0]),
        pltpu.make_async_copy(dt_send.at[place], dt_got.at[place], locals_.at[1]),
        pltpu.make_async_copy(wg_send.at[place], wg.at[row, place], locals_.at[2]),
        pltpu.make_async_copy(x_own, x_all.at[place], locals_.at[3]),
        pltpu.make_async_copy(cot_own, cot_all.at[place], locals_.at[4]),
        pltpu.make_async_copy(pack, packs.at[row, place], locals_.at[5]),
    ]
    for number in (0, 3):
        kept[number].start()

    out_home = lax.div(row, half) == core
    out_block = wo.at[lax.rem(row, half), core]
    out_kept = pltpu.make_async_copy(wo_own, out_block, locals_.at[6])
    out_pair = links.copy(wo_own, out_block, peer[1])
    order = (6, 2, 4, 7, 3, 5, 1)
    plane_x, plane_g = [], []
    for mask in order:
        target = peer[mask][1]
        plane_x.append(links.copy(wx_send.at[target], wx.at[row, place], peer[mask]))
        plane_g.append(links.copy(wg_send.at[target], wg.at[row, place], peer[mask]))
    for copy in plane_x:
        copy.start()
    pl.when(out_home)(out_kept.start)
    pl.when(jnp.logical_not(out_home))(out_pair.start)
    slot_rows = [pl.ds(slot * piece, piece) for slot in range(slots)]
    x_passes = [Pass(links, peer, place, x_own, x_all, at) for at in slot_rows]
    cot_passes = [Pass(links, peer, place, cot_own, cot_all, at) for at in slot_rows]
    x_passes[0].first()

    dt_own[...] = jnp.zeros_like(dt_own)
    last = in_weight.shape[1]
    dt_own[:, 0 : last - bc_cols - 2 * size] = in_weight[:, bc_cols + 2 * size : last]
    dt_pack[row] = dt_own[...]
    lines = [conv_w_in[...], conv_b_in[...], gate_in[...], norm_in[...]]
    small_rows = jnp.concatenate(
        [jnp.pad(v.astype(F32), ((0, 0), (0, 128 - v.shape[1]))) for v in lines]
        + [jnp.zeros((16 - sum(v.shape[0] for v in lines), 128), F32)],
        axis=0,
    )
    pack[...] = small_rows.astype(BF16)
    pack_line = [links.copy(pack, packs.at[row, place], device) for device in line_peers]
    pack_line += [
        links.copy(dt_own, dt_pack.at[row], device) for device in line_peers
    ]
    for copy in pack_line:
        copy.start()
    kept[5].start()
    head_params[...] = jnp.zeros_like(head_params)
    for k, v in enumerate((dt_bias_in, a_log_in, d_skip_in)):
        head_params[k : k + 1, 0 : v.shape[1]] = v[...]
    for target, at, to in runs_of(width, half, run):
        wg_send[target, :, at : at + run] = in_weight[:, to : to + run]
    kept[2].start()
    token = lax.broadcasted_iota(jnp.int32, (piece, model), 0) + place * piece
    for slot in range(slots):
        live = token < lengths[0:1, slot : slot + 1]
        part = slice(slot * piece, (slot + 1) * piece)
        cot_own[part, :] = jnp.where(live, cot_in[part, :].astype(F32), 0.0).astype(BF16)
    kept[4].start()
    out_line = Line(
        links,
        depth,
        row,
        place,
        lambda shard: [wo.at[lax.rem(shard, half)]],
        lambda shard: lax.div(shard, half) == core,
    )
    x_lines = [
        Line(links, depth, row, place, lambda shard, k=k: [wx.at[shard, pl.ds(k, width // 2)]])
        for k in (0, width // 2)
    ]
    gate_line = Line(links, depth, row, place, lambda shard: [wg.at[shard]])

    pl.when(out_home)(out_kept.wait)
    pl.when(out_home)(out_pair.wait_recv)
    out_line.send(0)
    kept[0].wait()
    for copy in plane_x:
        copy.wait_recv()
    for line in x_lines:
        line.send(0)
    x_passes[1].first()
    kept[5].wait()
    for copy in pack_line:
        copy.wait_recv()
    targets = jnp.concatenate(
        [head_choice(target, plane, half, run // head_size, heads)[:, :16] for target in range(width)],
        axis=1,
    ).astype(BF16)
    dt_rows = dot(targets, dt_pack[...].reshape(depth * in_rows, 128), ((0,), (1,)))
    dt_send[...] = jnp.zeros_like(dt_send)
    dt_send[:, :, 0 : depth * in_rows] = dt_rows.astype(BF16).reshape(width, 16, depth * in_rows)
    kept[1].start()
    mine = packs.at[:, place]
    pack_plane = [links.copy(mine, mine, peer[mask]) for mask in order]
    pack_plane += [
        links.copy(dt_send.at[peer[mask][1]], dt_got.at[place], peer[mask]) for mask in order
    ]
    for copy in pack_plane:
        copy.start()
    x_passes[0].relay()
    for copy in plane_g:
        copy.start()
    for line in x_lines:
        line.wait(0)
        if depth > 2:
            line.send(1)
    x_passes[0].last()
    x_passes[1].relay()
    cot_passes[0].first()

    def normalise(index, carry):
        for part in range(2):
            held = x_all[index, part * piece : (part + 1) * piece, :].astype(F32)
            inv = lax.rsqrt(jnp.mean(held * held, axis=1, keepdims=True) + EPS)
            normed_all[index, part * piece : (part + 1) * piece, :] = (
                held * inv * rows_out[0:1, :]
            ).astype(BF16)
        return carry

    for line in x_lines:
        if depth > 2:
            line.wait(1)
        if depth > 3:
            line.send(2)
    x_passes[1].last()
    cot_passes[1].first()
    kept[1].wait()
    for copy in pack_plane:
        copy.wait_recv()

    small = [
        packs[z, s].astype(F32)[:8]
        for z in range(depth)
        for s in range(width)
    ]
    choice = head_choice(place, plane, half, run // head_size, heads)
    tap_tiles = lay_out(small, 0, own_ch)
    for at, tile in enumerate(tap_tiles):
        full[:, at * 128 : (at + 1) * 128] = tile
    taps_out[:, :inner] = channel_windows(full, place, plane, half, run)
    taps_out[:, inner:] = full[:, inner_all : inner_all + 2 * size]
    gate_tiles = lay_out(small, 5, inner_all // (depth * width))
    for at, tile in enumerate(gate_tiles):
        full[:, at * 128 : (at + 1) * 128] = tile
    gate_gain = channel_windows(full, place, plane, half, run)[5:6]
    norm_tiles = lay_out(small, 6, model // (depth * width))
    norm_gain = jnp.concatenate([tile[6:7] for tile in norm_tiles], axis=1)
    chosen = dot(head_params[...], choice, ((1,), (0,)), lax.Precision.HIGHEST)
    lane = lax.broadcasted_iota(jnp.int32, (1, 128), 1)
    rates = jnp.where(lane < heads, -jnp.exp(chosen[1:2]), 0.0)
    skip = widen(chosen[2:3], heads, head_size)
    dt_tiles = lay_out(
        [
            pltpu.roll(dt_got[s].astype(F32), 256 - z * in_rows, 1)[:, :128]
            if z
            else dt_got[s].astype(F32)[:, :128]
            for z in range(depth)
            for s in range(width)
        ],
        0,
        in_rows,
    )
    w_dt_out[...] = jnp.zeros_like(w_dt_out)
    w_dt_out[0:16, :] = jnp.concatenate(dt_tiles, axis=1).astype(BF16)
    rows_out[...] = jnp.zeros_like(rows_out)
    rows_out[0:1, :] = norm_gain
    rows_out[1:2, :inner] = gate_gain
    rows_out[2:3, :inner] = skip
    rows_out[3:4, :128] = chosen[0:1]
    rows_out[4:5, :128] = rates

    for copy in plane_g:
        copy.wait_recv()
    kept[2].wait()
    if depth > 3:
        x_lines[0].wait(2)
    gate_line.send(0)
    if depth > 3:
        x_lines[1].wait(2)
    near_bc = wx.at[:, :, :, pl.ds(inner, size)]
    pair_bc = links.copy(near_bc, wb_far, peer[1])
    pair_bc.start()
    for each in x_passes:
        each.end()
    kept[3].wait()
    lax.fori_loop(0, width, normalise, 0)
    saves = [pltpu.make_async_copy(normed_all, normed_out, locals_.at[7])]
    saves[0].start()
    pair_bc.wait_recv()

    causal = triangles()
    ones_three = jnp.concatenate([causal.astype(BF16)] * 3, axis=1)

    def stored(index):
        at = pl.ds(pl.multiple_of(index * rows, rows), rows)
        pairs = [
            (conv_in.at[at], conv_out.at[at]),
            (pre_all.at[at], pre_out.at[at]),
            (dt_all.at[at], dt_out.at[at]),
            (y_all.at[at], y_out.at[at]),
            (
                states.at[pl.ds(index * (rows // CHUNK), rows // CHUNK)],
                states_out.at[pl.ds(index * (rows // CHUNK), rows // CHUNK)],
            ),
        ]
        return [
            pltpu.make_async_copy(source, target, stores.at[k, index])
            for k, (source, target) in enumerate(pairs)
        ]

    per_slot = blocks // slots

    def scan_block(index, carry):
        slot, block = lax.div(index, per_slot), lax.rem(index, per_slot)
        at = pl.multiple_of(index * rows, rows)

        @pl.when(block == 0)
        def _():
            ext[0:8, :] = jnp.zeros((8, ext.shape[1]), F32)
            state[...] = jnp.zeros_like(state)

        tokens = normed_all[
            pl.ds(2 * block, 2), pl.ds(pl.multiple_of(slot * piece, piece), piece), :
        ].reshape(rows, model)
        mine = mm(tokens, wx[...].reshape(model, inner + size))
        ext[8:, :inner] = mine[:, :inner]
        ext[8:, pl.ds(pl.multiple_of(inner + core * size, 128), size)] = mine[:, inner:]
        ext[8:, pl.ds(pl.multiple_of(inner + (1 - core) * size, 128), size)] = mm(
            tokens, wb_far[...].reshape(model, size)
        )
        dt_arg = mm_t(tokens, w_dt_out[...]) + rows_out[3:4, :128]
        dt_all[pl.ds(at, rows), :] = dt_arg
        pre = taps_out[kernel : kernel + 1, :] + sum(
            taps_out[k : k + 1, :] * ext[9 - kernel + k : 9 - kernel + k + rows, :]
            for k in range(kernel)
        )
        conv_in[pl.ds(at, rows), :] = ext[8:, :]
        ext[0:8, :] = ext[rows : rows + 8, :]
        pre_all[pl.ds(at, rows), :] = pre
        act = pre * sigmoid(pre)
        dt_block = softplus(dt_arg)
        steps_block = dt_block * rows_out[4:5, :128]
        subs = rows // CHUNK
        parts = [slice(sub * CHUNK, (sub + 1) * CHUNK) for sub in range(subs)]
        x = act[:, :inner]
        b = act[:, inner : inner + size].astype(BF16)
        c = act[:, inner + size :].astype(BF16)
        cums = [
            mm(ones_three, jnp.concatenate(in_parts(steps_block[part], 3), axis=0))
            for part in parts
        ]
        lasts = [cum[CHUNK - 1 : CHUNK, :] for cum in cums]
        x_dt = x * widen(dt_block, heads, head_size)
        x_dt16 = x_dt.astype(BF16)
        cum_wide = widen(jnp.exp(jnp.concatenate(cums, axis=0)), heads, head_size)
        out_wide = widen(
            jnp.exp(jnp.concatenate([last - cum for last, cum in zip(lasts, cums)], axis=0)),
            heads,
            head_size,
        )
        weighted = (x_dt * out_wide).astype(BF16)
        near, read = [], []
        for sub, part in enumerate(parts):
            cum_t = cums[sub].T
            cb = mm_t(c[part], b[part])
            pieces = []
            for pair in range(heads // 2):
                lanes = slice(2 * pair * head_size, 2 * (pair + 1) * head_size)
                mixing = jnp.concatenate(
                    [
                        (head_decays(cums[sub], cum_t, 2 * pair + k, causal) * cb).astype(BF16)
                        for k in range(2)
                    ],
                    axis=1,
                )
                pieces.append(
                    mm(
                        mixing,
                        jnp.concatenate(split_pair(x_dt16[part, lanes], head_size), axis=0),
                    )
                )
            near.append(jnp.concatenate(pieces, axis=1))
        for sub, part in enumerate(parts):
            held = state[...]
            held16 = held.astype(BF16)
            states[index * subs + sub] = held16
            read.append(mm(c[part], held16))
            state[...] = held * widen(jnp.exp(lasts[sub]), heads, head_size) + t_mm(
                b[part], weighted[part]
            )
        y_all[pl.ds(at, rows), :] = (
            jnp.concatenate(near, axis=0)
            + jnp.concatenate(read, axis=0) * cum_wide
            + rows_out[2:3, :inner] * x
        )
        for copy in stored(index):
            copy.start()

        @pl.when(index == 1)
        def _():
            gate_line.wait(0)
            gate_line.send(1) if depth > 2 else None
            out_line.wait(0)
            out_line.send(1) if depth > 2 else None

        @pl.when(index == 2)
        def _():
            cot_passes[0].relay()
            cot_passes[1].relay()

        @pl.when(index == 4)
        def _():
            gate_line.wait(1) if depth > 2 else None
            gate_line.send(2) if depth > 3 else None
            out_line.wait(1) if depth > 2 else None
            out_line.send(2) if depth > 3 else None

        @pl.when(index == 5)
        def _():
            cot_passes[0].last()
            cot_passes[1].last()

        @pl.when(index == 6)
        def _():
            gate_line.wait(2) if depth > 3 else None

        return carry

    lax.fori_loop(0, blocks, scan_block, 0)

    chunk_lane = lax.broadcasted_iota(jnp.int32, (CHUNK, 128), 1)
    sums[...] = jnp.zeros_like(sums)

    def gate_block(index, carry):
        slot, block = lax.div(index, per_slot), lax.rem(index, per_slot)
        at = pl.multiple_of(index * rows, rows)
        tokens = normed_all[
            pl.ds(2 * block, 2), pl.ds(pl.multiple_of(slot * piece, piece), piece), :
        ].reshape(rows, model)
        gate = mm(tokens, wg[...].reshape(model, inner))
        gate_all[pl.ds(at, rows), :] = gate
        gated = y_all[pl.ds(at, rows), :] * (gate * sigmoid(gate))
        for sub in range(rows // CHUNK):
            part = gated[sub * CHUNK : (sub + 1) * CHUNK]
            total = jnp.sum(part * part, axis=1, keepdims=True)
            sums[...] = jnp.where(chunk_lane == index * (rows // CHUNK) + sub, total, sums[...])
        return carry

    lax.fori_loop(0, blocks, gate_block, 0)
    squares = plane_total(links, sums, sums_in, peer, 2 * blocks)
    save_gate = pltpu.make_async_copy(gate_all, gate_out, locals_.at[8])
    save_gate.start()
    wg_flat, wx_flat = wg[...].reshape(model, inner), wx[...].reshape(model, inner + size)
    for at in range(0, model, 128):
        turned[:inner, at : at + 128] = wg_flat[at : at + 128, :].T
        turned[inner:, at : at + 128] = wx_flat[at : at + 128, :inner].T
    save_weights = [
        pltpu.make_async_copy(source, target, locals_.at[10 + k])
        for k, (source, target) in enumerate(
            (
                (turned, turned_out),
                (near_bc, wb_out.at[core]),
                (wb_far, wb_out.at[1 - core]),
                (wo, wo_out),
            )
        )
    ]
    for copy in save_weights[:3]:
        copy.start()
    kept[4].wait()
    save_cot = [
        pltpu.make_async_copy(cot_all.at[:, at], cot_out.at[:, at], locals_.at[9 + 5 * k])
        for k, at in enumerate(slot_rows)
    ]
    for each, copy in zip(cot_passes, save_cot):
        each.end()
        copy.start()
    if depth > 3:
        out_line.wait(2)
    save_weights[3].start()
    inv_gate = lax.rsqrt(squares() / inner_all + EPS)
    norms_out[...] = by_column(inv_gate)

    for copies in (plane_x, plane_g, pack_line, pack_plane, [pair_bc]):
        for copy in copies:
            copy.wait_send()
    pl.when(jnp.logical_not(out_home))(out_pair.wait_send)
    for line in [out_line, gate_line] + x_lines:
        line.drain()
    for each in x_passes + cot_passes:
        each.drain()
    for copy in saves + [save_gate] + save_cot + save_weights:
        copy.wait()

    def stores_end(index, carry):
        for copy in stored(index):
            copy.wait()
        return carry

    lax.fori_loop(0, blocks, stores_end, 0)


def forward(dims, arrays, collective):
    depth, width, heads, head_size, size, kernel, own_ch, inner_all = dims
    inner = heads * head_size
    x_own, _, _, in_weight, wo_own = arrays[:5]
    rows, model = x_own.shape
    in_rows = in_weight.shape[0]
    tokens = rows * width
    wide = inner + 2 * size
    shape = jax.ShapeDtypeStruct
    chunks = tokens // CHUNK
    weights = [
        ((depth, width, in_rows, inner), BF16),
        ((depth, width, in_rows, inner + size), BF16),
        ((depth, width, in_rows, size), BF16),
        ((depth // 2, 2) + wo_own.shape, BF16),
    ]
    passed = [
        ((2 * inner, model), BF16),
        ((2, depth, width, in_rows, size), BF16),
        ((depth // 2, 2) + wo_own.shape, BF16),
    ]
    kept = [
        ((tokens, wide), F32),
        ((tokens, wide), F32),
        ((tokens, 128), F32),
        ((tokens, inner), F32),
        ((tokens, inner), F32),
        ((chunks, size, inner), BF16),
    ]
    in_hbm = [((width, rows, model), BF16)] * 2 + passed + kept
    in_vmem = [((CHUNK, 128), F32), ((8, wide), F32), ((8, model), F32), ((128, model), BF16)]
    return pl.pallas_call(
        functools.partial(forward_kernel, dims),
        out_shape=tuple(shape(*s) for s in in_hbm + in_vmem),
        in_specs=[INVMEM] * len(arrays),
        out_specs=(ANY,) * len(in_hbm) + (INVMEM,) * len(in_vmem),
        scratch_shapes=[pltpu.VMEM((width, rows, model), BF16)] * 3
        + [pltpu.VMEM(*s) for s in weights]
        + [
            pltpu.VMEM((depth, width, 16, 128), BF16),
            pltpu.VMEM((width, 16, 256), BF16),
            pltpu.VMEM((2 * inner, model), BF16),
        ]
        + [pltpu.VMEM(*s) for s in kept]
        + [
            pltpu.VMEM((rows + 8, wide), F32),
            pltpu.VMEM((size, inner), F32),
            pltpu.VMEM((8, -(-own_ch * depth * width // 128) * 128), F32),
            pltpu.VMEM((CHUNK, 128), F32),
            pltpu.VMEM((width, chunks, 128), F32),
            pltpu.VMEM((rows, model), BF16),
            pltpu.VMEM((width, in_rows, inner), BF16),
            pltpu.VMEM((width, in_rows, inner + size), BF16),
            pltpu.VMEM((16, 128), BF16),
            pltpu.VMEM((in_rows, 128), BF16),
            pltpu.VMEM((depth, in_rows, 128), BF16),
            pltpu.VMEM((width, 16, 256), BF16),
            pltpu.VMEM((8, 128), F32),
            pltpu.SemaphoreType.DMA((160,)),
            pltpu.SemaphoreType.DMA((160,)),
            pltpu.SemaphoreType.DMA((16,)),
            pltpu.SemaphoreType.DMA((5, tokens // rows)),
        ],
        compiler_params=pltpu.CompilerParams(
            collective_id=collective, has_side_effects=True, vmem_limit_bytes=VMEM_LIMIT
        ),
        name="forward_fused",
    )(*arrays)


class PlaneRows:
    def __init__(self, links, row, place, parts, landed, at, local):
        mine = landed.at[place, :, at]
        peers = [(row, flip_all(place, mask)) for mask in (6, 7, 2, 3, 4, 5, 1)]
        self.copies = [links.copy(parts.at[peer[1], :, at], mine, peer) for peer in peers]
        self.kept = pltpu.make_async_copy(parts.at[place, :, at], mine, local)

    def begin(self):
        for copy in self.copies:
            copy.start()
        self.kept.start()

    def end(self):
        self.kept.wait()
        for copy in self.copies:
            copy.wait()


class SendBack:
    def __init__(self, links, row, place, sent, back, local):
        self.rows = back.shape[1]
        self.sent, self.back, self.place = sent, back, place
        mine = back.at[place]
        self.copies = [
            links.copy(self.block((row, flip_all(place, mask))[1]), mine, (row, flip_all(place, mask)))
            for mask in (6, 2, 4, 7, 3, 5, 1)
        ]
        self.kept = pltpu.make_async_copy(self.block(place), mine, local)

    def block(self, target):
        return self.sent.at[pl.ds(pl.multiple_of(target * self.rows, self.rows), self.rows)]

    def begin(self):
        for copy in self.copies:
            copy.start()
        self.kept.start()

    def end(self):
        self.kept.wait()
        for copy in self.copies:
            copy.wait()


def turn(target, source):
    for at in range(0, source.shape[0], 128):
        target[:, at : at + 128] = source[at : at + 128, :].T.astype(target.dtype)


def reverse_kernel(
    dims,
    cot_hbm,
    normed_hbm,
    gate_hbm,
    y_hbm,
    pre_hbm,
    conv_hbm,
    dt_hbm,
    states_hbm,
    wo_hbm,
    norms,
    taps,
    rows_in,
    x_own,
    d_gate_hbm,
    d_x_hbm,
    d_arg_hbm,
    output,
    gate_back,
    out_grad,
    channel_sums,
    head_sums,
    bc_landed,
    cot_all,
    normed_all,
    gate_all,
    y_all,
    d_y_all,
    wo,
    d_gate,
    d_x_all,
    d_arg_all,
    d_bc,
    g_out,
    g_gate,
    pre_two,
    conv_two,
    dt_two,
    states_two,
    later,
    d_ext,
    o_pair,
    o_sums,
    o_relay,
    o_last,
    out_up_in,
    out_up_out,
    out_down_in,
    out_down_out,
    gate_up_in,
    gate_up_out,
    gate_down_in,
    gate_down_out,
    out_sum,
    out_far,
    gate_sum,
    gate_sent,
    means,
    sums_in,
    sends,
    recvs,
    locals_,
    streams,
):
    depth, width, heads, head_size, size, kernel, own_ch, inner_all = dims
    half = depth // 2
    inner = heads * head_size
    model = cot_all.shape[2]
    piece = cot_all.shape[1] // 2
    rows = 2 * piece
    slots = 2
    blocks = slots * width // 2
    per_slot = blocks // slots
    subs = rows // CHUNK
    row, place = lax.axis_index("dp"), lax.axis_index("seq")
    core = lax.rem(place, 2)
    links = Links(sends, recvs)
    above, below = lax.min(row + 1, depth - 1), lax.max(row - 1, 0)
    peer = {mask: (row, flip_all(place, mask)) for mask in range(1, width)}

    loads = [
        pltpu.make_async_copy(source, target, locals_.at[k])
        for k, (source, target) in enumerate(
            (
                (y_hbm, y_all),
                (gate_hbm, gate_all),
                (cot_hbm, cot_all),
                (wo_hbm, wo),
                (normed_hbm, normed_all),
            )
        )
    ]
    for copy in loads:
        copy.start()

    def place_of(number):
        slot = lax.div(number, per_slot)
        return slot, per_slot - 1 - lax.rem(number, per_slot)

    def fetch(number):
        slot, block = place_of(number)
        index = slot * per_slot + block
        at = pl.ds(pl.multiple_of(index * rows, rows), rows)
        buffer = lax.rem(number, 2)
        pairs = (
            (pre_hbm.at[at], pre_two.at[buffer]),
            (conv_hbm.at[at, pl.ds(0, inner)], conv_two.at[buffer]),
            (dt_hbm.at[at], dt_two.at[buffer]),
            (states_hbm.at[pl.ds(index * subs, subs)], states_two.at[buffer]),
        )
        return [
            pltpu.make_async_copy(source, target, streams.at[buffer, k])
            for k, (source, target) in enumerate(pairs)
        ]

    for copy in fetch(0):
        copy.start()
    greet(
        [peer[mask] for mask in range(1, width)],
        [(row < depth - 1, (above, place)), (row > 0, (below, place))],
    )

    out_line = LineSum(
        links,
        depth,
        row,
        place,
        lambda q: g_out.at[pl.ds((q % half) * (inner // half), inner // half)],
        lambda q: core == q // half,
        out_up_in,
        out_up_out,
        out_down_in,
        out_down_out,
        half,
    )
    cols = model // depth
    gate_line = LineSum(
        links,
        depth,
        row,
        place,
        lambda q: g_gate.at[:, pl.ds(q * cols, cols)],
        lambda q: row >= 0,
        gate_up_in,
        gate_up_out,
        gate_down_in,
        gate_down_out,
    )
    o_plane = PlaneSum(links, row, place, cot_all, o_pair, o_sums, o_relay, o_last)
    send_gate = SendBack(links, row, place, gate_sent, gate_back, locals_.at[6])

    chunk_lane = lax.broadcasted_iota(jnp.int32, (CHUNK, 128), 1)

    def column(ref, index):
        parts = [
            jnp.sum(
                jnp.where(chunk_lane == index * subs + sub, ref[...], 0.0),
                axis=1,
                keepdims=True,
            )
            for sub in range(subs)
        ]
        return jnp.concatenate(parts, axis=0)

    def tokens_of(ref, index):
        slot, block = lax.div(index, per_slot), lax.rem(index, per_slot)
        return ref.at[pl.ds(2 * block, 2), pl.ds(pl.multiple_of(slot * piece, piece), piece), :]

    gate_gain = rows_in[1:2, :inner]
    skip = rows_in[2:3, :inner]

    def normed_block(index, carry):
        at = pl.ds(pl.multiple_of(index * rows, rows), rows)
        gate = gate_all[at, :]
        hat = y_all[at, :] * (gate * sigmoid(gate)) * column(norms, index)
        tokens_of(d_gate, index)[...] = (
            (hat * gate_gain).astype(BF16).reshape(2, piece, inner)
        )
        return carry

    loads[0].wait()
    loads[1].wait()
    lax.fori_loop(0, blocks, normed_block, 0)

    everything = slots * width * piece

    def out_grad_tile(number, carry):
        at = pl.ds(pl.multiple_of(number * 128, 128), 128)
        left = d_gate[:, :, at].reshape(everything, 128)
        g_out[at, :] = t_mm(left, cot_all[...].reshape(everything, model))
        return carry

    loads[2].wait()
    lax.fori_loop(0, inner // 128, out_grad_tile, 0)
    out_line.phase(0)

    def cot_block(index, carry):
        at = pl.ds(pl.multiple_of(index * rows, rows), rows)
        tokens = tokens_of(cot_all, index)[...].reshape(rows, model)
        dgn = mm_t(tokens, wo[...].reshape(inner, model))
        d_y_all[at, :] = dgn
        gate = gate_all[at, :]
        cross = dgn * gate_gain * y_all[at, :] * (gate * sigmoid(gate))
        for sub in range(subs):
            part = cross[sub * CHUNK : (sub + 1) * CHUNK]
            total = jnp.sum(part, axis=1, keepdims=True)
            means[...] = jnp.where(chunk_lane == index * subs + sub, total, means[...])
        return carry

    loads[3].wait()
    means[...] = jnp.zeros_like(means)
    lax.fori_loop(0, blocks, cot_block, 0)
    crosses = plane_total(links, means, sums_in, peer, 2 * blocks)

    def out_block(index):
        cot_all[index] = mm(d_gate[index], wo[...].reshape(inner, model)).astype(BF16)

    def for_pair(mask):
        out_block(peer[mask ^ 1][1])
        o_plane.pair[mask].start()

    for_pair(6)
    out_block(peer[6][1])
    for_pair(2)
    out_block(peer[2][1])
    o_plane.far()
    for_pair(4)
    out_block(peer[4][1])
    o_plane.near(2)
    for_pair(0)
    out_block(place)
    o_plane.near(4)
    if depth > 2:
        out_line.phase(1)
    means[...] = norms[...] * by_column(crosses() / inner_all)

    def gate_block(index, carry):
        at = pl.ds(pl.multiple_of(index * rows, rows), rows)
        gate = gate_all[at, :]
        sig = sigmoid(gate)
        gate_act = gate * sig
        y = y_all[at, :]
        inv = column(norms, index)
        hat = y * gate_act * inv
        d_gated = inv * (d_y_all[at, :] * gate_gain - hat * column(means, index))
        d_y_all[at, :] = d_gated * gate_act
        tokens_of(d_gate, index)[...] = (
            (d_gated * y * sig * (1.0 + gate * (1.0 - sig))).astype(BF16).reshape(2, piece, inner)
        )
        return carry

    lax.fori_loop(0, blocks, gate_block, 0)
    save_gate = pltpu.make_async_copy(d_gate, d_gate_hbm, locals_.at[7])
    save_gate.start()

    def gate_grad_tile(number, carry):
        at = pl.ds(pl.multiple_of(number * 128, 128), 128)
        left = d_gate[:, :, at].reshape(everything, 128)
        g_gate[at, :] = t_mm(left, normed_all[...].reshape(everything, model))
        return carry

    loads[4].wait()
    lax.fori_loop(0, inner // 128, gate_grad_tile, 0)
    gate_line.phase(0)
    o_plane.near(0)

    channel_sums[...] = jnp.zeros_like(channel_sums)
    head_sums[...] = jnp.zeros_like(head_sums)
    causal = triangles()
    ones = causal.astype(BF16)
    ones_three = jnp.concatenate([ones] * 3, axis=1)
    after = jnp.where(triangles_up(), 1.0, 0.0).astype(BF16)
    before = jnp.where(triangles_up(), 0.0, 1.0).astype(BF16)
    both_ways = jnp.concatenate([after, before] * 2, axis=1)
    of_head = head_of_channel(inner, head_size).astype(BF16)

    def head_totals(values):
        high, low = in_parts(values, 2)
        return mm(high, of_head) + mm(low, of_head)

    home = lax.div(row, half) == core
    rows_out = out_grad.shape[0]
    far = links.copy(out_far, out_grad, peer[1])

    def pump_gate():
        if depth > 2:
            gate_line.phase(1)

    def pump_gate_last():
        if depth > 3:
            gate_line.phase(2)

    def pump_out():
        out_line.finish(out_sum)
        for this in range(2):

            @pl.when(home & (core == this))
            def _():
                cast_rows(out_far, out_sum.at[pl.ds((1 - this) * rows_out, rows_out)])
                far.start()
                cast_rows(out_grad, out_sum.at[pl.ds(this * rows_out, rows_out)])

    def pump_back():
        gate_line.finish(gate_sum)
        turn(gate_sent, gate_sum)
        send_gate.begin()

    quarter = everything // 4
    bc_rows = [
        PlaneRows(
            links,
            row,
            place,
            d_bc,
            bc_landed,
            pl.ds((2 * (k // 2) + 1 - k % 2) * quarter, quarter),
            locals_.at[10 + k],
        )
        for k in range(4)
    ]

    def pump_out_last():
        if depth > 3:
            out_line.phase(2)

    pumps = {
        0: [o_plane.second, pump_out_last],
        1: [bc_rows[0].begin],
        2: [pump_gate],
        3: [bc_rows[1].begin, pump_out],
        4: [pump_gate_last],
        5: [bc_rows[2].begin, lambda: o_plane.finish(store_output)],
        7: [pump_back],
    }

    def store_output(at, total):
        output[at] = (x_own[at].astype(F32) + total).astype(BF16)

    def scan_block(number, carry):
        slot, block = place_of(number)
        index = slot * per_slot + block
        buffer = lax.rem(number, 2)
        for copy in fetch(number):
            copy.wait()

        @pl.when(number + 1 < blocks)
        def _():
            for copy in fetch(number + 1):
                copy.start()

        @pl.when(block == per_slot - 1)
        def _():
            later[...] = jnp.zeros_like(later)
            d_ext[rows:, :] = jnp.zeros((8, inner), F32)

        pre = pre_two[buffer]
        pre_sig = sigmoid(pre)
        act = pre * pre_sig
        slope = pre_sig[:, :inner] * (1.0 + pre[:, :inner] * (1.0 - pre_sig[:, :inner]))
        dt_arg = dt_two[buffer]
        dt_block = softplus(dt_arg)
        rates = rows_in[4:5, :128]
        steps_block = dt_block * rates
        parts = [slice(sub * CHUNK, (sub + 1) * CHUNK) for sub in range(subs)]
        at = pl.ds(pl.multiple_of(index * rows, rows), rows)
        x = act[:, :inner]
        b = act[:, inner : inner + size].astype(BF16)
        c = act[:, inner + size :].astype(BF16)
        cums = [
            mm(ones_three, jnp.concatenate(in_parts(steps_block[part], 3), axis=0))
            for part in parts
        ]
        lasts = [cum[CHUNK - 1 : CHUNK, :] for cum in cums]
        dt_wide = widen(dt_block, heads, head_size)
        cum_wide = widen(jnp.exp(jnp.concatenate(cums, axis=0)), heads, head_size)
        out_wide = widen(
            jnp.exp(jnp.concatenate([last - cum for last, cum in zip(lasts, cums)], axis=0)),
            heads,
            head_size,
        )
        x_dt = x * dt_wide
        x_dt16 = x_dt.astype(BF16)
        d_y = d_y_all[at, :]
        d_y16 = d_y.astype(BF16)
        d_read = (d_y * cum_wide).astype(BF16)
        sent = (x_dt * out_wide).astype(BF16)
        near, d_cbs = [], []
        for sub, part in enumerate(parts):
            cum_t = cums[sub].T
            cb = mm_t(c[part], b[part])
            d_cb = jnp.zeros((CHUNK, CHUNK), F32)
            pieces = []
            for pair in range(heads // 2):
                lanes = slice(2 * pair * head_size, 2 * (pair + 1) * head_size)
                d_y_split = split_pair(d_y16[part, lanes], head_size)
                mixing = []
                for k in range(2):
                    decay = head_decays(cums[sub], cum_t, 2 * pair + k, causal)
                    mixing.append((decay * cb).astype(BF16))
                    d_cb = d_cb + decay * mm_t(d_y_split[k], x_dt16[part, lanes])
                pieces.append(
                    t_mm(jnp.concatenate(mixing, axis=0), jnp.concatenate(d_y_split, axis=0))
                )
            near.append(jnp.concatenate(pieces, axis=1))
            d_cbs.append(d_cb.astype(BF16))
        later_rows, overs = [None] * subs, [None] * subs
        for sub in reversed(range(subs)):
            part = parts[sub]
            held16 = states_two[buffer, sub]
            grown = later[...]
            grown16 = grown.astype(BF16)
            later_rows[sub] = mm(b[part], grown16)
            column_at = pl.ds(pl.multiple_of(index * rows + sub * CHUNK, CHUNK), CHUNK)
            d_b = mm_t(grown16, sent[part]) + t_mm(c[part], d_cbs[sub])
            d_c = mm_t(held16, d_read[part]) + dot(b[part], d_cbs[sub], ((0,), (1,)))
            for first, value in ((0, d_b), (width // 2, d_c)):
                d_bc[first : first + width // 2, :, column_at] = value.astype(BF16).reshape(
                    width // 2, 2 * size // width, CHUNK
                )
            overs[sub] = jnp.sum(grown * held16.astype(F32), axis=0, keepdims=True)
            later[...] = grown * widen(jnp.exp(lasts[sub]), heads, head_size) + t_mm(
                c[part], d_read[part]
            )
        d_x_near = jnp.concatenate(near, axis=0)
        d_x_later = out_wide * jnp.concatenate(later_rows, axis=0)
        d_x_dt = d_x_later + d_x_near
        d_x = d_x_dt * dt_wide + skip * d_y
        d_ext[0:rows, :] = d_x * slope
        channel_sums[5:6, :] += jnp.sum(d_y * x, axis=0, keepdims=True)
        cross_wide = d_y16.astype(F32) * (y_all[at, :] - skip * x) - x_dt16.astype(F32) * d_x_near
        over_wide = jnp.concatenate(overs + [jnp.zeros((8 - subs, inner), F32)], axis=0)
        d_dt_direct = mm((x * d_x_dt).astype(BF16), of_head)
        d_cum = head_totals(cross_wide)
        through = mm((x_dt * d_x_later).astype(BF16), of_head)
        over = head_totals(over_wide)
        d_log = jnp.concatenate(
            [
                mm(
                    both_ways,
                    jnp.concatenate(
                        in_parts(jnp.concatenate([d_cum[part], through[part]], axis=0), 2), axis=0
                    ),
                )
                + over[sub : sub + 1] * jnp.exp(lasts[sub])
                for sub, part in enumerate(parts)
            ],
            axis=0,
        )
        d_arg = (d_dt_direct + rates * d_log) * sigmoid(dt_arg)
        d_arg_all[
            pl.ds(2 * block, 2), pl.ds(pl.multiple_of(slot * piece, piece), piece), :
        ] = d_arg.astype(BF16).reshape(2, piece, 128)
        head_sums[0:1, :] += jnp.sum(d_arg, axis=0, keepdims=True)
        head_sums[1:2, :] += jnp.sum(d_log * dt_block, axis=0, keepdims=True) * rates

        d_conv = jnp.zeros((rows, inner), F32)
        x_in = conv_two[buffer]
        for k in range(kernel):
            moved = d_ext[kernel - 1 - k : kernel - 1 - k + rows, :]
            d_conv = d_conv + taps[k : k + 1, :inner] * moved
            channel_sums[k : k + 1, :] += jnp.sum(moved * x_in, axis=0, keepdims=True)
        channel_sums[4:5, :] += jnp.sum(d_ext[0:rows, :], axis=0, keepdims=True)
        d_x_all[
            pl.ds(2 * block, 2), pl.ds(pl.multiple_of(slot * piece, piece), piece), :
        ] = d_conv.astype(BF16).reshape(2, piece, inner)
        d_ext[rows:, :] = d_ext[0:8, :]

        for at_step, actions in pumps.items():

            @pl.when(number == at_step)
            def _():
                for action in actions:
                    action()

        return carry

    lax.fori_loop(0, blocks, scan_block, 0)
    bc_rows[3].begin()
    saves = [
        pltpu.make_async_copy(source, target, locals_.at[8 + k])
        for k, (source, target) in enumerate(
            ((d_x_all, d_x_hbm), (d_arg_all, d_arg_hbm))
        )
    ]
    for copy in saves:
        copy.start()

    pl.when(jnp.logical_not(home))(far.wait_recv)
    pl.when(home)(far.wait_send)
    o_plane.drain()
    out_line.drain()
    gate_line.drain()
    send_gate.end()
    save_gate.wait()
    for copy in saves:
        copy.wait()
    for rows_ in bc_rows:
        rows_.end()


def line_buffers(count, extent):
    return [pltpu.VMEM((count,) + extent, BF16)] * 4


def plane_buffers(rows, model):
    return [
        pltpu.VMEM((4, rows, model), BF16),
        pltpu.VMEM((4, rows, model), BF16),
        pltpu.VMEM((2, rows // 2, model), BF16),
        pltpu.VMEM((2, rows, model), BF16),
    ]


def reverse(dims, hbm, vmem, collective):
    depth, width, heads, head_size, size, kernel, own_ch, inner_all = dims
    inner = heads * head_size
    _, rows, model = hbm[0].shape
    tokens = rows * width
    wide = inner + 2 * size
    shape = jax.ShapeDtypeStruct
    subs = rows // CHUNK
    half = depth // 2
    out_piece, in_piece = (inner // half, model), (inner, model // depth)
    saved = [
        ((width, rows, inner), BF16),
        ((width, rows, inner), BF16),
        ((width, rows, 128), BF16),
    ]
    bc = ((width, 2 * size // width, tokens), BF16)
    kept = [
        ((rows, model), BF16),
        ((width, model // depth // width, inner), BF16),
        ((out_piece[0] // 2, model), F32),
        ((8, inner), F32),
        ((8, 128), F32),
        bc,
    ]
    return pl.pallas_call(
        functools.partial(reverse_kernel, dims),
        out_shape=tuple(shape(*s) for s in saved + kept),
        in_specs=[ANY] * len(hbm) + [INVMEM] * len(vmem),
        out_specs=(ANY,) * len(saved) + (INVMEM,) * len(kept),
        scratch_shapes=[pltpu.VMEM((width, rows, model), BF16)] * 2
        + [pltpu.VMEM((tokens, inner), F32)] * 3
        + [pltpu.VMEM(hbm[-1].shape, BF16)]
        + [pltpu.VMEM(*s) for s in saved]
        + [
            pltpu.VMEM(*bc),
            pltpu.VMEM((inner, model), F32),
            pltpu.VMEM((inner, model), F32),
            pltpu.VMEM((2, rows, wide), F32),
            pltpu.VMEM((2, rows, inner), F32),
            pltpu.VMEM((2, rows, 128), F32),
            pltpu.VMEM((2, subs, size, inner), BF16),
            pltpu.VMEM((size, inner), F32),
            pltpu.VMEM((rows + 8, inner), F32),
        ]
        + plane_buffers(rows, model)
        + line_buffers(half, out_piece)
        + line_buffers(depth - 1, in_piece)
        + [
            pltpu.VMEM(out_piece, F32),
            pltpu.VMEM((out_piece[0] // 2, model), F32),
            pltpu.VMEM(in_piece, F32),
            pltpu.VMEM((in_piece[1], in_piece[0]), BF16),
            pltpu.VMEM((CHUNK, 128), F32),
            pltpu.VMEM((width, tokens // CHUNK, 128), F32),
            pltpu.SemaphoreType.DMA((80,)),
            pltpu.SemaphoreType.DMA((80,)),
            pltpu.SemaphoreType.DMA((14,)),
            pltpu.SemaphoreType.DMA((2, 4)),
        ],
        compiler_params=pltpu.CompilerParams(
            collective_id=collective, has_side_effects=True, vmem_limit_bytes=VMEM_LIMIT
        ),
        name="reverse_fused",
    )(*hbm, *vmem)


def runs_of(width, half, run):
    plane = width // 2
    for place in range(width):
        for j in range(half):
            yield place, j * run, (((place % 2) * half + j) * plane + place // 2) * run


def head_places(place, half, plane, group, heads, shift):
    lane = lax.broadcasted_iota(jnp.int32, (128, 128), 0) - shift
    head = lax.broadcasted_iota(jnp.int32, (128, 128), 1)
    part = sum(((lane >= j * group).astype(jnp.int32) for j in range(1, half)), jnp.zeros_like(lane))
    chosen = ((place % 2 * half + part) * plane + place // 2) * group + lane - part * group
    return jnp.where((head == chosen) & (lane >= 0) & (lane < heads), 1.0, 0.0)


def weights_kernel(
    dims,
    d_x_hbm,
    normed_hbm,
    turned_hbm,
    d_gate_hbm,
    pre_hbm,
    conv_hbm,
    d_arg_hbm,
    wb_hbm,
    cot_hbm,
    bc_landed,
    taps,
    channel_sums,
    head_sums,
    rows_in,
    x_own,
    w_dt,
    gate_back,
    input_grad,
    in_grad,
    smalls,
    d_x,
    normed_all,
    d_gate,
    pre_own,
    conv_own,
    d_arg,
    wb,
    cot_own,
    w_turned,
    d_small,
    g_x,
    g_small,
    d_parts,
    d_ext,
    bc_sums,
    d_pair,
    d_sums,
    d_relay,
    d_last,
    x_up_in,
    x_up_out,
    x_down_in,
    x_down_out,
    small_up_in,
    small_up_out,
    small_down_in,
    small_down_out,
    x_sum,
    x_sent,
    small_sum,
    small_sent,
    x_back,
    small_back,
    sums_own,
    sums_line,
    sums_all,
    full,
    sends,
    recvs,
    locals_,
):
    depth, width, heads, head_size, size, kernel, own_ch, inner_all = dims
    half, plane = depth // 2, width // 2
    inner = heads * head_size
    run = inner // half
    group = run // head_size
    model = normed_all.shape[2]
    piece = normed_all.shape[1] // 2
    rows = 2 * piece
    slots = 2
    blocks = slots * width // 2
    per_slot = blocks // slots
    everything = slots * width * piece
    own = 2 * size // width
    row, place = lax.axis_index("dp"), lax.axis_index("seq")
    links = Links(sends, recvs)
    peer = {mask: (row, flip_all(place, mask)) for mask in range(1, width)}
    order = (6, 2, 4, 7, 3, 5, 1)
    per_block = 128 // own
    bc_turn = 128 - own * lax.rem(place, per_block)
    window = pl.ds(pl.multiple_of(inner + lax.div(place, per_block) * 128, 128), 128)

    loads = [
        pltpu.make_async_copy(source, target, locals_.at[k])
        for k, (source, target) in enumerate(
            (
                (d_x_hbm, d_x),
                (normed_hbm, normed_all),
                (turned_hbm, w_turned.at[pl.ds(0, 2 * inner)]),
                (d_gate_hbm, d_gate),
                (pre_hbm.at[:, window], pre_own),
                (conv_hbm.at[:, window], conv_own),
                (d_arg_hbm, d_arg),
                (wb_hbm, wb),
                (cot_hbm.at[place], cot_own),
            )
        )
    ]
    for copy in loads:
        copy.start()
    line_peers = [(lax.rem(row + up, depth), place) for up in range(1, depth)]
    greet([peer[mask] for mask in range(1, width)] + line_peers)

    cols = model // depth

    def line(own_ref, buffers):
        return LineSum(
            links,
            depth,
            row,
            place,
            lambda q: own_ref.at[:, pl.ds(q * cols, cols)],
            lambda q: row >= 0,
            *buffers,
        )

    x_line = line(g_x, (x_up_in, x_up_out, x_down_in, x_down_out))
    small_line = line(g_small, (small_up_in, small_up_out, small_down_in, small_down_out))
    d_plane = PlaneSum(links, row, place, d_parts, d_pair, d_sums, d_relay, d_last)
    send_x = SendBack(links, row, place, x_sent, x_back, locals_.at[12])
    send_small = SendBack(links, row, place, small_sent, small_back, locals_.at[13])

    def x_grad_tile(number, carry):
        at = pl.ds(pl.multiple_of(number * 128, 128), 128)
        left = d_x[:, :, at].reshape(everything, 128)
        g_x[at, :] = t_mm(left, normed_all[...].reshape(everything, model))
        return carry

    loads[0].wait()
    loads[1].wait()
    lax.fori_loop(0, inner // 128, x_grad_tile, 0)
    x_line.phase(0)

    lane = lax.broadcasted_iota(jnp.int32, (1, 128), 1)
    mine = lane < own

    def to_front(values):
        return pltpu.roll(values, bc_turn, 1)

    own_taps = to_front(taps[:, window])
    for copy in loads[4:8]:
        copy.wait()
    bc_sums[...] = jnp.zeros_like(bc_sums)

    def small_block(number, carry):
        slot, block = lax.div(number, per_slot), per_slot - 1 - lax.rem(number, per_slot)
        at = pl.ds(pl.multiple_of((slot * per_slot + block) * rows, rows), rows)

        @pl.when(block == per_slot - 1)
        def _():
            d_ext[rows:, :] = jnp.zeros((8, 128), F32)

        total = sum(bc_landed[k, :, at].astype(F32) for k in range(width))
        total = jnp.concatenate([total, jnp.zeros((128 - own, rows), F32)], axis=0)
        pre = to_front(pre_own[at, :])
        sig = sigmoid(pre)
        d_pre = jnp.where(mine, total.T * (sig * (1.0 + pre * (1.0 - sig))), 0.0)
        d_ext[0:rows, :] = d_pre
        where = (pl.ds(2 * block, 2), pl.ds(pl.multiple_of(slot * piece, piece), piece))
        conv_in = to_front(conv_own[at, :])
        d_conv = jnp.zeros((rows, 128), F32)
        for k in range(kernel):
            moved = d_ext[kernel - 1 - k : kernel - 1 - k + rows, :]
            d_conv = d_conv + own_taps[k : k + 1, :] * moved
            bc_sums[k : k + 1, :] += jnp.sum(moved * conv_in, axis=0, keepdims=True)
        bc_sums[4:5, :] += jnp.sum(d_pre, axis=0, keepdims=True)
        d_ext[rows:, :] = d_ext[0:8, :]
        d_dt = pltpu.roll(
            d_arg[where[0], where[1], :].astype(F32).reshape(rows, 128), own, 1
        )
        both = jnp.where(mine, d_conv, jnp.where(lane < own + heads, d_dt, 0.0))
        d_small[where[0], where[1], :] = both.astype(BF16).reshape(2, piece, 128)
        return carry

    lax.fori_loop(0, blocks, small_block, 0)
    g_small[...] = t_mm(
        d_small[...].reshape(everything, 128), normed_all[...].reshape(everything, model)
    )
    small_line.phase(0)
    for copy in loads[2:4]:
        copy.wait()

    def turn_weights(number, carry):
        at = pl.ds(pl.multiple_of(number * 128, 128), 128)
        bc = to_front(wb[lax.div(place, per_block), at, :].astype(F32))
        w_turned[2 * inner :, at] = jnp.where(mine, bc, 0.0).T.astype(BF16)
        return carry

    lax.fori_loop(0, model // 128, turn_weights, 0)
    w_turned[2 * inner + own : 2 * inner + own + 16, :] = w_dt[0:16, :]

    def token_grads(index):
        both = jnp.concatenate([d_gate[index], d_x[index], d_small[index]], axis=1)
        d_parts[index] = mm(both, w_turned[...]).astype(BF16)

    def for_pair(mask):
        token_grads(peer[mask ^ 1][1])
        d_plane.pair[mask].start()

    for_pair(6)
    token_grads(peer[6][1])
    for_pair(2)
    d_plane.far()
    token_grads(peer[2][1])
    for_pair(4)
    d_plane.near(2)
    if depth > 2:
        x_line.phase(1)
    token_grads(peer[4][1])
    for_pair(0)
    d_plane.near(4)
    token_grads(place)
    d_plane.near(0)

    sums_own[:, :inner] = channel_sums[...]
    sums_own[:, inner : inner + 128] = bc_sums[...]
    sums_own[:, inner + 128 :] = head_sums[...]
    sums_own[2:3, inner + 128 :] = dot(
        channel_sums[...],
        head_of_channel(inner, head_size),
        ((1,), (0,)),
        lax.Precision.HIGHEST,
    )[5:6]
    sums_copies = [
        links.copy(sums_own, sums_line.at[k], device) for k, device in enumerate(line_peers)
    ]
    for copy in sums_copies:
        copy.start()
    d_plane.second()
    if depth > 3:
        x_line.phase(2)
    if depth > 2:
        small_line.phase(1)
    for copy in sums_copies:
        copy.wait()
    total = jnp.zeros(sums_own.shape, F32)
    for q in range(depth):
        term = jnp.zeros(sums_own.shape, F32)
        for up in range(1, depth):
            term = jnp.where(lax.rem(row + depth - up, depth) == q, sums_line[up - 1], term)
        total = total + jnp.where(row == q, sums_own[...], term)
    sums_all[place] = total
    mine_all = sums_all.at[place]
    spread_sums = [links.copy(mine_all, mine_all, peer[mask]) for mask in order]
    for copy in spread_sums:
        copy.start()

    x_line.finish(x_sum)
    turn(x_sent, x_sum)
    send_x.begin()
    if depth > 3:
        small_line.phase(2)

    for source, at, to in runs_of(width, half, run):
        in_grad[:, to : to + run] = gate_back[source, :, at : at + run].astype(F32)
    small_line.finish(small_sum)
    turn(small_sent, small_sum)
    send_small.begin()
    for copy in spread_sums:
        copy.wait()
    for source, at, to in runs_of(width, half, run):
        full[:, to : to + run] = sums_all[source, :, at : at + run]
    for source in range(width):
        to = inner_all + source * own
        full[:, to : to + own] = sums_all[source, :, inner : inner + own]
    first = (row * width + place) * own_ch
    base = pl.multiple_of(lax.div(first, 128) * 128, 128)
    view = pltpu.roll(full[:, pl.ds(base, 256)], 256 - lax.rem(first, 128), 1)
    smalls[0:8, :] = view[:, :128]
    smalls[8:16, :] = sum(
        dot(
            sums_all[source, :, inner + 128 :],
            head_places(source, half, plane, group, heads, 0),
            ((1,), (0,)),
            lax.Precision.HIGHEST,
        )
        for source in range(width)
    )
    send_x.end()
    for source, at, to in runs_of(width, half, run):
        in_grad[:, inner_all + to : inner_all + to + run] = x_back[
            source, :, at : at + run
        ].astype(F32)
    send_small.end()
    for source in range(width):
        to = 2 * inner_all + source * own
        in_grad[:, to : to + own] = small_back[source, :, :own].astype(F32)
    for source, at, to in runs_of(width, half, group):
        to = 2 * inner_all + 2 * size + to
        in_grad[:, to : to + group] = small_back[
            source, :, own + at : own + at + group
        ].astype(F32)

    norm_gain = rows_in[0:1, :]

    def store_grad(at, total):
        held = x_own[at].astype(F32)
        inv = lax.rsqrt(jnp.mean(held * held, axis=1, keepdims=True) + EPS)
        hat = held * inv
        d_h = total * norm_gain
        grad = inv * (d_h - hat * jnp.mean(d_h * hat, axis=1, keepdims=True))
        input_grad[at] = (grad + cot_own[at].astype(F32)).astype(BF16)

    loads[8].wait()
    d_plane.finish(store_grad)
    d_plane.drain()
    x_line.drain()
    small_line.drain()


def weights(dims, hbm, vmem, collective):
    depth, width, heads, head_size, size, kernel, own_ch, inner_all = dims
    inner = heads * head_size
    _, rows, model = hbm[1].shape
    tokens = rows * width
    shape = jax.ShapeDtypeStruct
    cols = model // depth
    owned = cols // width
    own = 2 * size // width
    kept = [
        ((rows, model), BF16),
        ((owned, 2 * inner_all + 2 * size + heads * width), F32),
        ((16, 128), F32),
    ]
    return pl.pallas_call(
        functools.partial(weights_kernel, dims),
        out_shape=tuple(shape(*s) for s in kept),
        in_specs=[ANY] * len(hbm) + [INVMEM] * len(vmem),
        out_specs=(INVMEM,) * len(kept),
        scratch_shapes=[pltpu.VMEM(v.shape, v.dtype) for v in (hbm[0], hbm[1], hbm[3])]
        + [
            pltpu.VMEM((tokens, 128), F32),
            pltpu.VMEM((tokens, 128), F32),
            pltpu.VMEM(hbm[6].shape, BF16),
            pltpu.VMEM(hbm[7].shape, BF16),
            pltpu.VMEM((rows, model), BF16),
            pltpu.VMEM((2 * inner + 128, model), BF16),
            pltpu.VMEM((width, rows, 128), BF16),
            pltpu.VMEM((inner, model), F32),
            pltpu.VMEM((128, model), F32),
            pltpu.VMEM((width, rows, model), BF16),
            pltpu.VMEM((rows + 8, 128), F32),
            pltpu.VMEM((8, 128), F32),
        ]
        + plane_buffers(rows, model)
        + line_buffers(depth - 1, (inner, cols))
        + line_buffers(depth - 1, (128, cols))
        + [
            pltpu.VMEM((inner, cols), F32),
            pltpu.VMEM((cols, inner), BF16),
            pltpu.VMEM((128, cols), F32),
            pltpu.VMEM((cols, 128), BF16),
            pltpu.VMEM((width, owned, inner), BF16),
            pltpu.VMEM((width, owned, 128), BF16),
            pltpu.VMEM((8, inner + 256), F32),
            pltpu.VMEM((depth - 1, 8, inner + 256), F32),
            pltpu.VMEM((width, 8, inner + 256), F32),
            pltpu.VMEM((8, inner_all + 2 * size + 256), F32),
            pltpu.SemaphoreType.DMA((88,)),
            pltpu.SemaphoreType.DMA((88,)),
            pltpu.SemaphoreType.DMA((14,)),
        ],
        compiler_params=pltpu.CompilerParams(
            collective_id=collective, has_side_effects=True, vmem_limit_bytes=VMEM_LIMIT
        ),
        name="weights_fused",
    )(*hbm, *vmem)


def fast_body(
    depth,
    width,
    block_input,
    cotangent,
    lengths,
    in_weight,
    out_weight,
    norm_gain,
    gate_gain,
    conv_weight,
    conv_bias,
    dt_bias,
    a_log,
    d_skip,
):
    slots, piece, model = block_input.shape
    heads_all = dt_bias.shape[0]
    out_rows = out_weight.shape[0]
    in_rows = in_weight.shape[0]
    inner_all = out_rows * depth * width
    head_size = inner_all // heads_all
    taps_count = conv_weight.shape[0]
    channels = conv_weight.shape[1] * depth * width
    size = (channels - inner_all) // 2
    heads = heads_all // width
    inner = heads * head_size
    plane = width // 2
    half = depth // 2
    pair_rows = 2 * out_rows
    row, place = lax.axis_index("dp"), lax.axis_index("seq")
    core, chip = lax.rem(place, 2), lax.div(place, 2)
    slot_len = piece * width
    tokens = slots * slot_len

    own_ch = conv_bias.shape[0]
    tokens_dev = slots * piece
    dims = (depth, width, heads, head_size, size, taps_count, own_ch, inner_all)
    (
        normed_all,
        cot_all,
        w_turned,
        w_bc,
        w_out,
        conv_in,
        pre,
        dt_arg,
        gate,
        y,
        states,
        norms,
        taps,
        param_rows,
        w_dt,
    ) = forward(
        dims,
        (
            block_input.reshape(tokens_dev, model),
            cotangent.reshape(tokens_dev, model),
            lengths[None],
            in_weight,
            out_weight,
            norm_gain[None],
            gate_gain[None],
            conv_weight,
            conv_bias[None],
            dt_bias[None],
            a_log[None],
            d_skip[None],
        ),
        2,
    )
    x_own = block_input.reshape(tokens_dev, model)
    (
        d_gate,
        d_x,
        d_arg,
        output,
        gate_back,
        out_grad,
        channel_sums,
        head_sums,
        d_bc,
    ) = reverse(
        dims,
        (cot_all, normed_all, gate, y, pre, conv_in, dt_arg, states, w_out),
        (norms, taps, param_rows, x_own),
        3,
    )
    input_grad, in_grad, smalls = weights(
        dims,
        (
            d_x,
            normed_all,
            w_turned,
            d_gate,
            pre,
            conv_in,
            d_arg,
            w_bc.reshape(2, model, size),
            cot_all,
        ),
        (
            d_bc,
            taps,
            channel_sums,
            head_sums,
            param_rows,
            x_own,
            w_dt,
            gate_back,
        ),
        4,
    )
    norm_grad = jnp.sum(in_grad * in_weight.astype(F32), axis=1) / norm_gain.astype(F32)
    gate_grad = jnp.sum(out_grad * out_weight.astype(F32), axis=1) / gate_gain.astype(F32)
    return (
        output.reshape(slots, piece, model),
        input_grad.reshape(slots, piece, model),
        in_grad,
        out_grad,
        norm_grad,
        gate_grad,
        smalls[:4, :own_ch],
        smalls[4, :own_ch],
        smalls[8, :heads_all],
        smalls[9, :heads_all],
        smalls[10, :heads_all],
    )


def heads_fit(depth, width, arrays):
    block_input, out_weight, dt_bias = arrays[0], arrays[4], arrays[9]
    pair_rows = 2 * out_weight.shape[0]
    head_size = out_weight.shape[0] * depth * width // dt_bias.shape[0]
    return (
        width == 8
        and depth % 2 == 0
        and pair_rows % head_size == 0
        and (depth // 2 * pair_rows) % 128 == 0
        and block_input.shape[1] % CHUNK == 0
        and 2 * head_size == CHUNK
    )


def solution(mesh):
    placed = (
        P("dp", "seq", None),
        P("dp", "seq", None),
        P("dp"),
        P(("dp", "seq"), None),
        P(("dp", "seq"), None),
        P(("dp", "seq")),
        P(("dp", "seq")),
        P(None, ("dp", "seq")),
        P(("dp", "seq")),
        P(),
        P(),
        P(),
    )
    depth, width = mesh.shape["dp"], mesh.shape["seq"]

    def either(*arrays):
        if heads_fit(depth, width, arrays):
            return fast_body(depth, width, *arrays)
        return body(*arrays)

    return jax.shard_map(
        either,
        mesh=mesh,
        in_specs=placed,
        out_specs=(
            P("dp", "seq", None),
            P("dp", "seq", None),
            P(("dp", "seq"), None),
            P(("dp", "seq"), None),
            P(("dp", "seq")),
            P(("dp", "seq")),
            P(None, ("dp", "seq")),
            P(("dp", "seq")),
            P(),
            P(),
            P(),
        ),
        check_vma=False,
    )
```

```python
import functools

import jax
import jax.numpy as jnp
from jax import lax
from jax.experimental import pallas as pl
from jax.experimental.pallas import tpu as pltpu
from jax.sharding import PartitionSpec as P

SLOTS_MB = 1


EPS = 1e-05
HIGH = lax.Precision.HIGHEST


def from_behind(value, axis, steps):
    count = lax.axis_size(axis)
    leading, last = (max(0, -steps), min(count, count - steps))
    return lax.ppermute(value, axis, [(source, source + steps) for source in range(leading, last)])


def carried_in(value, axis, join, neutral, backward):
    count = lax.axis_size(axis)
    place = lax.axis_index(axis)
    ahead = count - 1 - place if backward else place
    gathered = jax.tree.map(
        lambda a, kind: lax.all_gather(a.astype(kind), axis),
        value,
        jax.tree.map(lambda a: jnp.bfloat16 if a.dtype == jnp.float32 else a.dtype, value),
    )
    state = jax.tree.map(lambda a, e: jnp.zeros_like(a) + jnp.asarray(e, a.dtype), value, neutral)

    def one(lap, state):
        source = count - 1 - lap if backward else lap
        return join(
            state,
            jax.tree.map(
                lambda a, own: lax.dynamic_index_in_dim(a, source, 0, False).astype(own.dtype),
                gathered,
                value,
            ),
        )

    return lax.fori_loop(0, ahead, one, state)


def as_sent(value):

    def short(part):
        return part.astype(jnp.bfloat16) if part.dtype == jnp.float32 else part

    return jax.tree.map(short, value)


def link_states(earlier, later):
    return (earlier[0] * later[0], later[0][:, :, None, None] * earlier[1] + later[1])


def silu_slope(values):
    sigma = jax.nn.sigmoid(values)
    return sigma * (1.0 + values * (1.0 - sigma))


def rows_product(left, right):
    return lax.dot_general(
        left, right, (((0,), (0,)), ((), ())), preferred_element_type=jnp.float32
    )


def cols_product(left, right):
    return lax.dot_general(
        left, right, (((1,), (1,)), ((), ())), preferred_element_type=jnp.float32
    )


def add_pair(first, second):
    return first + second


def first_total(stacked):
    return jnp.sum(stacked, axis=0)


def owner_sums(grads):
    lifted = tuple((grad[None] for grad in grads))
    by_data = (
        lax.all_to_all(lifted[0], "dp", split_axis=1, concat_axis=0, tiled=True),
        lax.all_to_all(lifted[1], "dp", split_axis=1, concat_axis=0, tiled=True),
        lax.all_to_all(lifted[2], "dp", split_axis=1, concat_axis=0, tiled=True),
        lax.all_to_all(lifted[3], "dp", split_axis=1, concat_axis=0, tiled=True),
        lax.all_to_all(lifted[4], "dp", split_axis=1, concat_axis=0, tiled=True),
        lax.all_to_all(lifted[5], "dp", split_axis=1, concat_axis=0, tiled=True),
    )
    partial_value = tuple((first_total(stacked)[None] for stacked in by_data))
    by_piece = (
        lax.all_to_all(partial_value[0], "seq", split_axis=1, concat_axis=0, tiled=True),
        lax.all_to_all(partial_value[1], "seq", split_axis=1, concat_axis=0, tiled=True),
        lax.all_to_all(partial_value[2], "seq", split_axis=1, concat_axis=0, tiled=True),
        lax.all_to_all(partial_value[3], "seq", split_axis=1, concat_axis=0, tiled=True),
        lax.all_to_all(partial_value[4], "seq", split_axis=1, concat_axis=0, tiled=True),
        lax.all_to_all(partial_value[5], "seq", split_axis=1, concat_axis=0, tiled=True),
    )
    return tuple((first_total(stacked) for stacked in by_piece))


def forward_pass(slot_in, weights, head_params):
    in_full, out_full, norm_full, gate_full, conv_full, bias_full = weights
    dt_shift, log_rate, skip_gain = head_params
    slot_count, piece_len, model_width = slot_in.shape
    inner_width = out_full.shape[0]
    channels = conv_full.shape[1]
    kernel = conv_full.shape[0]
    head_count = dt_shift.shape[0]
    head_size = inner_width // head_count
    state_size = (channels - inner_width) // 2
    input_f = slot_in.astype(jnp.float32)
    inv_rms = lax.rsqrt(jnp.mean(input_f * input_f, axis=-1, keepdims=True) + EPS)
    normed = (input_f * inv_rms * norm_full.astype(jnp.float32)).astype(jnp.bfloat16)
    projected = jnp.dot(
        normed.reshape(-1, model_width), in_full, preferred_element_type=jnp.float32
    ).reshape(slot_count, piece_len, -1)
    gate_part = projected[..., :inner_width]
    conv_in = projected[..., inner_width : inner_width + channels]
    dt_arg = projected[..., inner_width + channels :] + dt_shift
    rim_rows = from_behind(
        conv_in[:, piece_len - kernel + 1 :].astype(jnp.bfloat16), "seq", 1
    ).astype(jnp.float32)
    extended = jnp.concatenate([rim_rows, conv_in], axis=1)
    conv_taps = conv_full.astype(jnp.float32)
    pre_act = bias_full.astype(jnp.float32) + sum(
        (
            conv_taps[tap_index] * extended[:, tap_index : tap_index + piece_len]
            for tap_index in range(kernel)
        )
    )
    activated = jax.nn.silu(pre_act)
    x_heads = activated[..., :inner_width].reshape(slot_count, piece_len, head_count, head_size)
    b_rows = activated[..., inner_width : inner_width + state_size]
    c_rows = activated[..., inner_width + state_size :]
    dt_vals = jax.nn.softplus(dt_arg)
    decay_rates = -jnp.exp(log_rate)
    log_cum = jnp.cumsum(dt_vals * decay_rates, axis=1)
    log_tot = log_cum[:, -1]
    weights_in = jnp.exp(log_tot[:, None] - log_cum) * dt_vals
    local_state = jnp.einsum(
        "sthp,stn->shpn", weights_in[..., None] * x_heads, b_rows, precision=HIGH
    )
    carry_decay = jnp.exp(log_tot)
    neutral = (jnp.ones_like(carry_decay), jnp.zeros_like(local_state))
    _, start_state = carried_in((carry_decay, local_state), "seq", link_states, neutral, False)
    spots = jnp.arange(piece_len)
    causal = spots[:, None] >= spots[None, :]
    cum_heads = jnp.swapaxes(log_cum, 1, 2)
    gap_vals = jnp.where(causal, cum_heads[..., :, None] - cum_heads[..., None, :], 0.0)
    decay_mat = jnp.where(causal, jnp.exp(gap_vals), 0.0)
    cb_mat = jnp.einsum("stn,sun->stu", c_rows, b_rows, precision=HIGH)
    dt_cols = jnp.swapaxes(dt_vals, 1, 2)[:, :, None, :]
    mixing = decay_mat * cb_mat[:, None] * dt_cols
    y_intra = jnp.einsum("shtu,suhp->sthp", mixing, x_heads, precision=HIGH)
    state_read = jnp.einsum("stn,shpn->sthp", c_rows, start_state, precision=HIGH)
    exp_cum = jnp.exp(log_cum)
    y_heads = y_intra + exp_cum[..., None] * state_read + skip_gain[:, None] * x_heads
    y_flat = y_heads.reshape(slot_count, piece_len, inner_width)
    gate_act = jax.nn.silu(gate_part)
    gated_out = y_flat * gate_act
    inv_gate = lax.rsqrt(jnp.mean(gated_out * gated_out, axis=-1, keepdims=True) + EPS)
    gate_normed = (gated_out * inv_gate * gate_full.astype(jnp.float32)).astype(jnp.bfloat16)
    mixed = jnp.dot(
        gate_normed.reshape(-1, inner_width), out_full, preferred_element_type=jnp.float32
    )
    output = (input_f + mixed.reshape(slot_count, piece_len, model_width)).astype(jnp.bfloat16)
    saved = dict(
        input_f=input_f,
        inv_rms=inv_rms,
        normed=normed,
        gate_part=gate_part,
        dt_arg=dt_arg,
        extended=extended,
        pre_act=pre_act,
        x_heads=x_heads,
        b_rows=b_rows,
        c_rows=c_rows,
        dt_vals=dt_vals,
        log_cum=log_cum,
        log_tot=log_tot,
        weights_in=weights_in,
        carry_decay=carry_decay,
        start_state=start_state,
        decay_mat=decay_mat,
        cb_mat=cb_mat,
        dt_cols=dt_cols,
        mixing=mixing,
        state_read=state_read,
        exp_cum=exp_cum,
        y_flat=y_flat,
        gate_act=gate_act,
        gated_out=gated_out,
        inv_gate=inv_gate,
        gate_normed=gate_normed,
    )
    return (output, saved)


def backward_pass(saved, slot_cot, live, weights, head_params):
    in_full, out_full, norm_full, gate_full, conv_full, bias_full = weights
    dt_shift, log_rate, skip_gain = head_params
    slot_count, piece_len, model_width = slot_cot.shape
    inner_width = out_full.shape[0]
    kernel = conv_full.shape[0]
    x_heads = saved["x_heads"]
    b_rows = saved["b_rows"]
    c_rows = saved["c_rows"]
    dt_vals = saved["dt_vals"]
    log_cum = saved["log_cum"]
    weights_in = saved["weights_in"]
    carry_decay = saved["carry_decay"]
    start_state = saved["start_state"]
    decay_mat = saved["decay_mat"]
    cb_mat = saved["cb_mat"]
    dt_cols = saved["dt_cols"]
    decay_rates = -jnp.exp(log_rate)
    masked_cot = slot_cot * live[..., None].astype(jnp.bfloat16)
    cot_rows = masked_cot.reshape(-1, model_width)
    d_gn = cols_product(cot_rows, out_full).reshape(slot_count, piece_len, inner_width)
    gate_hat = saved["gated_out"] * saved["inv_gate"]
    grad_ggain = jnp.sum(d_gn * gate_hat, axis=(0, 1))
    d_hat = d_gn * gate_full.astype(jnp.float32)
    d_gated = saved["inv_gate"] * (
        d_hat - gate_hat * jnp.mean(d_hat * gate_hat, axis=-1, keepdims=True)
    )
    d_gate_part = d_gated * saved["y_flat"] * silu_slope(saved["gate_part"])
    d_heads = (d_gated * saved["gate_act"]).reshape(x_heads.shape)
    grad_skip = jnp.sum(d_heads * x_heads, axis=(0, 1, 3))
    exp_cum = saved["exp_cum"]
    d_read = d_heads * exp_cum[..., None]
    d_cvals = jnp.einsum("sthp,shpn->stn", d_read, start_state, precision=HIGH)
    d_start = jnp.einsum("sthp,stn->shpn", d_read, c_rows, precision=HIGH)
    d_cum = jnp.sum(d_heads * saved["state_read"], axis=-1) * exp_cum
    d_mixing = jnp.einsum("sthp,suhp->shtu", d_heads, x_heads, precision=HIGH)
    d_x = skip_gain[:, None] * d_heads + jnp.einsum(
        "shtu,sthp->suhp", saved["mixing"], d_heads, precision=HIGH
    )
    d_decay = d_mixing * cb_mat[:, None] * dt_cols
    d_cb = jnp.sum(d_mixing * decay_mat * dt_cols, axis=1)
    d_dt = jnp.swapaxes(jnp.sum(d_mixing * decay_mat * cb_mat[:, None], axis=2), 1, 2)
    spread = d_decay * decay_mat
    d_cum = d_cum + jnp.swapaxes(jnp.sum(spread, axis=3) - jnp.sum(spread, axis=2), 1, 2)
    d_cvals = d_cvals + jnp.einsum("stu,sun->stn", d_cb, b_rows, precision=HIGH)
    d_bvals = jnp.einsum("stu,stn->sun", d_cb, c_rows, precision=HIGH)
    neutral = (jnp.ones_like(carry_decay), jnp.zeros_like(d_start))
    _, later_grad = carried_in((carry_decay, d_start), "seq", link_states, neutral, True)
    d_tot = jnp.sum(later_grad * start_state, axis=(2, 3)) * carry_decay
    grad_proj_b = jnp.einsum("shpn,stn->sthp", later_grad, b_rows, precision=HIGH)
    d_x = d_x + weights_in[..., None] * grad_proj_b
    d_weights = jnp.sum(grad_proj_b * x_heads, axis=-1)
    d_bvals = d_bvals + jnp.einsum(
        "sthp,shpn->stn", weights_in[..., None] * x_heads, later_grad, precision=HIGH
    )
    d_dt = d_dt + d_weights * jnp.exp(saved["log_tot"][:, None] - log_cum)
    through = d_weights * weights_in
    d_tot = d_tot + jnp.sum(through, axis=1)
    last_row = (jnp.arange(piece_len) == piece_len - 1).astype(jnp.float32)
    d_cum = d_cum - through + last_row[None, :, None] * d_tot[:, None, :]
    d_log = lax.cumsum(d_cum, axis=1, reverse=True)
    d_dt = d_dt + d_log * decay_rates
    grad_alog = jnp.sum(d_log * dt_vals, axis=(0, 1)) * decay_rates
    d_arg = d_dt * jax.nn.sigmoid(saved["dt_arg"])
    grad_dtb = jnp.sum(d_arg, axis=(0, 1))
    d_act = jnp.concatenate(
        [d_x.reshape(slot_count, piece_len, inner_width), d_bvals, d_cvals], axis=-1
    )
    d_pre = d_act * silu_slope(saved["pre_act"])
    grad_cbias = jnp.sum(d_pre, axis=(0, 1))
    extended = saved["extended"]
    grad_conv = jnp.stack(
        [
            jnp.sum(d_pre * extended[:, tap_index : tap_index + piece_len], axis=(0, 1))
            for tap_index in range(kernel)
        ]
    )
    conv_taps = conv_full.astype(jnp.float32)
    d_ext = sum(
        (
            jnp.pad(
                conv_taps[tap_index] * d_pre, ((0, 0), (tap_index, kernel - 1 - tap_index), (0, 0))
            )
            for tap_index in range(kernel)
        )
    )
    back_rim = from_behind(as_sent(d_ext[:, : kernel - 1]), "seq", -1)
    d_conv_in = d_ext[:, kernel - 1 :] + jnp.pad(
        back_rim, ((0, 0), (piece_len - kernel + 1, 0), (0, 0))
    )
    d_proj = jnp.concatenate([d_gate_part, d_conv_in, d_arg], axis=-1).astype(jnp.bfloat16)
    d_proj = d_proj.reshape(slot_count * piece_len, -1)
    d_normed = cols_product(d_proj, in_full).reshape(slot_count, piece_len, model_width)
    in_hat = saved["input_f"] * saved["inv_rms"]
    grad_ngain = jnp.sum(d_normed * in_hat, axis=(0, 1))
    d_norm_in = d_normed * norm_full.astype(jnp.float32)
    input_grad = saved["inv_rms"] * (
        d_norm_in - in_hat * jnp.mean(d_norm_in * in_hat, axis=-1, keepdims=True)
    )
    input_grad = input_grad + masked_cot.astype(jnp.float32)
    product_rows = (
        saved["normed"].reshape(-1, model_width),
        d_proj,
        saved["gate_normed"].reshape(-1, inner_width),
        cot_rows,
    )
    small_grads = (grad_ngain, grad_ggain, grad_conv, grad_cbias)
    return (
        input_grad.astype(jnp.bfloat16),
        product_rows,
        small_grads,
        (grad_dtb, grad_alog, grad_skip),
    )


def body(
    block_input,
    cotangent,
    lengths,
    in_weight,
    out_weight,
    norm_gain,
    gate_gain,
    conv_weight,
    conv_bias,
    dt_bias,
    a_log,
    d_skip,
):
    shards = (in_weight, out_weight, norm_gain, gate_gain, conv_weight, conv_bias)
    head_params = (dt_bias, a_log, d_skip)
    piece_len = block_input.shape[1]
    batches = block_input.shape[0] // SLOTS_MB
    positions = lax.axis_index("seq") * piece_len + jnp.arange(piece_len, dtype=jnp.int32)
    held = (
        lax.all_gather(shards[0], ("dp", "seq"), axis=0, tiled=True),
        lax.all_gather(shards[1], ("dp", "seq"), axis=0, tiled=True),
        lax.all_gather(shards[2], ("dp", "seq"), axis=0, tiled=True),
        lax.all_gather(shards[3], ("dp", "seq"), axis=0, tiled=True),
        lax.all_gather(shards[4], ("dp", "seq"), axis=1, tiled=True),
        lax.all_gather(shards[5], ("dp", "seq"), axis=0, tiled=True),
    )
    outputs = []
    input_grads = []
    kept_rows = []
    small_totals = None
    head_totals = None
    for batch_index in range(batches):
        first = batch_index * SLOTS_MB
        slot_in = block_input[first : first + SLOTS_MB]
        slot_cot = cotangent[first : first + SLOTS_MB]
        live = (positions[None, :] < lengths[first : first + SLOTS_MB, None]).astype(jnp.float32)
        output, saved = forward_pass(slot_in, held, head_params)
        input_grad, product_rows, small_grads, head_grads = backward_pass(
            saved, slot_cot, live, held, head_params
        )
        outputs.append(output)
        input_grads.append(input_grad)
        kept_rows.append(product_rows)
        small_totals = (
            small_grads
            if small_totals is None
            else jax.tree.map(add_pair, small_totals, small_grads)
        )
        head_totals = (
            head_grads if head_totals is None else jax.tree.map(add_pair, head_totals, head_grads)
        )
    normed_all = jnp.concatenate([rows[0] for rows in kept_rows], axis=0)
    dproj_all = jnp.concatenate([rows[1] for rows in kept_rows], axis=0)
    gnormed_all = jnp.concatenate([rows[2] for rows in kept_rows], axis=0)
    cot_all = jnp.concatenate([rows[3] for rows in kept_rows], axis=0)
    grad_win = rows_product(normed_all, dproj_all)
    grad_wout = rows_product(gnormed_all, cot_all)
    grad_ngain, grad_ggain, grad_conv, grad_cbias = small_totals
    owned = owner_sums((grad_win, grad_wout, grad_ngain, grad_ggain, grad_conv.T, grad_cbias))
    head_sums = lax.psum(head_totals, ("dp", "seq"))
    return (
        jnp.concatenate(outputs, axis=0),
        jnp.concatenate(input_grads, axis=0),
        owned[0],
        owned[1],
        owned[2],
        owned[3],
        owned[4].T,
        owned[5],
        head_sums[0],
        head_sums[1],
        head_sums[2],
    )


F32 = jnp.float32
BF16 = jnp.bfloat16
MESH_ID = pl.DeviceIdType.MESH
ANY = pl.BlockSpec(memory_space=pl.ANY)
INVMEM = pl.BlockSpec(memory_space=pltpu.VMEM)
VMEM_LIMIT = 63 * 1024 * 1024
CHUNK = 128


def flip(place, bit):
    return place + bit - 2 * bit * lax.rem(lax.div(place, bit), 2)


def flip_all(place, mask):
    for bit in (1, 2, 4):
        if mask & bit:
            place = flip(place, bit)
    return place


class Links:
    def __init__(self, sends, recvs):
        self.sends, self.recvs, self.used = sends, recvs, 0

    def copy(self, source, target, device):
        slot = self.used
        self.used += 1
        return pltpu.make_async_remote_copy(
            src_ref=source,
            dst_ref=target,
            send_sem=self.sends.at[slot],
            recv_sem=self.recvs.at[slot],
            device_id=device,
            device_id_type=MESH_ID,
        )


def greet(devices, conditions=(), between=None):
    barrier = pltpu.get_barrier_semaphore()
    for device in devices:
        pl.semaphore_signal(barrier, inc=1, device_id=device, device_id_type=MESH_ID)
    for condition, device in conditions:

        @pl.when(condition)
        def _():
            pl.semaphore_signal(barrier, inc=1, device_id=device, device_id_type=MESH_ID)

    count = len(devices)
    for condition, _ in conditions:
        count = count + jnp.where(condition, 1, 0)
    if between is not None:
        between()
    pl.semaphore_wait(barrier, count)


def add_rows(target, first, second, step=32):
    def one(number, carry):
        rows = pl.ds(pl.multiple_of(number * step, step), step)
        target[rows] = (first[rows].astype(F32) + second[rows].astype(F32)).astype(target.dtype)
        return carry

    lax.fori_loop(0, target.shape[0] // step, one, 0)


def cast_rows(target, source, step=32):
    def one(number, carry):
        rows = pl.ds(pl.multiple_of(number * step, step), step)
        target[rows] = source[rows].astype(target.dtype)
        return carry

    lax.fori_loop(0, target.shape[0] // step, one, 0)


class LineSum:
    def __init__(
        self, links, depth, row, place, own, valid, up_in, up_out, down_in, down_out, shared=None
    ):
        self.depth, self.row, self.own, self.valid = depth, row, own, valid
        above, below = lax.min(row + 1, depth - 1), lax.max(row - 1, 0)

        def slots(ref, shift):
            return {q: ref.at[q % shared if shared else q - shift] for q in range(shift, depth - 1 + shift)}

        self.up_in, self.up_out = slots(up_in, 1), slots(up_out, 1)
        self.down_in, self.down_out = slots(down_in, 0), slots(down_out, 0)
        self.ups = {
            q: links.copy(self.up_out[q], self.up_in[q], (above, place)) for q in self.up_in
        }
        self.downs = {
            q: links.copy(self.down_out[q], self.down_in[q], (below, place)) for q in self.down_in
        }

    def up(self, q, row):
        @pl.when(self.valid(q) & (self.row == row))
        def _():
            if row == 0:
                cast_rows(self.up_out[q], self.own(q))
            else:
                self.ups[q].wait_recv()
                add_rows(self.up_out[q], self.own(q), self.up_in[q])
            self.ups[q].start()

    def down(self, q, row):
        @pl.when(self.valid(q) & (self.row == row))
        def _():
            if row == self.depth - 1:
                cast_rows(self.down_out[q], self.own(q))
            else:
                self.downs[q].wait_recv()
                add_rows(self.down_out[q], self.own(q), self.down_in[q])
            self.downs[q].start()

    def phase(self, number):
        for row in range(self.depth):
            up_q = self.depth - 1 + row - number
            if row < up_q < self.depth:
                self.up(up_q, row)
            down_q = number - (self.depth - 1 - row)
            if 0 <= down_q < row:
                self.down(down_q, row)

    def finish(self, total):
        depth, row = self.depth, self.row
        for q in range(depth):

            @pl.when(self.valid(q) & (row == q))
            def _():
                if q > 0:
                    self.ups[q].wait_recv()
                if q < depth - 1:
                    self.downs[q].wait_recv()
                if 0 < q < depth - 1:
                    add_rows(total, self.up_in[q], self.down_in[q])
                    add_rows(total, total, self.own(q))
                elif q > 0:
                    add_rows(total, self.own(q), self.up_in[q])
                else:
                    add_rows(total, self.own(q), self.down_in[q])

    def drain(self):
        for q, copy in self.ups.items():
            pl.when(self.valid(q) & (self.row < q))(copy.wait_send)
        for q, copy in self.downs.items():
            pl.when(self.valid(q) & (self.row > q))(copy.wait_send)


class PlaneSum:
    def __init__(self, links, row, place, parts, pair_in, sums, relay_in, last_in):
        self.place, self.parts = place, parts
        self.pair_in, self.sums, self.relay_in, self.last_in = pair_in, sums, relay_in, last_in
        peer = {mask: (row, flip_all(place, mask)) for mask in range(1, 8)}
        self.peer = peer
        rows = last_in.shape[1] // 2
        self.halves = (pl.ds(0, rows), pl.ds(rows, rows))
        self.pair = {
            mask: links.copy(parts.at[peer[mask ^ 1][1]], pair_in.at[mask // 2], peer[1])
            for mask in (6, 2, 4, 0)
        }
        top, low = self.halves
        self.relay4 = links.copy(sums.at[3, top], relay_in.at[0], peer[4])
        self.relay2 = links.copy(sums.at[3, low], relay_in.at[1], peer[2])
        self.last2 = [
            links.copy(sums.at[1, half], last_in.at[0, half], peer[2]) for half in self.halves
        ]
        self.last4 = [
            links.copy(sums.at[2, half], last_in.at[1, half], peer[4]) for half in self.halves
        ]

    def begin(self):
        for copy in self.pair.values():
            copy.start()

    def chip(self, mask):
        index = mask // 2
        self.pair[mask].wait_recv()
        mine = self.parts.at[self.peer[mask][1] if mask else self.place]
        add_rows(self.sums.at[index], mine, self.pair_in.at[index])

    def far(self):
        self.chip(6)
        self.relay4.start()
        self.relay2.start()

    def near(self, mask):
        self.chip(mask)
        if mask:
            (self.last2[1] if mask == 2 else self.last4[0]).start()

    def first(self):
        self.far()
        for mask in (2, 4, 0):
            self.near(mask)

    def second(self):
        top, low = self.halves
        self.relay4.wait_recv()
        add_rows(self.sums.at[1, top], self.sums.at[1, top], self.relay_in.at[0])
        self.last2[0].start()
        self.relay2.wait_recv()
        add_rows(self.sums.at[2, low], self.sums.at[2, low], self.relay_in.at[1])
        self.last4[1].start()

    def finish(self, store):
        for copy in self.last2 + self.last4:
            copy.wait_recv()

        def one(number, carry):
            at = pl.ds(pl.multiple_of(number * 32, 32), 32)
            total = self.last_in[0, at].astype(F32) + self.last_in[1, at].astype(F32)
            store(at, total + self.sums[0, at].astype(F32))
            return carry

        lax.fori_loop(0, self.last_in.shape[1] // 32, one, 0)

    def drain(self):
        for copy in self.pair.values():
            copy.wait_send()
        for copy in [self.relay4, self.relay2] + self.last2 + self.last4:
            copy.wait_send()


def dot(left, right, contract, precision=None):
    return lax.dot_general(
        left, right, (contract, ((), ())), precision=precision, preferred_element_type=F32
    )


def mm(left, right):
    return dot(left, right, ((1,), (0,)))


def mm_t(left, right):
    return dot(left, right, ((1,), (1,)))


def t_mm(left, right):
    return dot(left, right, ((0,), (0,)))


def widen(values, heads, head_size):
    rows = values.shape[0]
    lane = lax.broadcasted_iota(jnp.int32, (rows, 2 * head_size), 1)
    parts = []
    for pair in range(heads // 2):
        low = jnp.broadcast_to(values[:, 2 * pair : 2 * pair + 1], (rows, 2 * head_size))
        high = jnp.broadcast_to(values[:, 2 * pair + 1 : 2 * pair + 2], (rows, 2 * head_size))
        parts.append(jnp.where(lane < head_size, low, high))
    return jnp.concatenate(parts, axis=1)


def head_of_channel(inner, head_size):
    channel = lax.broadcasted_iota(jnp.int32, (inner, 128), 0)
    first = lax.broadcasted_iota(jnp.int32, (inner, 128), 1) * head_size
    return jnp.where((channel >= first) & (channel < first + head_size), 1.0, 0.0)


def sigmoid(values):
    return 0.5 * jnp.tanh(0.5 * values) + 0.5


def in_parts(values, count):
    parts = []
    for _ in range(count):
        parts.append(values.astype(BF16))
        values = values - parts[-1].astype(F32)
    return parts


def softplus(values):
    return jnp.maximum(values, 0.0) + jnp.log1p(jnp.exp(-jnp.abs(values)))


def split_pair(values, head_size):
    lane = lax.broadcasted_iota(jnp.int32, values.shape, 1)
    zero = jnp.zeros_like(values)
    return jnp.where(lane < head_size, values, zero), jnp.where(lane < head_size, zero, values)


def triangles():
    rows = lax.broadcasted_iota(jnp.int32, (CHUNK, CHUNK), 0)
    cols = lax.broadcasted_iota(jnp.int32, (CHUNK, CHUNK), 1)
    return rows >= cols


def triangles_up():
    rows = lax.broadcasted_iota(jnp.int32, (CHUNK, CHUNK), 0)
    cols = lax.broadcasted_iota(jnp.int32, (CHUNK, CHUNK), 1)
    return cols >= rows


def head_decays(cum, cum_t, head, causal):
    gap = cum[:, head : head + 1] - cum_t[head : head + 1, :]
    return jnp.exp(jnp.where(causal, gap, -1e30))


def plane_total(links, sums, landed, peer, count):
    landed[0] = sums[...].T[:count]
    copies = [links.copy(landed.at[0], landed.at[mask], peer[mask]) for mask in peer]
    for copy in copies:
        copy.start()

    def end():
        for copy in copies:
            copy.wait()
        got = [landed[mask] for mask in range(len(peer) + 1)]
        while len(got) > 1:
            got = [got[k] + got[k + 1] for k in range(0, len(got), 2)]
        return got[0]

    return end


def by_column(values):
    return jnp.concatenate([values, jnp.zeros((128 - values.shape[0], CHUNK), F32)], axis=0).T


class Line:
    def __init__(self, links, depth, row, place, blocks, valid=None):
        self.depth, self.row = depth, row
        above, below = lax.min(row + 1, depth - 1), lax.max(row - 1, 0)
        self.steps = []
        for step in range(depth - 1):
            up_sent, up_got = row - step, row - 1 - step
            down_sent, down_got = row + step, row + 1 + step
            ways = []
            for sends, shard, gets, got, device in (
                ((row < depth - 1) & (up_sent >= 0), up_sent, (row > 0) & (up_got >= 0), up_got, above),
                ((row > 0) & (down_sent < depth), down_sent, (row < depth - 1) & (down_got < depth), down_got, below),
            ):
                shard = lax.clamp(0, shard, depth - 1)
                got = lax.clamp(0, got, depth - 1)
                if valid is not None:
                    sends, gets = sends & valid(shard), gets & valid(got)
                copies = [links.copy(block, block, (device, place)) for block in blocks(shard)]
                ways.append((sends, gets, copies))
            self.steps.append(ways)

    def send(self, number):
        for sends, _, copies in self.steps[number]:

            @pl.when(sends)
            def _():
                for copy in copies:
                    copy.start()

    def wait(self, number):
        for _, gets, copies in self.steps[number]:

            @pl.when(gets)
            def _():
                for copy in copies:
                    copy.wait_recv()

    def drain(self):
        for ways in self.steps:
            for sends, _, copies in ways:

                @pl.when(sends)
                def _():
                    for copy in copies:
                        copy.wait_send()


class Pass:
    def __init__(self, links, peer, place, own, everyone, at):
        own = own.at[at]
        rows = own.shape[0] // 2
        mine = everyone.at[place, at]
        from2, from4, far = (everyone.at[peer[mask][1], at] for mask in (2, 4, 6))
        top, low = pl.ds(0, rows), pl.ds(rows, rows)
        self.kept = None
        self.to2 = links.copy(own, mine, peer[2])
        self.to4 = links.copy(own, mine, peer[4])
        self.to1 = links.copy(own, mine, peer[1])
        self.relay4 = links.copy(from2.at[top], from2.at[top], peer[4])
        self.relay2 = links.copy(from4.at[low], from4.at[low], peer[2])
        self.pair2 = links.copy(from2, from2, peer[1])
        self.pair4 = links.copy(from4, from4, peer[1])
        self.pair6 = links.copy(far.at[top], far.at[top], peer[1])
        self.pair7 = links.copy(far.at[low], far.at[low], peer[1])

    def first(self):
        self.to2.start()
        self.to4.start()
        self.to1.start()

    def relay(self):
        self.to2.wait_recv()
        self.relay4.start()
        self.to4.wait_recv()
        self.relay2.start()
        self.pair2.start()
        self.pair4.start()

    def last(self):
        self.relay4.wait_recv()
        self.pair6.start()
        self.relay2.wait_recv()
        self.pair7.start()

    def end(self):
        for copy in (self.to1, self.pair2, self.pair4, self.pair6, self.pair7):
            copy.wait_recv()

    def drain(self):
        for copy in (
            self.to2,
            self.to4,
            self.to1,
            self.relay4,
            self.relay2,
            self.pair2,
            self.pair4,
            self.pair6,
            self.pair7,
        ):
            copy.wait_send()


def lay_out(pieces, row, count):
    tiles = [None] * -(-count * len(pieces) // 128)
    for index, piece in enumerate(pieces):
        tile, shift = divmod(index * count, 128)
        moved = pltpu.roll(piece, shift, 1) if shift else piece
        lane = lax.broadcasted_iota(jnp.int32, piece.shape, 1)
        parts = [(tile, jnp.where((lane >= shift) & (lane < shift + count), moved, 0.0))]
        if shift + count > 128:
            parts.append((tile + 1, jnp.where(lane < shift + count - 128, moved, 0.0)))
        for at, part in parts:
            tiles[at] = part if tiles[at] is None else tiles[at] + part
    return tiles


def channel_windows(ref, place, plane, half, run):
    core, chip = lax.rem(place, 2), lax.div(place, 2)
    parts = []
    for j in range(half):
        start = ((core * half + j) * plane + chip) * run
        base = pl.multiple_of(lax.div(start, 128) * 128, 128)
        window = ref[:, pl.ds(base, run + 64)]
        moved = pltpu.roll(window, run, 1)
        parts.append(jnp.where(lax.rem(start, 128) == 0, window, moved)[:, :run])
    return jnp.concatenate(parts, axis=1)


def head_choice(place, plane, half, group, heads):
    core, chip = lax.rem(place, 2), lax.div(place, 2)
    head = lax.broadcasted_iota(jnp.int32, (128, 128), 0)
    lane = lax.broadcasted_iota(jnp.int32, (128, 128), 1)
    part = sum(((lane >= j * group).astype(jnp.int32) for j in range(1, half)), jnp.zeros_like(lane))
    chosen = ((core * half + part) * plane + chip) * group + lane - part * group
    return jnp.where((head == chosen) & (lane < heads), 1.0, 0.0)


def forward_kernel(
    dims,
    x_own,
    cot_in,
    lengths,
    in_weight,
    wo_own,
    norm_in,
    gate_in,
    conv_w_in,
    conv_b_in,
    dt_bias_in,
    a_log_in,
    d_skip_in,
    normed_out,
    cot_out,
    turned_out,
    wb_out,
    wo_out,
    conv_out,
    pre_out,
    dt_out,
    gate_out,
    y_out,
    states_out,
    norms_out,
    taps_out,
    rows_out,
    w_dt_out,
    x_all,
    normed_all,
    cot_all,
    wg,
    wx,
    wb_far,
    wo,
    packs,
    dt_got,
    turned,
    conv_in,
    pre_all,
    dt_all,
    gate_all,
    y_all,
    states,
    ext,
    state,
    full,
    sums,
    sums_in,
    cot_own,
    wg_send,
    wx_send,
    pack,
    dt_own,
    dt_pack,
    dt_send,
    head_params,
    sends,
    recvs,
    locals_,
    stores,
):
    depth, width, heads, head_size, size, kernel, own_ch, inner_all = dims
    half, plane = depth // 2, width // 2
    inner = heads * head_size
    run = inner // half
    model = x_own.shape[1]
    piece = x_own.shape[0] // 2
    rows = 2 * piece
    slots = 2
    blocks = slots * width // 2
    row, place = lax.axis_index("dp"), lax.axis_index("seq")
    core = lax.rem(place, 2)
    links = Links(sends, recvs)
    peer = {mask: (row, flip_all(place, mask)) for mask in range(1, width)}
    line_peers = [(lax.rem(row + up, depth), place) for up in range(1, depth)]
    in_rows = in_weight.shape[0]
    bc_cols = 2 * inner_all

    def prepare():
        for target, at, to in runs_of(width, half, run):
            wx_send[target, :, at : at + run] = in_weight[:, inner_all + to : inner_all + to + run]
        for target in range(width):
            first = bc_cols + target % 2 * size
            wx_send[target, :, inner:] = in_weight[:, first : first + size]

    greet([peer[mask] for mask in range(1, width)] + line_peers, between=prepare)
    kept = [
        pltpu.make_async_copy(wx_send.at[place], wx.at[row, place], locals_.at[0]),
        pltpu.make_async_copy(dt_send.at[place], dt_got.at[place], locals_.at[1]),
        pltpu.make_async_copy(wg_send.at[place], wg.at[row, place], locals_.at[2]),
        pltpu.make_async_copy(x_own, x_all.at[place], locals_.at[3]),
        pltpu.make_async_copy(cot_own, cot_all.at[place], locals_.at[4]),
        pltpu.make_async_copy(pack, packs.at[row, place], locals_.at[5]),
    ]
    for number in (0, 3):
        kept[number].start()

    out_home = lax.div(row, half) == core
    out_block = wo.at[lax.rem(row, half), core]
    out_kept = pltpu.make_async_copy(wo_own, out_block, locals_.at[6])
    out_pair = links.copy(wo_own, out_block, peer[1])
    order = (6, 2, 4, 7, 3, 5, 1)
    plane_x, plane_g = [], []
    for mask in order:
        target = peer[mask][1]
        plane_x.append(links.copy(wx_send.at[target], wx.at[row, place], peer[mask]))
        plane_g.append(links.copy(wg_send.at[target], wg.at[row, place], peer[mask]))
    for copy in plane_x:
        copy.start()
    pl.when(out_home)(out_kept.start)
    pl.when(jnp.logical_not(out_home))(out_pair.start)
    slot_rows = [pl.ds(slot * piece, piece) for slot in range(slots)]
    x_passes = [Pass(links, peer, place, x_own, x_all, at) for at in slot_rows]
    cot_passes = [Pass(links, peer, place, cot_own, cot_all, at) for at in slot_rows]
    x_passes[0].first()

    dt_own[...] = jnp.zeros_like(dt_own)
    last = in_weight.shape[1]
    dt_own[:, 0 : last - bc_cols - 2 * size] = in_weight[:, bc_cols + 2 * size : last]
    dt_pack[row] = dt_own[...]
    lines = [conv_w_in[...], conv_b_in[...], gate_in[...], norm_in[...]]
    small_rows = jnp.concatenate(
        [jnp.pad(v.astype(F32), ((0, 0), (0, 128 - v.shape[1]))) for v in lines]
        + [jnp.zeros((16 - sum(v.shape[0] for v in lines), 128), F32)],
        axis=0,
    )
    pack[...] = small_rows.astype(BF16)
    pack_line = [links.copy(pack, packs.at[row, place], device) for device in line_peers]
    pack_line += [
        links.copy(dt_own, dt_pack.at[row], device) for device in line_peers
    ]
    for copy in pack_line:
        copy.start()
    kept[5].start()
    head_params[...] = jnp.zeros_like(head_params)
    for k, v in enumerate((dt_bias_in, a_log_in, d_skip_in)):
        head_params[k : k + 1, 0 : v.shape[1]] = v[...]
    for target, at, to in runs_of(width, half, run):
        wg_send[target, :, at : at + run] = in_weight[:, to : to + run]
    kept[2].start()
    token = lax.broadcasted_iota(jnp.int32, (piece, model), 0) + place * piece
    for slot in range(slots):
        live = token < lengths[0:1, slot : slot + 1]
        part = slice(slot * piece, (slot + 1) * piece)
        cot_own[part, :] = jnp.where(live, cot_in[part, :].astype(F32), 0.0).astype(BF16)
    kept[4].start()
    out_line = Line(
        links,
        depth,
        row,
        place,
        lambda shard: [wo.at[lax.rem(shard, half)]],
        lambda shard: lax.div(shard, half) == core,
    )
    x_lines = [
        Line(links, depth, row, place, lambda shard, k=k: [wx.at[shard, pl.ds(k, width // 2)]])
        for k in (0, width // 2)
    ]
    gate_line = Line(links, depth, row, place, lambda shard: [wg.at[shard]])

    pl.when(out_home)(out_kept.wait)
    pl.when(out_home)(out_pair.wait_recv)
    out_line.send(0)
    kept[0].wait()
    for copy in plane_x:
        copy.wait_recv()
    for line in x_lines:
        line.send(0)
    x_passes[1].first()
    kept[5].wait()
    for copy in pack_line:
        copy.wait_recv()
    targets = jnp.concatenate(
        [head_choice(target, plane, half, run // head_size, heads)[:, :16] for target in range(width)],
        axis=1,
    ).astype(BF16)
    dt_rows = dot(targets, dt_pack[...].reshape(depth * in_rows, 128), ((0,), (1,)))
    dt_send[...] = jnp.zeros_like(dt_send)
    dt_send[:, :, 0 : depth * in_rows] = dt_rows.astype(BF16).reshape(width, 16, depth * in_rows)
    kept[1].start()
    mine = packs.at[:, place]
    pack_plane = [links.copy(mine, mine, peer[mask]) for mask in order]
    pack_plane += [
        links.copy(dt_send.at[peer[mask][1]], dt_got.at[place], peer[mask]) for mask in order
    ]
    for copy in pack_plane:
        copy.start()
    x_passes[0].relay()
    for copy in plane_g:
        copy.start()
    for line in x_lines:
        line.wait(0)
        if depth > 2:
            line.send(1)
    x_passes[0].last()
    x_passes[1].relay()
    cot_passes[0].first()

    def normalise(index, carry):
        for part in range(2):
            held = x_all[index, part * piece : (part + 1) * piece, :].astype(F32)
            inv = lax.rsqrt(jnp.mean(held * held, axis=1, keepdims=True) + EPS)
            normed_all[index, part * piece : (part + 1) * piece, :] = (
                held * inv * rows_out[0:1, :]
            ).astype(BF16)
        return carry

    for line in x_lines:
        if depth > 2:
            line.wait(1)
        if depth > 3:
            line.send(2)
    x_passes[1].last()
    cot_passes[1].first()
    kept[1].wait()
    for copy in pack_plane:
        copy.wait_recv()

    small = [
        packs[z, s].astype(F32)[:8]
        for z in range(depth)
        for s in range(width)
    ]
    choice = head_choice(place, plane, half, run // head_size, heads)
    tap_tiles = lay_out(small, 0, own_ch)
    for at, tile in enumerate(tap_tiles):
        full[:, at * 128 : (at + 1) * 128] = tile
    taps_out[:, :inner] = channel_windows(full, place, plane, half, run)
    taps_out[:, inner:] = full[:, inner_all : inner_all + 2 * size]
    gate_tiles = lay_out(small, 5, inner_all // (depth * width))
    for at, tile in enumerate(gate_tiles):
        full[:, at * 128 : (at + 1) * 128] = tile
    gate_gain = channel_windows(full, place, plane, half, run)[5:6]
    norm_tiles = lay_out(small, 6, model // (depth * width))
    norm_gain = jnp.concatenate([tile[6:7] for tile in norm_tiles], axis=1)
    chosen = dot(head_params[...], choice, ((1,), (0,)), lax.Precision.HIGHEST)
    lane = lax.broadcasted_iota(jnp.int32, (1, 128), 1)
    rates = jnp.where(lane < heads, -jnp.exp(chosen[1:2]), 0.0)
    skip = widen(chosen[2:3], heads, head_size)
    dt_tiles = lay_out(
        [
            pltpu.roll(dt_got[s].astype(F32), 256 - z * in_rows, 1)[:, :128]
            if z
            else dt_got[s].astype(F32)[:, :128]
            for z in range(depth)
            for s in range(width)
        ],
        0,
        in_rows,
    )
    w_dt_out[...] = jnp.zeros_like(w_dt_out)
    w_dt_out[0:16, :] = jnp.concatenate(dt_tiles, axis=1).astype(BF16)
    rows_out[...] = jnp.zeros_like(rows_out)
    rows_out[0:1, :] = norm_gain
    rows_out[1:2, :inner] = gate_gain
    rows_out[2:3, :inner] = skip
    rows_out[3:4, :128] = chosen[0:1]
    rows_out[4:5, :128] = rates

    for copy in plane_g:
        copy.wait_recv()
    kept[2].wait()
    if depth > 3:
        x_lines[0].wait(2)
    gate_line.send(0)
    if depth > 3:
        x_lines[1].wait(2)
    near_bc = wx.at[:, :, :, pl.ds(inner, size)]
    pair_bc = links.copy(near_bc, wb_far, peer[1])
    pair_bc.start()
    for each in x_passes:
        each.end()
    kept[3].wait()
    lax.fori_loop(0, width, normalise, 0)
    saves = [pltpu.make_async_copy(normed_all, normed_out, locals_.at[7])]
    saves[0].start()
    pair_bc.wait_recv()

    causal = triangles()
    ones_three = jnp.concatenate([causal.astype(BF16)] * 3, axis=1)

    def stored(index):
        at = pl.ds(pl.multiple_of(index * rows, rows), rows)
        pairs = [
            (conv_in.at[at], conv_out.at[at]),
            (pre_all.at[at], pre_out.at[at]),
            (dt_all.at[at], dt_out.at[at]),
            (y_all.at[at], y_out.at[at]),
            (
                states.at[pl.ds(index * (rows // CHUNK), rows // CHUNK)],
                states_out.at[pl.ds(index * (rows // CHUNK), rows // CHUNK)],
            ),
        ]
        return [
            pltpu.make_async_copy(source, target, stores.at[k, index])
            for k, (source, target) in enumerate(pairs)
        ]

    per_slot = blocks // slots

    def scan_block(index, carry):
        slot, block = lax.div(index, per_slot), lax.rem(index, per_slot)
        at = pl.multiple_of(index * rows, rows)

        @pl.when(block == 0)
        def _():
            ext[0:8, :] = jnp.zeros((8, ext.shape[1]), F32)
            state[...] = jnp.zeros_like(state)

        tokens = normed_all[
            pl.ds(2 * block, 2), pl.ds(pl.multiple_of(slot * piece, piece), piece), :
        ].reshape(rows, model)
        mine = mm(tokens, wx[...].reshape(model, inner + size))
        ext[8:, :inner] = mine[:, :inner]
        ext[8:, pl.ds(pl.multiple_of(inner + core * size, 128), size)] = mine[:, inner:]
        ext[8:, pl.ds(pl.multiple_of(inner + (1 - core) * size, 128), size)] = mm(
            tokens, wb_far[...].reshape(model, size)
        )
        dt_arg = mm_t(tokens, w_dt_out[...]) + rows_out[3:4, :128]
        dt_all[pl.ds(at, rows), :] = dt_arg
        pre = taps_out[kernel : kernel + 1, :] + sum(
            taps_out[k : k + 1, :] * ext[9 - kernel + k : 9 - kernel + k + rows, :]
            for k in range(kernel)
        )
        conv_in[pl.ds(at, rows), :] = ext[8:, :]
        ext[0:8, :] = ext[rows : rows + 8, :]
        pre_all[pl.ds(at, rows), :] = pre
        act = pre * sigmoid(pre)
        dt_block = softplus(dt_arg)
        steps_block = dt_block * rows_out[4:5, :128]
        subs = rows // CHUNK
        parts = [slice(sub * CHUNK, (sub + 1) * CHUNK) for sub in range(subs)]
        x = act[:, :inner]
        b = act[:, inner : inner + size].astype(BF16)
        c = act[:, inner + size :].astype(BF16)
        cums = [
            mm(ones_three, jnp.concatenate(in_parts(steps_block[part], 3), axis=0))
            for part in parts
        ]
        lasts = [cum[CHUNK - 1 : CHUNK, :] for cum in cums]
        x_dt = x * widen(dt_block, heads, head_size)
        x_dt16 = x_dt.astype(BF16)
        cum_wide = widen(jnp.exp(jnp.concatenate(cums, axis=0)), heads, head_size)
        out_wide = widen(
            jnp.exp(jnp.concatenate([last - cum for last, cum in zip(lasts, cums)], axis=0)),
            heads,
            head_size,
        )
        weighted = (x_dt * out_wide).astype(BF16)
        near, read = [], []
        for sub, part in enumerate(parts):
            cum_t = cums[sub].T
            cb = mm_t(c[part], b[part])
            pieces = []
            for pair in range(heads // 2):
                lanes = slice(2 * pair * head_size, 2 * (pair + 1) * head_size)
                mixing = jnp.concatenate(
                    [
                        (head_decays(cums[sub], cum_t, 2 * pair + k, causal) * cb).astype(BF16)
                        for k in range(2)
                    ],
                    axis=1,
                )
                pieces.append(
                    mm(
                        mixing,
                        jnp.concatenate(split_pair(x_dt16[part, lanes], head_size), axis=0),
                    )
                )
            near.append(jnp.concatenate(pieces, axis=1))
        for sub, part in enumerate(parts):
            held = state[...]
            held16 = held.astype(BF16)
            states[index * subs + sub] = held16
            read.append(mm(c[part], held16))
            state[...] = held * widen(jnp.exp(lasts[sub]), heads, head_size) + t_mm(
                b[part], weighted[part]
            )
        y_all[pl.ds(at, rows), :] = (
            jnp.concatenate(near, axis=0)
            + jnp.concatenate(read, axis=0) * cum_wide
            + rows_out[2:3, :inner] * x
        )
        for copy in stored(index):
            copy.start()

        @pl.when(index == 1)
        def _():
            gate_line.wait(0)
            gate_line.send(1) if depth > 2 else None
            out_line.wait(0)
            out_line.send(1) if depth > 2 else None

        @pl.when(index == 2)
        def _():
            cot_passes[0].relay()
            cot_passes[1].relay()

        @pl.when(index == 4)
        def _():
            gate_line.wait(1) if depth > 2 else None
            gate_line.send(2) if depth > 3 else None
            out_line.wait(1) if depth > 2 else None
            out_line.send(2) if depth > 3 else None

        @pl.when(index == 5)
        def _():
            cot_passes[0].last()
            cot_passes[1].last()

        @pl.when(index == 6)
        def _():
            gate_line.wait(2) if depth > 3 else None

        return carry

    lax.fori_loop(0, blocks, scan_block, 0)

    chunk_lane = lax.broadcasted_iota(jnp.int32, (CHUNK, 128), 1)
    sums[...] = jnp.zeros_like(sums)

    def gate_block(index, carry):
        slot, block = lax.div(index, per_slot), lax.rem(index, per_slot)
        at = pl.multiple_of(index * rows, rows)
        tokens = normed_all[
            pl.ds(2 * block, 2), pl.ds(pl.multiple_of(slot * piece, piece), piece), :
        ].reshape(rows, model)
        gate = mm(tokens, wg[...].reshape(model, inner))
        gate_all[pl.ds(at, rows), :] = gate
        gated = y_all[pl.ds(at, rows), :] * (gate * sigmoid(gate))
        for sub in range(rows // CHUNK):
            part = gated[sub * CHUNK : (sub + 1) * CHUNK]
            total = jnp.sum(part * part, axis=1, keepdims=True)
            sums[...] = jnp.where(chunk_lane == index * (rows // CHUNK) + sub, total, sums[...])
        return carry

    lax.fori_loop(0, blocks, gate_block, 0)
    squares = plane_total(links, sums, sums_in, peer, 2 * blocks)
    save_gate = pltpu.make_async_copy(gate_all, gate_out, locals_.at[8])
    save_gate.start()
    wg_flat, wx_flat = wg[...].reshape(model, inner), wx[...].reshape(model, inner + size)
    for at in range(0, model, 128):
        turned[:inner, at : at + 128] = wg_flat[at : at + 128, :].T
        turned[inner:, at : at + 128] = wx_flat[at : at + 128, :inner].T
    save_weights = [
        pltpu.make_async_copy(source, target, locals_.at[10 + k])
        for k, (source, target) in enumerate(
            (
                (turned, turned_out),
                (near_bc, wb_out.at[core]),
                (wb_far, wb_out.at[1 - core]),
                (wo, wo_out),
            )
        )
    ]
    for copy in save_weights[:3]:
        copy.start()
    kept[4].wait()
    save_cot = [
        pltpu.make_async_copy(cot_all.at[:, at], cot_out.at[:, at], locals_.at[9 + 5 * k])
        for k, at in enumerate(slot_rows)
    ]
    for each, copy in zip(cot_passes, save_cot):
        each.end()
        copy.start()
    if depth > 3:
        out_line.wait(2)
    save_weights[3].start()
    inv_gate = lax.rsqrt(squares() / inner_all + EPS)
    norms_out[...] = by_column(inv_gate)

    for copies in (plane_x, plane_g, pack_line, pack_plane, [pair_bc]):
        for copy in copies:
            copy.wait_send()
    pl.when(jnp.logical_not(out_home))(out_pair.wait_send)
    for line in [out_line, gate_line] + x_lines:
        line.drain()
    for each in x_passes + cot_passes:
        each.drain()
    for copy in saves + [save_gate] + save_cot + save_weights:
        copy.wait()

    def stores_end(index, carry):
        for copy in stored(index):
            copy.wait()
        return carry

    lax.fori_loop(0, blocks, stores_end, 0)


def forward(dims, arrays, collective):
    depth, width, heads, head_size, size, kernel, own_ch, inner_all = dims
    inner = heads * head_size
    x_own, _, _, in_weight, wo_own = arrays[:5]
    rows, model = x_own.shape
    in_rows = in_weight.shape[0]
    tokens = rows * width
    wide = inner + 2 * size
    shape = jax.ShapeDtypeStruct
    chunks = tokens // CHUNK
    weights = [
        ((depth, width, in_rows, inner), BF16),
        ((depth, width, in_rows, inner + size), BF16),
        ((depth, width, in_rows, size), BF16),
        ((depth // 2, 2) + wo_own.shape, BF16),
    ]
    passed = [
        ((2 * inner, model), BF16),
        ((2, depth, width, in_rows, size), BF16),
        ((depth // 2, 2) + wo_own.shape, BF16),
    ]
    kept = [
        ((tokens, wide), F32),
        ((tokens, wide), F32),
        ((tokens, 128), F32),
        ((tokens, inner), F32),
        ((tokens, inner), F32),
        ((chunks, size, inner), BF16),
    ]
    in_hbm = [((width, rows, model), BF16)] * 2 + passed + kept
    in_vmem = [((CHUNK, 128), F32), ((8, wide), F32), ((8, model), F32), ((128, model), BF16)]
    return pl.pallas_call(
        functools.partial(forward_kernel, dims),
        out_shape=tuple(shape(*s) for s in in_hbm + in_vmem),
        in_specs=[INVMEM] * len(arrays),
        out_specs=(ANY,) * len(in_hbm) + (INVMEM,) * len(in_vmem),
        scratch_shapes=[pltpu.VMEM((width, rows, model), BF16)] * 3
        + [pltpu.VMEM(*s) for s in weights]
        + [
            pltpu.VMEM((depth, width, 16, 128), BF16),
            pltpu.VMEM((width, 16, 256), BF16),
            pltpu.VMEM((2 * inner, model), BF16),
        ]
        + [pltpu.VMEM(*s) for s in kept]
        + [
            pltpu.VMEM((rows + 8, wide), F32),
            pltpu.VMEM((size, inner), F32),
            pltpu.VMEM((8, -(-own_ch * depth * width // 128) * 128), F32),
            pltpu.VMEM((CHUNK, 128), F32),
            pltpu.VMEM((width, chunks, 128), F32),
            pltpu.VMEM((rows, model), BF16),
            pltpu.VMEM((width, in_rows, inner), BF16),
            pltpu.VMEM((width, in_rows, inner + size), BF16),
            pltpu.VMEM((16, 128), BF16),
            pltpu.VMEM((in_rows, 128), BF16),
            pltpu.VMEM((depth, in_rows, 128), BF16),
            pltpu.VMEM((width, 16, 256), BF16),
            pltpu.VMEM((8, 128), F32),
            pltpu.SemaphoreType.DMA((160,)),
            pltpu.SemaphoreType.DMA((160,)),
            pltpu.SemaphoreType.DMA((16,)),
            pltpu.SemaphoreType.DMA((5, tokens // rows)),
        ],
        compiler_params=pltpu.CompilerParams(
            collective_id=collective, has_side_effects=True, vmem_limit_bytes=VMEM_LIMIT
        ),
        name="forward_fused",
    )(*arrays)


class PlaneRows:
    def __init__(self, links, row, place, parts, landed, at, local):
        mine = landed.at[place, :, at]
        peers = [(row, flip_all(place, mask)) for mask in (6, 7, 2, 3, 4, 5, 1)]
        self.copies = [links.copy(parts.at[peer[1], :, at], mine, peer) for peer in peers]
        self.kept = pltpu.make_async_copy(parts.at[place, :, at], mine, local)

    def begin(self):
        for copy in self.copies:
            copy.start()
        self.kept.start()

    def end(self):
        self.kept.wait()
        for copy in self.copies:
            copy.wait()


class SendBack:
    def __init__(self, links, row, place, sent, back, local):
        self.rows = back.shape[1]
        self.sent, self.back, self.place = sent, back, place
        mine = back.at[place]
        self.copies = [
            links.copy(self.block((row, flip_all(place, mask))[1]), mine, (row, flip_all(place, mask)))
            for mask in (6, 2, 4, 7, 3, 5, 1)
        ]
        self.kept = pltpu.make_async_copy(self.block(place), mine, local)

    def block(self, target):
        return self.sent.at[pl.ds(pl.multiple_of(target * self.rows, self.rows), self.rows)]

    def begin(self):
        for copy in self.copies:
            copy.start()
        self.kept.start()

    def end(self):
        self.kept.wait()
        for copy in self.copies:
            copy.wait()


def turn(target, source):
    for at in range(0, source.shape[0], 128):
        target[:, at : at + 128] = source[at : at + 128, :].T.astype(target.dtype)


def reverse_kernel(
    dims,
    cot_hbm,
    normed_hbm,
    gate_hbm,
    y_hbm,
    pre_hbm,
    conv_hbm,
    dt_hbm,
    states_hbm,
    wo_hbm,
    norms,
    taps,
    rows_in,
    x_own,
    d_gate_hbm,
    d_x_hbm,
    d_arg_hbm,
    output,
    gate_back,
    out_grad,
    channel_sums,
    head_sums,
    bc_landed,
    cot_all,
    normed_all,
    gate_all,
    y_all,
    d_y_all,
    wo,
    d_gate,
    d_x_all,
    d_arg_all,
    d_bc,
    g_out,
    g_gate,
    pre_two,
    conv_two,
    dt_two,
    states_two,
    later,
    d_ext,
    o_pair,
    o_sums,
    o_relay,
    o_last,
    out_up_in,
    out_up_out,
    out_down_in,
    out_down_out,
    gate_up_in,
    gate_up_out,
    gate_down_in,
    gate_down_out,
    out_sum,
    out_far,
    gate_sum,
    gate_sent,
    means,
    sums_in,
    sends,
    recvs,
    locals_,
    streams,
):
    depth, width, heads, head_size, size, kernel, own_ch, inner_all = dims
    half = depth // 2
    inner = heads * head_size
    model = cot_all.shape[2]
    piece = cot_all.shape[1] // 2
    rows = 2 * piece
    slots = 2
    blocks = slots * width // 2
    per_slot = blocks // slots
    subs = rows // CHUNK
    row, place = lax.axis_index("dp"), lax.axis_index("seq")
    core = lax.rem(place, 2)
    links = Links(sends, recvs)
    above, below = lax.min(row + 1, depth - 1), lax.max(row - 1, 0)
    peer = {mask: (row, flip_all(place, mask)) for mask in range(1, width)}

    loads = [
        pltpu.make_async_copy(source, target, locals_.at[k])
        for k, (source, target) in enumerate(
            (
                (y_hbm, y_all),
                (gate_hbm, gate_all),
                (cot_hbm, cot_all),
                (wo_hbm, wo),
                (normed_hbm, normed_all),
            )
        )
    ]
    for copy in loads:
        copy.start()

    def place_of(number):
        slot = lax.div(number, per_slot)
        return slot, per_slot - 1 - lax.rem(number, per_slot)

    def fetch(number):
        slot, block = place_of(number)
        index = slot * per_slot + block
        at = pl.ds(pl.multiple_of(index * rows, rows), rows)
        buffer = lax.rem(number, 2)
        pairs = (
            (pre_hbm.at[at], pre_two.at[buffer]),
            (conv_hbm.at[at, pl.ds(0, inner)], conv_two.at[buffer]),
            (dt_hbm.at[at], dt_two.at[buffer]),
            (states_hbm.at[pl.ds(index * subs, subs)], states_two.at[buffer]),
        )
        return [
            pltpu.make_async_copy(source, target, streams.at[buffer, k])
            for k, (source, target) in enumerate(pairs)
        ]

    for copy in fetch(0):
        copy.start()
    greet(
        [peer[mask] for mask in range(1, width)],
        [(row < depth - 1, (above, place)), (row > 0, (below, place))],
    )

    out_line = LineSum(
        links,
        depth,
        row,
        place,
        lambda q: g_out.at[pl.ds((q % half) * (inner // half), inner // half)],
        lambda q: core == q // half,
        out_up_in,
        out_up_out,
        out_down_in,
        out_down_out,
        half,
    )
    cols = model // depth
    gate_line = LineSum(
        links,
        depth,
        row,
        place,
        lambda q: g_gate.at[:, pl.ds(q * cols, cols)],
        lambda q: row >= 0,
        gate_up_in,
        gate_up_out,
        gate_down_in,
        gate_down_out,
    )
    o_plane = PlaneSum(links, row, place, cot_all, o_pair, o_sums, o_relay, o_last)
    send_gate = SendBack(links, row, place, gate_sent, gate_back, locals_.at[6])

    chunk_lane = lax.broadcasted_iota(jnp.int32, (CHUNK, 128), 1)

    def column(ref, index):
        parts = [
            jnp.sum(
                jnp.where(chunk_lane == index * subs + sub, ref[...], 0.0),
                axis=1,
                keepdims=True,
            )
            for sub in range(subs)
        ]
        return jnp.concatenate(parts, axis=0)

    def tokens_of(ref, index):
        slot, block = lax.div(index, per_slot), lax.rem(index, per_slot)
        return ref.at[pl.ds(2 * block, 2), pl.ds(pl.multiple_of(slot * piece, piece), piece), :]

    gate_gain = rows_in[1:2, :inner]
    skip = rows_in[2:3, :inner]

    def normed_block(index, carry):
        at = pl.ds(pl.multiple_of(index * rows, rows), rows)
        gate = gate_all[at, :]
        hat = y_all[at, :] * (gate * sigmoid(gate)) * column(norms, index)
        tokens_of(d_gate, index)[...] = (
            (hat * gate_gain).astype(BF16).reshape(2, piece, inner)
        )
        return carry

    loads[0].wait()
    loads[1].wait()
    lax.fori_loop(0, blocks, normed_block, 0)

    everything = slots * width * piece

    def out_grad_tile(number, carry):
        at = pl.ds(pl.multiple_of(number * 128, 128), 128)
        left = d_gate[:, :, at].reshape(everything, 128)
        g_out[at, :] = t_mm(left, cot_all[...].reshape(everything, model))
        return carry

    loads[2].wait()
    lax.fori_loop(0, inner // 128, out_grad_tile, 0)
    out_line.phase(0)

    def cot_block(index, carry):
        at = pl.ds(pl.multiple_of(index * rows, rows), rows)
        tokens = tokens_of(cot_all, index)[...].reshape(rows, model)
        dgn = mm_t(tokens, wo[...].reshape(inner, model))
        d_y_all[at, :] = dgn
        gate = gate_all[at, :]
        cross = dgn * gate_gain * y_all[at, :] * (gate * sigmoid(gate))
        for sub in range(subs):
            part = cross[sub * CHUNK : (sub + 1) * CHUNK]
            total = jnp.sum(part, axis=1, keepdims=True)
            means[...] = jnp.where(chunk_lane == index * subs + sub, total, means[...])
        return carry

    loads[3].wait()
    means[...] = jnp.zeros_like(means)
    lax.fori_loop(0, blocks, cot_block, 0)
    crosses = plane_total(links, means, sums_in, peer, 2 * blocks)

    def out_block(index):
        cot_all[index] = mm(d_gate[index], wo[...].reshape(inner, model)).astype(BF16)

    def for_pair(mask):
        out_block(peer[mask ^ 1][1])
        o_plane.pair[mask].start()

    for_pair(6)
    out_block(peer[6][1])
    for_pair(2)
    out_block(peer[2][1])
    o_plane.far()
    for_pair(4)
    out_block(peer[4][1])
    o_plane.near(2)
    for_pair(0)
    out_block(place)
    o_plane.near(4)
    if depth > 2:
        out_line.phase(1)
    means[...] = norms[...] * by_column(crosses() / inner_all)

    def gate_block(index, carry):
        at = pl.ds(pl.multiple_of(index * rows, rows), rows)
        gate = gate_all[at, :]
        sig = sigmoid(gate)
        gate_act = gate * sig
        y = y_all[at, :]
        inv = column(norms, index)
        hat = y * gate_act * inv
        d_gated = inv * (d_y_all[at, :] * gate_gain - hat * column(means, index))
        d_y_all[at, :] = d_gated * gate_act
        tokens_of(d_gate, index)[...] = (
            (d_gated * y * sig * (1.0 + gate * (1.0 - sig))).astype(BF16).reshape(2, piece, inner)
        )
        return carry

    lax.fori_loop(0, blocks, gate_block, 0)
    save_gate = pltpu.make_async_copy(d_gate, d_gate_hbm, locals_.at[7])
    save_gate.start()

    def gate_grad_tile(number, carry):
        at = pl.ds(pl.multiple_of(number * 128, 128), 128)
        left = d_gate[:, :, at].reshape(everything, 128)
        g_gate[at, :] = t_mm(left, normed_all[...].reshape(everything, model))
        return carry

    loads[4].wait()
    lax.fori_loop(0, inner // 128, gate_grad_tile, 0)
    gate_line.phase(0)
    o_plane.near(0)

    channel_sums[...] = jnp.zeros_like(channel_sums)
    head_sums[...] = jnp.zeros_like(head_sums)
    causal = triangles()
    ones = causal.astype(BF16)
    ones_three = jnp.concatenate([ones] * 3, axis=1)
    after = jnp.where(triangles_up(), 1.0, 0.0).astype(BF16)
    before = jnp.where(triangles_up(), 0.0, 1.0).astype(BF16)
    both_ways = jnp.concatenate([after, before] * 2, axis=1)
    of_head = head_of_channel(inner, head_size).astype(BF16)

    def head_totals(values):
        high, low = in_parts(values, 2)
        return mm(high, of_head) + mm(low, of_head)

    home = lax.div(row, half) == core
    rows_out = out_grad.shape[0]
    far = links.copy(out_far, out_grad, peer[1])

    def pump_gate():
        if depth > 2:
            gate_line.phase(1)

    def pump_gate_last():
        if depth > 3:
            gate_line.phase(2)

    def pump_out():
        out_line.finish(out_sum)
        for this in range(2):

            @pl.when(home & (core == this))
            def _():
                cast_rows(out_far, out_sum.at[pl.ds((1 - this) * rows_out, rows_out)])
                far.start()
                cast_rows(out_grad, out_sum.at[pl.ds(this * rows_out, rows_out)])

    def pump_back():
        gate_line.finish(gate_sum)
        turn(gate_sent, gate_sum)
        send_gate.begin()

    quarter = everything // 4
    bc_rows = [
        PlaneRows(
            links,
            row,
            place,
            d_bc,
            bc_landed,
            pl.ds(first, count),
            locals_.at[10 + k],
        )
        for k, (first, count) in enumerate(
            (
                (quarter, quarter),
                (0, quarter),
                (3 * quarter, quarter),
                (2 * quarter + quarter // 2, quarter // 2),
                (2 * quarter, quarter // 2),
            )
        )
    ]

    def pump_out_last():
        if depth > 3:
            out_line.phase(2)

    pumps = {
        0: [o_plane.second, pump_out_last],
        1: [bc_rows[0].begin],
        2: [pump_gate],
        3: [bc_rows[1].begin, pump_out],
        4: [pump_gate_last],
        5: [bc_rows[2].begin, lambda: o_plane.finish(store_output)],
        6: [bc_rows[3].begin],
        7: [pump_back],
    }

    def store_output(at, total):
        output[at] = (x_own[at].astype(F32) + total).astype(BF16)

    def scan_block(number, carry):
        slot, block = place_of(number)
        index = slot * per_slot + block
        buffer = lax.rem(number, 2)
        for copy in fetch(number):
            copy.wait()

        @pl.when(number + 1 < blocks)
        def _():
            for copy in fetch(number + 1):
                copy.start()

        @pl.when(block == per_slot - 1)
        def _():
            later[...] = jnp.zeros_like(later)
            d_ext[rows:, :] = jnp.zeros((8, inner), F32)

        pre = pre_two[buffer]
        pre_sig = sigmoid(pre)
        act = pre * pre_sig
        slope = pre_sig[:, :inner] * (1.0 + pre[:, :inner] * (1.0 - pre_sig[:, :inner]))
        dt_arg = dt_two[buffer]
        dt_block = softplus(dt_arg)
        rates = rows_in[4:5, :128]
        steps_block = dt_block * rates
        parts = [slice(sub * CHUNK, (sub + 1) * CHUNK) for sub in range(subs)]
        at = pl.ds(pl.multiple_of(index * rows, rows), rows)
        x = act[:, :inner]
        b = act[:, inner : inner + size].astype(BF16)
        c = act[:, inner + size :].astype(BF16)
        cums = [
            mm(ones_three, jnp.concatenate(in_parts(steps_block[part], 3), axis=0))
            for part in parts
        ]
        lasts = [cum[CHUNK - 1 : CHUNK, :] for cum in cums]
        dt_wide = widen(dt_block, heads, head_size)
        cum_wide = widen(jnp.exp(jnp.concatenate(cums, axis=0)), heads, head_size)
        out_wide = widen(
            jnp.exp(jnp.concatenate([last - cum for last, cum in zip(lasts, cums)], axis=0)),
            heads,
            head_size,
        )
        x_dt = x * dt_wide
        x_dt16 = x_dt.astype(BF16)
        d_y = d_y_all[at, :]
        d_y16 = d_y.astype(BF16)
        d_read = (d_y * cum_wide).astype(BF16)
        sent = (x_dt * out_wide).astype(BF16)
        near, d_cbs = [], []
        for sub, part in enumerate(parts):
            cum_t = cums[sub].T
            cb = mm_t(c[part], b[part])
            d_cb = jnp.zeros((CHUNK, CHUNK), F32)
            pieces = []
            for pair in range(heads // 2):
                lanes = slice(2 * pair * head_size, 2 * (pair + 1) * head_size)
                d_y_split = split_pair(d_y16[part, lanes], head_size)
                mixing = []
                for k in range(2):
                    decay = head_decays(cums[sub], cum_t, 2 * pair + k, causal)
                    mixing.append((decay * cb).astype(BF16))
                    d_cb = d_cb + decay * mm_t(d_y_split[k], x_dt16[part, lanes])
                pieces.append(
                    t_mm(jnp.concatenate(mixing, axis=0), jnp.concatenate(d_y_split, axis=0))
                )
            near.append(jnp.concatenate(pieces, axis=1))
            d_cbs.append(d_cb.astype(BF16))
        later_rows, overs = [None] * subs, [None] * subs
        for sub in reversed(range(subs)):
            part = parts[sub]
            held16 = states_two[buffer, sub]
            grown = later[...]
            grown16 = grown.astype(BF16)
            later_rows[sub] = mm(b[part], grown16)
            column_at = pl.ds(pl.multiple_of(index * rows + sub * CHUNK, CHUNK), CHUNK)
            d_b = mm_t(grown16, sent[part]) + t_mm(c[part], d_cbs[sub])
            d_c = mm_t(held16, d_read[part]) + dot(b[part], d_cbs[sub], ((0,), (1,)))
            for first, value in ((0, d_b), (width // 2, d_c)):
                d_bc[first : first + width // 2, :, column_at] = value.astype(BF16).reshape(
                    width // 2, 2 * size // width, CHUNK
                )
            overs[sub] = jnp.sum(grown * held16.astype(F32), axis=0, keepdims=True)
            later[...] = grown * widen(jnp.exp(lasts[sub]), heads, head_size) + t_mm(
                c[part], d_read[part]
            )
        d_x_near = jnp.concatenate(near, axis=0)
        d_x_later = out_wide * jnp.concatenate(later_rows, axis=0)
        d_x_dt = d_x_later + d_x_near
        d_x = d_x_dt * dt_wide + skip * d_y
        d_ext[0:rows, :] = d_x * slope
        channel_sums[5:6, :] += jnp.sum(d_y * x, axis=0, keepdims=True)
        cross_wide = d_y16.astype(F32) * (y_all[at, :] - skip * x) - x_dt16.astype(F32) * d_x_near
        over_wide = jnp.concatenate(overs + [jnp.zeros((8 - subs, inner), F32)], axis=0)
        d_dt_direct = mm((x * d_x_dt).astype(BF16), of_head)
        d_cum = head_totals(cross_wide)
        through = mm((x_dt * d_x_later).astype(BF16), of_head)
        over = head_totals(over_wide)
        d_log = jnp.concatenate(
            [
                mm(
                    both_ways,
                    jnp.concatenate(
                        in_parts(jnp.concatenate([d_cum[part], through[part]], axis=0), 2), axis=0
                    ),
                )
                + over[sub : sub + 1] * jnp.exp(lasts[sub])
                for sub, part in enumerate(parts)
            ],
            axis=0,
        )
        d_arg = (d_dt_direct + rates * d_log) * sigmoid(dt_arg)
        d_arg_all[
            pl.ds(2 * block, 2), pl.ds(pl.multiple_of(slot * piece, piece), piece), :
        ] = d_arg.astype(BF16).reshape(2, piece, 128)
        head_sums[0:1, :] += jnp.sum(d_arg, axis=0, keepdims=True)
        head_sums[1:2, :] += jnp.sum(d_log * dt_block, axis=0, keepdims=True) * rates

        d_conv = jnp.zeros((rows, inner), F32)
        x_in = conv_two[buffer]
        for k in range(kernel):
            moved = d_ext[kernel - 1 - k : kernel - 1 - k + rows, :]
            d_conv = d_conv + taps[k : k + 1, :inner] * moved
            channel_sums[k : k + 1, :] += jnp.sum(moved * x_in, axis=0, keepdims=True)
        channel_sums[4:5, :] += jnp.sum(d_ext[0:rows, :], axis=0, keepdims=True)
        d_x_all[
            pl.ds(2 * block, 2), pl.ds(pl.multiple_of(slot * piece, piece), piece), :
        ] = d_conv.astype(BF16).reshape(2, piece, inner)
        d_ext[rows:, :] = d_ext[0:8, :]

        for at_step, actions in pumps.items():

            @pl.when(number == at_step)
            def _():
                for action in actions:
                    action()

        return carry

    lax.fori_loop(0, blocks, scan_block, 0)
    bc_rows[4].begin()
    saves = [
        pltpu.make_async_copy(source, target, locals_.at[8 + k])
        for k, (source, target) in enumerate(
            ((d_x_all, d_x_hbm), (d_arg_all, d_arg_hbm))
        )
    ]
    for copy in saves:
        copy.start()

    pl.when(jnp.logical_not(home))(far.wait_recv)
    pl.when(home)(far.wait_send)
    o_plane.drain()
    out_line.drain()
    gate_line.drain()
    send_gate.end()
    save_gate.wait()
    for copy in saves:
        copy.wait()
    for rows_ in bc_rows:
        rows_.end()


def line_buffers(count, extent):
    return [pltpu.VMEM((count,) + extent, BF16)] * 4


def plane_buffers(rows, model):
    return [
        pltpu.VMEM((4, rows, model), BF16),
        pltpu.VMEM((4, rows, model), BF16),
        pltpu.VMEM((2, rows // 2, model), BF16),
        pltpu.VMEM((2, rows, model), BF16),
    ]


def reverse(dims, hbm, vmem, collective):
    depth, width, heads, head_size, size, kernel, own_ch, inner_all = dims
    inner = heads * head_size
    _, rows, model = hbm[0].shape
    tokens = rows * width
    wide = inner + 2 * size
    shape = jax.ShapeDtypeStruct
    subs = rows // CHUNK
    half = depth // 2
    out_piece, in_piece = (inner // half, model), (inner, model // depth)
    saved = [
        ((width, rows, inner), BF16),
        ((width, rows, inner), BF16),
        ((width, rows, 128), BF16),
    ]
    bc = ((width, 2 * size // width, tokens), BF16)
    kept = [
        ((rows, model), BF16),
        ((width, model // depth // width, inner), BF16),
        ((out_piece[0] // 2, model), F32),
        ((8, inner), F32),
        ((8, 128), F32),
        bc,
    ]
    return pl.pallas_call(
        functools.partial(reverse_kernel, dims),
        out_shape=tuple(shape(*s) for s in saved + kept),
        in_specs=[ANY] * len(hbm) + [INVMEM] * len(vmem),
        out_specs=(ANY,) * len(saved) + (INVMEM,) * len(kept),
        scratch_shapes=[pltpu.VMEM((width, rows, model), BF16)] * 2
        + [pltpu.VMEM((tokens, inner), F32)] * 3
        + [pltpu.VMEM(hbm[-1].shape, BF16)]
        + [pltpu.VMEM(*s) for s in saved]
        + [
            pltpu.VMEM(*bc),
            pltpu.VMEM((inner, model), F32),
            pltpu.VMEM((inner, model), F32),
            pltpu.VMEM((2, rows, wide), F32),
            pltpu.VMEM((2, rows, inner), F32),
            pltpu.VMEM((2, rows, 128), F32),
            pltpu.VMEM((2, subs, size, inner), BF16),
            pltpu.VMEM((size, inner), F32),
            pltpu.VMEM((rows + 8, inner), F32),
        ]
        + plane_buffers(rows, model)
        + line_buffers(half, out_piece)
        + line_buffers(depth - 1, in_piece)
        + [
            pltpu.VMEM(out_piece, F32),
            pltpu.VMEM((out_piece[0] // 2, model), F32),
            pltpu.VMEM(in_piece, F32),
            pltpu.VMEM((in_piece[1], in_piece[0]), BF16),
            pltpu.VMEM((CHUNK, 128), F32),
            pltpu.VMEM((width, tokens // CHUNK, 128), F32),
            pltpu.SemaphoreType.DMA((80,)),
            pltpu.SemaphoreType.DMA((80,)),
            pltpu.SemaphoreType.DMA((15,)),
            pltpu.SemaphoreType.DMA((2, 4)),
        ],
        compiler_params=pltpu.CompilerParams(
            collective_id=collective, has_side_effects=True, vmem_limit_bytes=VMEM_LIMIT
        ),
        name="reverse_fused",
    )(*hbm, *vmem)


def runs_of(width, half, run):
    plane = width // 2
    for place in range(width):
        for j in range(half):
            yield place, j * run, (((place % 2) * half + j) * plane + place // 2) * run


def head_places(place, half, plane, group, heads, shift):
    lane = lax.broadcasted_iota(jnp.int32, (128, 128), 0) - shift
    head = lax.broadcasted_iota(jnp.int32, (128, 128), 1)
    part = sum(((lane >= j * group).astype(jnp.int32) for j in range(1, half)), jnp.zeros_like(lane))
    chosen = ((place % 2 * half + part) * plane + place // 2) * group + lane - part * group
    return jnp.where((head == chosen) & (lane >= 0) & (lane < heads), 1.0, 0.0)


def weights_kernel(
    dims,
    d_x_hbm,
    normed_hbm,
    turned_hbm,
    d_gate_hbm,
    pre_hbm,
    conv_hbm,
    d_arg_hbm,
    wb_hbm,
    cot_hbm,
    bc_landed,
    taps,
    channel_sums,
    head_sums,
    rows_in,
    x_own,
    w_dt,
    gate_back,
    input_grad,
    in_grad,
    smalls,
    d_x,
    normed_all,
    d_gate,
    pre_own,
    conv_own,
    d_arg,
    wb,
    cot_own,
    w_turned,
    d_small,
    g_x,
    g_small,
    d_parts,
    d_ext,
    bc_sums,
    d_pair,
    d_sums,
    d_relay,
    d_last,
    x_up_in,
    x_up_out,
    x_down_in,
    x_down_out,
    small_up_in,
    small_up_out,
    small_down_in,
    small_down_out,
    x_sum,
    x_sent,
    small_sum,
    small_sent,
    x_back,
    small_back,
    sums_own,
    sums_line,
    sums_all,
    full,
    sends,
    recvs,
    locals_,
):
    depth, width, heads, head_size, size, kernel, own_ch, inner_all = dims
    half, plane = depth // 2, width // 2
    inner = heads * head_size
    run = inner // half
    group = run // head_size
    model = normed_all.shape[2]
    piece = normed_all.shape[1] // 2
    rows = 2 * piece
    slots = 2
    blocks = slots * width // 2
    per_slot = blocks // slots
    everything = slots * width * piece
    own = 2 * size // width
    row, place = lax.axis_index("dp"), lax.axis_index("seq")
    links = Links(sends, recvs)
    peer = {mask: (row, flip_all(place, mask)) for mask in range(1, width)}
    order = (6, 2, 4, 7, 3, 5, 1)
    per_block = 128 // own
    bc_turn = 128 - own * lax.rem(place, per_block)
    window = pl.ds(pl.multiple_of(inner + lax.div(place, per_block) * 128, 128), 128)

    loads = [
        pltpu.make_async_copy(source, target, locals_.at[k])
        for k, (source, target) in enumerate(
            (
                (d_x_hbm, d_x),
                (normed_hbm, normed_all),
                (turned_hbm, w_turned.at[pl.ds(0, 2 * inner)]),
                (d_gate_hbm, d_gate),
                (pre_hbm.at[:, window], pre_own),
                (conv_hbm.at[:, window], conv_own),
                (d_arg_hbm, d_arg),
                (wb_hbm, wb),
                (cot_hbm.at[place], cot_own),
            )
        )
    ]
    for copy in loads:
        copy.start()
    line_peers = [(lax.rem(row + up, depth), place) for up in range(1, depth)]
    greet([peer[mask] for mask in range(1, width)] + line_peers)

    cols = model // depth

    def line(own_ref, buffers):
        return LineSum(
            links,
            depth,
            row,
            place,
            lambda q: own_ref.at[:, pl.ds(q * cols, cols)],
            lambda q: row >= 0,
            *buffers,
        )

    x_line = line(g_x, (x_up_in, x_up_out, x_down_in, x_down_out))
    small_line = line(g_small, (small_up_in, small_up_out, small_down_in, small_down_out))
    d_plane = PlaneSum(links, row, place, d_parts, d_pair, d_sums, d_relay, d_last)
    send_x = SendBack(links, row, place, x_sent, x_back, locals_.at[12])
    send_small = SendBack(links, row, place, small_sent, small_back, locals_.at[13])

    def x_grad_tile(number, carry):
        at = pl.ds(pl.multiple_of(number * 128, 128), 128)
        left = d_x[:, :, at].reshape(everything, 128)
        g_x[at, :] = t_mm(left, normed_all[...].reshape(everything, model))
        return carry

    loads[0].wait()
    loads[1].wait()
    lax.fori_loop(0, inner // 128, x_grad_tile, 0)
    x_line.phase(0)

    lane = lax.broadcasted_iota(jnp.int32, (1, 128), 1)
    mine = lane < own

    def to_front(values):
        return pltpu.roll(values, bc_turn, 1)

    own_taps = to_front(taps[:, window])
    for copy in loads[4:8]:
        copy.wait()
    bc_sums[...] = jnp.zeros_like(bc_sums)

    def small_block(number, carry):
        slot, block = lax.div(number, per_slot), per_slot - 1 - lax.rem(number, per_slot)
        at = pl.ds(pl.multiple_of((slot * per_slot + block) * rows, rows), rows)

        @pl.when(block == per_slot - 1)
        def _():
            d_ext[rows:, :] = jnp.zeros((8, 128), F32)

        total = sum(bc_landed[k, :, at].astype(F32) for k in range(width))
        total = jnp.concatenate([total, jnp.zeros((128 - own, rows), F32)], axis=0)
        pre = to_front(pre_own[at, :])
        sig = sigmoid(pre)
        d_pre = jnp.where(mine, total.T * (sig * (1.0 + pre * (1.0 - sig))), 0.0)
        d_ext[0:rows, :] = d_pre
        where = (pl.ds(2 * block, 2), pl.ds(pl.multiple_of(slot * piece, piece), piece))
        conv_in = to_front(conv_own[at, :])
        d_conv = jnp.zeros((rows, 128), F32)
        for k in range(kernel):
            moved = d_ext[kernel - 1 - k : kernel - 1 - k + rows, :]
            d_conv = d_conv + own_taps[k : k + 1, :] * moved
            bc_sums[k : k + 1, :] += jnp.sum(moved * conv_in, axis=0, keepdims=True)
        bc_sums[4:5, :] += jnp.sum(d_pre, axis=0, keepdims=True)
        d_ext[rows:, :] = d_ext[0:8, :]
        d_dt = pltpu.roll(
            d_arg[where[0], where[1], :].astype(F32).reshape(rows, 128), own, 1
        )
        both = jnp.where(mine, d_conv, jnp.where(lane < own + heads, d_dt, 0.0))
        d_small[where[0], where[1], :] = both.astype(BF16).reshape(2, piece, 128)
        return carry

    lax.fori_loop(0, blocks, small_block, 0)
    g_small[...] = t_mm(
        d_small[...].reshape(everything, 128), normed_all[...].reshape(everything, model)
    )
    small_line.phase(0)
    for copy in loads[2:4]:
        copy.wait()

    def turn_weights(number, carry):
        at = pl.ds(pl.multiple_of(number * 128, 128), 128)
        bc = to_front(wb[lax.div(place, per_block), at, :].astype(F32))
        w_turned[2 * inner :, at] = jnp.where(mine, bc, 0.0).T.astype(BF16)
        return carry

    lax.fori_loop(0, model // 128, turn_weights, 0)
    w_turned[2 * inner + own : 2 * inner + own + 16, :] = w_dt[0:16, :]

    def token_grads(index):
        both = jnp.concatenate([d_gate[index], d_x[index], d_small[index]], axis=1)
        d_parts[index] = mm(both, w_turned[...]).astype(BF16)

    def for_pair(mask):
        token_grads(peer[mask ^ 1][1])
        d_plane.pair[mask].start()

    for_pair(6)
    token_grads(peer[6][1])
    for_pair(2)
    d_plane.far()
    token_grads(peer[2][1])
    for_pair(4)
    d_plane.near(2)
    if depth > 2:
        x_line.phase(1)
    token_grads(peer[4][1])
    for_pair(0)
    d_plane.near(4)
    token_grads(place)
    d_plane.near(0)

    sums_own[:, :inner] = channel_sums[...]
    sums_own[:, inner : inner + 128] = bc_sums[...]
    sums_own[:, inner + 128 :] = head_sums[...]
    sums_own[2:3, inner + 128 :] = dot(
        channel_sums[...],
        head_of_channel(inner, head_size),
        ((1,), (0,)),
        lax.Precision.HIGHEST,
    )[5:6]
    sums_copies = [
        links.copy(sums_own, sums_line.at[k], device) for k, device in enumerate(line_peers)
    ]
    for copy in sums_copies:
        copy.start()
    if depth > 3:
        x_line.phase(2)
    d_plane.second()
    if depth > 2:
        small_line.phase(1)
    for copy in sums_copies:
        copy.wait()
    total = jnp.zeros(sums_own.shape, F32)
    for q in range(depth):
        term = jnp.zeros(sums_own.shape, F32)
        for up in range(1, depth):
            term = jnp.where(lax.rem(row + depth - up, depth) == q, sums_line[up - 1], term)
        total = total + jnp.where(row == q, sums_own[...], term)
    sums_all[place] = total
    mine_all = sums_all.at[place]
    spread_sums = [links.copy(mine_all, mine_all, peer[mask]) for mask in order]
    for copy in spread_sums:
        copy.start()

    x_line.finish(x_sum)
    turn(x_sent, x_sum)
    send_x.begin()
    if depth > 3:
        small_line.phase(2)

    for source, at, to in runs_of(width, half, run):
        in_grad[:, to : to + run] = gate_back[source, :, at : at + run].astype(F32)
    small_line.finish(small_sum)
    turn(small_sent, small_sum)
    send_small.begin()
    for copy in spread_sums:
        copy.wait()
    for source, at, to in runs_of(width, half, run):
        full[:, to : to + run] = sums_all[source, :, at : at + run]
    for source in range(width):
        to = inner_all + source * own
        full[:, to : to + own] = sums_all[source, :, inner : inner + own]
    first = (row * width + place) * own_ch
    base = pl.multiple_of(lax.div(first, 128) * 128, 128)
    view = pltpu.roll(full[:, pl.ds(base, 256)], 256 - lax.rem(first, 128), 1)
    smalls[0:8, :] = view[:, :128]
    smalls[8:16, :] = sum(
        dot(
            sums_all[source, :, inner + 128 :],
            head_places(source, half, plane, group, heads, 0),
            ((1,), (0,)),
            lax.Precision.HIGHEST,
        )
        for source in range(width)
    )
    send_x.end()
    for source, at, to in runs_of(width, half, run):
        in_grad[:, inner_all + to : inner_all + to + run] = x_back[
            source, :, at : at + run
        ].astype(F32)
    send_small.end()
    for source in range(width):
        to = 2 * inner_all + source * own
        in_grad[:, to : to + own] = small_back[source, :, :own].astype(F32)
    for source, at, to in runs_of(width, half, group):
        to = 2 * inner_all + 2 * size + to
        in_grad[:, to : to + group] = small_back[
            source, :, own + at : own + at + group
        ].astype(F32)

    norm_gain = rows_in[0:1, :]

    def store_grad(at, total):
        held = x_own[at].astype(F32)
        inv = lax.rsqrt(jnp.mean(held * held, axis=1, keepdims=True) + EPS)
        hat = held * inv
        d_h = total * norm_gain
        grad = inv * (d_h - hat * jnp.mean(d_h * hat, axis=1, keepdims=True))
        input_grad[at] = (grad + cot_own[at].astype(F32)).astype(BF16)

    loads[8].wait()
    d_plane.finish(store_grad)
    d_plane.drain()
    x_line.drain()
    small_line.drain()


def weights(dims, hbm, vmem, collective):
    depth, width, heads, head_size, size, kernel, own_ch, inner_all = dims
    inner = heads * head_size
    _, rows, model = hbm[1].shape
    tokens = rows * width
    shape = jax.ShapeDtypeStruct
    cols = model // depth
    owned = cols // width
    own = 2 * size // width
    kept = [
        ((rows, model), BF16),
        ((owned, 2 * inner_all + 2 * size + heads * width), F32),
        ((16, 128), F32),
    ]
    return pl.pallas_call(
        functools.partial(weights_kernel, dims),
        out_shape=tuple(shape(*s) for s in kept),
        in_specs=[ANY] * len(hbm) + [INVMEM] * len(vmem),
        out_specs=(INVMEM,) * len(kept),
        scratch_shapes=[pltpu.VMEM(v.shape, v.dtype) for v in (hbm[0], hbm[1], hbm[3])]
        + [
            pltpu.VMEM((tokens, 128), F32),
            pltpu.VMEM((tokens, 128), F32),
            pltpu.VMEM(hbm[6].shape, BF16),
            pltpu.VMEM(hbm[7].shape, BF16),
            pltpu.VMEM((rows, model), BF16),
            pltpu.VMEM((2 * inner + 128, model), BF16),
            pltpu.VMEM((width, rows, 128), BF16),
            pltpu.VMEM((inner, model), F32),
            pltpu.VMEM((128, model), F32),
            pltpu.VMEM((width, rows, model), BF16),
            pltpu.VMEM((rows + 8, 128), F32),
            pltpu.VMEM((8, 128), F32),
        ]
        + plane_buffers(rows, model)
        + line_buffers(depth - 1, (inner, cols))
        + line_buffers(depth - 1, (128, cols))
        + [
            pltpu.VMEM((inner, cols), F32),
            pltpu.VMEM((cols, inner), BF16),
            pltpu.VMEM((128, cols), F32),
            pltpu.VMEM((cols, 128), BF16),
            pltpu.VMEM((width, owned, inner), BF16),
            pltpu.VMEM((width, owned, 128), BF16),
            pltpu.VMEM((8, inner + 256), F32),
            pltpu.VMEM((depth - 1, 8, inner + 256), F32),
            pltpu.VMEM((width, 8, inner + 256), F32),
            pltpu.VMEM((8, inner_all + 2 * size + 256), F32),
            pltpu.SemaphoreType.DMA((88,)),
            pltpu.SemaphoreType.DMA((88,)),
            pltpu.SemaphoreType.DMA((14,)),
        ],
        compiler_params=pltpu.CompilerParams(
            collective_id=collective, has_side_effects=True, vmem_limit_bytes=VMEM_LIMIT
        ),
        name="weights_fused",
    )(*hbm, *vmem)


def fast_body(
    depth,
    width,
    block_input,
    cotangent,
    lengths,
    in_weight,
    out_weight,
    norm_gain,
    gate_gain,
    conv_weight,
    conv_bias,
    dt_bias,
    a_log,
    d_skip,
):
    slots, piece, model = block_input.shape
    heads_all = dt_bias.shape[0]
    out_rows = out_weight.shape[0]
    in_rows = in_weight.shape[0]
    inner_all = out_rows * depth * width
    head_size = inner_all // heads_all
    taps_count = conv_weight.shape[0]
    channels = conv_weight.shape[1] * depth * width
    size = (channels - inner_all) // 2
    heads = heads_all // width
    inner = heads * head_size
    plane = width // 2
    half = depth // 2
    pair_rows = 2 * out_rows
    row, place = lax.axis_index("dp"), lax.axis_index("seq")
    core, chip = lax.rem(place, 2), lax.div(place, 2)
    slot_len = piece * width
    tokens = slots * slot_len

    own_ch = conv_bias.shape[0]
    tokens_dev = slots * piece
    dims = (depth, width, heads, head_size, size, taps_count, own_ch, inner_all)
    (
        normed_all,
        cot_all,
        w_turned,
        w_bc,
        w_out,
        conv_in,
        pre,
        dt_arg,
        gate,
        y,
        states,
        norms,
        taps,
        param_rows,
        w_dt,
    ) = forward(
        dims,
        (
            block_input.reshape(tokens_dev, model),
            cotangent.reshape(tokens_dev, model),
            lengths[None],
            in_weight,
            out_weight,
            norm_gain[None],
            gate_gain[None],
            conv_weight,
            conv_bias[None],
            dt_bias[None],
            a_log[None],
            d_skip[None],
        ),
        2,
    )
    x_own = block_input.reshape(tokens_dev, model)
    (
        d_gate,
        d_x,
        d_arg,
        output,
        gate_back,
        out_grad,
        channel_sums,
        head_sums,
        d_bc,
    ) = reverse(
        dims,
        (cot_all, normed_all, gate, y, pre, conv_in, dt_arg, states, w_out),
        (norms, taps, param_rows, x_own),
        3,
    )
    input_grad, in_grad, smalls = weights(
        dims,
        (
            d_x,
            normed_all,
            w_turned,
            d_gate,
            pre,
            conv_in,
            d_arg,
            w_bc.reshape(2, model, size),
            cot_all,
        ),
        (
            d_bc,
            taps,
            channel_sums,
            head_sums,
            param_rows,
            x_own,
            w_dt,
            gate_back,
        ),
        4,
    )
    norm_grad = jnp.sum(in_grad * in_weight.astype(F32), axis=1) / norm_gain.astype(F32)
    gate_grad = jnp.sum(out_grad * out_weight.astype(F32), axis=1) / gate_gain.astype(F32)
    return (
        output.reshape(slots, piece, model),
        input_grad.reshape(slots, piece, model),
        in_grad,
        out_grad,
        norm_grad,
        gate_grad,
        smalls[:4, :own_ch],
        smalls[4, :own_ch],
        smalls[8, :heads_all],
        smalls[9, :heads_all],
        smalls[10, :heads_all],
    )


def heads_fit(depth, width, arrays):
    block_input, out_weight, dt_bias = arrays[0], arrays[4], arrays[9]
    pair_rows = 2 * out_weight.shape[0]
    head_size = out_weight.shape[0] * depth * width // dt_bias.shape[0]
    return (
        width == 8
        and depth % 2 == 0
        and pair_rows % head_size == 0
        and (depth // 2 * pair_rows) % 128 == 0
        and block_input.shape[1] % CHUNK == 0
        and 2 * head_size == CHUNK
    )


def solution(mesh):
    placed = (
        P("dp", "seq", None),
        P("dp", "seq", None),
        P("dp"),
        P(("dp", "seq"), None),
        P(("dp", "seq"), None),
        P(("dp", "seq")),
        P(("dp", "seq")),
        P(None, ("dp", "seq")),
        P(("dp", "seq")),
        P(),
        P(),
        P(),
    )
    depth, width = mesh.shape["dp"], mesh.shape["seq"]

    def either(*arrays):
        if heads_fit(depth, width, arrays):
            return fast_body(depth, width, *arrays)
        return body(*arrays)

    return jax.shard_map(
        either,
        mesh=mesh,
        in_specs=placed,
        out_specs=(
            P("dp", "seq", None),
            P("dp", "seq", None),
            P(("dp", "seq"), None),
            P(("dp", "seq"), None),
            P(("dp", "seq")),
            P(("dp", "seq")),
            P(None, ("dp", "seq")),
            P(("dp", "seq")),
            P(),
            P(),
            P(),
        ),
        check_vma=False,
    )
```
